32 devices in a mesh: feat: 2 (over core), dom: 16 (over z, y, x).
Axes of the slice: x: 2, y: 2, z: 4, core: 2. Of those that a mesh axis runs over, the one named last changes fastest.
Arguments:
- features: bfloat16 [16384, 1024], P('dom', 'feat'), may hold values from -6 to 6
- tile_weight: bfloat16 [2048, 128, 128], P('dom'), may hold values from 0 to 0.029907227
- tile_dst: int32 [2048], P('dom'), may hold values from 0 to 15
- tile_src: int32 [2048], P('dom'), may hold values from 0 to 7
- tile_rows: int32 [2048], P('dom'), may hold values from 1 to 128
- w_self1: bfloat16 [1024, 256], P('feat'), may hold values from -0.1875 to 0.1875
- neighbour_weight_first: bfloat16 [1024, 256], P('feat'), may hold values from -0.1875 to 0.1875
- send_list: int32 [16, 16, 8], replicated, may hold values from 0 to 127
- send_count: int32 [16, 16], replicated, may hold values from 1 to 8
- adj_two: bfloat16 [1024, 256], P('dom'), may hold values from 0 to 0.0049743652
- w_self2: bfloat16 [256, 172], replicated, may hold values from -0.375 to 0.375
- w_neigh2: bfloat16 [256, 172], replicated, may hold values from -0.375 to 0.375
Outputs:
- logits: float32 [1024, 172], P('dom')
The draws below stay inside these ranges and needn't reach their ends.
Inputs may be any that keep to these rules, and one draw needn't show every extreme that they name: `send_list`: every send list slot names a local hidden row of the sender.
All inputs are finite; a program needn't handle non-finite values.
Results may differ from the reference program's by a relative error of at most 0.0012.
The reference program's roundings to bfloat16 on the way count: a program that leaves them out, or rounds other values in their place, can miss the bound.
Values may be sent and summed in bfloat16 or wider, within the bound.
No kernel may reach another device: no remote copies, remote signals or barrier semaphores. Data moves between devices by JAX's collectives and lax.ppermute only.
A program may use at most 128 MiB of HBM per device.

```python
import math
import jax
import jax.numpy as jnp
import numpy as np
from jax import lax

F = 1024
H = 256
C = 172
TILE = 128
HID_DEV = 128
ROWS_DEV = 1024
TILES = 128
OUT_DEV = 64
SEND_MAX = 8
N_NODES = 16384
N_TILES = 2048
BATCH = 1024
POOL = 256
N_DOM = 16


def plant(drawn, stream_key, least, high):
    longest = drawn.shape.index(max(drawn.shape))
    spots = []
    for shift in (0, 1):
        where = [jax.random.randint(jax.random.fold_in(stream_key, axis), (), 0, length) for axis, length in enumerate(drawn.shape)]
        where[longest] = (where[longest] + shift) % drawn.shape[longest]
        spots.append(tuple(where))
    return drawn.at[spots[0]].set(least).at[spots[1]].set(high)


def block_scale(rng, extent, shards, low, top_value):
    loudness = 1.0
    for axis_at, blocks in shards:
        steps = jax.random.uniform(jax.random.fold_in(jax.random.fold_in(rng, 6), axis_at), (blocks,), jnp.float32, low / len(shards), top_value / len(shards))
        loudness = loudness * jnp.repeat(jnp.exp(steps), extent[axis_at] // blocks).reshape((-1,) + (1,) * (len(extent) - 1 - axis_at))
    return loudness


def rank_bounds(number_of, skew):
    portions = [(1 << 20) // math.isqrt(grade ** skew) + 1 for grade in range(1, number_of + 1)]
    scale = 1 + sum(portions) // (1 << 30)
    return np.cumsum(np.array([max(1, weight // scale) for weight in portions]))


def ranked_ids(own_key, dims, number_of, slope):
    table = rank_bounds(number_of, slope)
    pick = jax.random.randint(jax.random.fold_in(own_key, 1), dims, 0, int(table[number_of - 1]))
    standing = jnp.searchsorted(jnp.asarray(table, jnp.int32), pick, side="right")
    return jax.random.permutation(jax.random.fold_in(own_key, 2), number_of)[standing].astype(jnp.int32)


def normal_values(rng, extent, width, most, split=(), kind=jnp.bfloat16):
    values = jax.random.normal(rng, extent, jnp.float32) * width
    if len(split) > 0:
        values = block_scale(rng, extent, split, -0.22, 0.18) * values
    return jnp.clip(values, min=-most, max=most).astype(kind)


def setup_inputs(seed: int = 0) -> dict:
    arg_keys = jax.random.split(jax.random.key(seed), 13)
    return {
        "features": normal_values(arg_keys[0], (N_NODES, F), 1.0, 6.0, ((0, 16), (1, 2))),
        "tile_weight": jnp.clip(0.029907227 * jax.random.uniform(arg_keys[1], (N_TILES, TILE, TILE), jnp.float32) ** block_scale(arg_keys[1], (N_TILES, TILE, TILE), ((0, 16),), -0.2, 0.2), 0.0, 0.029907227).astype(jnp.bfloat16),
        "tile_dst": plant(ranked_ids(arg_keys[2], (N_TILES,), N_DOM, 2), jax.random.fold_in(arg_keys[2], 3), 0, N_DOM - 1).astype(jnp.int32),
        "tile_src": plant(jax.random.randint(arg_keys[3], (N_TILES,), 0, ROWS_DEV // TILE), jax.random.fold_in(arg_keys[3], 1), 0, (ROWS_DEV // TILE) - 1).astype(jnp.int32),
        "tile_rows": plant(jax.random.randint(arg_keys[4], (N_TILES,), 1, TILE + 1), jax.random.fold_in(arg_keys[4], 1), 1, TILE).astype(jnp.int32),
        "w_self1": normal_values(arg_keys[5], (F, H), F ** -0.5, 0.1875, ((0, 2),)),
        "neighbour_weight_first": normal_values(arg_keys[6], (F, H), F ** -0.5, 0.1875, ((0, 2),)),
        "send_list": plant(jax.random.randint(arg_keys[7], (N_DOM, N_DOM, SEND_MAX), 0, HID_DEV), jax.random.fold_in(arg_keys[7], 1), 0, HID_DEV - 1).astype(jnp.int32),
        "send_count": plant(jax.random.randint(arg_keys[8], (N_DOM, N_DOM), 1, SEND_MAX + 1), jax.random.fold_in(arg_keys[8], 1), 1, SEND_MAX).astype(jnp.int32),
        "adj_two": jnp.clip(0.0049743652 * jax.random.uniform(arg_keys[9], (BATCH, POOL), jnp.float32) ** block_scale(arg_keys[9], (BATCH, POOL), ((0, 16),), -0.2, 0.2), 0.0, 0.0049743652).astype(jnp.bfloat16),
        "w_self2": normal_values(arg_keys[10], (H, C), H ** -0.5, 0.375),
        "w_neigh2": normal_values(arg_keys[11], (H, C), H ** -0.5, 0.375),
    }


def reference(features, tile_weight, tile_dst, tile_src, tile_rows, w_self1, neighbour_weight_first, send_list, send_count, adj_two, w_self2, w_neigh2):
    blocks_all = features.reshape(N_DOM, ROWS_DEV // TILE, TILE, F)
    weight_pieces = tile_weight.reshape(N_DOM, TILES, TILE, TILE)
    dst_parts = tile_dst.reshape(N_DOM, TILES)
    src_parts = tile_src.reshape(N_DOM, TILES)
    rows_parts = tile_rows.reshape(N_DOM, TILES)
    row_indices = jnp.arange(TILE, dtype=jnp.int32)
    block_ids = jnp.arange(N_DOM, dtype=jnp.int32)

    def partition(total, index):
        blocks = blocks_all[index]
        valid = row_indices[None, :, None] < rows_parts[index][:, None, None]
        masked_features = jnp.where(valid, weight_pieces[index], jnp.zeros_like(weight_pieces[index]))
        source_nodes = blocks[src_parts[index]]
        collected_rows = jnp.einsum('zvx,zxm->zvm', masked_features.astype(jnp.float32), source_nodes.astype(jnp.float32)).astype(jnp.bfloat16)
        neighbour_rows = jnp.einsum('kys,sj->kyj', collected_rows.astype(jnp.float32), neighbour_weight_first.astype(jnp.float32))
        onehot = (dst_parts[index][:, None] == block_ids[None, :]).astype(jnp.float32)
        term = jnp.einsum('tb,trh->brh', onehot, neighbour_rows, precision=lax.Precision.HIGHEST)
        return total + term, 0

    start = jnp.zeros((N_DOM, TILE, H), jnp.float32)
    neigh_sum, unused = lax.scan(partition, start, jnp.arange(N_DOM, dtype=jnp.int32))
    own = blocks_all[:, 0].reshape(N_DOM * TILE, F)
    pre = jnp.dot(own, w_self1, preferred_element_type=jnp.float32) + neigh_sum.reshape(N_DOM * TILE, H)
    hidden = jnp.maximum(pre, 0.0).astype(jnp.bfloat16)
    hidden_parts = hidden.reshape(N_DOM, HID_DEV, H)
    slots = jnp.arange(SEND_MAX, dtype=jnp.int32)

    def second(receiver):
        lists = send_list[:, receiver, :]
        counts = send_count[:, receiver]
        flat = (block_ids[:, None] * HID_DEV + lists).reshape(N_DOM * SEND_MAX)
        rows = hidden[flat].reshape(N_DOM, SEND_MAX, H)
        rows = jnp.where((slots[None, :] < counts[:, None])[:, :, None], rows, jnp.zeros_like(rows))
        pool = jnp.concatenate([hidden_parts[receiver], rows.reshape(N_DOM * SEND_MAX, H)], axis=0)
        adjacency = lax.dynamic_slice_in_dim(adj_two, receiver * OUT_DEV, OUT_DEV, 0)
        neighbour_mean = jnp.dot(adjacency, pool, preferred_element_type=jnp.float32).astype(jnp.bfloat16)
        selfrows = hidden_parts[receiver][:OUT_DEV]
        return jnp.dot(selfrows, w_self2, preferred_element_type=jnp.float32) + jnp.dot(neighbour_mean, w_neigh2, preferred_element_type=jnp.float32)

    logits = lax.map(second, jnp.arange(N_DOM, dtype=jnp.int32))
    return logits.reshape(N_DOM * OUT_DEV, C)
```

```python
import functools

import jax
import jax.numpy as jnp
from jax import lax
from jax.experimental import pallas as pl
from jax.experimental.pallas import tpu as pltpu
from jax.sharding import PartitionSpec as P

UNIT = 16
CHUNKS = 1


def group_of(core, place, groups):
    pair = 2 * (place // 2) + core
    return pair if place % 2 == 0 else groups - 1 - pair


def plan(src_row, rows_row, tops, tiles, n_blocks):
    units = len(tops) * tiles
    keys = []
    lane = lax.broadcasted_iota(jnp.int32, (1, tiles), 1)
    for j, top in enumerate(tops):
        keys.append(jnp.where(rows_row > top, src_row, n_blocks) * units + j * tiles + lane)
    key_row = jnp.concatenate(keys, axis=1)
    sub_i = lax.broadcasted_iota(jnp.int32, (units, units), 0)
    lane_i = lax.broadcasted_iota(jnp.int32, (units, units), 1)
    key_mat = jnp.broadcast_to(key_row, (units, units))
    key_col = jnp.sum(jnp.where(sub_i == lane_i, key_mat, 0).astype(jnp.float32), axis=1, keepdims=True).astype(jnp.int32)
    key_col_mat = jnp.broadcast_to(key_col, (units, units))
    rank_col = jnp.sum(jnp.where(key_mat < key_col_mat, 1.0, 0.0), axis=1, keepdims=True).astype(jnp.int32)
    inv = jnp.sum(jnp.where(rank_col == lane_i, sub_i, 0).astype(jnp.float32), axis=0, keepdims=True).astype(jnp.int32)
    starts = jnp.sum(jnp.where(key_col_mat < lane_i * units, 1.0, 0.0), axis=0, keepdims=True).astype(jnp.int32)
    return inv, starts


def tiles_kernel(
    chunk, per, n, radix,
    ids, src_s, dst_s, rows_s, src_v, rows_v, tw, xo, xp, wo, wp, so, sp,
    *rest,
):
    outs, rest = rest[:radix], rest[radix:]
    tbuf, xbuf, wbuf, sbuf, packed, gath, res, acc, plan_v, plan_s, sems = rest
    tiles, groups = tw.shape[0], tw.shape[1]
    tile = tw.shape[3]
    width = xo.shape[1]
    n_blocks = xo.shape[0] // tile
    hidden = wo.shape[1]
    units = per * tiles
    core, me = ids[0], ids[1]
    gs = [group_of(core, chunk * per + j, groups) for j in range(per)]
    copies = [pltpu.make_async_copy(tw.at[:, gs[j]], tbuf.at[j], sems.at[j]) for j in range(per)]
    extra = [
        pltpu.make_async_copy(a, b, sems.at[per + i])
        for i, (a, b) in enumerate([
            (xo, xbuf.at[0]), (xp, xbuf.at[1]), (wo, wbuf.at[0]), (wp, wbuf.at[1]), (so, sbuf.at[0]), (sp, sbuf.at[1]),
        ])
    ]
    for c in copies + extra:
        c.start()

    inv, starts = plan(src_v[...], rows_v[...], [UNIT * g for g in gs], tiles, n_blocks)
    plan_v[0:1, :] = inv
    plan_v[1:2, :] = starts
    to_scalar = pltpu.make_async_copy(plan_v, plan_s, sems.at[per + 6])
    to_scalar.start()
    acc[...] = jnp.zeros_like(acc)
    to_scalar.wait()
    n_valid = plan_s[1, n_blocks]
    for c in copies:
        c.wait()

    row_i = lax.broadcasted_iota(jnp.int32, (UNIT, tile), 0)

    def pack(b, carry):
        for i in range(8):
            p = b * 8 + i
            u = plan_s[0, p]
            t = lax.rem(u, tiles)
            j = lax.div(u, tiles)
            g = gs[0]
            for q in range(1, per):
                g = jnp.where(j == q, gs[q], g)
            value = tbuf[j, t].astype(jnp.float32)
            value = jnp.where(row_i < rows_s[t] - UNIT * g, value, 0.0).astype(jnp.bfloat16)
            packed[pl.ds(pl.multiple_of(p * UNIT, UNIT), UNIT), :] = value
        return carry

    lax.fori_loop(0, lax.div(n_valid + 7, 8), pack, 0)
    for c in extra:
        c.wait()

    def first(s, carry):
        lo, hi = plan_s[1, s], plan_s[1, s + 1]
        base = pl.multiple_of(s * tile, tile)

        def block(b, inner):
            at = pl.multiple_of((lo + 8 * b) * UNIT, UNIT)
            lhs = packed[pl.ds(at, 8 * UNIT), :]
            for h in range(2):
                got = jnp.dot(lhs, xbuf[h, pl.ds(base, tile), :], preferred_element_type=jnp.float32)
                gath[pl.ds(at, 8 * UNIT), h * width:(h + 1) * width] = got.astype(jnp.bfloat16)
            return inner

        return lax.fori_loop(0, lax.div(hi - lo + 7, 8), block, carry)

    lax.fori_loop(0, n_blocks, first, 0)

    for j in range(per):
        at = pl.multiple_of(gs[j] * UNIT, UNIT)
        own = jnp.dot(xbuf[0, pl.ds(at, UNIT), :], sbuf[0], preferred_element_type=jnp.float32)
        own = own + jnp.dot(xbuf[1, pl.ds(at, UNIT), :], sbuf[1], preferred_element_type=jnp.float32)
        acc[0, j * UNIT:(j + 1) * UNIT, :] = own

    def second(b, carry):
        at = pl.multiple_of(b * 16 * UNIT, 16 * UNIT)
        got = jnp.dot(gath[pl.ds(at, 16 * UNIT), :width], wbuf[0], preferred_element_type=jnp.float32)
        got = got + jnp.dot(gath[pl.ds(at, 16 * UNIT), width:], wbuf[1], preferred_element_type=jnp.float32)
        res[...] = got
        for i in range(16):
            p = b * 16 + i
            u = plan_s[0, p]
            t = lax.rem(u, tiles)
            j = lax.div(u, tiles)
            slot = jnp.bitwise_xor(dst_s[t], me)
            slot = lax.rem(slot, radix) * (n // radix) + lax.div(slot, radix)
            slot = jnp.where(p < n_valid, slot, n)
            where = pl.ds(pl.multiple_of(j * UNIT, UNIT), UNIT)
            acc[slot, where, :] += res[i * UNIT:(i + 1) * UNIT, :]
        return carry

    lax.fori_loop(0, lax.div(n_valid + 15, 16), second, 0)
    span = n // radix
    back = [pltpu.make_async_copy(acc.at[pl.ds(k * span, span)], outs[k], sems.at[per + 7 + k]) for k in range(radix)]
    for c in back:
        c.start()
    for c in back:
        c.wait()


def neighbour_terms(chunk, per, n, radix, ids, src, dst, rows, tw, xo, xp, wo, wp, so, sp):
    tiles, groups, _, tile = tw.shape
    units = per * tiles
    hidden = wo.shape[1]
    width = xo.shape[1]
    smem = pl.BlockSpec(memory_space=pltpu.SMEM)
    vmem = pl.BlockSpec(memory_space=pltpu.VMEM)
    anym = pl.BlockSpec(memory_space=pl.ANY)
    flops = 2 * units * UNIT * (tile * 2 * width + 2 * width * hidden)
    return pl.pallas_call(
        functools.partial(tiles_kernel, chunk, per, n, radix),
        out_shape=[jax.ShapeDtypeStruct((n // radix, per * UNIT, hidden), jnp.float32)] * radix,
        in_specs=[smem] * 4 + [vmem] * 2 + [anym] * 7,
        out_specs=[anym] * radix,
        scratch_shapes=[
            pltpu.VMEM((per, tiles, UNIT, tile), tw.dtype),
            pltpu.VMEM((2,) + xo.shape, xo.dtype),
            pltpu.VMEM((2,) + wo.shape, wo.dtype),
            pltpu.VMEM((2,) + so.shape, so.dtype),
            pltpu.VMEM(((units + 8) * UNIT, tile), jnp.bfloat16),
            pltpu.VMEM(((units + 16) * UNIT, 2 * width), jnp.bfloat16),
            pltpu.VMEM((16 * UNIT, hidden), jnp.float32),
            pltpu.VMEM((n + 1, per * UNIT, hidden), jnp.float32),
            pltpu.VMEM((2, units), jnp.int32),
            pltpu.SMEM((2, units), jnp.int32),
            pltpu.SemaphoreType.DMA((per + 7 + radix,)),
        ],
        compiler_params=pltpu.CompilerParams(vmem_limit_bytes=56 * 1024 * 1024),
        cost_estimate=pl.CostEstimate(flops=flops, bytes_accessed=8 << 20, transcendentals=0),
        name="neighbour_terms",
    )(ids, src, dst, rows, src.reshape(1, tiles), rows.reshape(1, tiles), tw, xo, xp, wo, wp, so, sp)


def select_kernel(tile, places, ids, lists, counts, out):
    core, me = ids[0], ids[1]
    slots, n = lists.shape[1], lists.shape[2]
    total = n * slots
    q_n = lax.broadcasted_iota(jnp.int32, (total, n), 0)
    r_n = lax.broadcasted_iota(jnp.int32, (total, n), 1)
    mine = lists[me].astype(jnp.float32)
    cnt = counts[pl.ds(me, 1), :]
    picked = jnp.zeros((total, n), jnp.float32)
    slot = jnp.bitwise_and(q_n, slots - 1)
    for k in range(slots):
        picked = jnp.where(slot == k, mine[k:k + 1, :], picked)
    good = jnp.logical_and(q_n // slots == r_n, slot < cnt)
    row = jnp.sum(jnp.where(good, picked + 1.0, 0.0), axis=1, keepdims=True) - 1.0
    held = len(places) * UNIT
    lane = lax.broadcasted_iota(jnp.int32, (1, held), 1)
    name = jnp.zeros((1, held), jnp.int32)
    for i, place in enumerate(places):
        g = group_of(core, place, tile // UNIT)
        name = jnp.where(lane // UNIT == i, g * UNIT + lane % UNIT, name)
    out[...] = jnp.where(row == name.astype(jnp.float32), 1.0, 0.0).astype(jnp.bfloat16)


def selection(ids, send_list, send_count, tile, places):
    n, _, slots = send_list.shape
    smem = pl.BlockSpec(memory_space=pltpu.SMEM)
    vmem = pl.BlockSpec(memory_space=pltpu.VMEM)
    return pl.pallas_call(
        functools.partial(select_kernel, tile, places),
        out_shape=jax.ShapeDtypeStruct((n * slots, len(places) * UNIT), jnp.bfloat16),
        in_specs=[smem, vmem, vmem],
        out_specs=vmem,
        compiler_params=pltpu.CompilerParams(vmem_limit_bytes=32 * 1024 * 1024),
        name="selection",
    )(ids, jnp.swapaxes(send_list, 1, 2), send_count)


def hidden_kernel(chunks, parts, *refs):
    sel, (own, send) = refs[chunks * parts], refs[chunks * parts + 1:]
    rows = refs[0].shape[1]
    for c in range(chunks):
        total = refs[c * parts][0]
        for k in range(1, parts):
            total = total + refs[c * parts + k][0]
        own[c * rows:(c + 1) * rows, :] = jnp.maximum(total, 0.0).astype(jnp.bfloat16)
    picked = jnp.dot(sel[...], own[...], preferred_element_type=jnp.float32).astype(jnp.bfloat16)
    half = picked.shape[0]
    send[:half, :] = picked
    send[half:, :] = picked


def hidden_rows(chunk_parts, sel):
    chunks, parts = len(chunk_parts), len(chunk_parts[0])
    held = sel.shape[1]
    width = chunk_parts[0][0].shape[2]
    vmem = pl.BlockSpec(memory_space=pltpu.VMEM)
    flat = [a for part in chunk_parts for a in part]
    return pl.pallas_call(
        functools.partial(hidden_kernel, chunks, parts),
        out_shape=[
            jax.ShapeDtypeStruct((held, width), jnp.bfloat16),
            jax.ShapeDtypeStruct((2 * sel.shape[0], width), jnp.bfloat16),
        ],
        in_specs=[vmem] * (len(flat) + 1),
        out_specs=[vmem] * 2,
        compiler_params=pltpu.CompilerParams(vmem_limit_bytes=32 * 1024 * 1024),
        name="hidden_rows",
    )(*flat, sel)


def logits_kernel(tile, places, ids, own, other, received, adj, w_self, w_neigh, out, pool):
    core = ids[0]
    groups = tile // UNIT
    for i, place in enumerate(places):
        mine = group_of(core, place, groups)
        theirs = group_of(1 - core, place, groups)
        pool[pl.ds(pl.multiple_of(mine * UNIT, UNIT), UNIT), :] = own[i * UNIT:(i + 1) * UNIT, :]
        pool[pl.ds(pl.multiple_of(theirs * UNIT, UNIT), UNIT), :] = other[i * UNIT:(i + 1) * UNIT, :]
    half = received.shape[0] // 2
    both = received[:half, :].astype(jnp.float32) + received[half:, :].astype(jnp.float32)
    pool[tile:, :] = both.astype(jnp.bfloat16)
    mean = jnp.dot(adj[...], pool[...], preferred_element_type=jnp.float32).astype(jnp.bfloat16)
    dims = (((1,), (1,)), ((), ()))
    rows = adj.shape[0]
    got = lax.dot_general(pool[:rows, :], w_self[...], dims, preferred_element_type=jnp.float32)
    out[...] = got + lax.dot_general(mean, w_neigh[...], dims, preferred_element_type=jnp.float32)


def logits_of(ids, own, other, received, adj, w_self, w_neigh, tile, places):
    smem = pl.BlockSpec(memory_space=pltpu.SMEM)
    vmem = pl.BlockSpec(memory_space=pltpu.VMEM)
    return pl.pallas_call(
        functools.partial(logits_kernel, tile, places),
        out_shape=jax.ShapeDtypeStruct((adj.shape[0], w_self.shape[1]), jnp.float32),
        in_specs=[smem] + [vmem] * 6,
        out_specs=vmem,
        scratch_shapes=[pltpu.VMEM((adj.shape[1], own.shape[1]), jnp.bfloat16)],
        compiler_params=pltpu.CompilerParams(vmem_limit_bytes=32 * 1024 * 1024),
        name="logits",
    )(ids, own, other, received, adj, w_self.T, w_neigh.T)


def exchange(parts, stride, n):
    got = [parts[0]]
    for k in range(1, len(parts)):
        got.append(lax.ppermute(parts[k], "dom", [(i, i ^ (k * stride)) for i in range(n)]))
    return got


def body(
    features,
    tile_weight,
    tile_dst,
    tile_src,
    tile_rows,
    w_self1,
    neighbour_weight_first,
    send_list,
    send_count,
    adj_two,
    w_self2,
    w_neigh2,
):
    n = lax.axis_size("dom")
    tile = tile_weight.shape[1]
    groups = tile // UNIT
    per = groups // 2 // CHUNKS
    places = list(range(groups // 2))
    bits = n.bit_length() - 1
    assert n == 1 << bits and bits >= 2
    radices = [2] * (bits // 2) + [1] * (bits % 2)
    ids = jnp.stack([lax.axis_index("feat"), lax.axis_index("dom")]).astype(jnp.int32)
    swap = [(0, 1), (1, 0)]
    xp = lax.ppermute(features, "feat", swap)
    wp = lax.ppermute(neighbour_weight_first, "feat", swap)
    sp = lax.ppermute(w_self1, "feat", swap)
    sel = selection(ids, send_list, send_count, tile, places)
    tw = tile_weight.reshape(tile_weight.shape[0], groups, UNIT, tile)
    done = []
    for chunk in range(CHUNKS):
        parts = neighbour_terms(
            chunk, per, n, 4, ids, tile_src, tile_dst, tile_rows, tw, features, xp,
            neighbour_weight_first, wp, w_self1, sp,
        )
        got = exchange(parts, 1, n)
        stride = 4
        for radix in radices[1:]:
            ways = 1 << radix
            parts = []
            for k in range(ways):
                total = got[0][k::ways]
                for a in got[1:]:
                    total = total + a[k::ways]
                parts.append(total)
            got = exchange(parts, stride, n)
            stride *= ways
        done.append(got)
    own, send = hidden_rows(done, sel)
    other = lax.ppermute(own, "feat", swap)
    received = lax.all_to_all(send, ("feat", "dom"), 0, 0, tiled=True)
    return logits_of(ids, own, other, received, adj_two, w_self2, w_neigh2, tile, places)


def solution(mesh):
    in_specs = (
        P("dom", "feat"),
        P("dom", None, None),
        P("dom"),
        P("dom"),
        P("dom"),
        P("feat", None),
        P("feat", None),
        P(),
        P(),
        P("dom", None),
        P(),
        P(),
    )
    out_specs = P("dom", None)
    return jax.shard_map(body, mesh=mesh, in_specs=in_specs, out_specs=out_specs, check_vma=False)
```

```python
import functools

import jax
import jax.numpy as jnp
from jax import lax
from jax.experimental import pallas as pl
from jax.experimental.pallas import tpu as pltpu
from jax.sharding import PartitionSpec as P

UNIT = 16
BLOCK = 16
LEAD = 3
CHUNKS = 1


def group_of(core, place, groups):
    pair = 2 * (place // 2) + core
    return pair if place % 2 == 0 else groups - 1 - pair


def plan_kernel(chunks, per, n, radix, n_src, ids, src_v, rows_v, dst_v, lists, counts, *outs):
    core, me = ids[0], ids[1]
    tiles = src_v.shape[1]
    tables, sel = outs[:chunks], outs[chunks]
    n_pos = tables[0].shape[1]
    units = per * tiles
    groups = 2 * per * chunks
    lead = LEAD * BLOCK
    src, rows = src_v[...], rows_v[...]
    slot = jnp.bitwise_xor(dst_v[...], me)
    slot = jnp.bitwise_and(slot, radix - 1) * (n // radix) + lax.div(slot, radix)
    lane = lax.broadcasted_iota(jnp.int32, (1, tiles), 1)
    block_i = lax.broadcasted_iota(jnp.int32, (n_src, tiles), 0)
    before = lax.broadcasted_iota(jnp.int32, (units, units), 0) < lax.broadcasted_iota(jnp.int32, (units, units), 1)
    before = jnp.where(before, 1.0, 0.0).astype(jnp.bfloat16)
    pos_i = lax.broadcasted_iota(jnp.int32, (tiles, n_pos), 1).astype(jnp.float32)
    place_i = lax.broadcasted_iota(jnp.int32, (1, n_pos), 1)
    trash = float(n * per << 14)
    for c in range(chunks):
        hot, words, valid = [], [], []
        for j in range(per):
            g = group_of(core, c * per + j, groups)
            limit = jnp.clip(rows - UNIT * g, 0, UNIT)
            ok = limit > 0
            valid.append(ok)
            words.append(((slot * per + j) * 512 + (j * tiles + lane)) * 32 + limit)
            hot.append(jnp.where(jnp.logical_and(block_i == src, ok), 1.0, 0.0))
        hot = jnp.concatenate(hot, axis=1)
        earlier = jnp.dot(hot.astype(jnp.bfloat16), before, preferred_element_type=jnp.float32)
        blocks = jnp.floor((jnp.sum(hot, axis=1, keepdims=True) + (BLOCK - 1)) * (1.0 / BLOCK))
        run = jnp.zeros((1, 1), jnp.float32)
        pos = jnp.zeros((1, units), jnp.float32)
        owner = jnp.zeros((1, n_pos), jnp.float32)
        for s in range(n_src):
            pos = pos + hot[s:s + 1, :] * (earlier[s:s + 1, :] + (run * BLOCK + lead))
            run = run + blocks[s:s + 1, :]
            owner = owner + jnp.where(place_i.astype(jnp.float32) >= run, 1.0, 0.0)
        stack = [jnp.where(valid[j], pos[:, j * tiles:(j + 1) * tiles], -1.0) for j in range(per)]
        stack += [w.astype(jnp.float32) - trash for w in words]
        stack += [jnp.zeros((1, tiles), jnp.float32)] * (-len(stack) % 8)
        cols = jnp.concatenate(stack, axis=0).T
        found = jnp.zeros((tiles, n_pos), jnp.float32)
        for j in range(per):
            found = found + jnp.where(cols[:, j:j + 1] == pos_i, cols[:, per + j:per + j + 1], 0.0)
        word = jnp.sum(found, axis=0, keepdims=True) + trash
        owner = jnp.where(place_i == n_pos - 1, run, jnp.minimum(owner, n_src - 1.0))
        tables[c][0:1, :] = word.astype(jnp.int32)
        tables[c][1:2, :] = owner.astype(jnp.int32)

    slots = lists.shape[1]
    total = n * slots
    q_n = lax.broadcasted_iota(jnp.int32, (total, n), 0)
    r_n = lax.broadcasted_iota(jnp.int32, (total, n), 1)
    mine = lists[me].astype(jnp.float32)
    cnt = counts[pl.ds(me, 1), :]
    picked = jnp.zeros((total, n), jnp.float32)
    k_n = jnp.bitwise_and(q_n, slots - 1)
    for k in range(slots):
        picked = jnp.where(k_n == k, mine[k:k + 1, :], picked)
    good = jnp.logical_and(lax.div(q_n, slots) == r_n, k_n < cnt)
    row = jnp.sum(jnp.where(good, picked + 1.0, 0.0), axis=1, keepdims=True) - 1.0
    held = groups // 2 * UNIT
    lane = lax.broadcasted_iota(jnp.int32, (1, held), 1)
    name = jnp.zeros((1, held), jnp.int32)
    for i in range(groups // 2):
        g = group_of(core, i, groups)
        name = jnp.where(lax.div(lane, UNIT) == i, g * UNIT + jnp.bitwise_and(lane, UNIT - 1), name)
    sel[...] = jnp.where(row == name.astype(jnp.float32), 1.0, 0.0).astype(jnp.bfloat16)


def plan(chunks, per, n, radix, n_src, ids, src, rows, dst, send_list, send_count):
    tiles = src.shape[0]
    slots = send_list.shape[2]
    n_pos = -(-(LEAD * BLOCK + per * tiles + (n_src + LEAD) * BLOCK) // 128) * 128
    smem = pl.BlockSpec(memory_space=pltpu.SMEM)
    vmem = pl.BlockSpec(memory_space=pltpu.VMEM)
    return pl.pallas_call(
        functools.partial(plan_kernel, chunks, per, n, radix, n_src),
        out_shape=[jax.ShapeDtypeStruct((2, n_pos), jnp.int32)] * chunks
        + [jax.ShapeDtypeStruct((n * slots, chunks * per * UNIT), jnp.bfloat16)],
        in_specs=[smem] + [vmem] * 5,
        out_specs=[vmem] * (chunks + 1),
        compiler_params=pltpu.CompilerParams(vmem_limit_bytes=32 * 1024 * 1024),
        name="plan",
    )(ids, src.reshape(1, tiles), rows.reshape(1, tiles), dst.reshape(1, tiles), jnp.swapaxes(send_list, 1, 2), send_count)


def tiles_kernel(chunk, per, n, radix, ids, table, tw, xo, xp, wo, wp, so, sp, *rest):
    outs, rest = rest[:radix], rest[radix:]
    tbuf, xbuf, wbuf, sbuf, masks, packed, gath, res, acc, sems = rest
    tiles, groups = tw.shape[0], tw.shape[1]
    tile = tw.shape[3]
    width = xo.shape[1]
    core = ids[0]
    gs = [group_of(core, chunk * per + j, groups) for j in range(per)]
    copies = [
        pltpu.make_async_copy(a, b, sems.at[i])
        for i, (a, b) in enumerate(
            [(tw.at[:, gs[j]], tbuf.at[pl.ds(j * tiles, tiles)]) for j in range(per)]
            + [
                (xo, xbuf.at[:, pl.ds(0, width)]),
                (xp, xbuf.at[:, pl.ds(width, width)]),
                (wo, wbuf.at[pl.ds(0, width)]),
                (wp, wbuf.at[pl.ds(width, width)]),
                (so, sbuf.at[pl.ds(0, width)]),
                (sp, sbuf.at[pl.ds(width, width)]),
            ]
        )
    ]
    for c in copies:
        c.start()
    acc[...] = jnp.zeros_like(acc)
    row_i = lax.broadcasted_iota(jnp.int32, (UNIT, tile), 0)
    for m in range(UNIT + 1):
        masks[m] = jnp.where(row_i < m, 1.0, 0.0).astype(jnp.bfloat16)
    n_blocks = table[1, table.shape[1] - 1]
    for c in copies:
        c.wait()
    for j in range(per):
        at = pl.multiple_of(gs[j] * UNIT, UNIT)
        own = jnp.dot(xbuf[pl.ds(at, UNIT), :], sbuf[...], preferred_element_type=jnp.float32)
        acc[j * UNIT:(j + 1) * UNIT, :] = own

    def step(i, carry):
        for k in range(BLOCK):
            word = table[0, i * BLOCK + k]
            at = pl.multiple_of(lax.shift_right_logical(word, 14) * UNIT, UNIT)
            acc[pl.ds(at, UNIT), :] += res[k * UNIT:(k + 1) * UNIT, :]
        res[...] = jnp.dot(gath[...], wbuf[...], preferred_element_type=jnp.float32)
        s = table[1, jnp.maximum(i - 1, 0)]
        base = pl.multiple_of(s * tile, tile)
        for h in range(0, 2 * width, 256):
            got = jnp.dot(packed[...], xbuf[pl.ds(base, tile), h:h + 256], preferred_element_type=jnp.float32)
            gath[:, h:h + 256] = got.astype(jnp.bfloat16)
        for k in range(BLOCK):
            word = table[0, (i + LEAD) * BLOCK + k]
            u = jnp.bitwise_and(lax.shift_right_logical(word, 5), 511)
            packed[k * UNIT:(k + 1) * UNIT, :] = tbuf[u] * masks[jnp.bitwise_and(word, 31)]
        return carry

    lax.fori_loop(0, n_blocks + LEAD, step, 0)
    span = n // radix * per * UNIT
    back = [pltpu.make_async_copy(acc.at[pl.ds(k * span, span)], outs[k], sems.at[per + 6 + k]) for k in range(radix)]
    for c in back:
        c.start()
    for c in back:
        c.wait()


def neighbour_terms(chunk, per, n, radix, ids, table, tw, xo, xp, wo, wp, so, sp):
    tiles, groups, _, tile = tw.shape
    units = per * tiles
    hidden = wo.shape[1]
    rows, width = xo.shape
    smem = pl.BlockSpec(memory_space=pltpu.SMEM)
    anym = pl.BlockSpec(memory_space=pl.ANY)
    flops = 2 * units * UNIT * (tile * 2 * width + 2 * width * hidden)
    return pl.pallas_call(
        functools.partial(tiles_kernel, chunk, per, n, radix),
        out_shape=[jax.ShapeDtypeStruct((n // radix * per * UNIT, hidden), jnp.float32)] * radix,
        in_specs=[smem] * 2 + [anym] * 7,
        out_specs=[anym] * radix,
        scratch_shapes=[
            pltpu.VMEM((units, UNIT, tile), tw.dtype),
            pltpu.VMEM((rows, 2 * width), xo.dtype),
            pltpu.VMEM((2 * width, hidden), wo.dtype),
            pltpu.VMEM((2 * width, hidden), so.dtype),
            pltpu.VMEM((UNIT + 1, UNIT, tile), jnp.bfloat16),
            pltpu.VMEM((BLOCK * UNIT, tile), jnp.bfloat16),
            pltpu.VMEM((BLOCK * UNIT, 2 * width), jnp.bfloat16),
            pltpu.VMEM((BLOCK * UNIT, hidden), jnp.float32),
            pltpu.VMEM(((n * per + 1) * UNIT, hidden), jnp.float32),
            pltpu.SemaphoreType.DMA((per + 6 + radix,)),
        ],
        compiler_params=pltpu.CompilerParams(vmem_limit_bytes=40 * 1024 * 1024),
        cost_estimate=pl.CostEstimate(flops=flops, bytes_accessed=8 << 20, transcendentals=0),
        name="neighbour_terms",
    )(ids, table, tw, xo, xp, wo, wp, so, sp)


def hidden_kernel(chunks, parts, *refs):
    sel, (own, send) = refs[chunks * parts], refs[chunks * parts + 1:]
    rows = refs[0].shape[0]
    for c in range(chunks):
        total = refs[c * parts][...]
        for k in range(1, parts):
            total = total + refs[c * parts + k][...]
        own[c * rows:(c + 1) * rows, :] = jnp.maximum(total, 0.0).astype(jnp.bfloat16)
    picked = jnp.dot(sel[...], own[...], preferred_element_type=jnp.float32).astype(jnp.bfloat16)
    half = picked.shape[0]
    send[:half, :] = picked
    send[half:, :] = picked


def hidden_rows(chunk_parts, sel):
    chunks, parts = len(chunk_parts), len(chunk_parts[0])
    held = sel.shape[1]
    width = chunk_parts[0][0].shape[1]
    vmem = pl.BlockSpec(memory_space=pltpu.VMEM)
    flat = [a for part in chunk_parts for a in part]
    return pl.pallas_call(
        functools.partial(hidden_kernel, chunks, parts),
        out_shape=[
            jax.ShapeDtypeStruct((held, width), jnp.bfloat16),
            jax.ShapeDtypeStruct((2 * sel.shape[0], width), jnp.bfloat16),
        ],
        in_specs=[vmem] * (len(flat) + 1),
        out_specs=[vmem] * 2,
        compiler_params=pltpu.CompilerParams(vmem_limit_bytes=32 * 1024 * 1024),
        name="hidden_rows",
    )(*flat, sel)


def logits_kernel(tile, places, ids, own, other, received, adj, w_self, w_neigh, out, pool):
    core = ids[0]
    groups = tile // UNIT
    for i, place in enumerate(places):
        mine = group_of(core, place, groups)
        theirs = group_of(1 - core, place, groups)
        pool[pl.ds(pl.multiple_of(mine * UNIT, UNIT), UNIT), :] = own[i * UNIT:(i + 1) * UNIT, :]
        pool[pl.ds(pl.multiple_of(theirs * UNIT, UNIT), UNIT), :] = other[i * UNIT:(i + 1) * UNIT, :]
    half = received.shape[0] // 2
    both = received[:half, :].astype(jnp.float32) + received[half:, :].astype(jnp.float32)
    pool[tile:, :] = both.astype(jnp.bfloat16)
    mean = jnp.dot(adj[...], pool[...], preferred_element_type=jnp.float32).astype(jnp.bfloat16)
    dims = (((1,), (1,)), ((), ()))
    rows = adj.shape[0]
    got = lax.dot_general(pool[:rows, :], w_self[...], dims, preferred_element_type=jnp.float32)
    out[...] = got + lax.dot_general(mean, w_neigh[...], dims, preferred_element_type=jnp.float32)


def logits_of(ids, own, other, received, adj, w_self, w_neigh, tile, places):
    smem = pl.BlockSpec(memory_space=pltpu.SMEM)
    vmem = pl.BlockSpec(memory_space=pltpu.VMEM)
    return pl.pallas_call(
        functools.partial(logits_kernel, tile, places),
        out_shape=jax.ShapeDtypeStruct((adj.shape[0], w_self.shape[1]), jnp.float32),
        in_specs=[smem] + [vmem] * 6,
        out_specs=vmem,
        scratch_shapes=[pltpu.VMEM((adj.shape[1], own.shape[1]), jnp.bfloat16)],
        compiler_params=pltpu.CompilerParams(vmem_limit_bytes=32 * 1024 * 1024),
        name="logits",
    )(ids, own, other, received, adj, w_self.T, w_neigh.T)


def exchange(parts, stride, n):
    got = [parts[0]]
    for k in range(1, len(parts)):
        got.append(lax.ppermute(parts[k], "dom", [(i, i ^ (k * stride)) for i in range(n)]))
    return got


def body(
    features,
    tile_weight,
    tile_dst,
    tile_src,
    tile_rows,
    w_self1,
    neighbour_weight_first,
    send_list,
    send_count,
    adj_two,
    w_self2,
    w_neigh2,
):
    n = lax.axis_size("dom")
    tile = tile_weight.shape[1]
    groups = tile // UNIT
    per = groups // 2 // CHUNKS
    places = list(range(groups // 2))
    bits = n.bit_length() - 1
    assert n == 1 << bits and bits >= 2
    radices = [2] * (bits // 2) + [1] * (bits % 2)
    ids = jnp.stack([lax.axis_index("feat"), lax.axis_index("dom")]).astype(jnp.int32)
    swap = [(0, 1), (1, 0)]
    xp = lax.ppermute(features, "feat", swap)
    wp = lax.ppermute(neighbour_weight_first, "feat", swap)
    sp = lax.ppermute(w_self1, "feat", swap)
    tw = tile_weight.reshape(tile_weight.shape[0], groups, UNIT, tile)
    *tables, sel = plan(CHUNKS, per, n, 4, features.shape[0] // tile, ids, tile_src, tile_rows, tile_dst, send_list, send_count)
    done = []
    for chunk in range(CHUNKS):
        parts = neighbour_terms(
            chunk, per, n, 4, ids, tables[chunk], tw, features, xp, neighbour_weight_first, wp, w_self1, sp,
        )
        got = exchange(parts, 1, n)
        stride = 4
        left = n // 4
        for radix in radices[1:]:
            ways = 1 << radix
            got = [a.reshape(left, per * UNIT, -1) for a in got]
            left //= ways
            parts = []
            for k in range(ways):
                total = got[0][k::ways]
                for a in got[1:]:
                    total = total + a[k::ways]
                parts.append(total.reshape(left * per * UNIT, -1))
            got = exchange(parts, stride, n)
            stride *= ways
        done.append(got)
    own, send = hidden_rows(done, sel)
    other = lax.ppermute(own, "feat", swap)
    received = lax.all_to_all(send, ("feat", "dom"), 0, 0, tiled=True)
    return logits_of(ids, own, other, received, adj_two, w_self2, w_neigh2, tile, places)


def solution(mesh):
    in_specs = (
        P("dom", "feat"),
        P("dom", None, None),
        P("dom"),
        P("dom"),
        P("dom"),
        P("feat", None),
        P("feat", None),
        P(),
        P(),
        P("dom", None),
        P(),
        P(),
    )
    out_specs = P("dom", None)
    return jax.shard_map(body, mesh=mesh, in_specs=in_specs, out_specs=out_specs, check_vma=False)
```

```python
import functools

import jax
import jax.numpy as jnp
from jax import lax
from jax.experimental import pallas as pl
from jax.experimental.pallas import tpu as pltpu
from jax.sharding import PartitionSpec as P

UNIT = 16
BLOCK = 16
LEAD = 2
CHUNKS = 1


def group_of(core, place, groups):
    pair = 2 * (place // 2) + core
    return pair if place % 2 == 0 else groups - 1 - pair


def plan_kernel(chunks, per, n, radix, n_src, ids, src_h, rows_h, dst_h, lists_h, counts_h, tw, xo, wo, so, *rest):
    tables, rest = rest[:chunks], rest[chunks:]
    packs, rest = rest[:chunks], rest[chunks:]
    sel, xo_out, wo_out, so_out = rest[:4]
    src_v, rows_v, dst_v, lists, counts, tbuf, masks, table_s, sems = rest[4:]
    core, me = ids[0], ids[1]
    tiles = src_v.shape[1]
    tile = tw.shape[3]
    lead = LEAD * BLOCK
    n_pos = tables[0].shape[1]
    units = per * tiles
    groups = 2 * per * chunks
    half = groups // 2
    gs = [group_of(core, i, groups) for i in range(half)]
    small = [(src_h, src_v), (rows_h, rows_v), (dst_h, dst_v), (lists_h, lists), (counts_h, counts)]
    large = [(tw.at[:, g], tbuf.at[pl.ds(i * tiles, tiles)]) for i, g in enumerate(gs)]
    large += [(xo, xo_out), (wo, wo_out), (so, so_out)]
    copies = [pltpu.make_async_copy(a, b, sems.at[i]) for i, (a, b) in enumerate(small + large)]
    for c in copies:
        c.start()
    row_i = lax.broadcasted_iota(jnp.int32, (UNIT, tile), 0)
    for m in range(UNIT + 1):
        masks[m] = jnp.where(row_i < m, 1.0, 0.0).astype(jnp.bfloat16)
    lane = lax.broadcasted_iota(jnp.int32, (1, tiles), 1)
    block_i = lax.broadcasted_iota(jnp.int32, (n_src, tiles), 0)
    before = lax.broadcasted_iota(jnp.int32, (units, units), 0) < lax.broadcasted_iota(jnp.int32, (units, units), 1)
    before = jnp.where(before, 1.0, 0.0).astype(jnp.bfloat16)
    pos_i = lax.broadcasted_iota(jnp.int32, (tiles, n_pos), 1).astype(jnp.float32)
    place_i = lax.broadcasted_iota(jnp.int32, (1, n_pos), 1)
    trash = float(n * per << 14)
    for c in copies[:5]:
        c.wait()
    src, rows = src_v[...], rows_v[...]
    slot = jnp.bitwise_xor(dst_v[...], me)
    slot = jnp.bitwise_and(slot, radix - 1) * (n // radix) + lax.div(slot, radix)
    to_scalar = []
    for c in range(chunks):
        hot, words, valid = [], [], []
        for j in range(per):
            limit = jnp.clip(rows - UNIT * gs[c * per + j], 0, UNIT)
            ok = limit > 0
            valid.append(ok)
            words.append(((slot * per + j) * 512 + (j * tiles + lane)) * 32 + limit)
            hot.append(jnp.where(jnp.logical_and(block_i == src, ok), 1.0, 0.0))
        hot = jnp.concatenate(hot, axis=1)
        earlier = jnp.dot(hot.astype(jnp.bfloat16), before, preferred_element_type=jnp.float32)
        blocks = jnp.floor((jnp.sum(hot, axis=1, keepdims=True) + (BLOCK - 1)) * (1.0 / BLOCK))
        run = jnp.zeros((1, 1), jnp.float32)
        pos = jnp.zeros((1, units), jnp.float32)
        owner = jnp.zeros((1, n_pos), jnp.float32)
        for s in range(n_src):
            pos = pos + hot[s:s + 1, :] * (earlier[s:s + 1, :] + (run * BLOCK + lead))
            run = run + blocks[s:s + 1, :]
            owner = owner + jnp.where(place_i.astype(jnp.float32) >= run, 1.0, 0.0)
        stack = [jnp.where(valid[j], pos[:, j * tiles:(j + 1) * tiles], -1.0) for j in range(per)]
        stack += [w.astype(jnp.float32) - trash for w in words]
        stack += [jnp.zeros((1, tiles), jnp.float32)] * (-len(stack) % 8)
        cols = jnp.concatenate(stack, axis=0).T
        found = jnp.zeros((tiles, n_pos), jnp.float32)
        for j in range(per):
            found = found + jnp.where(cols[:, j:j + 1] == pos_i, cols[:, per + j:per + j + 1], 0.0)
        word = jnp.sum(found, axis=0, keepdims=True) + trash
        owner = jnp.where(place_i == n_pos - 1, run, jnp.minimum(owner, n_src - 1.0))
        tables[c][0:1, :] = word.astype(jnp.int32)
        tables[c][1:2, :] = owner.astype(jnp.int32)
        copy = pltpu.make_async_copy(tables[c], table_s.at[c], sems.at[len(copies) + c])
        copy.start()
        to_scalar.append(copy)

    slots = lists.shape[1]
    total = n * slots
    q_n = lax.broadcasted_iota(jnp.int32, (total, n), 0)
    r_n = lax.broadcasted_iota(jnp.int32, (total, n), 1)
    mine = lists[me].astype(jnp.float32)
    cnt = counts[pl.ds(me, 1), :]
    picked = jnp.zeros((total, n), jnp.float32)
    k_n = jnp.bitwise_and(q_n, slots - 1)
    for k in range(slots):
        picked = jnp.where(k_n == k, mine[k:k + 1, :], picked)
    good = jnp.logical_and(lax.div(q_n, slots) == r_n, k_n < cnt)
    row = jnp.sum(jnp.where(good, picked + 1.0, 0.0), axis=1, keepdims=True) - 1.0
    lane = lax.broadcasted_iota(jnp.int32, (1, half * UNIT), 1)
    name = jnp.zeros((1, half * UNIT), jnp.int32)
    for i in range(half):
        name = jnp.where(lax.div(lane, UNIT) == i, gs[i] * UNIT + jnp.bitwise_and(lane, UNIT - 1), name)
    sel[...] = jnp.where(row == name.astype(jnp.float32), 1.0, 0.0).astype(jnp.bfloat16)

    for c in copies[5:5 + half]:
        c.wait()
    for c in range(chunks):
        to_scalar[c].wait()

        def block(b, carry):
            for k in range(BLOCK):
                word = table_s[c, 0, lead + b * BLOCK + k]
                u = jnp.bitwise_and(lax.shift_right_logical(word, 5), 511) + c * units
                at = pl.multiple_of((b * BLOCK + k) * UNIT, UNIT)
                packs[c][pl.ds(at, UNIT), :] = tbuf[u] * masks[jnp.bitwise_and(word, 31)]
            return carry

        lax.fori_loop(0, table_s[c, 1, n_pos - 1], block, 0)
    for c in copies[5 + half:]:
        c.wait()


def plan(chunks, per, n, radix, ids, src, rows, dst, send_list, send_count, tw, xo, wo, so):
    tiles, _, _, tile = tw.shape
    slots = send_list.shape[2]
    n_src = xo.shape[0] // tile
    blocks = per * tiles // BLOCK + n_src + LEAD
    n_pos = -(-((LEAD + blocks) * BLOCK + 1) // 128) * 128
    smem = pl.BlockSpec(memory_space=pltpu.SMEM)
    vmem = pl.BlockSpec(memory_space=pltpu.VMEM)
    hbm = pl.BlockSpec(memory_space=pltpu.HBM)
    lists = jnp.swapaxes(send_list, 1, 2)
    half = chunks * per
    return pl.pallas_call(
        functools.partial(plan_kernel, chunks, per, n, radix, n_src),
        out_shape=[jax.ShapeDtypeStruct((2, n_pos), jnp.int32)] * chunks
        + [jax.ShapeDtypeStruct((blocks * BLOCK * UNIT, tile), tw.dtype)] * chunks
        + [
            jax.ShapeDtypeStruct((n * slots, half * UNIT), jnp.bfloat16),
            jax.ShapeDtypeStruct(xo.shape, xo.dtype),
            jax.ShapeDtypeStruct(wo.shape, wo.dtype),
            jax.ShapeDtypeStruct(so.shape, so.dtype),
        ],
        in_specs=[smem] + [hbm] * 9,
        out_specs=[vmem] * (2 * chunks + 4),
        scratch_shapes=[
            pltpu.VMEM((1, tiles), jnp.int32),
            pltpu.VMEM((1, tiles), jnp.int32),
            pltpu.VMEM((1, tiles), jnp.int32),
            pltpu.VMEM(lists.shape, jnp.int32),
            pltpu.VMEM(send_count.shape, jnp.int32),
            pltpu.VMEM((half * tiles, UNIT, tile), tw.dtype),
            pltpu.VMEM((UNIT + 1, UNIT, tile), jnp.bfloat16),
            pltpu.SMEM((chunks, 2, n_pos), jnp.int32),
            pltpu.SemaphoreType.DMA((5 + half + 3 + chunks,)),
        ],
        compiler_params=pltpu.CompilerParams(vmem_limit_bytes=32 * 1024 * 1024),
        name="plan",
    )(ids, *[
        pltpu.with_memory_space_constraint(a, pltpu.HBM)
        for a in (src.reshape(1, tiles), rows.reshape(1, tiles), dst.reshape(1, tiles), lists, send_count, tw, xo, wo, so)
    ])


def tiles_kernel(chunk, per, n, radix, groups, ids, table, packed, xo, xp, wo, wp, so, sp, *rest):
    outs, rest = rest[:radix], rest[radix:]
    wbuf, gath, res, acc, sems = rest
    tile = packed.shape[1]
    width = xo.shape[1]
    core = ids[0]
    copies = [
        pltpu.make_async_copy(wo, wbuf.at[pl.ds(0, width)], sems.at[0]),
        pltpu.make_async_copy(wp, wbuf.at[pl.ds(width, width)], sems.at[1]),
    ]
    for c in copies:
        c.start()
    acc[...] = jnp.zeros_like(acc)
    for j in range(per):
        at = pl.multiple_of(group_of(core, chunk * per + j, groups) * UNIT, UNIT)
        own = jnp.dot(xo[pl.ds(at, UNIT), :], so[...], preferred_element_type=jnp.float32)
        own = own + jnp.dot(xp[pl.ds(at, UNIT), :], sp[...], preferred_element_type=jnp.float32)
        acc[j * UNIT:(j + 1) * UNIT, :] = own
    for c in copies:
        c.wait()

    def step(i, carry):
        for k in range(BLOCK):
            word = table[0, i * BLOCK + k]
            at = pl.multiple_of(lax.shift_right_logical(word, 14) * UNIT, UNIT)
            acc[pl.ds(at, UNIT), :] += res[k * UNIT:(k + 1) * UNIT, :]
        res[...] = jnp.dot(gath[...], wbuf[...], preferred_element_type=jnp.float32)
        base = pl.multiple_of(table[1, i] * tile, tile)
        lhs = packed[pl.ds(pl.multiple_of(i * BLOCK * UNIT, BLOCK * UNIT), BLOCK * UNIT), :]
        for q, x in enumerate((xo, xp)):
            for h in range(0, width, 256):
                got = jnp.dot(lhs, x[pl.ds(base, tile), h:h + 256], preferred_element_type=jnp.float32)
                gath[:, q * width + h:q * width + h + 256] = got.astype(jnp.bfloat16)
        return carry

    lax.fori_loop(0, table[1, table.shape[1] - 1] + LEAD, step, 0)
    span = n // radix * per * UNIT
    back = [pltpu.make_async_copy(acc.at[pl.ds(k * span, span)], outs[k], sems.at[2 + k]) for k in range(radix)]
    for c in back:
        c.start()
    for c in back:
        c.wait()


def neighbour_terms(chunk, per, n, radix, groups, ids, table, packed, xo, xp, wo, wp, so, sp):
    hidden = wo.shape[1]
    width = xo.shape[1]
    tile = packed.shape[1]
    smem = pl.BlockSpec(memory_space=pltpu.SMEM)
    vmem = pl.BlockSpec(memory_space=pltpu.VMEM)
    anym = pl.BlockSpec(memory_space=pl.ANY)
    flops = 2 * packed.shape[0] * (tile * 2 * width + 2 * width * hidden)
    sums = (n * per + 1) * UNIT * hidden * 4
    return pl.pallas_call(
        functools.partial(tiles_kernel, chunk, per, n, radix, groups),
        out_shape=[jax.ShapeDtypeStruct((n // radix * per * UNIT, hidden), jnp.float32)] * radix,
        in_specs=[smem] * 2 + [vmem] * 7,
        out_specs=[anym] * radix,
        scratch_shapes=[
            pltpu.VMEM((2 * width, hidden), wo.dtype),
            pltpu.VMEM((BLOCK * UNIT, 2 * width), jnp.bfloat16),
            pltpu.VMEM((BLOCK * UNIT, hidden), jnp.float32),
            pltpu.VMEM(((n * per + 1) * UNIT, hidden), jnp.float32),
            pltpu.SemaphoreType.DMA((2 + radix,)),
        ],
        compiler_params=pltpu.CompilerParams(vmem_limit_bytes=(16 << 20) + sums),
        cost_estimate=pl.CostEstimate(flops=flops, bytes_accessed=8 << 20, transcendentals=0),
        name="neighbour_terms",
    )(ids, table, packed, xo, xp, wo, wp, so, sp)


def hidden_kernel(chunks, parts, *refs):
    sel, (own, send) = refs[chunks * parts], refs[chunks * parts + 1:]
    rows = refs[0].shape[0]
    for c in range(chunks):
        total = refs[c * parts][...]
        for k in range(1, parts):
            total = total + refs[c * parts + k][...]
        own[c * rows:(c + 1) * rows, :] = jnp.maximum(total, 0.0).astype(jnp.bfloat16)
    picked = jnp.dot(sel[...], own[...], preferred_element_type=jnp.float32).astype(jnp.bfloat16)
    half = picked.shape[0]
    send[:half, :] = picked
    send[half:, :] = picked


def hidden_rows(chunk_parts, sel):
    chunks, parts = len(chunk_parts), len(chunk_parts[0])
    held = sel.shape[1]
    width = chunk_parts[0][0].shape[1]
    vmem = pl.BlockSpec(memory_space=pltpu.VMEM)
    flat = [a for part in chunk_parts for a in part]
    return pl.pallas_call(
        functools.partial(hidden_kernel, chunks, parts),
        out_shape=[
            jax.ShapeDtypeStruct((held, width), jnp.bfloat16),
            jax.ShapeDtypeStruct((2 * sel.shape[0], width), jnp.bfloat16),
        ],
        in_specs=[vmem] * (len(flat) + 1),
        out_specs=[vmem] * 2,
        compiler_params=pltpu.CompilerParams(vmem_limit_bytes=32 * 1024 * 1024),
        name="hidden_rows",
    )(*flat, sel)


def logits_kernel(tile, places, ids, own, other, received, adj, w_self, w_neigh, out, pool):
    core = ids[0]
    groups = tile // UNIT
    for i, place in enumerate(places):
        mine = group_of(core, place, groups)
        theirs = group_of(1 - core, place, groups)
        pool[pl.ds(pl.multiple_of(mine * UNIT, UNIT), UNIT), :] = own[i * UNIT:(i + 1) * UNIT, :]
        pool[pl.ds(pl.multiple_of(theirs * UNIT, UNIT), UNIT), :] = other[i * UNIT:(i + 1) * UNIT, :]
    half = received.shape[0] // 2
    both = received[:half, :].astype(jnp.float32) + received[half:, :].astype(jnp.float32)
    pool[tile:, :] = both.astype(jnp.bfloat16)
    mean = jnp.dot(adj[...], pool[...], preferred_element_type=jnp.float32).astype(jnp.bfloat16)
    dims = (((1,), (1,)), ((), ()))
    rows = adj.shape[0]
    got = lax.dot_general(pool[:rows, :], w_self[...], dims, preferred_element_type=jnp.float32)
    out[...] = got + lax.dot_general(mean, w_neigh[...], dims, preferred_element_type=jnp.float32)


def logits_of(ids, own, other, received, adj, w_self, w_neigh, tile, places):
    smem = pl.BlockSpec(memory_space=pltpu.SMEM)
    vmem = pl.BlockSpec(memory_space=pltpu.VMEM)
    return pl.pallas_call(
        functools.partial(logits_kernel, tile, places),
        out_shape=jax.ShapeDtypeStruct((adj.shape[0], w_self.shape[1]), jnp.float32),
        in_specs=[smem] + [vmem] * 6,
        out_specs=vmem,
        scratch_shapes=[pltpu.VMEM((adj.shape[1], own.shape[1]), jnp.bfloat16)],
        compiler_params=pltpu.CompilerParams(vmem_limit_bytes=32 * 1024 * 1024),
        name="logits",
    )(ids, own, other, received, adj, w_self.T, w_neigh.T)


def exchange(parts, stride, n):
    got = [parts[0]]
    for k in range(1, len(parts)):
        got.append(lax.ppermute(parts[k], "dom", [(i, i ^ (k * stride)) for i in range(n)]))
    return got


def body(
    features,
    tile_weight,
    tile_dst,
    tile_src,
    tile_rows,
    w_self1,
    neighbour_weight_first,
    send_list,
    send_count,
    adj_two,
    w_self2,
    w_neigh2,
):
    n = lax.axis_size("dom")
    tile = tile_weight.shape[1]
    groups = tile // UNIT
    per = groups // 2 // CHUNKS
    places = list(range(groups // 2))
    bits = n.bit_length() - 1
    assert n == 1 << bits and bits >= 2
    radices = [2] * (bits // 2) + [1] * (bits % 2)
    ids = jnp.stack([lax.axis_index("feat"), lax.axis_index("dom")]).astype(jnp.int32)
    swap = [(0, 1), (1, 0)]
    xp = lax.ppermute(features, "feat", swap)
    wp = lax.ppermute(neighbour_weight_first, "feat", swap)
    sp = lax.ppermute(w_self1, "feat", swap)
    tw = tile_weight.reshape(tile_weight.shape[0], groups, UNIT, tile)
    planned = plan(
        CHUNKS, per, n, 4, ids, tile_src, tile_rows, tile_dst, send_list, send_count, tw, features,
        neighbour_weight_first, w_self1,
    )
    tables, packs, (sel, xo, wo, so) = planned[:CHUNKS], planned[CHUNKS:2 * CHUNKS], planned[2 * CHUNKS:]
    done = []
    for chunk in range(CHUNKS):
        parts = neighbour_terms(chunk, per, n, 4, groups, ids, tables[chunk], packs[chunk], xo, xp, wo, wp, so, sp)
        got = exchange(parts, 1, n)
        stride = 4
        left = n // 4
        for radix in radices[1:]:
            ways = 1 << radix
            got = [a.reshape(left, per * UNIT, -1) for a in got]
            left //= ways
            parts = []
            for k in range(ways):
                total = got[0][k::ways]
                for a in got[1:]:
                    total = total + a[k::ways]
                parts.append(total.reshape(left * per * UNIT, -1))
            got = exchange(parts, stride, n)
            stride *= ways
        done.append(got)
    own, send = hidden_rows(done, sel)
    other = lax.ppermute(own, "feat", swap)
    received = lax.all_to_all(send, ("feat", "dom"), 0, 0, tiled=True)
    return logits_of(ids, own, other, received, adj_two, w_self2, w_neigh2, tile, places)


def solution(mesh):
    in_specs = (
        P("dom", "feat"),
        P("dom", None, None),
        P("dom"),
        P("dom"),
        P("dom"),
        P("feat", None),
        P("feat", None),
        P(),
        P(),
        P("dom", None),
        P(),
        P(),
    )
    out_specs = P("dom", None)
    return jax.shard_map(body, mesh=mesh, in_specs=in_specs, out_specs=out_specs, check_vma=False)
```

```python
import functools

import jax
import jax.numpy as jnp
from jax import lax
from jax.experimental import pallas as pl
from jax.experimental.pallas import tpu as pltpu
from jax.sharding import PartitionSpec as P

UNIT = 16
BLOCK = 8
STEP = 4
LEAD = 2
CHUNKS = 1


def group_of(core, place, groups):
    pair = 2 * (place // 2) + core
    return pair if place % 2 == 0 else groups - 1 - pair


def plan_kernel(chunks, per, n, radix, n_src, ids, src_h, rows_h, dst_h, lists_h, counts_h, tw, xo, wo, so, *rest):
    tables, rest = rest[:chunks], rest[chunks:]
    packs, rest = rest[:chunks], rest[chunks:]
    sel, xo_out, wo_out, so_out = rest[:4]
    src_v, rows_v, dst_v, lists, counts, tbuf, masks, table_s, sems = rest[4:]
    core, me = ids[0], ids[1]
    tiles = src_v.shape[1]
    tile = tw.shape[3]
    lead = LEAD * STEP * BLOCK
    n_pos = tables[0].shape[1]
    units = per * tiles
    groups = 2 * per * chunks
    half = groups // 2
    gs = [group_of(core, i, groups) for i in range(half)]
    small = [(src_h, src_v), (rows_h, rows_v), (dst_h, dst_v), (lists_h, lists), (counts_h, counts)]
    large = [(tw.at[:, g], tbuf.at[pl.ds(i * tiles, tiles)]) for i, g in enumerate(gs)]
    large += [(xo, xo_out), (wo, wo_out), (so, so_out)]
    copies = [pltpu.make_async_copy(a, b, sems.at[i]) for i, (a, b) in enumerate(small + large)]
    for c in copies:
        c.start()
    row_i = lax.broadcasted_iota(jnp.int32, (UNIT, tile), 0)
    for m in range(UNIT + 1):
        masks[m] = jnp.where(row_i < m, 1.0, 0.0).astype(jnp.bfloat16)
    lane = lax.broadcasted_iota(jnp.int32, (1, tiles), 1)
    block_i = lax.broadcasted_iota(jnp.int32, (n_src, tiles), 0)
    before = lax.broadcasted_iota(jnp.int32, (units, units), 0) < lax.broadcasted_iota(jnp.int32, (units, units), 1)
    before = jnp.where(before, 1.0, 0.0).astype(jnp.bfloat16)
    pos_i = lax.broadcasted_iota(jnp.int32, (tiles, n_pos), 1).astype(jnp.float32)
    place_i = lax.broadcasted_iota(jnp.int32, (1, n_pos), 1)
    trash = float(n * per << 14)
    for c in copies[:5]:
        c.wait()
    src, rows = src_v[...], rows_v[...]
    slot = jnp.bitwise_xor(dst_v[...], me)
    slot = jnp.bitwise_and(slot, radix - 1) * (n // radix) + lax.div(slot, radix)
    to_scalar = []
    for c in range(chunks):
        hot, words, valid = [], [], []
        for j in range(per):
            limit = jnp.clip(rows - UNIT * gs[c * per + j], 0, UNIT)
            ok = limit > 0
            valid.append(ok)
            words.append(((slot * per + j) * 512 + (j * tiles + lane)) * 32 + limit)
            hot.append(jnp.where(jnp.logical_and(block_i == src, ok), 1.0, 0.0))
        hot = jnp.concatenate(hot, axis=1)
        earlier = jnp.dot(hot.astype(jnp.bfloat16), before, preferred_element_type=jnp.float32)
        blocks = jnp.floor((jnp.sum(hot, axis=1, keepdims=True) + (BLOCK - 1)) * (1.0 / BLOCK))
        run = jnp.zeros((1, 1), jnp.float32)
        pos = jnp.zeros((1, units), jnp.float32)
        owner = jnp.zeros((1, n_pos), jnp.float32)
        for s in range(n_src):
            pos = pos + hot[s:s + 1, :] * (earlier[s:s + 1, :] + (run * BLOCK + lead))
            run = run + blocks[s:s + 1, :]
            owner = owner + jnp.where(place_i.astype(jnp.float32) >= run, 1.0, 0.0)
        stack = [jnp.where(valid[j], pos[:, j * tiles:(j + 1) * tiles], -1.0) for j in range(per)]
        stack += [w.astype(jnp.float32) - trash for w in words]
        stack += [jnp.zeros((1, tiles), jnp.float32)] * (-len(stack) % 8)
        cols = jnp.concatenate(stack, axis=0).T
        found = jnp.zeros((tiles, n_pos), jnp.float32)
        for j in range(per):
            found = found + jnp.where(cols[:, j:j + 1] == pos_i, cols[:, per + j:per + j + 1], 0.0)
        word = jnp.sum(found, axis=0, keepdims=True) + trash
        owner = jnp.where(place_i == n_pos - 1, run, jnp.minimum(owner, n_src - 1.0))
        tables[c][0:1, :] = word.astype(jnp.int32)
        tables[c][1:2, :] = owner.astype(jnp.int32)
        copy = pltpu.make_async_copy(tables[c], table_s.at[c], sems.at[len(copies) + c])
        copy.start()
        to_scalar.append(copy)

    slots = lists.shape[1]
    total = n * slots
    q_n = lax.broadcasted_iota(jnp.int32, (total, n), 0)
    r_n = lax.broadcasted_iota(jnp.int32, (total, n), 1)
    mine = lists[me].astype(jnp.float32)
    cnt = counts[pl.ds(me, 1), :]
    picked = jnp.zeros((total, n), jnp.float32)
    k_n = jnp.bitwise_and(q_n, slots - 1)
    for k in range(slots):
        picked = jnp.where(k_n == k, mine[k:k + 1, :], picked)
    good = jnp.logical_and(lax.div(q_n, slots) == r_n, k_n < cnt)
    row = jnp.sum(jnp.where(good, picked + 1.0, 0.0), axis=1, keepdims=True) - 1.0
    lane = lax.broadcasted_iota(jnp.int32, (1, sel.shape[1]), 1).astype(jnp.float32)
    sel[...] = jnp.where(row == lane, 1.0, 0.0).astype(jnp.bfloat16)

    for c in copies[5:5 + half]:
        c.wait()
    for c in range(chunks):
        to_scalar[c].wait()

        def block(b, carry):
            for k in range(BLOCK):
                word = table_s[c, 0, lead + b * BLOCK + k]
                u = jnp.bitwise_and(lax.shift_right_logical(word, 5), 511) + c * units
                at = pl.multiple_of((b * BLOCK + k) * UNIT, UNIT)
                packs[c][pl.ds(at, UNIT), :] = tbuf[u] * masks[jnp.bitwise_and(word, 31)]
            return carry

        lax.fori_loop(0, table_s[c, 1, n_pos - 1], block, 0)
    for c in copies[5 + half:]:
        c.wait()


def plan(chunks, per, n, radix, ids, src, rows, dst, send_list, send_count, tw, xo, wo, so):
    tiles, _, _, tile = tw.shape
    slots = send_list.shape[2]
    n_src = xo.shape[0] // tile
    blocks = -(-(per * tiles // BLOCK + n_src) // STEP + -LEAD) * STEP
    n_pos = -(-((LEAD * STEP + blocks) * BLOCK + 1) // 128) * 128
    smem = pl.BlockSpec(memory_space=pltpu.SMEM)
    vmem = pl.BlockSpec(memory_space=pltpu.VMEM)
    hbm = pl.BlockSpec(memory_space=pltpu.HBM)
    lists = jnp.swapaxes(send_list, 1, 2)
    half = chunks * per
    return pl.pallas_call(
        functools.partial(plan_kernel, chunks, per, n, radix, n_src),
        out_shape=[jax.ShapeDtypeStruct((2, n_pos), jnp.int32)] * chunks
        + [jax.ShapeDtypeStruct((blocks * BLOCK * UNIT, tile), tw.dtype)] * chunks
        + [
            jax.ShapeDtypeStruct((n * slots, 2 * half * UNIT), jnp.bfloat16),
            jax.ShapeDtypeStruct(xo.shape, xo.dtype),
            jax.ShapeDtypeStruct(wo.shape, wo.dtype),
            jax.ShapeDtypeStruct(so.shape, so.dtype),
        ],
        in_specs=[smem] + [hbm] * 9,
        out_specs=[vmem] * (2 * chunks + 4),
        scratch_shapes=[
            pltpu.VMEM((1, tiles), jnp.int32),
            pltpu.VMEM((1, tiles), jnp.int32),
            pltpu.VMEM((1, tiles), jnp.int32),
            pltpu.VMEM(lists.shape, jnp.int32),
            pltpu.VMEM(send_count.shape, jnp.int32),
            pltpu.VMEM((half * tiles, UNIT, tile), tw.dtype),
            pltpu.VMEM((UNIT + 1, UNIT, tile), jnp.bfloat16),
            pltpu.SMEM((chunks, 2, n_pos), jnp.int32),
            pltpu.SemaphoreType.DMA((5 + half + 3 + chunks,)),
        ],
        compiler_params=pltpu.CompilerParams(vmem_limit_bytes=32 * 1024 * 1024),
        name="plan",
    )(ids, *[
        pltpu.with_memory_space_constraint(a, pltpu.HBM)
        for a in (src.reshape(1, tiles), rows.reshape(1, tiles), dst.reshape(1, tiles), lists, send_count, tw, xo, wo, so)
    ])


def tiles_kernel(chunk, per, n, radix, groups, ids, table, packed, xo, xp, wo, wp, so, sp, *rest):
    outs, rest = rest[:radix], rest[radix:]
    wbuf, gath, res, acc, sems = rest
    tile = packed.shape[1]
    width = xo.shape[1]
    core = ids[0]
    copies = [
        pltpu.make_async_copy(wo, wbuf.at[pl.ds(0, width)], sems.at[0]),
        pltpu.make_async_copy(wp, wbuf.at[pl.ds(width, width)], sems.at[1]),
    ]
    for c in copies:
        c.start()
    acc[...] = jnp.zeros_like(acc)
    for j in range(per):
        at = pl.multiple_of(group_of(core, chunk * per + j, groups) * UNIT, UNIT)
        own = jnp.dot(xo[pl.ds(at, UNIT), :], so[...], preferred_element_type=jnp.float32)
        own = own + jnp.dot(xp[pl.ds(at, UNIT), :], sp[...], preferred_element_type=jnp.float32)
        acc[j * UNIT:(j + 1) * UNIT, :] = own
    for c in copies:
        c.wait()

    size = BLOCK * UNIT

    def step(i, carry):
        for k in range(STEP * BLOCK):
            word = table[0, i * (STEP * BLOCK) + k]
            at = pl.multiple_of(lax.shift_right_logical(word, 14) * UNIT, UNIT)
            acc[pl.ds(at, UNIT), :] += res[k * UNIT:(k + 1) * UNIT, :]
        res[...] = jnp.dot(gath[...], wbuf[...], preferred_element_type=jnp.float32)
        for m in range(STEP):
            base = pl.multiple_of(table[1, i * STEP + m] * tile, tile)
            lhs = packed[pl.ds(pl.multiple_of((i * STEP + m) * size, size), size), :]
            for q, x in enumerate((xo, xp)):
                for h in range(0, width, 256):
                    got = jnp.dot(lhs, x[pl.ds(base, tile), h:h + 256], preferred_element_type=jnp.float32)
                    gath[m * size:(m + 1) * size, q * width + h:q * width + h + 256] = got.astype(jnp.bfloat16)
        return carry

    steps = lax.div(table[1, table.shape[1] - 1] + STEP - 1, STEP)
    lax.fori_loop(0, steps + LEAD, step, 0)
    span = n // radix * per * UNIT
    back = [pltpu.make_async_copy(acc.at[pl.ds(k * span, span)], outs[k], sems.at[2 + k]) for k in range(radix)]
    for c in back:
        c.start()
    for c in back:
        c.wait()


def neighbour_terms(chunk, per, n, radix, groups, ids, table, packed, xo, xp, wo, wp, so, sp):
    hidden = wo.shape[1]
    width = xo.shape[1]
    tile = packed.shape[1]
    smem = pl.BlockSpec(memory_space=pltpu.SMEM)
    vmem = pl.BlockSpec(memory_space=pltpu.VMEM)
    anym = pl.BlockSpec(memory_space=pl.ANY)
    flops = 2 * packed.shape[0] * (tile * 2 * width + 2 * width * hidden)
    sums = (n * per + 1) * UNIT * hidden * 4
    return pl.pallas_call(
        functools.partial(tiles_kernel, chunk, per, n, radix, groups),
        out_shape=[jax.ShapeDtypeStruct((n // radix * per * UNIT, hidden), jnp.float32)] * radix,
        in_specs=[smem] * 2 + [vmem] * 7,
        out_specs=[anym] * radix,
        scratch_shapes=[
            pltpu.VMEM((2 * width, hidden), wo.dtype),
            pltpu.VMEM((STEP * BLOCK * UNIT, 2 * width), jnp.bfloat16),
            pltpu.VMEM((STEP * BLOCK * UNIT, hidden), jnp.float32),
            pltpu.VMEM(((n * per + 1) * UNIT, hidden), jnp.float32),
            pltpu.SemaphoreType.DMA((2 + radix,)),
        ],
        compiler_params=pltpu.CompilerParams(vmem_limit_bytes=(16 << 20) + sums),
        cost_estimate=pl.CostEstimate(flops=flops, bytes_accessed=8 << 20, transcendentals=0),
        name="neighbour_terms",
    )(ids, table, packed, xo, xp, wo, wp, so, sp)


def hidden_kernel(chunks, parts, *refs):
    own = refs[chunks * parts]
    rows = refs[0].shape[0]
    for c in range(chunks):
        total = refs[c * parts][...]
        for k in range(1, parts):
            total = total + refs[c * parts + k][...]
        own[c * rows:(c + 1) * rows, :] = jnp.maximum(total, 0.0).astype(jnp.bfloat16)


def hidden_rows(chunk_parts):
    chunks, parts = len(chunk_parts), len(chunk_parts[0])
    rows, width = chunk_parts[0][0].shape
    vmem = pl.BlockSpec(memory_space=pltpu.VMEM)
    flat = [a for part in chunk_parts for a in part]
    return pl.pallas_call(
        functools.partial(hidden_kernel, chunks, parts),
        out_shape=jax.ShapeDtypeStruct((chunks * rows, width), jnp.bfloat16),
        in_specs=[vmem] * len(flat),
        out_specs=vmem,
        compiler_params=pltpu.CompilerParams(vmem_limit_bytes=32 * 1024 * 1024),
        name="hidden_rows",
    )(*flat)


def send_kernel(groups, ids, own, other, sel, hidden, send):
    core = ids[0]
    for i in range(groups // 2):
        mine = group_of(core, i, groups)
        theirs = group_of(1 - core, i, groups)
        hidden[pl.ds(pl.multiple_of(mine * UNIT, UNIT), UNIT), :] = own[i * UNIT:(i + 1) * UNIT, :]
        hidden[pl.ds(pl.multiple_of(theirs * UNIT, UNIT), UNIT), :] = other[i * UNIT:(i + 1) * UNIT, :]
    send[...] = jnp.dot(sel[...], hidden[...], preferred_element_type=jnp.float32).astype(jnp.bfloat16)


def rows_to_send(groups, ids, own, other, sel):
    smem = pl.BlockSpec(memory_space=pltpu.SMEM)
    vmem = pl.BlockSpec(memory_space=pltpu.VMEM)
    width = own.shape[1]
    return pl.pallas_call(
        functools.partial(send_kernel, groups),
        out_shape=[
            jax.ShapeDtypeStruct((groups * UNIT, width), jnp.bfloat16),
            jax.ShapeDtypeStruct((sel.shape[0], width), jnp.bfloat16),
        ],
        in_specs=[smem] + [vmem] * 3,
        out_specs=[vmem] * 2,
        compiler_params=pltpu.CompilerParams(vmem_limit_bytes=32 * 1024 * 1024),
        name="rows_to_send",
    )(ids, own, other, sel)


def logits_kernel(hidden, received, adj, w_self, w_neigh, out):
    tile, rows = hidden.shape[0], adj.shape[0]
    mean = jnp.dot(adj[:, :tile], hidden[...], preferred_element_type=jnp.float32)
    mean = mean + jnp.dot(adj[:, tile:], received[...], preferred_element_type=jnp.float32)
    dims = (((1,), (1,)), ((), ()))
    got = lax.dot_general(hidden[:rows, :], w_self[...], dims, preferred_element_type=jnp.float32)
    got = got + lax.dot_general(mean.astype(jnp.bfloat16), w_neigh[...], dims, preferred_element_type=jnp.float32)
    out[...] = got


def logits_of(hidden, received, adj, w_self, w_neigh):
    vmem = pl.BlockSpec(memory_space=pltpu.VMEM)
    return pl.pallas_call(
        logits_kernel,
        out_shape=jax.ShapeDtypeStruct((adj.shape[0], w_self.shape[1]), jnp.float32),
        in_specs=[vmem] * 5,
        out_specs=vmem,
        compiler_params=pltpu.CompilerParams(vmem_limit_bytes=32 * 1024 * 1024),
        name="logits",
    )(hidden, received, adj, w_self.T, w_neigh.T)


def exchange(parts, stride, n):
    got = [parts[0]]
    for k in range(1, len(parts)):
        got.append(lax.ppermute(parts[k], "dom", [(i, i ^ (k * stride)) for i in range(n)]))
    return got


def body(
    features,
    tile_weight,
    tile_dst,
    tile_src,
    tile_rows,
    w_self1,
    neighbour_weight_first,
    send_list,
    send_count,
    adj_two,
    w_self2,
    w_neigh2,
):
    n = lax.axis_size("dom")
    tile = tile_weight.shape[1]
    groups = tile // UNIT
    per = groups // 2 // CHUNKS
    bits = n.bit_length() - 1
    assert n == 1 << bits and bits >= 2
    radices = [2] * (bits // 2) + [1] * (bits % 2)
    ids = jnp.stack([lax.axis_index("feat"), lax.axis_index("dom")]).astype(jnp.int32)
    swap = [(0, 1), (1, 0)]
    xp = lax.ppermute(features, "feat", swap)
    wp = lax.ppermute(neighbour_weight_first, "feat", swap)
    sp = lax.ppermute(w_self1, "feat", swap)
    tw = tile_weight.reshape(tile_weight.shape[0], groups, UNIT, tile)
    planned = plan(
        CHUNKS, per, n, 4, ids, tile_src, tile_rows, tile_dst, send_list, send_count, tw, features,
        neighbour_weight_first, w_self1,
    )
    tables, packs, (sel, xo, wo, so) = planned[:CHUNKS], planned[CHUNKS:2 * CHUNKS], planned[2 * CHUNKS:]
    done = []
    for chunk in range(CHUNKS):
        parts = neighbour_terms(chunk, per, n, 4, groups, ids, tables[chunk], packs[chunk], xo, xp, wo, wp, so, sp)
        got = exchange(parts, 1, n)
        stride = 4
        left = n // 4
        for radix in radices[1:]:
            ways = 1 << radix
            got = [a.reshape(left, per * UNIT, -1) for a in got]
            left //= ways
            parts = []
            for k in range(ways):
                total = got[0][k::ways]
                for a in got[1:]:
                    total = total + a[k::ways]
                parts.append(total.reshape(left * per * UNIT, -1))
            got = exchange(parts, stride, n)
            stride *= ways
        done.append(got)
    own = hidden_rows(done)
    other = lax.ppermute(own, "feat", swap)
    hidden, send = rows_to_send(groups, ids, own, other, sel)
    received = lax.all_to_all(send, "dom", 0, 0, tiled=True)
    return logits_of(hidden, received, adj_two, w_self2, w_neigh2)


def solution(mesh):
    in_specs = (
        P("dom", "feat"),
        P("dom", None, None),
        P("dom"),
        P("dom"),
        P("dom"),
        P("feat", None),
        P("feat", None),
        P(),
        P(),
        P("dom", None),
        P(),
        P(),
    )
    out_specs = P("dom", None)
    return jax.shard_map(body, mesh=mesh, in_specs=in_specs, out_specs=out_specs, check_vma=False)
```

```python
import functools

import jax
import jax.numpy as jnp
from jax import lax
from jax.experimental import pallas as pl
from jax.experimental.pallas import tpu as pltpu
from jax.sharding import PartitionSpec as P

UNIT = 16
BLOCK = 8
STEP = 4
LEAD = 2
CHUNKS = 1


def group_of(core, place, groups):
    pair = 2 * (place // 2) + core
    return pair if place % 2 == 0 else groups - 1 - pair


LN2 = 0.6931471805599453


def tail_rows(slots):
    return -(-slots // 16) * 16


def encode(x):
    top = jnp.max(jnp.abs(x), axis=0, keepdims=True)
    power = jnp.ceil(jnp.log(jnp.maximum(top, 1e-30)) * (1.0 / LN2) + 1e-3) - 15.0
    return jnp.floor(x * jnp.exp(power * -LN2) + 0.5), power


def to_int16(x):
    return x.astype(jnp.int32).astype(jnp.int16)


def write_coded(out, tail, slots, rows, value_of):
    tail[...] = jnp.zeros_like(tail)
    for s in range(slots):
        whole, power = encode(value_of(s))
        out[s * rows:(s + 1) * rows, :] = to_int16(whole)
        tail[s:s + 1, :] = power
    out[slots * rows:, :] = to_int16(tail[...])


def read_coded(ref, slots, rows):
    powers = ref[slots * rows:, :].astype(jnp.int32).astype(jnp.float32)

    def value_of(s):
        whole = ref[s * rows:(s + 1) * rows, :].astype(jnp.int32).astype(jnp.float32)
        return whole * jnp.exp(powers[s:s + 1, :] * LN2)

    return value_of


def plan_kernel(chunks, per, n, radix, n_src, ids, src_h, rows_h, dst_h, lists_h, counts_h, tw, xo, wo, so, *rest):
    tables, rest = rest[:chunks], rest[chunks:]
    packs, rest = rest[:chunks], rest[chunks:]
    sel, xo_out, wo_out, so_out = rest[:4]
    src_v, rows_v, dst_v, lists, counts, tbuf, masks, table_s, sems = rest[4:]
    core, me = ids[0], ids[1]
    tiles = src_v.shape[1]
    tile = tw.shape[3]
    lead = LEAD * STEP * BLOCK
    n_pos = tables[0].shape[1]
    units = per * tiles
    groups = 2 * per * chunks
    half = groups // 2
    gs = [group_of(core, i, groups) for i in range(half)]
    small = [(src_h, src_v), (rows_h, rows_v), (dst_h, dst_v), (lists_h, lists), (counts_h, counts)]
    large = [(tw.at[:, g], tbuf.at[pl.ds(i * tiles, tiles)]) for i, g in enumerate(gs)]
    large += [(xo, xo_out), (wo, wo_out), (so, so_out)]
    copies = [pltpu.make_async_copy(a, b, sems.at[i]) for i, (a, b) in enumerate(small + large)]
    for c in copies:
        c.start()
    row_i = lax.broadcasted_iota(jnp.int32, (UNIT, tile), 0)
    for m in range(UNIT + 1):
        masks[m] = jnp.where(row_i < m, 1.0, 0.0).astype(jnp.bfloat16)
    lane = lax.broadcasted_iota(jnp.int32, (1, tiles), 1)
    block_i = lax.broadcasted_iota(jnp.int32, (n_src, tiles), 0)
    before = lax.broadcasted_iota(jnp.int32, (units, units), 0) < lax.broadcasted_iota(jnp.int32, (units, units), 1)
    before = jnp.where(before, 1.0, 0.0).astype(jnp.bfloat16)
    pos_i = lax.broadcasted_iota(jnp.int32, (tiles, n_pos), 1).astype(jnp.float32)
    place_i = lax.broadcasted_iota(jnp.int32, (1, n_pos), 1)
    trash = float(n * per << 14)
    for c in copies[:5]:
        c.wait()
    src, rows = src_v[...], rows_v[...]
    slot = jnp.bitwise_xor(dst_v[...], me)
    slot = jnp.bitwise_and(slot, radix - 1) * (n // radix) + lax.div(slot, radix)
    to_scalar = []
    for c in range(chunks):
        hot, words, valid = [], [], []
        for j in range(per):
            limit = jnp.clip(rows - UNIT * gs[c * per + j], 0, UNIT)
            ok = limit > 0
            valid.append(ok)
            words.append(((slot * per + j) * 512 + (j * tiles + lane)) * 32 + limit)
            hot.append(jnp.where(jnp.logical_and(block_i == src, ok), 1.0, 0.0))
        hot = jnp.concatenate(hot, axis=1)
        earlier = jnp.dot(hot.astype(jnp.bfloat16), before, preferred_element_type=jnp.float32)
        blocks = jnp.floor((jnp.sum(hot, axis=1, keepdims=True) + (BLOCK - 1)) * (1.0 / BLOCK))
        run = jnp.zeros((1, 1), jnp.float32)
        pos = jnp.zeros((1, units), jnp.float32)
        owner = jnp.zeros((1, n_pos), jnp.float32)
        for s in range(n_src):
            pos = pos + hot[s:s + 1, :] * (earlier[s:s + 1, :] + (run * BLOCK + lead))
            run = run + blocks[s:s + 1, :]
            owner = owner + jnp.where(place_i.astype(jnp.float32) >= run, 1.0, 0.0)
        stack = [jnp.where(valid[j], pos[:, j * tiles:(j + 1) * tiles], -1.0) for j in range(per)]
        stack += [w.astype(jnp.float32) - trash for w in words]
        stack += [jnp.zeros((1, tiles), jnp.float32)] * (-len(stack) % 8)
        cols = jnp.concatenate(stack, axis=0).T
        found = jnp.zeros((tiles, n_pos), jnp.float32)
        for j in range(per):
            found = found + jnp.where(cols[:, j:j + 1] == pos_i, cols[:, per + j:per + j + 1], 0.0)
        word = jnp.sum(found, axis=0, keepdims=True) + trash
        owner = jnp.where(place_i == n_pos - 1, run, jnp.minimum(owner, n_src - 1.0))
        tables[c][0:1, :] = word.astype(jnp.int32)
        tables[c][1:2, :] = owner.astype(jnp.int32)
        copy = pltpu.make_async_copy(tables[c], table_s.at[c], sems.at[len(copies) + c])
        copy.start()
        to_scalar.append(copy)

    slots = lists.shape[1]
    total = n * slots
    q_n = lax.broadcasted_iota(jnp.int32, (total, n), 0)
    r_n = lax.broadcasted_iota(jnp.int32, (total, n), 1)
    mine = lists[me].astype(jnp.float32)
    cnt = counts[pl.ds(me, 1), :]
    picked = jnp.zeros((total, n), jnp.float32)
    k_n = jnp.bitwise_and(q_n, slots - 1)
    for k in range(slots):
        picked = jnp.where(k_n == k, mine[k:k + 1, :], picked)
    good = jnp.logical_and(lax.div(q_n, slots) == r_n, k_n < cnt)
    row = jnp.sum(jnp.where(good, picked + 1.0, 0.0), axis=1, keepdims=True) - 1.0
    lane = lax.broadcasted_iota(jnp.int32, (1, sel.shape[1]), 1).astype(jnp.float32)
    sel[...] = jnp.where(row == lane, 1.0, 0.0).astype(jnp.bfloat16)

    for c in copies[5:5 + half]:
        c.wait()
    for c in range(chunks):
        to_scalar[c].wait()

        def block(b, carry):
            for k in range(BLOCK):
                word = table_s[c, 0, lead + b * BLOCK + k]
                u = jnp.bitwise_and(lax.shift_right_logical(word, 5), 511) + c * units
                at = pl.multiple_of((b * BLOCK + k) * UNIT, UNIT)
                packs[c][pl.ds(at, UNIT), :] = tbuf[u] * masks[jnp.bitwise_and(word, 31)]
            return carry

        lax.fori_loop(0, table_s[c, 1, n_pos - 1], block, 0)
    for c in copies[5 + half:]:
        c.wait()


def plan(chunks, per, n, radix, ids, src, rows, dst, send_list, send_count, tw, xo, wo, so):
    tiles, _, _, tile = tw.shape
    slots = send_list.shape[2]
    n_src = xo.shape[0] // tile
    blocks = -(-(per * tiles // BLOCK + n_src) // STEP + -LEAD) * STEP
    n_pos = -(-((LEAD * STEP + blocks) * BLOCK + 1) // 128) * 128
    smem = pl.BlockSpec(memory_space=pltpu.SMEM)
    vmem = pl.BlockSpec(memory_space=pltpu.VMEM)
    hbm = pl.BlockSpec(memory_space=pltpu.HBM)
    lists = jnp.swapaxes(send_list, 1, 2)
    half = chunks * per
    return pl.pallas_call(
        functools.partial(plan_kernel, chunks, per, n, radix, n_src),
        out_shape=[jax.ShapeDtypeStruct((2, n_pos), jnp.int32)] * chunks
        + [jax.ShapeDtypeStruct((blocks * BLOCK * UNIT, tile), tw.dtype)] * chunks
        + [
            jax.ShapeDtypeStruct((n * slots, 2 * half * UNIT), jnp.bfloat16),
            jax.ShapeDtypeStruct(xo.shape, xo.dtype),
            jax.ShapeDtypeStruct(wo.shape, wo.dtype),
            jax.ShapeDtypeStruct(so.shape, so.dtype),
        ],
        in_specs=[smem] + [hbm] * 9,
        out_specs=[vmem] * (2 * chunks + 4),
        scratch_shapes=[
            pltpu.VMEM((1, tiles), jnp.int32),
            pltpu.VMEM((1, tiles), jnp.int32),
            pltpu.VMEM((1, tiles), jnp.int32),
            pltpu.VMEM(lists.shape, jnp.int32),
            pltpu.VMEM(send_count.shape, jnp.int32),
            pltpu.VMEM((half * tiles, UNIT, tile), tw.dtype),
            pltpu.VMEM((UNIT + 1, UNIT, tile), jnp.bfloat16),
            pltpu.SMEM((chunks, 2, n_pos), jnp.int32),
            pltpu.SemaphoreType.DMA((5 + half + 3 + chunks,)),
        ],
        compiler_params=pltpu.CompilerParams(vmem_limit_bytes=32 * 1024 * 1024),
        name="plan",
    )(ids, *[
        pltpu.with_memory_space_constraint(a, pltpu.HBM)
        for a in (src.reshape(1, tiles), rows.reshape(1, tiles), dst.reshape(1, tiles), lists, send_count, tw, xo, wo, so)
    ])


def tiles_kernel(chunk, per, n, radix, groups, ids, table, packed, xo, xp, wo, wp, so, sp, *rest):
    acc, outs, rest = rest[0], rest[1:radix], rest[radix:]
    wbuf, gath, res, tail, sems = rest
    tile = packed.shape[1]
    width = xo.shape[1]
    core = ids[0]
    copies = [
        pltpu.make_async_copy(wo, wbuf.at[pl.ds(0, width)], sems.at[0]),
        pltpu.make_async_copy(wp, wbuf.at[pl.ds(width, width)], sems.at[1]),
    ]
    for c in copies:
        c.start()
    acc[...] = jnp.zeros_like(acc)
    for j in range(per):
        at = pl.multiple_of(group_of(core, chunk * per + j, groups) * UNIT, UNIT)
        own = jnp.dot(xo[pl.ds(at, UNIT), :], so[...], preferred_element_type=jnp.float32)
        own = own + jnp.dot(xp[pl.ds(at, UNIT), :], sp[...], preferred_element_type=jnp.float32)
        acc[j * UNIT:(j + 1) * UNIT, :] = own
    for c in copies:
        c.wait()

    size = BLOCK * UNIT

    def step(i, carry):
        for k in range(STEP * BLOCK):
            word = table[0, i * (STEP * BLOCK) + k]
            at = pl.multiple_of(lax.shift_right_logical(word, 14) * UNIT, UNIT)
            acc[pl.ds(at, UNIT), :] += res[k * UNIT:(k + 1) * UNIT, :]
        res[...] = jnp.dot(gath[...], wbuf[...], preferred_element_type=jnp.float32)
        for m in range(STEP):
            base = pl.multiple_of(table[1, i * STEP + m] * tile, tile)
            lhs = packed[pl.ds(pl.multiple_of((i * STEP + m) * size, size), size), :]
            for q, x in enumerate((xo, xp)):
                for h in range(0, width, 256):
                    got = jnp.dot(lhs, x[pl.ds(base, tile), h:h + 256], preferred_element_type=jnp.float32)
                    gath[m * size:(m + 1) * size, q * width + h:q * width + h + 256] = got.astype(jnp.bfloat16)
        return carry

    steps = lax.div(table[1, table.shape[1] - 1] + STEP - 1, STEP)
    lax.fori_loop(0, steps + LEAD, step, 0)
    slots, rows = n // radix, per * UNIT
    for k, out in enumerate(outs, 1):
        write_coded(out, tail, slots, rows, lambda s: acc[(k * slots + s) * rows:(k * slots + s + 1) * rows, :])


def neighbour_terms(chunk, per, n, radix, groups, ids, table, packed, xo, xp, wo, wp, so, sp):
    hidden = wo.shape[1]
    width = xo.shape[1]
    tile = packed.shape[1]
    smem = pl.BlockSpec(memory_space=pltpu.SMEM)
    vmem = pl.BlockSpec(memory_space=pltpu.VMEM)
    flops = 2 * packed.shape[0] * (tile * 2 * width + 2 * width * hidden)
    sums = (n * per + 1) * UNIT * hidden * 4
    slots, rows = n // radix, per * UNIT
    coded = jax.ShapeDtypeStruct((slots * rows + tail_rows(slots), hidden), jnp.int16)
    return pl.pallas_call(
        functools.partial(tiles_kernel, chunk, per, n, radix, groups),
        out_shape=[jax.ShapeDtypeStruct(((n * per + 1) * UNIT, hidden), jnp.float32)] + [coded] * (radix - 1),
        in_specs=[smem] * 2 + [vmem] * 7,
        out_specs=[vmem] * radix,
        scratch_shapes=[
            pltpu.VMEM((2 * width, hidden), wo.dtype),
            pltpu.VMEM((STEP * BLOCK * UNIT, 2 * width), jnp.bfloat16),
            pltpu.VMEM((STEP * BLOCK * UNIT, hidden), jnp.float32),
            pltpu.VMEM((tail_rows(slots), hidden), jnp.float32),
            pltpu.SemaphoreType.DMA((2,)),
        ],
        compiler_params=pltpu.CompilerParams(vmem_limit_bytes=(16 << 20) + 2 * sums),
        cost_estimate=pl.CostEstimate(flops=flops, bytes_accessed=8 << 20, transcendentals=0),
        name="neighbour_terms",
    )(ids, table, packed, xo, xp, wo, wp, so, sp)


def combine_kernel(slots, rows, ways, own, *refs):
    parts = len(refs) - ways - 1
    coded, outs, tail = refs[:parts], refs[parts:parts + ways], refs[parts + ways]
    values = [read_coded(a, slots, rows) for a in coded]

    def total(s):
        got = own[s * rows:(s + 1) * rows, :]
        for value in values:
            got = got + value(s)
        return got

    for i in range(slots // ways):
        outs[0][i * rows:(i + 1) * rows, :] = total(i * ways)
    for k in range(1, ways):
        write_coded(outs[k], tail, slots // ways, rows, lambda s: total(s * ways + k))


def combine(slots, rows, ways, own, coded):
    width = own.shape[1]
    left = slots // ways
    vmem = pl.BlockSpec(memory_space=pltpu.VMEM)
    out = jax.ShapeDtypeStruct((left * rows + tail_rows(left), width), jnp.int16)
    return pl.pallas_call(
        functools.partial(combine_kernel, slots, rows, ways),
        out_shape=[jax.ShapeDtypeStruct((left * rows, width), jnp.float32)] + [out] * (ways - 1),
        in_specs=[vmem] * (1 + len(coded)),
        out_specs=[vmem] * ways,
        scratch_shapes=[pltpu.VMEM((tail_rows(left), width), jnp.float32)],
        compiler_params=pltpu.CompilerParams(vmem_limit_bytes=32 * 1024 * 1024),
        name="combine",
    )(own, *coded)


def hidden_kernel(chunks, parts, rows, *refs):
    out = refs[chunks * parts]
    for c in range(chunks):
        own, coded = refs[c * parts], refs[c * parts + 1:(c + 1) * parts]
        total = own[:rows, :]
        for a in coded:
            total = total + read_coded(a, 1, rows)(0)
        out[c * rows:(c + 1) * rows, :] = jnp.maximum(total, 0.0).astype(jnp.bfloat16)


def hidden_rows(chunk_parts, rows):
    chunks, parts = len(chunk_parts), len(chunk_parts[0])
    width = chunk_parts[0][0].shape[1]
    vmem = pl.BlockSpec(memory_space=pltpu.VMEM)
    flat = [a for part in chunk_parts for a in part]
    return pl.pallas_call(
        functools.partial(hidden_kernel, chunks, parts, rows),
        out_shape=jax.ShapeDtypeStruct((chunks * rows, width), jnp.bfloat16),
        in_specs=[vmem] * len(flat),
        out_specs=vmem,
        compiler_params=pltpu.CompilerParams(vmem_limit_bytes=32 * 1024 * 1024),
        name="hidden_rows",
    )(*flat)


def send_kernel(groups, ids, own, other, sel, hidden, send):
    core = ids[0]
    for i in range(groups // 2):
        mine = group_of(core, i, groups)
        theirs = group_of(1 - core, i, groups)
        hidden[pl.ds(pl.multiple_of(mine * UNIT, UNIT), UNIT), :] = own[i * UNIT:(i + 1) * UNIT, :]
        hidden[pl.ds(pl.multiple_of(theirs * UNIT, UNIT), UNIT), :] = other[i * UNIT:(i + 1) * UNIT, :]
    send[...] = jnp.dot(sel[...], hidden[...], preferred_element_type=jnp.float32).astype(jnp.bfloat16)


def rows_to_send(groups, ids, own, other, sel):
    smem = pl.BlockSpec(memory_space=pltpu.SMEM)
    vmem = pl.BlockSpec(memory_space=pltpu.VMEM)
    width = own.shape[1]
    return pl.pallas_call(
        functools.partial(send_kernel, groups),
        out_shape=[
            jax.ShapeDtypeStruct((groups * UNIT, width), jnp.bfloat16),
            jax.ShapeDtypeStruct((sel.shape[0], width), jnp.bfloat16),
        ],
        in_specs=[smem] + [vmem] * 3,
        out_specs=[vmem] * 2,
        compiler_params=pltpu.CompilerParams(vmem_limit_bytes=32 * 1024 * 1024),
        name="rows_to_send",
    )(ids, own, other, sel)


def logits_kernel(hidden, received, adj, w_self, w_neigh, out):
    tile, rows = hidden.shape[0], adj.shape[0]
    mean = jnp.dot(adj[:, :tile], hidden[...], preferred_element_type=jnp.float32)
    mean = mean + jnp.dot(adj[:, tile:], received[...], preferred_element_type=jnp.float32)
    dims = (((1,), (1,)), ((), ()))
    got = lax.dot_general(hidden[:rows, :], w_self[...], dims, preferred_element_type=jnp.float32)
    got = got + lax.dot_general(mean.astype(jnp.bfloat16), w_neigh[...], dims, preferred_element_type=jnp.float32)
    out[...] = got


def logits_of(hidden, received, adj, w_self, w_neigh):
    vmem = pl.BlockSpec(memory_space=pltpu.VMEM)
    return pl.pallas_call(
        logits_kernel,
        out_shape=jax.ShapeDtypeStruct((adj.shape[0], w_self.shape[1]), jnp.float32),
        in_specs=[vmem] * 5,
        out_specs=vmem,
        compiler_params=pltpu.CompilerParams(vmem_limit_bytes=32 * 1024 * 1024),
        name="logits",
    )(hidden, received, adj, w_self.T, w_neigh.T)


def exchange(parts, stride, n):
    got = [parts[0]]
    for k in range(1, len(parts)):
        got.append(lax.ppermute(parts[k], "dom", [(i, i ^ (k * stride)) for i in range(n)]))
    return got


def body(
    features,
    tile_weight,
    tile_dst,
    tile_src,
    tile_rows,
    w_self1,
    neighbour_weight_first,
    send_list,
    send_count,
    adj_two,
    w_self2,
    w_neigh2,
):
    n = lax.axis_size("dom")
    tile = tile_weight.shape[1]
    groups = tile // UNIT
    per = groups // 2 // CHUNKS
    bits = n.bit_length() - 1
    assert n == 1 << bits and bits >= 2
    radices = [2] * (bits // 2) + [1] * (bits % 2)
    ids = jnp.stack([lax.axis_index("feat"), lax.axis_index("dom")]).astype(jnp.int32)
    swap = [(0, 1), (1, 0)]
    xp = lax.ppermute(features, "feat", swap)
    wp = lax.ppermute(neighbour_weight_first, "feat", swap)
    sp = lax.ppermute(w_self1, "feat", swap)
    tw = tile_weight.reshape(tile_weight.shape[0], groups, UNIT, tile)
    planned = plan(
        CHUNKS, per, n, 4, ids, tile_src, tile_rows, tile_dst, send_list, send_count, tw, features,
        neighbour_weight_first, w_self1,
    )
    tables, packs, (sel, xo, wo, so) = planned[:CHUNKS], planned[CHUNKS:2 * CHUNKS], planned[2 * CHUNKS:]
    done = []
    for chunk in range(CHUNKS):
        parts = neighbour_terms(chunk, per, n, 4, groups, ids, tables[chunk], packs[chunk], xo, xp, wo, wp, so, sp)
        got = exchange(parts, 1, n)
        stride = 4
        for radix in radices[1:]:
            ways = 1 << radix
            parts = combine(n // stride, per * UNIT, ways, got[0], got[1:])
            got = exchange(parts, stride, n)
            stride *= ways
        done.append(got)
    own = hidden_rows(done, per * UNIT)
    other = lax.ppermute(own, "feat", swap)
    hidden, send = rows_to_send(groups, ids, own, other, sel)
    received = lax.all_to_all(send, "dom", 0, 0, tiled=True)
    return logits_of(hidden, received, adj_two, w_self2, w_neigh2)


def solution(mesh):
    in_specs = (
        P("dom", "feat"),
        P("dom", None, None),
        P("dom"),
        P("dom"),
        P("dom"),
        P("feat", None),
        P("feat", None),
        P(),
        P(),
        P("dom", None),
        P(),
        P(),
    )
    out_specs = P("dom", None)
    return jax.shard_map(body, mesh=mesh, in_specs=in_specs, out_specs=out_specs, check_vma=False)
```

```python
import functools

import jax
import jax.numpy as jnp
from jax import lax
from jax.experimental import pallas as pl
from jax.experimental.pallas import tpu as pltpu
from jax.sharding import PartitionSpec as P

UNIT = 16
BLOCK = 8
STEP = 4
LEAD = 2
CHUNKS = 1


def group_of(core, place, groups):
    pair = 2 * (place // 2) + core
    return pair if place % 2 == 0 else groups - 1 - pair


LN2 = 0.6931471805599453


def tail_rows(slots):
    return -(-slots // 16) * 16


def encode(x):
    top = jnp.max(jnp.abs(x), axis=0, keepdims=True)
    power = jnp.ceil(jnp.log(jnp.maximum(top, 1e-30)) * (1.0 / LN2) + 1e-3) - 15.0
    return jnp.floor(x * jnp.exp(power * -LN2) + 0.5), power


def to_int16(x):
    return x.astype(jnp.int32).astype(jnp.int16)


def write_coded(out, tail, slots, rows, value_of):
    tail[...] = jnp.zeros_like(tail)
    for s in range(slots):
        whole, power = encode(value_of(s))
        out[s * rows:(s + 1) * rows, :] = to_int16(whole)
        tail[s:s + 1, :] = power
    out[slots * rows:, :] = to_int16(tail[...])


def read_coded(ref, slots, rows):
    powers = ref[slots * rows:, :].astype(jnp.int32).astype(jnp.float32)

    def value_of(s):
        whole = ref[s * rows:(s + 1) * rows, :].astype(jnp.int32).astype(jnp.float32)
        return whole * jnp.exp(powers[s:s + 1, :] * LN2)

    return value_of


def plan_kernel(chunks, per, n, radix, n_src, ids, src_h, rows_h, dst_h, lists_h, counts_h, tw, xo, wo, so, *rest):
    tables, rest = rest[:chunks], rest[chunks:]
    packs, rest = rest[:chunks], rest[chunks:]
    sel, xo_out, wo_out, so_out = rest[:4]
    src_v, rows_v, dst_v, lists, counts, tbuf, masks, table_s, sems = rest[4:]
    core, me = ids[0], ids[1]
    tiles = src_v.shape[1]
    tile = tw.shape[3]
    lead = LEAD * STEP * BLOCK
    n_pos = tables[0].shape[1]
    units = per * tiles
    groups = 2 * per * chunks
    half = groups // 2
    gs = [group_of(core, i, groups) for i in range(half)]
    small = [(src_h, src_v), (rows_h, rows_v), (dst_h, dst_v), (lists_h, lists), (counts_h, counts)]
    large = [(tw.at[:, g], tbuf.at[pl.ds(i * tiles, tiles)]) for i, g in enumerate(gs)]
    large += [(xo, xo_out), (wo, wo_out), (so, so_out)]
    copies = [pltpu.make_async_copy(a, b, sems.at[i]) for i, (a, b) in enumerate(small + large)]
    for c in copies:
        c.start()
    row_i = lax.broadcasted_iota(jnp.int32, (UNIT, tile), 0)
    for m in range(UNIT + 1):
        masks[m] = jnp.where(row_i < m, 1.0, 0.0).astype(jnp.bfloat16)
    lane = lax.broadcasted_iota(jnp.int32, (1, tiles), 1)
    block_i = lax.broadcasted_iota(jnp.int32, (n_src, tiles), 0)
    before = lax.broadcasted_iota(jnp.int32, (units, units), 0) < lax.broadcasted_iota(jnp.int32, (units, units), 1)
    before = jnp.where(before, 1.0, 0.0).astype(jnp.bfloat16)
    pos_i = lax.broadcasted_iota(jnp.int32, (tiles, n_pos), 1).astype(jnp.float32)
    place_i = lax.broadcasted_iota(jnp.int32, (1, n_pos), 1)
    trash = float(n * per << 14)
    for c in copies[:5]:
        c.wait()
    src, rows = src_v[...], rows_v[...]
    slot = jnp.bitwise_xor(dst_v[...], me)
    slot = jnp.bitwise_and(slot, radix - 1) * (n // radix) + lax.div(slot, radix)
    to_scalar = []
    for c in range(chunks):
        hot, words, valid = [], [], []
        for j in range(per):
            limit = jnp.clip(rows - UNIT * gs[c * per + j], 0, UNIT)
            ok = limit > 0
            valid.append(ok)
            words.append(((slot * per + j) * 512 + (j * tiles + lane)) * 32 + limit)
            hot.append(jnp.where(jnp.logical_and(block_i == src, ok), 1.0, 0.0))
        hot = jnp.concatenate(hot, axis=1)
        earlier = jnp.dot(hot.astype(jnp.bfloat16), before, preferred_element_type=jnp.float32)
        blocks = jnp.floor((jnp.sum(hot, axis=1, keepdims=True) + (BLOCK - 1)) * (1.0 / BLOCK))
        run = jnp.zeros((1, 1), jnp.float32)
        pos = jnp.zeros((1, units), jnp.float32)
        owner = jnp.zeros((1, n_pos), jnp.float32)
        for s in range(n_src):
            pos = pos + hot[s:s + 1, :] * (earlier[s:s + 1, :] + (run * BLOCK + lead))
            run = run + blocks[s:s + 1, :]
            owner = owner + jnp.where(place_i.astype(jnp.float32) >= run, 1.0, 0.0)
        stack = [jnp.where(valid[j], pos[:, j * tiles:(j + 1) * tiles], -1.0) for j in range(per)]
        stack += [w.astype(jnp.float32) - trash for w in words]
        stack += [jnp.zeros((1, tiles), jnp.float32)] * (-len(stack) % 8)
        cols = jnp.concatenate(stack, axis=0).T
        found = jnp.zeros((tiles, n_pos), jnp.float32)
        for j in range(per):
            found = found + jnp.where(cols[:, j:j + 1] == pos_i, cols[:, per + j:per + j + 1], 0.0)
        word = jnp.sum(found, axis=0, keepdims=True) + trash
        owner = jnp.where(place_i == n_pos - 1, run, jnp.minimum(owner, n_src - 1.0))
        tables[c][0:1, :] = word.astype(jnp.int32)
        tables[c][1:2, :] = owner.astype(jnp.int32)
        copy = pltpu.make_async_copy(tables[c], table_s.at[c], sems.at[len(copies) + c])
        copy.start()
        to_scalar.append(copy)

    slots = lists.shape[1]
    total = n * slots
    q_n = lax.broadcasted_iota(jnp.int32, (total, n), 0)
    r_n = lax.broadcasted_iota(jnp.int32, (total, n), 1)
    mine = lists[me].astype(jnp.float32)
    cnt = counts[pl.ds(me, 1), :]
    picked = jnp.zeros((total, n), jnp.float32)
    k_n = jnp.bitwise_and(q_n, slots - 1)
    for k in range(slots):
        picked = jnp.where(k_n == k, mine[k:k + 1, :], picked)
    block = lax.div(q_n, slots)
    apart = jnp.bitwise_and(block, n // radix - 1) * radix + lax.div(block, n // radix)
    good = jnp.logical_and(jnp.bitwise_xor(apart, me) == r_n, k_n < cnt)
    row = jnp.sum(jnp.where(good, picked + 1.0, 0.0), axis=1, keepdims=True) - 1.0
    lane = lax.broadcasted_iota(jnp.int32, (1, sel.shape[1]), 1).astype(jnp.float32)
    sel[...] = jnp.where(row == lane, 1.0, 0.0).astype(jnp.bfloat16)

    for c in copies[5:5 + half]:
        c.wait()
    for c in range(chunks):
        to_scalar[c].wait()

        def block(b, carry):
            for k in range(BLOCK):
                word = table_s[c, 0, lead + b * BLOCK + k]
                u = jnp.bitwise_and(lax.shift_right_logical(word, 5), 511) + c * units
                at = pl.multiple_of((b * BLOCK + k) * UNIT, UNIT)
                packs[c][pl.ds(at, UNIT), :] = tbuf[u] * masks[jnp.bitwise_and(word, 31)]
            return carry

        lax.fori_loop(0, table_s[c, 1, n_pos - 1], block, 0)
    for c in copies[5 + half:]:
        c.wait()


def plan(chunks, per, n, radix, ids, src, rows, dst, send_list, send_count, tw, xo, wo, so):
    tiles, _, _, tile = tw.shape
    slots = send_list.shape[2]
    n_src = xo.shape[0] // tile
    blocks = -(-(per * tiles // BLOCK + n_src) // STEP + -LEAD) * STEP
    n_pos = -(-((LEAD * STEP + blocks) * BLOCK + 1) // 128) * 128
    smem = pl.BlockSpec(memory_space=pltpu.SMEM)
    vmem = pl.BlockSpec(memory_space=pltpu.VMEM)
    hbm = pl.BlockSpec(memory_space=pltpu.HBM)
    lists = jnp.swapaxes(send_list, 1, 2)
    half = chunks * per
    return pl.pallas_call(
        functools.partial(plan_kernel, chunks, per, n, radix, n_src),
        out_shape=[jax.ShapeDtypeStruct((2, n_pos), jnp.int32)] * chunks
        + [jax.ShapeDtypeStruct((blocks * BLOCK * UNIT, tile), tw.dtype)] * chunks
        + [
            jax.ShapeDtypeStruct((n * slots, 2 * half * UNIT), jnp.bfloat16),
            jax.ShapeDtypeStruct(xo.shape, xo.dtype),
            jax.ShapeDtypeStruct(wo.shape, wo.dtype),
            jax.ShapeDtypeStruct(so.shape, so.dtype),
        ],
        in_specs=[smem] + [hbm] * 9,
        out_specs=[vmem] * (2 * chunks + 4),
        scratch_shapes=[
            pltpu.VMEM((1, tiles), jnp.int32),
            pltpu.VMEM((1, tiles), jnp.int32),
            pltpu.VMEM((1, tiles), jnp.int32),
            pltpu.VMEM(lists.shape, jnp.int32),
            pltpu.VMEM(send_count.shape, jnp.int32),
            pltpu.VMEM((half * tiles, UNIT, tile), tw.dtype),
            pltpu.VMEM((UNIT + 1, UNIT, tile), jnp.bfloat16),
            pltpu.SMEM((chunks, 2, n_pos), jnp.int32),
            pltpu.SemaphoreType.DMA((5 + half + 3 + chunks,)),
        ],
        compiler_params=pltpu.CompilerParams(vmem_limit_bytes=32 * 1024 * 1024),
        name="plan",
    )(ids, *[
        pltpu.with_memory_space_constraint(a, pltpu.HBM)
        for a in (src.reshape(1, tiles), rows.reshape(1, tiles), dst.reshape(1, tiles), lists, send_count, tw, xo, wo, so)
    ])


def tiles_kernel(chunk, per, n, radix, groups, ids, table, packed, xo, xp, wo, wp, so, sp, *rest):
    acc, outs, rest = rest[0], rest[1:radix], rest[radix:]
    wbuf, gath, res, tail, sems = rest
    tile = packed.shape[1]
    width = xo.shape[1]
    core = ids[0]
    copies = [
        pltpu.make_async_copy(wo, wbuf.at[pl.ds(0, width)], sems.at[0]),
        pltpu.make_async_copy(wp, wbuf.at[pl.ds(width, width)], sems.at[1]),
    ]
    for c in copies:
        c.start()
    acc[...] = jnp.zeros_like(acc)
    for j in range(per):
        at = pl.multiple_of(group_of(core, chunk * per + j, groups) * UNIT, UNIT)
        own = jnp.dot(xo[pl.ds(at, UNIT), :], so[...], preferred_element_type=jnp.float32)
        own = own + jnp.dot(xp[pl.ds(at, UNIT), :], sp[...], preferred_element_type=jnp.float32)
        acc[j * UNIT:(j + 1) * UNIT, :] = own
    for c in copies:
        c.wait()

    size = BLOCK * UNIT

    def step(i, carry):
        for k in range(STEP * BLOCK):
            word = table[0, i * (STEP * BLOCK) + k]
            at = pl.multiple_of(lax.shift_right_logical(word, 14) * UNIT, UNIT)
            acc[pl.ds(at, UNIT), :] += res[k * UNIT:(k + 1) * UNIT, :]
        res[...] = jnp.dot(gath[...], wbuf[...], preferred_element_type=jnp.float32)
        for m in range(STEP):
            base = pl.multiple_of(table[1, i * STEP + m] * tile, tile)
            lhs = packed[pl.ds(pl.multiple_of((i * STEP + m) * size, size), size), :]
            for q, x in enumerate((xo, xp)):
                for h in range(0, width, 256):
                    got = jnp.dot(lhs, x[pl.ds(base, tile), h:h + 256], preferred_element_type=jnp.float32)
                    gath[m * size:(m + 1) * size, q * width + h:q * width + h + 256] = got.astype(jnp.bfloat16)
        return carry

    steps = lax.div(table[1, table.shape[1] - 1] + STEP - 1, STEP)
    lax.fori_loop(0, steps + LEAD, step, 0)
    slots, rows = n // radix, per * UNIT
    for k, out in enumerate(outs, 1):
        write_coded(out, tail, slots, rows, lambda s: acc[(k * slots + s) * rows:(k * slots + s + 1) * rows, :])


def neighbour_terms(chunk, per, n, radix, groups, ids, table, packed, xo, xp, wo, wp, so, sp):
    hidden = wo.shape[1]
    width = xo.shape[1]
    tile = packed.shape[1]
    smem = pl.BlockSpec(memory_space=pltpu.SMEM)
    vmem = pl.BlockSpec(memory_space=pltpu.VMEM)
    flops = 2 * packed.shape[0] * (tile * 2 * width + 2 * width * hidden)
    sums = (n * per + 1) * UNIT * hidden * 4
    slots, rows = n // radix, per * UNIT
    coded = jax.ShapeDtypeStruct((slots * rows + tail_rows(slots), hidden), jnp.int16)
    return pl.pallas_call(
        functools.partial(tiles_kernel, chunk, per, n, radix, groups),
        out_shape=[jax.ShapeDtypeStruct(((n * per + 1) * UNIT, hidden), jnp.float32)] + [coded] * (radix - 1),
        in_specs=[smem] * 2 + [vmem] * 7,
        out_specs=[vmem] * radix,
        scratch_shapes=[
            pltpu.VMEM((2 * width, hidden), wo.dtype),
            pltpu.VMEM((STEP * BLOCK * UNIT, 2 * width), jnp.bfloat16),
            pltpu.VMEM((STEP * BLOCK * UNIT, hidden), jnp.float32),
            pltpu.VMEM((tail_rows(slots), hidden), jnp.float32),
            pltpu.SemaphoreType.DMA((2,)),
        ],
        compiler_params=pltpu.CompilerParams(vmem_limit_bytes=(16 << 20) + 2 * sums),
        cost_estimate=pl.CostEstimate(flops=flops, bytes_accessed=8 << 20, transcendentals=0),
        name="neighbour_terms",
    )(ids, table, packed, xo, xp, wo, wp, so, sp)


def combine_kernel(slots, rows, ways, own, *refs):
    parts = len(refs) - ways - 1
    coded, outs, tail = refs[:parts], refs[parts:parts + ways], refs[parts + ways]
    values = [read_coded(a, slots, rows) for a in coded]

    def total(s):
        got = own[s * rows:(s + 1) * rows, :]
        for value in values:
            got = got + value(s)
        return got

    for i in range(slots // ways):
        outs[0][i * rows:(i + 1) * rows, :] = total(i * ways)
    for k in range(1, ways):
        write_coded(outs[k], tail, slots // ways, rows, lambda s: total(s * ways + k))


def combine(slots, rows, ways, own, coded):
    width = own.shape[1]
    left = slots // ways
    vmem = pl.BlockSpec(memory_space=pltpu.VMEM)
    out = jax.ShapeDtypeStruct((left * rows + tail_rows(left), width), jnp.int16)
    return pl.pallas_call(
        functools.partial(combine_kernel, slots, rows, ways),
        out_shape=[jax.ShapeDtypeStruct((left * rows, width), jnp.float32)] + [out] * (ways - 1),
        in_specs=[vmem] * (1 + len(coded)),
        out_specs=[vmem] * ways,
        scratch_shapes=[pltpu.VMEM((tail_rows(left), width), jnp.float32)],
        compiler_params=pltpu.CompilerParams(vmem_limit_bytes=32 * 1024 * 1024),
        name="combine",
    )(own, *coded)


def hidden_kernel(chunks, parts, rows, *refs):
    out = refs[chunks * parts]
    for c in range(chunks):
        own, coded = refs[c * parts], refs[c * parts + 1:(c + 1) * parts]
        total = own[:rows, :]
        for a in coded:
            total = total + read_coded(a, 1, rows)(0)
        out[c * rows:(c + 1) * rows, :] = jnp.maximum(total, 0.0).astype(jnp.bfloat16)


def hidden_rows(chunk_parts, rows):
    chunks, parts = len(chunk_parts), len(chunk_parts[0])
    width = chunk_parts[0][0].shape[1]
    vmem = pl.BlockSpec(memory_space=pltpu.VMEM)
    flat = [a for part in chunk_parts for a in part]
    return pl.pallas_call(
        functools.partial(hidden_kernel, chunks, parts, rows),
        out_shape=jax.ShapeDtypeStruct((chunks * rows, width), jnp.bfloat16),
        in_specs=[vmem] * len(flat),
        out_specs=vmem,
        compiler_params=pltpu.CompilerParams(vmem_limit_bytes=32 * 1024 * 1024),
        name="hidden_rows",
    )(*flat)


def send_kernel(groups, ways, ids, own, other, sel, hidden, *sends):
    core = ids[0]
    for i in range(groups // 2):
        mine = group_of(core, i, groups)
        theirs = group_of(1 - core, i, groups)
        hidden[pl.ds(pl.multiple_of(mine * UNIT, UNIT), UNIT), :] = own[i * UNIT:(i + 1) * UNIT, :]
        hidden[pl.ds(pl.multiple_of(theirs * UNIT, UNIT), UNIT), :] = other[i * UNIT:(i + 1) * UNIT, :]
    picked = jnp.dot(sel[...], hidden[...], preferred_element_type=jnp.float32).astype(jnp.bfloat16)
    rows = sel.shape[0] // ways
    for k in range(ways):
        sends[k][...] = picked[k * rows:(k + 1) * rows, :]


def rows_to_send(groups, ways, ids, own, other, sel):
    smem = pl.BlockSpec(memory_space=pltpu.SMEM)
    vmem = pl.BlockSpec(memory_space=pltpu.VMEM)
    width = own.shape[1]
    return pl.pallas_call(
        functools.partial(send_kernel, groups, ways),
        out_shape=[jax.ShapeDtypeStruct((groups * UNIT, width), jnp.bfloat16)]
        + [jax.ShapeDtypeStruct((sel.shape[0] // ways, width), jnp.bfloat16)] * ways,
        in_specs=[smem] + [vmem] * 3,
        out_specs=[vmem] * (1 + ways),
        compiler_params=pltpu.CompilerParams(vmem_limit_bytes=32 * 1024 * 1024),
        name="rows_to_send",
    )(ids, own, other, sel)


def regroup_kernel(had, left, ways, slots, *refs):
    parts = len(refs) - ways
    values = [a[...].astype(jnp.float32) for a in refs[:parts]]
    for k in range(ways):
        pieces = []
        for value in values:
            for p in range(had):
                for r in range(left // ways):
                    at = (p * left + r * ways + k) * slots
                    pieces.append(value[at:at + slots, :])
        refs[parts + k][...] = jnp.concatenate(pieces, axis=0).astype(jnp.bfloat16)


def regroup(had, left, ways, slots, arrays):
    rows, width = arrays[0].shape
    vmem = pl.BlockSpec(memory_space=pltpu.VMEM)
    out = jax.ShapeDtypeStruct((len(arrays) * rows // ways, width), jnp.bfloat16)
    return pl.pallas_call(
        functools.partial(regroup_kernel, had, left, ways, slots),
        out_shape=[out] * ways,
        in_specs=[vmem] * len(arrays),
        out_specs=[vmem] * ways,
        compiler_params=pltpu.CompilerParams(vmem_limit_bytes=32 * 1024 * 1024),
        name="regroup",
    )(*arrays)


def logits_kernel(order, slots, ids, hidden, adj, w_self, w_neigh, *refs):
    arrived, (out, pool) = refs[:-2], refs[-2:]
    me = ids[1]
    tile, rows = hidden.shape[0], adj.shape[0]
    at = 0
    for a in arrived:
        value = a[...].astype(jnp.float32)
        for i in range(a.shape[0] // slots):
            sender = jnp.bitwise_xor(me, order[at])
            pool[pl.ds(pl.multiple_of(sender * slots, slots), slots), :] = value[i * slots:(i + 1) * slots, :]
            at += 1
    mean = jnp.dot(adj[:, :tile], hidden[...], preferred_element_type=jnp.float32)
    mean = mean + jnp.dot(adj[:, tile:], pool[...].astype(jnp.bfloat16), preferred_element_type=jnp.float32)
    dims = (((1,), (1,)), ((), ()))
    got = lax.dot_general(hidden[:rows, :], w_self[...], dims, preferred_element_type=jnp.float32)
    got = got + lax.dot_general(mean.astype(jnp.bfloat16), w_neigh[...], dims, preferred_element_type=jnp.float32)
    out[...] = got


def logits_of(order, slots, ids, hidden, adj, w_self, w_neigh, arrived):
    smem = pl.BlockSpec(memory_space=pltpu.SMEM)
    vmem = pl.BlockSpec(memory_space=pltpu.VMEM)
    return pl.pallas_call(
        functools.partial(logits_kernel, order, slots),
        out_shape=jax.ShapeDtypeStruct((adj.shape[0], w_self.shape[1]), jnp.float32),
        in_specs=[smem] + [vmem] * (4 + len(arrived)),
        out_specs=vmem,
        scratch_shapes=[pltpu.VMEM((len(order) * slots, hidden.shape[1]), jnp.float32)],
        compiler_params=pltpu.CompilerParams(vmem_limit_bytes=32 * 1024 * 1024),
        name="logits",
    )(ids, hidden, adj, w_self.T, w_neigh.T, *arrived)


def exchange(parts, stride, n):
    got = [parts[0]]
    for k in range(1, len(parts)):
        got.append(lax.ppermute(parts[k], "dom", [(i, i ^ (k * stride)) for i in range(n)]))
    return got


def body(
    features,
    tile_weight,
    tile_dst,
    tile_src,
    tile_rows,
    w_self1,
    neighbour_weight_first,
    send_list,
    send_count,
    adj_two,
    w_self2,
    w_neigh2,
):
    n = lax.axis_size("dom")
    tile = tile_weight.shape[1]
    groups = tile // UNIT
    per = groups // 2 // CHUNKS
    bits = n.bit_length() - 1
    assert n == 1 << bits and bits >= 2
    radices = [2] * (bits // 2) + [1] * (bits % 2)
    ids = jnp.stack([lax.axis_index("feat"), lax.axis_index("dom")]).astype(jnp.int32)
    swap = [(0, 1), (1, 0)]
    xp = lax.ppermute(features, "feat", swap)
    wp = lax.ppermute(neighbour_weight_first, "feat", swap)
    sp = lax.ppermute(w_self1, "feat", swap)
    tw = tile_weight.reshape(tile_weight.shape[0], groups, UNIT, tile)
    planned = plan(
        CHUNKS, per, n, 4, ids, tile_src, tile_rows, tile_dst, send_list, send_count, tw, features,
        neighbour_weight_first, w_self1,
    )
    tables, packs, (sel, xo, wo, so) = planned[:CHUNKS], planned[CHUNKS:2 * CHUNKS], planned[2 * CHUNKS:]
    done = []
    for chunk in range(CHUNKS):
        parts = neighbour_terms(chunk, per, n, 4, groups, ids, tables[chunk], packs[chunk], xo, xp, wo, wp, so, sp)
        got = exchange(parts, 1, n)
        stride = 4
        for radix in radices[1:]:
            ways = 1 << radix
            parts = combine(n // stride, per * UNIT, ways, got[0], got[1:])
            got = exchange(parts, stride, n)
            stride *= ways
        done.append(got)
    own = hidden_rows(done, per * UNIT)
    other = lax.ppermute(own, "feat", swap)
    hidden, *sends = rows_to_send(groups, 4, ids, own, other, sel)
    slots = send_list.shape[2]
    arrived = exchange(sends, 1, n)
    stride, order = 4, [0]
    last = [k for k in range(4)]
    for radix in radices[1:]:
        ways = 1 << radix
        sends = regroup(len(order), n // stride, ways, slots, arrived)
        order = [k + v for k in last for v in order]
        arrived = exchange(sends, stride, n)
        last = [k * stride for k in range(ways)]
        stride *= ways
    order = tuple(k + v for k in last for v in order)
    return logits_of(order, slots, ids, hidden, adj_two, w_self2, w_neigh2, arrived)


def solution(mesh):
    in_specs = (
        P("dom", "feat"),
        P("dom", None, None),
        P("dom"),
        P("dom"),
        P("dom"),
        P("feat", None),
        P("feat", None),
        P(),
        P(),
        P("dom", None),
        P(),
        P(),
    )
    out_specs = P("dom", None)
    return jax.shard_map(body, mesh=mesh, in_specs=in_specs, out_specs=out_specs, check_vma=False)
```

```python
import functools

import jax
import jax.numpy as jnp
from jax import lax
from jax.experimental import pallas as pl
from jax.experimental.pallas import tpu as pltpu
from jax.sharding import PartitionSpec as P

UNIT = 16
BLOCK = 8
STEP = 8
PART = 256
CHUNKS = 1


def group_of(core, place, groups):
    pair = 2 * (place // 2) + core
    return pair if place % 2 == 0 else groups - 1 - pair


LN2 = 0.6931471805599453


def tail_rows(slots):
    return -(-slots // 16) * 16


def encode(x):
    top = jnp.max(jnp.abs(x), axis=0, keepdims=True)
    power = jnp.ceil(jnp.log(jnp.maximum(top, 1e-30)) * (1.0 / LN2) + 1e-3) - 15.0
    return jnp.floor(x * jnp.exp(power * -LN2) + 0.5), power


def to_int16(x):
    return x.astype(jnp.int32).astype(jnp.int16)


def write_coded(out, tail, slots, rows, value_of):
    tail[...] = jnp.zeros_like(tail)
    for s in range(slots):
        whole, power = encode(value_of(s))
        out[s * rows:(s + 1) * rows, :] = to_int16(whole)
        tail[s:s + 1, :] = power
    out[slots * rows:, :] = to_int16(tail[...])


def read_coded(ref, slots, rows):
    powers = ref[slots * rows:, :].astype(jnp.int32).astype(jnp.float32)

    def value_of(s):
        whole = ref[s * rows:(s + 1) * rows, :].astype(jnp.int32).astype(jnp.float32)
        return whole * jnp.exp(powers[s:s + 1, :] * LN2)

    return value_of


def plan_kernel(chunks, per, n, radix, n_src, ids, src_h, rows_h, dst_h, lists_h, counts_h, tw, xo, wo, so, *rest):
    tables, rest = rest[:chunks], rest[chunks:]
    tbufs, rest = rest[:chunks], rest[chunks:]
    sel, xo_out, wo_out, so_out = rest[:4]
    src_v, rows_v, dst_v, lists, counts, sems = rest[4:]
    core, me = ids[0], ids[1]
    tiles = src_v.shape[1]
    n_pos = tables[0].shape[1]
    units = per * tiles
    groups = 2 * per * chunks
    half = groups // 2
    gs = [group_of(core, i, groups) for i in range(half)]
    small = [(src_h, src_v), (rows_h, rows_v), (dst_h, dst_v), (lists_h, lists), (counts_h, counts)]
    large = [(tw.at[:, g], tbufs[i // per].at[pl.ds(i % per * tiles, tiles)]) for i, g in enumerate(gs)]
    large += [(xo, xo_out), (wo, wo_out), (so, so_out)]
    copies = [pltpu.make_async_copy(a, b, sems.at[i]) for i, (a, b) in enumerate(small + large)]
    for c in copies:
        c.start()
    lane = lax.broadcasted_iota(jnp.int32, (1, tiles), 1)
    block_i = lax.broadcasted_iota(jnp.int32, (n_src, tiles), 0)
    before = lax.broadcasted_iota(jnp.int32, (units, units), 0) < lax.broadcasted_iota(jnp.int32, (units, units), 1)
    before = jnp.where(before, 1.0, 0.0).astype(jnp.bfloat16)
    pos_i = lax.broadcasted_iota(jnp.int32, (tiles, n_pos), 1).astype(jnp.float32)
    place_i = lax.broadcasted_iota(jnp.int32, (1, n_pos), 1)
    trash = float(n * per << 14)
    for c in copies[:5]:
        c.wait()
    src, rows = src_v[...], rows_v[...]
    slot = jnp.bitwise_xor(dst_v[...], me)
    slot = jnp.bitwise_and(slot, radix - 1) * (n // radix) + lax.div(slot, radix)
    for c in range(chunks):
        hot, words, valid = [], [], []
        for j in range(per):
            limit = jnp.clip(rows - UNIT * gs[c * per + j], 0, UNIT)
            ok = limit > 0
            valid.append(ok)
            words.append(((slot * per + j) * 512 + (j * tiles + lane)) * 32 + limit)
            hot.append(jnp.where(jnp.logical_and(block_i == src, ok), 1.0, 0.0))
        hot = jnp.concatenate(hot, axis=1)
        earlier = jnp.dot(hot.astype(jnp.bfloat16), before, preferred_element_type=jnp.float32)
        blocks = jnp.floor((jnp.sum(hot, axis=1, keepdims=True) + (BLOCK - 1)) * (1.0 / BLOCK))
        run = jnp.zeros((1, 1), jnp.float32)
        pos = jnp.zeros((1, units), jnp.float32)
        owner = jnp.zeros((1, n_pos), jnp.float32)
        for s in range(n_src):
            pos = pos + hot[s:s + 1, :] * (earlier[s:s + 1, :] + run * BLOCK)
            run = run + blocks[s:s + 1, :]
            owner = owner + jnp.where(place_i.astype(jnp.float32) >= run, 1.0, 0.0)
        stack = [jnp.where(valid[j], pos[:, j * tiles:(j + 1) * tiles], -1.0) for j in range(per)]
        stack += [w.astype(jnp.float32) - trash for w in words]
        stack += [jnp.zeros((1, tiles), jnp.float32)] * (-len(stack) % 8)
        cols = jnp.concatenate(stack, axis=0).T
        found = jnp.zeros((tiles, n_pos), jnp.float32)
        for j in range(per):
            found = found + jnp.where(cols[:, j:j + 1] == pos_i, cols[:, per + j:per + j + 1], 0.0)
        word = jnp.sum(found, axis=0, keepdims=True) + trash
        owner = jnp.where(place_i == n_pos - 1, run, jnp.minimum(owner, n_src - 1.0))
        tables[c][0:1, :] = word.astype(jnp.int32)
        tables[c][1:2, :] = owner.astype(jnp.int32)

    slots = lists.shape[1]
    total = n * slots
    q_n = lax.broadcasted_iota(jnp.int32, (total, n), 0)
    r_n = lax.broadcasted_iota(jnp.int32, (total, n), 1)
    mine = lists[me].astype(jnp.float32)
    cnt = counts[pl.ds(me, 1), :]
    picked = jnp.zeros((total, n), jnp.float32)
    k_n = jnp.bitwise_and(q_n, slots - 1)
    for k in range(slots):
        picked = jnp.where(k_n == k, mine[k:k + 1, :], picked)
    good = jnp.logical_and(lax.div(q_n, slots) == r_n, k_n < cnt)
    row = jnp.sum(jnp.where(good, picked + 1.0, 0.0), axis=1, keepdims=True) - 1.0
    lane = lax.broadcasted_iota(jnp.int32, (1, sel.shape[1]), 1).astype(jnp.float32)
    sel[...] = jnp.where(row == lane, 1.0, 0.0).astype(jnp.bfloat16)

    for c in copies[5:]:
        c.wait()


def plan(chunks, per, n, radix, ids, src, rows, dst, send_list, send_count, tw, xo, wo, so):
    tiles, _, _, tile = tw.shape
    slots = send_list.shape[2]
    n_src = xo.shape[0] // tile
    blocks = -(-(per * tiles // BLOCK + n_src) // STEP) * STEP
    n_pos = -(-(blocks * BLOCK + 1) // 128) * 128
    smem = pl.BlockSpec(memory_space=pltpu.SMEM)
    vmem = pl.BlockSpec(memory_space=pltpu.VMEM)
    hbm = pl.BlockSpec(memory_space=pltpu.HBM)
    lists = jnp.swapaxes(send_list, 1, 2)
    half = chunks * per
    return pl.pallas_call(
        functools.partial(plan_kernel, chunks, per, n, radix, n_src),
        out_shape=[jax.ShapeDtypeStruct((2, n_pos), jnp.int32)] * chunks
        + [jax.ShapeDtypeStruct((per * tiles, UNIT, tile), tw.dtype)] * chunks
        + [
            jax.ShapeDtypeStruct((n * slots, 2 * half * UNIT), jnp.bfloat16),
            jax.ShapeDtypeStruct(xo.shape, xo.dtype),
            jax.ShapeDtypeStruct(wo.shape, wo.dtype),
            jax.ShapeDtypeStruct(so.shape, so.dtype),
        ],
        in_specs=[smem] + [hbm] * 9,
        out_specs=[vmem] * (2 * chunks + 4),
        scratch_shapes=[
            pltpu.VMEM((1, tiles), jnp.int32),
            pltpu.VMEM((1, tiles), jnp.int32),
            pltpu.VMEM((1, tiles), jnp.int32),
            pltpu.VMEM(lists.shape, jnp.int32),
            pltpu.VMEM(send_count.shape, jnp.int32),
            pltpu.SemaphoreType.DMA((5 + half + 3,)),
        ],
        compiler_params=pltpu.CompilerParams(vmem_limit_bytes=32 * 1024 * 1024),
        name="plan",
    )(ids, *[
        pltpu.with_memory_space_constraint(a, pltpu.HBM)
        for a in (src.reshape(1, tiles), rows.reshape(1, tiles), dst.reshape(1, tiles), lists, send_count, tw, xo, wo, so)
    ])


def tiles_kernel(chunk, per, n, radix, groups, ids, table, tbuf, xo, xp, wo, wp, so, sp, *rest):
    own, outs, rest = rest[0], rest[1:radix], rest[radix:]
    masks, sums, tail, accs = rest[0], rest[1], rest[2], rest[3:]
    tile = tbuf.shape[2]
    width = xo.shape[1]
    core = ids[0]
    for acc in accs:
        acc[...] = jnp.zeros_like(acc)
    row_i = lax.broadcasted_iota(jnp.int32, (UNIT, tile), 0)
    for m in range(UNIT + 1):
        masks[m] = jnp.where(row_i < m, 1.0, 0.0).astype(jnp.bfloat16)
    parts = [(x, w, h) for x, w in ((xo, wo), (xp, wp)) for h in range(0, width, PART)]

    def step(i, carry):
        for m in range(STEP):
            b = i * STEP + m
            base = pl.multiple_of(table[1, b] * tile, tile)
            rows, places = [], []
            for k in range(BLOCK):
                word = table[0, b * BLOCK + k]
                u = jnp.bitwise_and(lax.shift_right_logical(word, 5), 511)
                rows.append(tbuf[u] * masks[jnp.bitwise_and(word, 31)])
                places.append(pl.multiple_of(lax.shift_right_logical(word, 14) * UNIT, UNIT))
            lhs = jnp.concatenate(rows, axis=0)
            for acc, (x, _, h) in zip(accs, parts):
                got = jnp.dot(lhs, x[pl.ds(base, tile), h:h + PART], preferred_element_type=jnp.float32)
                got = got.astype(jnp.bfloat16).astype(jnp.float32)
                for k in range(BLOCK):
                    acc[pl.ds(places[k], UNIT), :] += got[k * UNIT:(k + 1) * UNIT, :]
        return carry

    steps = lax.div(table[1, table.shape[1] - 1] + STEP - 1, STEP)
    lax.fori_loop(0, steps, step, 0)

    slots, rows = n // radix, per * UNIT
    size = min(256, slots * rows)
    for k in range(radix):
        out = own if k == 0 else sums

        def weigh(r, carry):
            at = pl.multiple_of(r * size, size)
            got = jnp.zeros((size, out.shape[1]), jnp.float32)
            for acc, (_, w, h) in zip(accs, parts):
                value = acc[pl.ds(k * slots * rows + at, size), :]
                high = value.astype(jnp.bfloat16)
                low = (value - high.astype(jnp.float32)).astype(jnp.bfloat16)
                got = got + jnp.dot(high, w[h:h + PART, :], preferred_element_type=jnp.float32)
                got = got + jnp.dot(low, w[h:h + PART, :], preferred_element_type=jnp.float32)
            out[pl.ds(at, size), :] = got
            return carry

        lax.fori_loop(0, slots * rows // size, weigh, 0)
        if k == 0:
            for j in range(per):
                at = pl.multiple_of(group_of(core, chunk * per + j, groups) * UNIT, UNIT)
                self = jnp.dot(xo[pl.ds(at, UNIT), :], so[...], preferred_element_type=jnp.float32)
                self = self + jnp.dot(xp[pl.ds(at, UNIT), :], sp[...], preferred_element_type=jnp.float32)
                out[j * UNIT:(j + 1) * UNIT, :] += self
        else:
            write_coded(outs[k - 1], tail, slots, rows, lambda s: sums[s * rows:(s + 1) * rows, :])


def neighbour_terms(chunk, per, n, radix, groups, ids, table, tbuf, xo, xp, wo, wp, so, sp):
    hidden = wo.shape[1]
    width = xo.shape[1]
    tile = tbuf.shape[2]
    smem = pl.BlockSpec(memory_space=pltpu.SMEM)
    vmem = pl.BlockSpec(memory_space=pltpu.VMEM)
    flops = 2 * tbuf.shape[0] * UNIT * tile * 2 * width + 4 * n * per * UNIT * 2 * width * hidden
    slots, rows = n // radix, per * UNIT
    held = (n * per + 1) * UNIT * 2 * width * 4
    coded = jax.ShapeDtypeStruct((slots * rows + tail_rows(slots), hidden), jnp.int16)
    return pl.pallas_call(
        functools.partial(tiles_kernel, chunk, per, n, radix, groups),
        out_shape=[jax.ShapeDtypeStruct((slots * rows, hidden), jnp.float32)] + [coded] * (radix - 1),
        in_specs=[smem] * 2 + [vmem] * 7,
        out_specs=[vmem] * radix,
        scratch_shapes=[
            pltpu.VMEM((UNIT + 1, UNIT, tile), jnp.bfloat16),
            pltpu.VMEM((slots * rows, hidden), jnp.float32),
            pltpu.VMEM((tail_rows(slots), hidden), jnp.float32),
        ]
        + [pltpu.VMEM(((n * per + 1) * UNIT, PART), jnp.float32)] * (2 * width // PART),
        compiler_params=pltpu.CompilerParams(vmem_limit_bytes=(16 << 20) + held),
        cost_estimate=pl.CostEstimate(flops=flops, bytes_accessed=8 << 20, transcendentals=0),
        name="neighbour_terms",
    )(ids, table, tbuf, xo, xp, wo, wp, so, sp)


def combine_kernel(slots, rows, ways, own, *refs):
    parts = len(refs) - ways - 1
    coded, outs, tail = refs[:parts], refs[parts:parts + ways], refs[parts + ways]
    values = [read_coded(a, slots, rows) for a in coded]

    def total(s):
        got = own[s * rows:(s + 1) * rows, :]
        for value in values:
            got = got + value(s)
        return got

    for i in range(slots // ways):
        outs[0][i * rows:(i + 1) * rows, :] = total(i * ways)
    for k in range(1, ways):
        write_coded(outs[k], tail, slots // ways, rows, lambda s: total(s * ways + k))


def combine(slots, rows, ways, own, coded):
    width = own.shape[1]
    left = slots // ways
    vmem = pl.BlockSpec(memory_space=pltpu.VMEM)
    out = jax.ShapeDtypeStruct((left * rows + tail_rows(left), width), jnp.int16)
    return pl.pallas_call(
        functools.partial(combine_kernel, slots, rows, ways),
        out_shape=[jax.ShapeDtypeStruct((left * rows, width), jnp.float32)] + [out] * (ways - 1),
        in_specs=[vmem] * (1 + len(coded)),
        out_specs=[vmem] * ways,
        scratch_shapes=[pltpu.VMEM((tail_rows(left), width), jnp.float32)],
        compiler_params=pltpu.CompilerParams(vmem_limit_bytes=32 * 1024 * 1024),
        name="combine",
    )(own, *coded)


def hidden_kernel(chunks, parts, rows, *refs):
    out = refs[chunks * parts]
    for c in range(chunks):
        own, coded = refs[c * parts], refs[c * parts + 1:(c + 1) * parts]
        total = own[:rows, :]
        for a in coded:
            total = total + read_coded(a, 1, rows)(0)
        out[c * rows:(c + 1) * rows, :] = jnp.maximum(total, 0.0).astype(jnp.bfloat16)


def hidden_rows(chunk_parts, rows):
    chunks, parts = len(chunk_parts), len(chunk_parts[0])
    width = chunk_parts[0][0].shape[1]
    vmem = pl.BlockSpec(memory_space=pltpu.VMEM)
    flat = [a for part in chunk_parts for a in part]
    return pl.pallas_call(
        functools.partial(hidden_kernel, chunks, parts, rows),
        out_shape=jax.ShapeDtypeStruct((chunks * rows, width), jnp.bfloat16),
        in_specs=[vmem] * len(flat),
        out_specs=vmem,
        compiler_params=pltpu.CompilerParams(vmem_limit_bytes=32 * 1024 * 1024),
        name="hidden_rows",
    )(*flat)


def send_kernel(groups, ids, own, other, sel, hidden, send):
    core = ids[0]
    for i in range(groups // 2):
        mine = group_of(core, i, groups)
        theirs = group_of(1 - core, i, groups)
        hidden[pl.ds(pl.multiple_of(mine * UNIT, UNIT), UNIT), :] = own[i * UNIT:(i + 1) * UNIT, :]
        hidden[pl.ds(pl.multiple_of(theirs * UNIT, UNIT), UNIT), :] = other[i * UNIT:(i + 1) * UNIT, :]
    send[...] = jnp.dot(sel[...], hidden[...], preferred_element_type=jnp.float32).astype(jnp.bfloat16)


def rows_to_send(groups, ids, own, other, sel):
    smem = pl.BlockSpec(memory_space=pltpu.SMEM)
    vmem = pl.BlockSpec(memory_space=pltpu.VMEM)
    width = own.shape[1]
    return pl.pallas_call(
        functools.partial(send_kernel, groups),
        out_shape=[
            jax.ShapeDtypeStruct((groups * UNIT, width), jnp.bfloat16),
            jax.ShapeDtypeStruct((sel.shape[0], width), jnp.bfloat16),
        ],
        in_specs=[smem] + [vmem] * 3,
        out_specs=[vmem] * 2,
        compiler_params=pltpu.CompilerParams(vmem_limit_bytes=32 * 1024 * 1024),
        name="rows_to_send",
    )(ids, own, other, sel)


def logits_kernel(hidden, received, adj, w_self, w_neigh, out):
    tile, rows = hidden.shape[0], adj.shape[0]
    mean = jnp.dot(adj[:, :tile], hidden[...], preferred_element_type=jnp.float32)
    mean = mean + jnp.dot(adj[:, tile:], received[...], preferred_element_type=jnp.float32)
    dims = (((1,), (1,)), ((), ()))
    got = lax.dot_general(hidden[:rows, :], w_self[...], dims, preferred_element_type=jnp.float32)
    got = got + lax.dot_general(mean.astype(jnp.bfloat16), w_neigh[...], dims, preferred_element_type=jnp.float32)
    out[...] = got


def logits_of(hidden, received, adj, w_self, w_neigh):
    vmem = pl.BlockSpec(memory_space=pltpu.VMEM)
    return pl.pallas_call(
        logits_kernel,
        out_shape=jax.ShapeDtypeStruct((adj.shape[0], w_self.shape[1]), jnp.float32),
        in_specs=[vmem] * 5,
        out_specs=vmem,
        compiler_params=pltpu.CompilerParams(vmem_limit_bytes=32 * 1024 * 1024),
        name="logits",
    )(hidden, received, adj, w_self.T, w_neigh.T)


def exchange(parts, stride, n):
    got = [parts[0]]
    for k in range(1, len(parts)):
        got.append(lax.ppermute(parts[k], "dom", [(i, i ^ (k * stride)) for i in range(n)]))
    return got


def body(
    features,
    tile_weight,
    tile_dst,
    tile_src,
    tile_rows,
    w_self1,
    neighbour_weight_first,
    send_list,
    send_count,
    adj_two,
    w_self2,
    w_neigh2,
):
    n = lax.axis_size("dom")
    tile = tile_weight.shape[1]
    groups = tile // UNIT
    per = groups // 2 // CHUNKS
    bits = n.bit_length() - 1
    assert n == 1 << bits and bits >= 2
    radices = [2] * (bits // 2) + [1] * (bits % 2)
    ids = jnp.stack([lax.axis_index("feat"), lax.axis_index("dom")]).astype(jnp.int32)
    swap = [(0, 1), (1, 0)]
    xp = lax.ppermute(features, "feat", swap)
    wp = lax.ppermute(neighbour_weight_first, "feat", swap)
    sp = lax.ppermute(w_self1, "feat", swap)
    tw = tile_weight.reshape(tile_weight.shape[0], groups, UNIT, tile)
    planned = plan(
        CHUNKS, per, n, 4, ids, tile_src, tile_rows, tile_dst, send_list, send_count, tw, features,
        neighbour_weight_first, w_self1,
    )
    tables, tbufs, (sel, xo, wo, so) = planned[:CHUNKS], planned[CHUNKS:2 * CHUNKS], planned[2 * CHUNKS:]
    done = []
    for chunk in range(CHUNKS):
        parts = neighbour_terms(chunk, per, n, 4, groups, ids, tables[chunk], tbufs[chunk], xo, xp, wo, wp, so, sp)
        got = exchange(parts, 1, n)
        stride = 4
        for radix in radices[1:]:
            ways = 1 << radix
            parts = combine(n // stride, per * UNIT, ways, got[0], got[1:])
            got = exchange(parts, stride, n)
            stride *= ways
        done.append(got)
    own = hidden_rows(done, per * UNIT)
    other = lax.ppermute(own, "feat", swap)
    hidden, send = rows_to_send(groups, ids, own, other, sel)
    received = lax.all_to_all(send, "dom", 0, 0, tiled=True)
    return logits_of(hidden, received, adj_two, w_self2, w_neigh2)


def solution(mesh):
    in_specs = (
        P("dom", "feat"),
        P("dom", None, None),
        P("dom"),
        P("dom"),
        P("dom"),
        P("feat", None),
        P("feat", None),
        P(),
        P(),
        P("dom", None),
        P(),
        P(),
    )
    out_specs = P("dom", None)
    return jax.shard_map(body, mesh=mesh, in_specs=in_specs, out_specs=out_specs, check_vma=False)
```

```python
import functools

import jax
import jax.numpy as jnp
from jax import lax
from jax.experimental import pallas as pl
from jax.experimental.pallas import tpu as pltpu
from jax.sharding import PartitionSpec as P

UNIT = 16
BLOCK = 8
STEP = 8
PART = 256
CHUNKS = 1


def group_of(core, place, groups):
    pair = 2 * (place // 2) + core
    return pair if place % 2 == 0 else groups - 1 - pair


LN2 = 0.6931471805599453


def tail_rows(slots):
    return -(-slots // 16) * 16


def encode(x):
    top = jnp.max(jnp.abs(x), axis=0, keepdims=True)
    power = jnp.ceil(jnp.log(jnp.maximum(top, 1e-30)) * (1.0 / LN2) + 1e-3) - 15.0
    return jnp.floor(x * jnp.exp(power * -LN2) + 0.5), power


def to_int16(x):
    return x.astype(jnp.int32).astype(jnp.int16)


def write_coded(out, tail, slots, rows, value_of):
    tail[...] = jnp.zeros_like(tail)
    for s in range(slots):
        whole, power = encode(value_of(s))
        out[s * rows:(s + 1) * rows, :] = to_int16(whole)
        tail[s:s + 1, :] = power
    out[slots * rows:, :] = to_int16(tail[...])


def read_coded(ref, slots, rows):
    powers = ref[slots * rows:, :].astype(jnp.int32).astype(jnp.float32)

    def value_of(s):
        whole = ref[s * rows:(s + 1) * rows, :].astype(jnp.int32).astype(jnp.float32)
        return whole * jnp.exp(powers[s:s + 1, :] * LN2)

    return value_of


def plan_kernel(chunks, per, n, radix, n_src, ids, src_h, rows_h, dst_h, lists_h, counts_h, tw, xo, wo, so, *rest):
    tables, rest = rest[:chunks], rest[chunks:]
    tbufs, rest = rest[:chunks], rest[chunks:]
    sel, xo_out, wo_out, so_out = rest[:4]
    src_v, rows_v, dst_v, lists, counts, sems = rest[4:]
    core, me = ids[0], ids[1]
    tiles = src_v.shape[1]
    n_pos = tables[0].shape[1]
    units = per * tiles
    groups = 2 * per * chunks
    half = groups // 2
    gs = [group_of(core, i, groups) for i in range(half)]
    small = [(src_h, src_v), (rows_h, rows_v), (dst_h, dst_v), (lists_h, lists), (counts_h, counts)]
    large = [(tw.at[:, g], tbufs[i // per].at[pl.ds(i % per * tiles, tiles)]) for i, g in enumerate(gs)]
    large += [(xo, xo_out), (wo, wo_out), (so, so_out)]
    copies = [pltpu.make_async_copy(a, b, sems.at[i]) for i, (a, b) in enumerate(small + large)]
    for c in copies:
        c.start()
    lane = lax.broadcasted_iota(jnp.int32, (1, tiles), 1)
    block_i = lax.broadcasted_iota(jnp.int32, (n_src, tiles), 0)
    before = lax.broadcasted_iota(jnp.int32, (units, units), 0) < lax.broadcasted_iota(jnp.int32, (units, units), 1)
    before = jnp.where(before, 1.0, 0.0).astype(jnp.bfloat16)
    pos_i = lax.broadcasted_iota(jnp.int32, (tiles, n_pos), 1).astype(jnp.float32)
    place_i = lax.broadcasted_iota(jnp.int32, (1, n_pos), 1)
    trash = float(n * per << 14)
    for c in copies[:5]:
        c.wait()
    src, rows = src_v[...], rows_v[...]
    slot = jnp.bitwise_xor(dst_v[...], me)
    slot = jnp.bitwise_and(slot, radix - 1) * (n // radix) + lax.div(slot, radix)
    for c in range(chunks):
        hot, words, valid = [], [], []
        for j in range(per):
            limit = jnp.clip(rows - UNIT * gs[c * per + j], 0, UNIT)
            ok = limit > 0
            valid.append(ok)
            words.append(((slot * per + j) * 512 + (j * tiles + lane)) * 32 + limit)
            hot.append(jnp.where(jnp.logical_and(block_i == src, ok), 1.0, 0.0))
        hot = jnp.concatenate(hot, axis=1)
        earlier = jnp.dot(hot.astype(jnp.bfloat16), before, preferred_element_type=jnp.float32)
        blocks = jnp.floor((jnp.sum(hot, axis=1, keepdims=True) + (BLOCK - 1)) * (1.0 / BLOCK))
        run = jnp.zeros((1, 1), jnp.float32)
        pos = jnp.zeros((1, units), jnp.float32)
        owner = jnp.zeros((1, n_pos), jnp.float32)
        for s in range(n_src):
            pos = pos + hot[s:s + 1, :] * (earlier[s:s + 1, :] + run * BLOCK)
            run = run + blocks[s:s + 1, :]
            owner = owner + jnp.where(place_i.astype(jnp.float32) >= run, 1.0, 0.0)
        stack = [jnp.where(valid[j], pos[:, j * tiles:(j + 1) * tiles], -1.0) for j in range(per)]
        stack += [w.astype(jnp.float32) - trash for w in words]
        stack += [jnp.zeros((1, tiles), jnp.float32)] * (-len(stack) % 8)
        cols = jnp.concatenate(stack, axis=0).T
        found = jnp.zeros((tiles, n_pos), jnp.float32)
        for j in range(per):
            found = found + jnp.where(cols[:, j:j + 1] == pos_i, cols[:, per + j:per + j + 1], 0.0)
        word = jnp.sum(found, axis=0, keepdims=True) + trash
        owner = jnp.where(place_i == n_pos - 1, run, jnp.minimum(owner, n_src - 1.0))
        tables[c][0:1, :] = word.astype(jnp.int32)
        tables[c][1:2, :] = owner.astype(jnp.int32)

    slots = lists.shape[1]
    total = n * slots
    q_n = lax.broadcasted_iota(jnp.int32, (total, n), 0)
    r_n = lax.broadcasted_iota(jnp.int32, (total, n), 1)
    mine = lists[me].astype(jnp.float32)
    cnt = counts[pl.ds(me, 1), :]
    picked = jnp.zeros((total, n), jnp.float32)
    k_n = jnp.bitwise_and(q_n, slots - 1)
    for k in range(slots):
        picked = jnp.where(k_n == k, mine[k:k + 1, :], picked)
    good = jnp.logical_and(lax.div(q_n, slots) == r_n, k_n < cnt)
    row = jnp.sum(jnp.where(good, picked + 1.0, 0.0), axis=1, keepdims=True) - 1.0
    lane = lax.broadcasted_iota(jnp.int32, (1, sel.shape[1]), 1).astype(jnp.float32)
    sel[...] = jnp.where(row == lane, 1.0, 0.0).astype(jnp.bfloat16)

    for c in copies[5:]:
        c.wait()


def plan(chunks, per, n, radix, ids, src, rows, dst, send_list, send_count, tw, xo, wo, so):
    tiles, _, _, tile = tw.shape
    slots = send_list.shape[2]
    n_src = xo.shape[0] // tile
    blocks = -(-(per * tiles // BLOCK + n_src) // STEP) * STEP
    n_pos = -(-(blocks * BLOCK + 1) // 128) * 128
    smem = pl.BlockSpec(memory_space=pltpu.SMEM)
    vmem = pl.BlockSpec(memory_space=pltpu.VMEM)
    hbm = pl.BlockSpec(memory_space=pltpu.HBM)
    lists = jnp.swapaxes(send_list, 1, 2)
    half = chunks * per
    return pl.pallas_call(
        functools.partial(plan_kernel, chunks, per, n, radix, n_src),
        out_shape=[jax.ShapeDtypeStruct((2, n_pos), jnp.int32)] * chunks
        + [jax.ShapeDtypeStruct((per * tiles, UNIT, tile), tw.dtype)] * chunks
        + [
            jax.ShapeDtypeStruct((n * slots, 2 * half * UNIT), jnp.bfloat16),
            jax.ShapeDtypeStruct(xo.shape, xo.dtype),
            jax.ShapeDtypeStruct(wo.shape, wo.dtype),
            jax.ShapeDtypeStruct(so.shape, so.dtype),
        ],
        in_specs=[smem] + [hbm] * 9,
        out_specs=[vmem] * (2 * chunks + 4),
        scratch_shapes=[
            pltpu.VMEM((1, tiles), jnp.int32),
            pltpu.VMEM((1, tiles), jnp.int32),
            pltpu.VMEM((1, tiles), jnp.int32),
            pltpu.VMEM(lists.shape, jnp.int32),
            pltpu.VMEM(send_count.shape, jnp.int32),
            pltpu.SemaphoreType.DMA((5 + half + 3,)),
        ],
        compiler_params=pltpu.CompilerParams(vmem_limit_bytes=32 * 1024 * 1024),
        name="plan",
    )(ids, *[
        pltpu.with_memory_space_constraint(a, pltpu.HBM)
        for a in (src.reshape(1, tiles), rows.reshape(1, tiles), dst.reshape(1, tiles), lists, send_count, tw, xo, wo, so)
    ])


def tiles_kernel(chunk, per, n, radix, groups, ids, table, tbuf, xo, xp, wo, wp, so, sp, *rest):
    own, outs, rest = rest[0], rest[1:radix], rest[radix:]
    masks, sums, tail, accs = rest[0], rest[1], rest[2], rest[3:]
    tile = tbuf.shape[2]
    width = xo.shape[1]
    core = ids[0]
    for acc in accs:
        acc[...] = jnp.zeros_like(acc)
    row_i = lax.broadcasted_iota(jnp.int32, (UNIT, tile), 0)
    for m in range(UNIT + 1):
        masks[m] = jnp.where(row_i < m, 1.0, 0.0).astype(jnp.bfloat16)
    parts = [(x, w, h) for x, w in ((xo, wo), (xp, wp)) for h in range(0, width, PART)]

    def step(i, carry):
        for m in range(STEP):
            b = i * STEP + m
            base = pl.multiple_of(table[1, b] * tile, tile)
            rows, places = [], []
            for k in range(BLOCK):
                word = table[0, b * BLOCK + k]
                u = jnp.bitwise_and(lax.shift_right_logical(word, 5), 511)
                rows.append(tbuf[u] * masks[jnp.bitwise_and(word, 31)])
                places.append(pl.multiple_of(lax.shift_right_logical(word, 14) * UNIT, UNIT))
            lhs = jnp.concatenate(rows, axis=0)
            for acc, (x, _, h) in zip(accs, parts):
                got = jnp.dot(lhs, x[pl.ds(base, tile), h:h + PART], preferred_element_type=jnp.float32)
                got = got.astype(jnp.bfloat16).astype(jnp.float32)
                for k in range(BLOCK):
                    acc[pl.ds(places[k], UNIT), :] += got[k * UNIT:(k + 1) * UNIT, :]
        return carry

    steps = lax.div(table[1, table.shape[1] - 1] + STEP - 1, STEP)
    lax.fori_loop(0, steps, step, 0)

    slots, rows = n // radix, per * UNIT
    size = min(256, slots * rows)
    for k in range(radix):
        out = own if k == 0 else sums

        def weigh(r, carry):
            at = pl.multiple_of(r * size, size)
            got = jnp.zeros((size, out.shape[1]), jnp.float32)
            for acc, (_, w, h) in zip(accs, parts):
                value = acc[pl.ds(k * slots * rows + at, size), :]
                high = value.astype(jnp.bfloat16)
                low = (value - high.astype(jnp.float32)).astype(jnp.bfloat16)
                got = got + jnp.dot(high, w[h:h + PART, :], preferred_element_type=jnp.float32)
                got = got + jnp.dot(low, w[h:h + PART, :], preferred_element_type=jnp.float32)
            out[pl.ds(at, size), :] = got
            return carry

        lax.fori_loop(0, slots * rows // size, weigh, 0)
        if k == 0:
            for j in range(per):
                at = pl.multiple_of(group_of(core, chunk * per + j, groups) * UNIT, UNIT)
                self = jnp.dot(xo[pl.ds(at, UNIT), :], so[...], preferred_element_type=jnp.float32)
                self = self + jnp.dot(xp[pl.ds(at, UNIT), :], sp[...], preferred_element_type=jnp.float32)
                out[j * UNIT:(j + 1) * UNIT, :] += self
        else:
            write_coded(outs[k - 1], tail, slots, rows, lambda s: sums[s * rows:(s + 1) * rows, :])


def neighbour_terms(chunk, per, n, radix, groups, ids, table, tbuf, xo, xp, wo, wp, so, sp):
    hidden = wo.shape[1]
    width = xo.shape[1]
    tile = tbuf.shape[2]
    smem = pl.BlockSpec(memory_space=pltpu.SMEM)
    vmem = pl.BlockSpec(memory_space=pltpu.VMEM)
    flops = 2 * tbuf.shape[0] * UNIT * tile * 2 * width + 4 * n * per * UNIT * 2 * width * hidden
    slots, rows = n // radix, per * UNIT
    held = (n * per + 1) * UNIT * 2 * width * 4
    coded = jax.ShapeDtypeStruct((slots * rows + tail_rows(slots), hidden), jnp.int16)
    return pl.pallas_call(
        functools.partial(tiles_kernel, chunk, per, n, radix, groups),
        out_shape=[jax.ShapeDtypeStruct((slots * rows, hidden), jnp.float32)] + [coded] * (radix - 1),
        in_specs=[smem] * 2 + [vmem] * 7,
        out_specs=[vmem] * radix,
        scratch_shapes=[
            pltpu.VMEM((UNIT + 1, UNIT, tile), jnp.bfloat16),
            pltpu.VMEM((slots * rows, hidden), jnp.float32),
            pltpu.VMEM((tail_rows(slots), hidden), jnp.float32),
        ]
        + [pltpu.VMEM(((n * per + 1) * UNIT, PART), jnp.float32)] * (2 * width // PART),
        compiler_params=pltpu.CompilerParams(vmem_limit_bytes=(16 << 20) + held),
        cost_estimate=pl.CostEstimate(flops=flops, bytes_accessed=8 << 20, transcendentals=0),
        name="neighbour_terms",
    )(ids, table, tbuf, xo, xp, wo, wp, so, sp)


def combine_kernel(slots, rows, ways, own, *refs):
    parts = len(refs) - ways - 1
    coded, outs, tail = refs[:parts], refs[parts:parts + ways], refs[parts + ways]
    values = [read_coded(a, slots, rows) for a in coded]

    def total(s):
        got = own[s * rows:(s + 1) * rows, :]
        for value in values:
            got = got + value(s)
        return got

    for i in range(slots // ways):
        outs[0][i * rows:(i + 1) * rows, :] = total(i * ways)
    for k in range(1, ways):
        write_coded(outs[k], tail, slots // ways, rows, lambda s: total(s * ways + k))


def combine(slots, rows, ways, own, coded):
    width = own.shape[1]
    left = slots // ways
    vmem = pl.BlockSpec(memory_space=pltpu.VMEM)
    out = jax.ShapeDtypeStruct((left * rows + tail_rows(left), width), jnp.int16)
    return pl.pallas_call(
        functools.partial(combine_kernel, slots, rows, ways),
        out_shape=[jax.ShapeDtypeStruct((left * rows, width), jnp.float32)] + [out] * (ways - 1),
        in_specs=[vmem] * (1 + len(coded)),
        out_specs=[vmem] * ways,
        scratch_shapes=[pltpu.VMEM((tail_rows(left), width), jnp.float32)],
        compiler_params=pltpu.CompilerParams(vmem_limit_bytes=32 * 1024 * 1024),
        name="combine",
    )(own, *coded)


def hidden_kernel(chunks, parts, rows, *refs):
    out = refs[chunks * parts]
    for c in range(chunks):
        own, coded = refs[c * parts], refs[c * parts + 1:(c + 1) * parts]
        total = own[:rows, :]
        for a in coded:
            total = total + read_coded(a, 1, rows)(0)
        out[c * rows:(c + 1) * rows, :] = jnp.maximum(total, 0.0).astype(jnp.bfloat16)


def hidden_rows(chunk_parts, rows):
    chunks, parts = len(chunk_parts), len(chunk_parts[0])
    width = chunk_parts[0][0].shape[1]
    vmem = pl.BlockSpec(memory_space=pltpu.VMEM)
    flat = [a for part in chunk_parts for a in part]
    return pl.pallas_call(
        functools.partial(hidden_kernel, chunks, parts, rows),
        out_shape=jax.ShapeDtypeStruct((chunks * rows, width), jnp.bfloat16),
        in_specs=[vmem] * len(flat),
        out_specs=vmem,
        compiler_params=pltpu.CompilerParams(vmem_limit_bytes=32 * 1024 * 1024),
        name="hidden_rows",
    )(*flat)


def send_kernel(groups, ids, own, other, sel, hidden, send):
    core = ids[0]
    for i in range(groups // 2):
        mine = group_of(core, i, groups)
        theirs = group_of(1 - core, i, groups)
        hidden[pl.ds(pl.multiple_of(mine * UNIT, UNIT), UNIT), :] = own[i * UNIT:(i + 1) * UNIT, :]
        hidden[pl.ds(pl.multiple_of(theirs * UNIT, UNIT), UNIT), :] = other[i * UNIT:(i + 1) * UNIT, :]
    send[...] = jnp.dot(sel[...], hidden[...], preferred_element_type=jnp.float32).astype(jnp.bfloat16)


def rows_to_send(groups, ids, own, other, sel):
    smem = pl.BlockSpec(memory_space=pltpu.SMEM)
    vmem = pl.BlockSpec(memory_space=pltpu.VMEM)
    width = own.shape[1]
    return pl.pallas_call(
        functools.partial(send_kernel, groups),
        out_shape=[
            jax.ShapeDtypeStruct((groups * UNIT, width), jnp.bfloat16),
            jax.ShapeDtypeStruct((sel.shape[0], width), jnp.bfloat16),
        ],
        in_specs=[smem] + [vmem] * 3,
        out_specs=[vmem] * 2,
        compiler_params=pltpu.CompilerParams(vmem_limit_bytes=32 * 1024 * 1024),
        name="rows_to_send",
    )(ids, own, other, sel)


def logits_kernel(hidden, received, adj, w_self, w_neigh, out):
    tile, rows = hidden.shape[0], adj.shape[0]
    mean = jnp.dot(adj[:, :tile], hidden[...], preferred_element_type=jnp.float32)
    mean = mean + jnp.dot(adj[:, tile:], received[...], preferred_element_type=jnp.float32)
    dims = (((1,), (1,)), ((), ()))
    got = lax.dot_general(hidden[:rows, :], w_self[...], dims, preferred_element_type=jnp.float32)
    got = got + lax.dot_general(mean.astype(jnp.bfloat16), w_neigh[...], dims, preferred_element_type=jnp.float32)
    out[...] = got


def logits_of(hidden, received, adj, w_self, w_neigh):
    vmem = pl.BlockSpec(memory_space=pltpu.VMEM)
    return pl.pallas_call(
        logits_kernel,
        out_shape=jax.ShapeDtypeStruct((adj.shape[0], w_self.shape[1]), jnp.float32),
        in_specs=[vmem] * 5,
        out_specs=vmem,
        compiler_params=pltpu.CompilerParams(vmem_limit_bytes=32 * 1024 * 1024),
        name="logits",
    )(hidden, received, adj, w_self.T, w_neigh.T)


def exchange(parts, stride, n):
    got = [parts[0]]
    for k in reversed(range(1, len(parts))):
        got.append(lax.ppermute(parts[k], "dom", [(i, i ^ (k * stride)) for i in range(n)]))
    return got


def body(
    features,
    tile_weight,
    tile_dst,
    tile_src,
    tile_rows,
    w_self1,
    neighbour_weight_first,
    send_list,
    send_count,
    adj_two,
    w_self2,
    w_neigh2,
):
    n = lax.axis_size("dom")
    tile = tile_weight.shape[1]
    groups = tile // UNIT
    per = groups // 2 // CHUNKS
    bits = n.bit_length() - 1
    assert n == 1 << bits and bits >= 2
    radices = [2] * (bits // 2) + [1] * (bits % 2)
    ids = jnp.stack([lax.axis_index("feat"), lax.axis_index("dom")]).astype(jnp.int32)
    swap = [(0, 1), (1, 0)]
    xp = lax.ppermute(features, "feat", swap)
    wp = lax.ppermute(neighbour_weight_first, "feat", swap)
    sp = lax.ppermute(w_self1, "feat", swap)
    tw = tile_weight.reshape(tile_weight.shape[0], groups, UNIT, tile)
    planned = plan(
        CHUNKS, per, n, 4, ids, tile_src, tile_rows, tile_dst, send_list, send_count, tw, features,
        neighbour_weight_first, w_self1,
    )
    tables, tbufs, (sel, xo, wo, so) = planned[:CHUNKS], planned[CHUNKS:2 * CHUNKS], planned[2 * CHUNKS:]
    done = []
    for chunk in range(CHUNKS):
        parts = neighbour_terms(chunk, per, n, 4, groups, ids, tables[chunk], tbufs[chunk], xo, xp, wo, wp, so, sp)
        got = exchange(parts, 1, n)
        stride = 4
        for radix in radices[1:]:
            ways = 1 << radix
            parts = combine(n // stride, per * UNIT, ways, got[0], got[1:])
            got = exchange(parts, stride, n)
            stride *= ways
        done.append(got)
    own = hidden_rows(done, per * UNIT)
    other = lax.ppermute(own, "feat", swap)
    hidden, send = rows_to_send(groups, ids, own, other, sel)
    received = lax.all_to_all(send, "dom", 0, 0, tiled=True)
    return logits_of(hidden, received, adj_two, w_self2, w_neigh2)


def solution(mesh):
    in_specs = (
        P("dom", "feat"),
        P("dom", None, None),
        P("dom"),
        P("dom"),
        P("dom"),
        P("feat", None),
        P("feat", None),
        P(),
        P(),
        P("dom", None),
        P(),
        P(),
    )
    out_specs = P("dom", None)
    return jax.shard_map(body, mesh=mesh, in_specs=in_specs, out_specs=out_specs, check_vma=False)
```

```python
import functools

import jax
import jax.numpy as jnp
from jax import lax
from jax.experimental import pallas as pl
from jax.experimental.pallas import tpu as pltpu
from jax.sharding import PartitionSpec as P

UNIT = 16
BLOCK = 8
STEP = 8
PART = 256
CHUNKS = 1


def group_of(core, place, groups):
    pair = 2 * (place // 2) + core
    return pair if place % 2 == 0 else groups - 1 - pair


LN2 = 0.6931471805599453


def tail_rows(slots):
    return -(-slots // 16) * 16


def encode(x):
    top = jnp.max(jnp.abs(x), axis=0, keepdims=True)
    power = jnp.ceil(jnp.log(jnp.maximum(top, 1e-30)) * (1.0 / LN2) + 1e-3) - 15.0
    return jnp.floor(x * jnp.exp(power * -LN2) + 0.5), power


def to_int16(x):
    return x.astype(jnp.int32).astype(jnp.int16)


def write_coded(out, tail, slots, rows, value_of):
    tail[...] = jnp.zeros_like(tail)
    for s in range(slots):
        whole, power = encode(value_of(s))
        out[s * rows:(s + 1) * rows, :] = to_int16(whole)
        tail[s:s + 1, :] = power
    out[slots * rows:, :] = to_int16(tail[...])


def read_coded(ref, slots, rows):
    powers = ref[slots * rows:, :].astype(jnp.int32).astype(jnp.float32)

    def value_of(s):
        whole = ref[s * rows:(s + 1) * rows, :].astype(jnp.int32).astype(jnp.float32)
        return whole * jnp.exp(powers[s:s + 1, :] * LN2)

    return value_of


def plan_kernel(chunks, per, n, radix, n_src, ids, src_h, rows_h, dst_h, lists_h, counts_h, tw, xo, wo, so, *rest):
    tables, rest = rest[:chunks], rest[chunks:]
    tbufs, rest = rest[:chunks], rest[chunks:]
    sel, xo_out, wo_out, so_out = rest[:4]
    src_v, rows_v, dst_v, lists, counts, sems = rest[4:]
    core, me = ids[0], ids[1]
    tiles = src_v.shape[1]
    n_pos = tables[0].shape[1]
    units = per * tiles
    groups = 2 * per * chunks
    half = groups // 2
    gs = [group_of(core, i, groups) for i in range(half)]
    small = [(src_h, src_v), (rows_h, rows_v), (dst_h, dst_v), (lists_h, lists), (counts_h, counts)]
    large = [(tw.at[:, g], tbufs[i // per].at[pl.ds(i % per * tiles, tiles)]) for i, g in enumerate(gs)]
    large += [(xo, xo_out), (wo, wo_out), (so, so_out)]
    copies = [pltpu.make_async_copy(a, b, sems.at[i]) for i, (a, b) in enumerate(small + large)]
    for c in copies:
        c.start()
    lane = lax.broadcasted_iota(jnp.int32, (1, tiles), 1)
    block_i = lax.broadcasted_iota(jnp.int32, (n_src, tiles), 0)
    before = lax.broadcasted_iota(jnp.int32, (units, units), 0) < lax.broadcasted_iota(jnp.int32, (units, units), 1)
    before = jnp.where(before, 1.0, 0.0).astype(jnp.bfloat16)
    pos_i = lax.broadcasted_iota(jnp.int32, (tiles, n_pos), 1).astype(jnp.float32)
    place_i = lax.broadcasted_iota(jnp.int32, (1, n_pos), 1)
    trash = float(n * per << 14)
    for c in copies[:5]:
        c.wait()
    src, rows = src_v[...], rows_v[...]
    slot = jnp.bitwise_xor(dst_v[...], me)
    slot = jnp.bitwise_and(slot, radix - 1) * (n // radix) + lax.div(slot, radix)
    for c in range(chunks):
        hot, words, valid = [], [], []
        for j in range(per):
            limit = jnp.clip(rows - UNIT * gs[c * per + j], 0, UNIT)
            ok = limit > 0
            valid.append(ok)
            words.append(((slot * per + j) * 512 + (j * tiles + lane)) * 32 + limit)
            hot.append(jnp.where(jnp.logical_and(block_i == src, ok), 1.0, 0.0))
        hot = jnp.concatenate(hot, axis=1)
        earlier = jnp.dot(hot.astype(jnp.bfloat16), before, preferred_element_type=jnp.float32)
        blocks = jnp.floor((jnp.sum(hot, axis=1, keepdims=True) + (BLOCK - 1)) * (1.0 / BLOCK))
        run = jnp.zeros((1, 1), jnp.float32)
        pos = jnp.zeros((1, units), jnp.float32)
        owner = jnp.zeros((1, n_pos), jnp.float32)
        for s in range(n_src):
            pos = pos + hot[s:s + 1, :] * (earlier[s:s + 1, :] + run * BLOCK)
            run = run + blocks[s:s + 1, :]
            owner = owner + jnp.where(place_i.astype(jnp.float32) >= run, 1.0, 0.0)
        stack = [jnp.where(valid[j], pos[:, j * tiles:(j + 1) * tiles], -1.0) for j in range(per)]
        stack += [w.astype(jnp.float32) - trash for w in words]
        stack += [jnp.zeros((1, tiles), jnp.float32)] * (-len(stack) % 8)
        cols = jnp.concatenate(stack, axis=0).T
        found = jnp.zeros((tiles, n_pos), jnp.float32)
        for j in range(per):
            found = found + jnp.where(cols[:, j:j + 1] == pos_i, cols[:, per + j:per + j + 1], 0.0)
        word = jnp.sum(found, axis=0, keepdims=True) + trash
        owner = jnp.where(place_i == n_pos - 1, run, jnp.minimum(owner, n_src - 1.0))
        tables[c][0:1, :] = word.astype(jnp.int32)
        tables[c][1:2, :] = owner.astype(jnp.int32)

    slots = lists.shape[1]
    total = n * slots
    q_n = lax.broadcasted_iota(jnp.int32, (total, n), 0)
    r_n = lax.broadcasted_iota(jnp.int32, (total, n), 1)
    mine = lists[me].astype(jnp.float32)
    cnt = counts[pl.ds(me, 1), :]
    picked = jnp.zeros((total, n), jnp.float32)
    k_n = jnp.bitwise_and(q_n, slots - 1)
    for k in range(slots):
        picked = jnp.where(k_n == k, mine[k:k + 1, :], picked)
    block = lax.div(q_n, slots)
    apart = jnp.bitwise_and(block, n // 2 - 1) * 2 + lax.div(block, n // 2)
    good = jnp.logical_and(jnp.bitwise_xor(apart, me) == r_n, k_n < cnt)
    row = jnp.sum(jnp.where(good, picked + 1.0, 0.0), axis=1, keepdims=True) - 1.0
    lane = lax.broadcasted_iota(jnp.int32, (1, sel.shape[1]), 1).astype(jnp.float32)
    sel[...] = jnp.where(row == lane, 1.0, 0.0).astype(jnp.bfloat16)

    for c in copies[5:]:
        c.wait()


def plan(chunks, per, n, radix, ids, src, rows, dst, send_list, send_count, tw, xo, wo, so):
    tiles, _, _, tile = tw.shape
    slots = send_list.shape[2]
    n_src = xo.shape[0] // tile
    blocks = -(-(per * tiles // BLOCK + n_src) // STEP) * STEP
    n_pos = -(-(blocks * BLOCK + 1) // 128) * 128
    smem = pl.BlockSpec(memory_space=pltpu.SMEM)
    vmem = pl.BlockSpec(memory_space=pltpu.VMEM)
    hbm = pl.BlockSpec(memory_space=pltpu.HBM)
    lists = jnp.swapaxes(send_list, 1, 2)
    half = chunks * per
    return pl.pallas_call(
        functools.partial(plan_kernel, chunks, per, n, radix, n_src),
        out_shape=[jax.ShapeDtypeStruct((2, n_pos), jnp.int32)] * chunks
        + [jax.ShapeDtypeStruct((per * tiles, UNIT, tile), tw.dtype)] * chunks
        + [
            jax.ShapeDtypeStruct((n * slots, 2 * half * UNIT), jnp.bfloat16),
            jax.ShapeDtypeStruct(xo.shape, xo.dtype),
            jax.ShapeDtypeStruct(wo.shape, wo.dtype),
            jax.ShapeDtypeStruct(so.shape, so.dtype),
        ],
        in_specs=[smem] + [hbm] * 9,
        out_specs=[vmem] * (2 * chunks + 4),
        scratch_shapes=[
            pltpu.VMEM((1, tiles), jnp.int32),
            pltpu.VMEM((1, tiles), jnp.int32),
            pltpu.VMEM((1, tiles), jnp.int32),
            pltpu.VMEM(lists.shape, jnp.int32),
            pltpu.VMEM(send_count.shape, jnp.int32),
            pltpu.SemaphoreType.DMA((5 + half + 3,)),
        ],
        compiler_params=pltpu.CompilerParams(vmem_limit_bytes=32 * 1024 * 1024),
        name="plan",
    )(ids, *[
        pltpu.with_memory_space_constraint(a, pltpu.HBM)
        for a in (src.reshape(1, tiles), rows.reshape(1, tiles), dst.reshape(1, tiles), lists, send_count, tw, xo, wo, so)
    ])


def tiles_kernel(chunk, per, n, radix, groups, ids, table, tbuf, xo, xp, wo, wp, so, sp, *rest):
    own, outs, rest = rest[0], rest[1:radix], rest[radix:]
    masks, sums, tail, accs = rest[0], rest[1], rest[2], rest[3:]
    tile = tbuf.shape[2]
    width = xo.shape[1]
    core = ids[0]
    for acc in accs:
        acc[...] = jnp.zeros_like(acc)
    row_i = lax.broadcasted_iota(jnp.int32, (UNIT, tile), 0)
    for m in range(UNIT + 1):
        masks[m] = jnp.where(row_i < m, 1.0, 0.0).astype(jnp.bfloat16)
    parts = [(x, w, h) for x, w in ((xo, wo), (xp, wp)) for h in range(0, width, PART)]

    def step(i, carry):
        for m in range(STEP):
            b = i * STEP + m
            base = pl.multiple_of(table[1, b] * tile, tile)
            rows, places = [], []
            for k in range(BLOCK):
                word = table[0, b * BLOCK + k]
                u = jnp.bitwise_and(lax.shift_right_logical(word, 5), 511)
                rows.append(tbuf[u] * masks[jnp.bitwise_and(word, 31)])
                places.append(pl.multiple_of(lax.shift_right_logical(word, 14) * UNIT, UNIT))
            lhs = jnp.concatenate(rows, axis=0)
            for acc, (x, _, h) in zip(accs, parts):
                got = jnp.dot(lhs, x[pl.ds(base, tile), h:h + PART], preferred_element_type=jnp.float32)
                got = got.astype(jnp.bfloat16).astype(jnp.float32)
                for k in range(BLOCK):
                    acc[pl.ds(places[k], UNIT), :] += got[k * UNIT:(k + 1) * UNIT, :]
        return carry

    steps = lax.div(table[1, table.shape[1] - 1] + STEP - 1, STEP)
    lax.fori_loop(0, steps, step, 0)

    slots, rows = n // radix, per * UNIT
    size = min(256, slots * rows)
    for k in range(radix):
        out = own if k == 0 else sums

        def weigh(r, carry):
            at = pl.multiple_of(r * size, size)
            got = jnp.zeros((size, out.shape[1]), jnp.float32)
            for acc, (_, w, h) in zip(accs, parts):
                value = acc[pl.ds(k * slots * rows + at, size), :]
                high = value.astype(jnp.bfloat16)
                low = (value - high.astype(jnp.float32)).astype(jnp.bfloat16)
                got = got + jnp.dot(high, w[h:h + PART, :], preferred_element_type=jnp.float32)
                got = got + jnp.dot(low, w[h:h + PART, :], preferred_element_type=jnp.float32)
            out[pl.ds(at, size), :] = got
            return carry

        lax.fori_loop(0, slots * rows // size, weigh, 0)
        if k == 0:
            for j in range(per):
                at = pl.multiple_of(group_of(core, chunk * per + j, groups) * UNIT, UNIT)
                self = jnp.dot(xo[pl.ds(at, UNIT), :], so[...], preferred_element_type=jnp.float32)
                self = self + jnp.dot(xp[pl.ds(at, UNIT), :], sp[...], preferred_element_type=jnp.float32)
                out[j * UNIT:(j + 1) * UNIT, :] += self
        else:
            write_coded(outs[k - 1], tail, slots, rows, lambda s: sums[s * rows:(s + 1) * rows, :])


def neighbour_terms(chunk, per, n, radix, groups, ids, table, tbuf, xo, xp, wo, wp, so, sp):
    hidden = wo.shape[1]
    width = xo.shape[1]
    tile = tbuf.shape[2]
    smem = pl.BlockSpec(memory_space=pltpu.SMEM)
    vmem = pl.BlockSpec(memory_space=pltpu.VMEM)
    flops = 2 * tbuf.shape[0] * UNIT * tile * 2 * width + 4 * n * per * UNIT * 2 * width * hidden
    slots, rows = n // radix, per * UNIT
    held = (n * per + 1) * UNIT * 2 * width * 4
    coded = jax.ShapeDtypeStruct((slots * rows + tail_rows(slots), hidden), jnp.int16)
    return pl.pallas_call(
        functools.partial(tiles_kernel, chunk, per, n, radix, groups),
        out_shape=[jax.ShapeDtypeStruct((slots * rows, hidden), jnp.float32)] + [coded] * (radix - 1),
        in_specs=[smem] * 2 + [vmem] * 7,
        out_specs=[vmem] * radix,
        scratch_shapes=[
            pltpu.VMEM((UNIT + 1, UNIT, tile), jnp.bfloat16),
            pltpu.VMEM((slots * rows, hidden), jnp.float32),
            pltpu.VMEM((tail_rows(slots), hidden), jnp.float32),
        ]
        + [pltpu.VMEM(((n * per + 1) * UNIT, PART), jnp.float32)] * (2 * width // PART),
        compiler_params=pltpu.CompilerParams(vmem_limit_bytes=(16 << 20) + held),
        cost_estimate=pl.CostEstimate(flops=flops, bytes_accessed=8 << 20, transcendentals=0),
        name="neighbour_terms",
    )(ids, table, tbuf, xo, xp, wo, wp, so, sp)


def combine_kernel(slots, rows, ways, own, *refs):
    parts = len(refs) - ways - 1
    coded, outs, tail = refs[:parts], refs[parts:parts + ways], refs[parts + ways]
    values = [read_coded(a, slots, rows) for a in coded]

    def total(s):
        got = own[s * rows:(s + 1) * rows, :]
        for value in values:
            got = got + value(s)
        return got

    for i in range(slots // ways):
        outs[0][i * rows:(i + 1) * rows, :] = total(i * ways)
    for k in range(1, ways):
        write_coded(outs[k], tail, slots // ways, rows, lambda s: total(s * ways + k))


def combine(slots, rows, ways, own, coded):
    width = own.shape[1]
    left = slots // ways
    vmem = pl.BlockSpec(memory_space=pltpu.VMEM)
    out = jax.ShapeDtypeStruct((left * rows + tail_rows(left), width), jnp.int16)
    return pl.pallas_call(
        functools.partial(combine_kernel, slots, rows, ways),
        out_shape=[jax.ShapeDtypeStruct((left * rows, width), jnp.float32)] + [out] * (ways - 1),
        in_specs=[vmem] * (1 + len(coded)),
        out_specs=[vmem] * ways,
        scratch_shapes=[pltpu.VMEM((tail_rows(left), width), jnp.float32)],
        compiler_params=pltpu.CompilerParams(vmem_limit_bytes=32 * 1024 * 1024),
        name="combine",
    )(own, *coded)


def hidden_kernel(chunks, parts, rows, *refs):
    out = refs[chunks * parts]
    for c in range(chunks):
        own, coded = refs[c * parts], refs[c * parts + 1:(c + 1) * parts]
        total = own[:rows, :]
        for a in coded:
            total = total + read_coded(a, 1, rows)(0)
        out[c * rows:(c + 1) * rows, :] = jnp.maximum(total, 0.0).astype(jnp.bfloat16)


def hidden_rows(chunk_parts, rows):
    chunks, parts = len(chunk_parts), len(chunk_parts[0])
    width = chunk_parts[0][0].shape[1]
    vmem = pl.BlockSpec(memory_space=pltpu.VMEM)
    flat = [a for part in chunk_parts for a in part]
    return pl.pallas_call(
        functools.partial(hidden_kernel, chunks, parts, rows),
        out_shape=jax.ShapeDtypeStruct((chunks * rows, width), jnp.bfloat16),
        in_specs=[vmem] * len(flat),
        out_specs=vmem,
        compiler_params=pltpu.CompilerParams(vmem_limit_bytes=32 * 1024 * 1024),
        name="hidden_rows",
    )(*flat)


def send_kernel(groups, ways, ids, own, other, sel, hidden, *sends):
    core = ids[0]
    for i in range(groups // 2):
        mine = group_of(core, i, groups)
        theirs = group_of(1 - core, i, groups)
        hidden[pl.ds(pl.multiple_of(mine * UNIT, UNIT), UNIT), :] = own[i * UNIT:(i + 1) * UNIT, :]
        hidden[pl.ds(pl.multiple_of(theirs * UNIT, UNIT), UNIT), :] = other[i * UNIT:(i + 1) * UNIT, :]
    picked = jnp.dot(sel[...], hidden[...], preferred_element_type=jnp.float32).astype(jnp.bfloat16)
    rows = sel.shape[0] // ways
    for k in range(ways):
        sends[k][...] = picked[k * rows:(k + 1) * rows, :]


def rows_to_send(groups, ways, ids, own, other, sel):
    smem = pl.BlockSpec(memory_space=pltpu.SMEM)
    vmem = pl.BlockSpec(memory_space=pltpu.VMEM)
    width = own.shape[1]
    return pl.pallas_call(
        functools.partial(send_kernel, groups, ways),
        out_shape=[jax.ShapeDtypeStruct((groups * UNIT, width), jnp.bfloat16)]
        + [jax.ShapeDtypeStruct((sel.shape[0] // ways, width), jnp.bfloat16)] * ways,
        in_specs=[smem] + [vmem] * 3,
        out_specs=[vmem] * (1 + ways),
        compiler_params=pltpu.CompilerParams(vmem_limit_bytes=32 * 1024 * 1024),
        name="rows_to_send",
    )(ids, own, other, sel)


def regroup_kernel(had, left, ways, slots, *refs):
    parts = len(refs) - ways
    values = [a[...].astype(jnp.float32) for a in refs[:parts]]
    for k in range(ways):
        pieces = []
        for value in values:
            for p in range(had):
                for r in range(left // ways):
                    at = (p * left + r * ways + k) * slots
                    pieces.append(value[at:at + slots, :])
        refs[parts + k][...] = jnp.concatenate(pieces, axis=0).astype(jnp.bfloat16)


def regroup(had, left, ways, slots, arrays):
    rows, width = arrays[0].shape
    vmem = pl.BlockSpec(memory_space=pltpu.VMEM)
    out = jax.ShapeDtypeStruct((len(arrays) * rows // ways, width), jnp.bfloat16)
    return pl.pallas_call(
        functools.partial(regroup_kernel, had, left, ways, slots),
        out_shape=[out] * ways,
        in_specs=[vmem] * len(arrays),
        out_specs=[vmem] * ways,
        compiler_params=pltpu.CompilerParams(vmem_limit_bytes=32 * 1024 * 1024),
        name="regroup",
    )(*arrays)


def logits_kernel(order, slots, ids, hidden, adj, w_self, w_neigh, *refs):
    arrived, (out, pool) = refs[:-2], refs[-2:]
    me = ids[1]
    tile, rows = hidden.shape[0], adj.shape[0]
    at = 0
    for a in arrived:
        value = a[...].astype(jnp.float32)
        for i in range(a.shape[0] // slots):
            sender = jnp.bitwise_xor(me, order[at])
            pool[pl.ds(pl.multiple_of(sender * slots, slots), slots), :] = value[i * slots:(i + 1) * slots, :]
            at += 1
    mean = jnp.dot(adj[:, :tile], hidden[...], preferred_element_type=jnp.float32)
    mean = mean + jnp.dot(adj[:, tile:], pool[...].astype(jnp.bfloat16), preferred_element_type=jnp.float32)
    dims = (((1,), (1,)), ((), ()))
    got = lax.dot_general(hidden[:rows, :], w_self[...], dims, preferred_element_type=jnp.float32)
    got = got + lax.dot_general(mean.astype(jnp.bfloat16), w_neigh[...], dims, preferred_element_type=jnp.float32)
    out[...] = got


def logits_of(order, slots, ids, hidden, adj, w_self, w_neigh, arrived):
    smem = pl.BlockSpec(memory_space=pltpu.SMEM)
    vmem = pl.BlockSpec(memory_space=pltpu.VMEM)
    return pl.pallas_call(
        functools.partial(logits_kernel, order, slots),
        out_shape=jax.ShapeDtypeStruct((adj.shape[0], w_self.shape[1]), jnp.float32),
        in_specs=[smem] + [vmem] * (4 + len(arrived)),
        out_specs=vmem,
        scratch_shapes=[pltpu.VMEM((len(order) * slots, hidden.shape[1]), jnp.float32)],
        compiler_params=pltpu.CompilerParams(vmem_limit_bytes=32 * 1024 * 1024),
        name="logits",
    )(ids, hidden, adj, w_self.T, w_neigh.T, *arrived)


def exchange(parts, stride, n):
    got = [parts[0]]
    for k in reversed(range(1, len(parts))):
        got.append(lax.ppermute(parts[k], "dom", [(i, i ^ (k * stride)) for i in range(n)]))
    return got


def body(
    features,
    tile_weight,
    tile_dst,
    tile_src,
    tile_rows,
    w_self1,
    neighbour_weight_first,
    send_list,
    send_count,
    adj_two,
    w_self2,
    w_neigh2,
):
    n = lax.axis_size("dom")
    tile = tile_weight.shape[1]
    groups = tile // UNIT
    per = groups // 2 // CHUNKS
    bits = n.bit_length() - 1
    assert n == 1 << bits and bits >= 2
    radices = [2] * (bits // 2) + [1] * (bits % 2)
    ids = jnp.stack([lax.axis_index("feat"), lax.axis_index("dom")]).astype(jnp.int32)
    swap = [(0, 1), (1, 0)]
    xp = lax.ppermute(features, "feat", swap)
    wp = lax.ppermute(neighbour_weight_first, "feat", swap)
    sp = lax.ppermute(w_self1, "feat", swap)
    tw = tile_weight.reshape(tile_weight.shape[0], groups, UNIT, tile)
    planned = plan(
        CHUNKS, per, n, 4, ids, tile_src, tile_rows, tile_dst, send_list, send_count, tw, features,
        neighbour_weight_first, w_self1,
    )
    tables, tbufs, (sel, xo, wo, so) = planned[:CHUNKS], planned[CHUNKS:2 * CHUNKS], planned[2 * CHUNKS:]
    done = []
    for chunk in range(CHUNKS):
        parts = neighbour_terms(chunk, per, n, 4, groups, ids, tables[chunk], tbufs[chunk], xo, xp, wo, wp, so, sp)
        got = exchange(parts, 1, n)
        stride = 4
        for radix in radices[1:]:
            ways = 1 << radix
            parts = combine(n // stride, per * UNIT, ways, got[0], got[1:])
            got = exchange(parts, stride, n)
            stride *= ways
        done.append(got)
    own = hidden_rows(done, per * UNIT)
    other = lax.ppermute(own, "feat", swap)
    hidden, *sends = rows_to_send(groups, 2, ids, own, other, sel)
    slots = send_list.shape[2]
    arrived = exchange(sends, 1, n)
    stride, order, last = 2, [0], [0, 1]
    while stride < n:
        sends = regroup(len(order), n // stride, 2, slots, arrived)
        order = [k + v for k in last for v in order]
        arrived = exchange(sends, stride, n)
        last = [0, stride]
        stride *= 2
    order = tuple(k + v for k in last for v in order)
    return logits_of(order, slots, ids, hidden, adj_two, w_self2, w_neigh2, arrived)


def solution(mesh):
    in_specs = (
        P("dom", "feat"),
        P("dom", None, None),
        P("dom"),
        P("dom"),
        P("dom"),
        P("feat", None),
        P("feat", None),
        P(),
        P(),
        P("dom", None),
        P(),
        P(),
    )
    out_specs = P("dom", None)
    return jax.shard_map(body, mesh=mesh, in_specs=in_specs, out_specs=out_specs, check_vma=False)
```

```python
import functools

import jax
import jax.numpy as jnp
from jax import lax
from jax.experimental import pallas as pl
from jax.experimental.pallas import tpu as pltpu
from jax.sharding import PartitionSpec as P

UNIT = 16
BLOCK = 8
STEP = 8
PART = 256
CHUNKS = 1


def group_of(core, place, groups):
    pair = 2 * (place // 2) + core
    return pair if place % 2 == 0 else groups - 1 - pair


LN2 = 0.6931471805599453


def tail_rows(slots):
    return -(-slots // 16) * 16


def encode(x):
    top = jnp.max(jnp.abs(x), axis=0, keepdims=True)
    power = jnp.ceil(jnp.log(jnp.maximum(top, 1e-30)) * (1.0 / LN2) + 1e-3) - 15.0
    return jnp.floor(x * jnp.exp(power * -LN2) + 0.5), power


def to_int16(x):
    return x.astype(jnp.int32).astype(jnp.int16)


def write_coded(out, tail, slots, rows, value_of):
    tail[...] = jnp.zeros_like(tail)
    for s in range(slots):
        whole, power = encode(value_of(s))
        out[s * rows:(s + 1) * rows, :] = to_int16(whole)
        tail[s:s + 1, :] = power
    out[slots * rows:, :] = to_int16(tail[...])


def read_coded(ref, slots, rows):
    powers = ref[slots * rows:, :].astype(jnp.int32).astype(jnp.float32)

    def value_of(s):
        whole = ref[s * rows:(s + 1) * rows, :].astype(jnp.int32).astype(jnp.float32)
        return whole * jnp.exp(powers[s:s + 1, :] * LN2)

    return value_of


def plan_kernel(chunks, per, n, radix, n_src, ids, src_h, rows_h, dst_h, lists_h, counts_h, tw, xo, wo, so, *rest):
    tables, rest = rest[:chunks], rest[chunks:]
    tbufs, rest = rest[:chunks], rest[chunks:]
    sel, xo_out, wo_out, so_out = rest[:4]
    src_v, rows_v, dst_v, lists, counts, sems = rest[4:]
    core, me = ids[0], ids[1]
    tiles = src_v.shape[1]
    n_pos = tables[0].shape[1]
    units = per * tiles
    groups = 2 * per * chunks
    half = groups // 2
    gs = [group_of(core, i, groups) for i in range(half)]
    small = [(src_h, src_v), (rows_h, rows_v), (dst_h, dst_v), (lists_h, lists), (counts_h, counts)]
    large = [(tw.at[:, g], tbufs[i // per].at[pl.ds(i % per * tiles, tiles)]) for i, g in enumerate(gs)]
    large += [(xo, xo_out), (wo, wo_out), (so, so_out)]
    copies = [pltpu.make_async_copy(a, b, sems.at[i]) for i, (a, b) in enumerate(small + large)]
    for c in copies:
        c.start()
    lane = lax.broadcasted_iota(jnp.int32, (1, tiles), 1)
    block_i = lax.broadcasted_iota(jnp.int32, (n_src, tiles), 0)
    before = lax.broadcasted_iota(jnp.int32, (units, units), 0) < lax.broadcasted_iota(jnp.int32, (units, units), 1)
    before = jnp.where(before, 1.0, 0.0).astype(jnp.bfloat16)
    pos_i = lax.broadcasted_iota(jnp.int32, (tiles, n_pos), 1).astype(jnp.float32)
    place_i = lax.broadcasted_iota(jnp.int32, (1, n_pos), 1)
    trash = float(n * per << 14)
    for c in copies[:5]:
        c.wait()
    src, rows = src_v[...], rows_v[...]
    slot = jnp.bitwise_xor(dst_v[...], me)
    slot = jnp.bitwise_and(slot, radix - 1) * (n // radix) + lax.div(slot, radix)
    for c in range(chunks):
        hot, words, valid = [], [], []
        for j in range(per):
            limit = jnp.clip(rows - UNIT * gs[c * per + j], 0, UNIT)
            ok = limit > 0
            valid.append(ok)
            words.append(((slot * per + j) * 512 + (j * tiles + lane)) * 32 + limit)
            hot.append(jnp.where(jnp.logical_and(block_i == src, ok), 1.0, 0.0))
        hot = jnp.concatenate(hot, axis=1)
        earlier = jnp.dot(hot.astype(jnp.bfloat16), before, preferred_element_type=jnp.float32)
        blocks = jnp.floor((jnp.sum(hot, axis=1, keepdims=True) + (BLOCK - 1)) * (1.0 / BLOCK))
        run = jnp.zeros((1, 1), jnp.float32)
        pos = jnp.zeros((1, units), jnp.float32)
        owner = jnp.zeros((1, n_pos), jnp.float32)
        for s in range(n_src):
            pos = pos + hot[s:s + 1, :] * (earlier[s:s + 1, :] + run * BLOCK)
            run = run + blocks[s:s + 1, :]
            owner = owner + jnp.where(place_i.astype(jnp.float32) >= run, 1.0, 0.0)
        stack = [jnp.where(valid[j], pos[:, j * tiles:(j + 1) * tiles], -1.0) for j in range(per)]
        stack += [w.astype(jnp.float32) - trash for w in words]
        stack += [jnp.zeros((1, tiles), jnp.float32)] * (-len(stack) % 8)
        cols = jnp.concatenate(stack, axis=0).T
        found = jnp.zeros((tiles, n_pos), jnp.float32)
        for j in range(per):
            found = found + jnp.where(cols[:, j:j + 1] == pos_i, cols[:, per + j:per + j + 1], 0.0)
        word = jnp.sum(found, axis=0, keepdims=True) + trash
        owner = jnp.where(place_i == n_pos - 1, run, jnp.minimum(owner, n_src - 1.0))
        tables[c][0:1, :] = word.astype(jnp.int32)
        tables[c][1:2, :] = owner.astype(jnp.int32)

    slots = lists.shape[1]
    total = n * slots
    q_n = lax.broadcasted_iota(jnp.int32, (total, n), 0)
    r_n = lax.broadcasted_iota(jnp.int32, (total, n), 1)
    mine = lists[me].astype(jnp.float32)
    cnt = counts[pl.ds(me, 1), :]
    picked = jnp.zeros((total, n), jnp.float32)
    k_n = jnp.bitwise_and(q_n, slots - 1)
    for k in range(slots):
        picked = jnp.where(k_n == k, mine[k:k + 1, :], picked)
    good = jnp.logical_and(lax.div(q_n, slots) == r_n, k_n < cnt)
    row = jnp.sum(jnp.where(good, picked + 1.0, 0.0), axis=1, keepdims=True) - 1.0
    lane = lax.broadcasted_iota(jnp.int32, (1, sel.shape[1]), 1)
    name = jnp.zeros(lane.shape, jnp.int32)
    for i, g in enumerate(gs + [group_of(1 - core, i, groups) for i in range(half)]):
        name = jnp.where(lax.div(lane, UNIT) == i, g * UNIT + jnp.bitwise_and(lane, UNIT - 1), name)
    sel[...] = jnp.where(row == name.astype(jnp.float32), 1.0, 0.0).astype(jnp.bfloat16)

    for c in copies[5:]:
        c.wait()


def plan(chunks, per, n, radix, ids, src, rows, dst, send_list, send_count, tw, xo, wo, so):
    tiles, _, _, tile = tw.shape
    slots = send_list.shape[2]
    n_src = xo.shape[0] // tile
    blocks = -(-(per * tiles // BLOCK + n_src) // STEP) * STEP
    n_pos = -(-(blocks * BLOCK + 1) // 128) * 128
    smem = pl.BlockSpec(memory_space=pltpu.SMEM)
    vmem = pl.BlockSpec(memory_space=pltpu.VMEM)
    hbm = pl.BlockSpec(memory_space=pltpu.HBM)
    lists = jnp.swapaxes(send_list, 1, 2)
    half = chunks * per
    return pl.pallas_call(
        functools.partial(plan_kernel, chunks, per, n, radix, n_src),
        out_shape=[jax.ShapeDtypeStruct((2, n_pos), jnp.int32)] * chunks
        + [jax.ShapeDtypeStruct((per * tiles, UNIT, tile), tw.dtype)] * chunks
        + [
            jax.ShapeDtypeStruct((n * slots, 2 * half * UNIT), jnp.bfloat16),
            jax.ShapeDtypeStruct(xo.shape, xo.dtype),
            jax.ShapeDtypeStruct(wo.shape, wo.dtype),
            jax.ShapeDtypeStruct(so.shape, so.dtype),
        ],
        in_specs=[smem] + [hbm] * 9,
        out_specs=[vmem] * (2 * chunks + 4),
        scratch_shapes=[
            pltpu.VMEM((1, tiles), jnp.int32),
            pltpu.VMEM((1, tiles), jnp.int32),
            pltpu.VMEM((1, tiles), jnp.int32),
            pltpu.VMEM(lists.shape, jnp.int32),
            pltpu.VMEM(send_count.shape, jnp.int32),
            pltpu.SemaphoreType.DMA((5 + half + 3,)),
        ],
        compiler_params=pltpu.CompilerParams(vmem_limit_bytes=32 * 1024 * 1024),
        name="plan",
    )(ids, *[
        pltpu.with_memory_space_constraint(a, pltpu.HBM)
        for a in (src.reshape(1, tiles), rows.reshape(1, tiles), dst.reshape(1, tiles), lists, send_count, tw, xo, wo, so)
    ])


def tiles_kernel(table_v, tbuf, xo, xp, *rest):
    parts = len(rest) - 3
    accs, (masks, table, sem) = rest[:parts], rest[parts:]
    tile = tbuf.shape[2]
    width = xo.shape[1]
    to_scalar = pltpu.make_async_copy(table_v, table, sem)
    to_scalar.start()
    for acc in accs:
        acc[...] = jnp.zeros_like(acc)
    row_i = lax.broadcasted_iota(jnp.int32, (UNIT, tile), 0)
    for m in range(UNIT + 1):
        masks[m] = jnp.where(row_i < m, 1.0, 0.0).astype(jnp.bfloat16)
    columns = [(x, h) for x in (xo, xp) for h in range(0, width, PART)]
    to_scalar.wait()

    def step(i, carry):
        for m in range(STEP):
            b = i * STEP + m
            base = pl.multiple_of(table[1, b] * tile, tile)
            rows, places = [], []
            for k in range(BLOCK):
                word = table[0, b * BLOCK + k]
                u = jnp.bitwise_and(lax.shift_right_logical(word, 5), 511)
                rows.append(tbuf[u] * masks[jnp.bitwise_and(word, 31)])
                places.append(pl.multiple_of(lax.shift_right_logical(word, 14) * UNIT, UNIT))
            lhs = jnp.concatenate(rows, axis=0)
            for acc, (x, h) in zip(accs, columns):
                got = jnp.dot(lhs, x[pl.ds(base, tile), h:h + PART], preferred_element_type=jnp.float32)
                got = got.astype(jnp.bfloat16).astype(jnp.float32)
                for k in range(BLOCK):
                    acc[pl.ds(places[k], UNIT), :] += got[k * UNIT:(k + 1) * UNIT, :]
        return carry

    steps = lax.div(table[1, table.shape[1] - 1] + STEP - 1, STEP)
    lax.fori_loop(0, steps, step, 0)


def gathered_sums(per, n, table, tbuf, xo, xp):
    width = xo.shape[1]
    tile = tbuf.shape[2]
    vmem = pl.BlockSpec(memory_space=pltpu.VMEM)
    flops = 2 * tbuf.shape[0] * UNIT * tile * 2 * width
    parts = 2 * width // PART
    sums = jax.ShapeDtypeStruct(((n * per + 1) * UNIT, PART), jnp.float32)
    return pl.pallas_call(
        tiles_kernel,
        out_shape=[sums] * parts,
        in_specs=[vmem] * 4,
        out_specs=[vmem] * parts,
        scratch_shapes=[
            pltpu.VMEM((UNIT + 1, UNIT, tile), jnp.bfloat16),
            pltpu.SMEM(table.shape, jnp.int32),
            pltpu.SemaphoreType.DMA,
        ],
        compiler_params=pltpu.CompilerParams(vmem_limit_bytes=(12 << 20) + sums.size * 4 * parts),
        cost_estimate=pl.CostEstimate(flops=flops, bytes_accessed=8 << 20, transcendentals=0),
        name="gathered_sums",
    )(table, tbuf, xo, xp)


def weigh(accs, weights, first, count, out):
    size = min(256, count)

    def piece(r, carry):
        at = pl.multiple_of(r * size, size)
        got = jnp.zeros((size, out.shape[1]), jnp.float32)
        for i, acc in enumerate(accs):
            w, h = weights[i * PART // weights[0].shape[0]], i * PART % weights[0].shape[0]
            value = acc[pl.ds(first + at, size), :]
            high = value.astype(jnp.bfloat16)
            low = (value - high.astype(jnp.float32)).astype(jnp.bfloat16)
            got = got + jnp.dot(high, w[h:h + PART, :], preferred_element_type=jnp.float32)
            got = got + jnp.dot(low, w[h:h + PART, :], preferred_element_type=jnp.float32)
        out[pl.ds(at, size), :] = got
        return carry

    lax.fori_loop(0, count // size, piece, 0)


def sent_kernel(k, slots, rows, parts, wo, wp, *refs):
    accs, (out, sums, tail) = refs[:parts], refs[parts:]
    weigh(accs, (wo, wp), k * slots * rows, slots * rows, sums)
    write_coded(out, tail, slots, rows, lambda s: sums[s * rows:(s + 1) * rows, :])


def sent_terms(k, slots, rows, accs, wo, wp):
    hidden = wo.shape[1]
    vmem = pl.BlockSpec(memory_space=pltpu.VMEM)
    return pl.pallas_call(
        functools.partial(sent_kernel, k, slots, rows, len(accs)),
        out_shape=jax.ShapeDtypeStruct((slots * rows + tail_rows(slots), hidden), jnp.int16),
        in_specs=[vmem] * (2 + len(accs)),
        out_specs=vmem,
        scratch_shapes=[
            pltpu.VMEM((slots * rows, hidden), jnp.float32),
            pltpu.VMEM((tail_rows(slots), hidden), jnp.float32),
        ],
        compiler_params=pltpu.CompilerParams(vmem_limit_bytes=(12 << 20) + accs[0].size * 4 * len(accs)),
        cost_estimate=pl.CostEstimate(
            flops=4 * slots * rows * PART * len(accs) * hidden, bytes_accessed=2 << 20, transcendentals=0),
        name="sent_terms",
    )(wo, wp, *accs)


def own_kernel(chunk, per, groups, parts, ids, wo, wp, xo, xp, so, sp, *refs):
    accs, out = refs[:parts], refs[parts]
    weigh(accs, (wo, wp), 0, out.shape[0], out)
    for j in range(per):
        at = pl.multiple_of(group_of(ids[0], chunk * per + j, groups) * UNIT, UNIT)
        self = jnp.dot(xo[pl.ds(at, UNIT), :], so[...], preferred_element_type=jnp.float32)
        self = self + jnp.dot(xp[pl.ds(at, UNIT), :], sp[...], preferred_element_type=jnp.float32)
        out[j * UNIT:(j + 1) * UNIT, :] += self


def own_terms(chunk, per, groups, slots, ids, accs, wo, wp, xo, xp, so, sp):
    hidden = wo.shape[1]
    rows = per * UNIT
    smem = pl.BlockSpec(memory_space=pltpu.SMEM)
    vmem = pl.BlockSpec(memory_space=pltpu.VMEM)
    return pl.pallas_call(
        functools.partial(own_kernel, chunk, per, groups, len(accs)),
        out_shape=jax.ShapeDtypeStruct((slots * rows, hidden), jnp.float32),
        in_specs=[smem] + [vmem] * (6 + len(accs)),
        out_specs=vmem,
        compiler_params=pltpu.CompilerParams(vmem_limit_bytes=(12 << 20) + accs[0].size * 4 * len(accs)),
        cost_estimate=pl.CostEstimate(
            flops=4 * slots * rows * PART * len(accs) * hidden, bytes_accessed=2 << 20, transcendentals=0),
        name="own_terms",
    )(ids, wo, wp, xo, xp, so, sp, *accs)


def combine_kernel(slots, rows, ways, own, *refs):
    parts = len(refs) - ways - 1
    coded, outs, tail = refs[:parts], refs[parts:parts + ways], refs[parts + ways]
    values = [read_coded(a, slots, rows) for a in coded]

    def total(s):
        got = own[s * rows:(s + 1) * rows, :]
        for value in values:
            got = got + value(s)
        return got

    for i in range(slots // ways):
        outs[0][i * rows:(i + 1) * rows, :] = total(i * ways)
    for k in range(1, ways):
        write_coded(outs[k], tail, slots // ways, rows, lambda s: total(s * ways + k))


def combine(slots, rows, ways, own, coded):
    width = own.shape[1]
    left = slots // ways
    vmem = pl.BlockSpec(memory_space=pltpu.VMEM)
    out = jax.ShapeDtypeStruct((left * rows + tail_rows(left), width), jnp.int16)
    return pl.pallas_call(
        functools.partial(combine_kernel, slots, rows, ways),
        out_shape=[jax.ShapeDtypeStruct((left * rows, width), jnp.float32)] + [out] * (ways - 1),
        in_specs=[vmem] * (1 + len(coded)),
        out_specs=[vmem] * ways,
        scratch_shapes=[pltpu.VMEM((tail_rows(left), width), jnp.float32)],
        compiler_params=pltpu.CompilerParams(vmem_limit_bytes=32 * 1024 * 1024),
        name="combine",
    )(own, *coded)


def hidden_kernel(chunks, parts, rows, *refs):
    out = refs[chunks * parts]
    for c in range(chunks):
        own, coded = refs[c * parts], refs[c * parts + 1:(c + 1) * parts]
        total = own[:rows, :]
        for a in coded:
            total = total + read_coded(a, 1, rows)(0)
        out[c * rows:(c + 1) * rows, :] = jnp.maximum(total, 0.0).astype(jnp.bfloat16)


def hidden_rows(chunk_parts, rows):
    chunks, parts = len(chunk_parts), len(chunk_parts[0])
    width = chunk_parts[0][0].shape[1]
    vmem = pl.BlockSpec(memory_space=pltpu.VMEM)
    flat = [a for part in chunk_parts for a in part]
    return pl.pallas_call(
        functools.partial(hidden_kernel, chunks, parts, rows),
        out_shape=jax.ShapeDtypeStruct((chunks * rows, width), jnp.bfloat16),
        in_specs=[vmem] * len(flat),
        out_specs=vmem,
        compiler_params=pltpu.CompilerParams(vmem_limit_bytes=32 * 1024 * 1024),
        name="hidden_rows",
    )(*flat)


def send_kernel(own, other, sel, send):
    both = jnp.concatenate([own[...], other[...]], axis=0)
    send[...] = jnp.dot(sel[...], both, preferred_element_type=jnp.float32).astype(jnp.bfloat16)


def rows_to_send(own, other, sel):
    vmem = pl.BlockSpec(memory_space=pltpu.VMEM)
    return pl.pallas_call(
        send_kernel,
        out_shape=jax.ShapeDtypeStruct((sel.shape[0], own.shape[1]), jnp.bfloat16),
        in_specs=[vmem] * 3,
        out_specs=vmem,
        compiler_params=pltpu.CompilerParams(vmem_limit_bytes=32 * 1024 * 1024),
        name="rows_to_send",
    )(own, other, sel)


def local_kernel(groups, ids, own, other, adj, w_self, part, logits, hidden):
    core = ids[0]
    for i in range(groups // 2):
        mine = group_of(core, i, groups)
        theirs = group_of(1 - core, i, groups)
        hidden[pl.ds(pl.multiple_of(mine * UNIT, UNIT), UNIT), :] = own[i * UNIT:(i + 1) * UNIT, :]
        hidden[pl.ds(pl.multiple_of(theirs * UNIT, UNIT), UNIT), :] = other[i * UNIT:(i + 1) * UNIT, :]
    tile, rows = hidden.shape[0], adj.shape[0]
    part[...] = jnp.dot(adj[:, :tile], hidden[...], preferred_element_type=jnp.float32)
    dims = (((1,), (1,)), ((), ()))
    logits[...] = lax.dot_general(hidden[:rows, :], w_self[...], dims, preferred_element_type=jnp.float32)


def local_terms(groups, ids, own, other, adj, w_self):
    smem = pl.BlockSpec(memory_space=pltpu.SMEM)
    vmem = pl.BlockSpec(memory_space=pltpu.VMEM)
    width = own.shape[1]
    return pl.pallas_call(
        functools.partial(local_kernel, groups),
        out_shape=[
            jax.ShapeDtypeStruct((adj.shape[0], width), jnp.float32),
            jax.ShapeDtypeStruct((adj.shape[0], w_self.shape[1]), jnp.float32),
        ],
        in_specs=[smem] + [vmem] * 4,
        out_specs=[vmem] * 2,
        scratch_shapes=[pltpu.VMEM((groups * UNIT, width), jnp.bfloat16)],
        compiler_params=pltpu.CompilerParams(vmem_limit_bytes=32 * 1024 * 1024),
        name="local_terms",
    )(ids, own, other, adj, w_self.T)


def logits_kernel(part, logits, received, adj, w_neigh, out):
    tile = adj.shape[1] - received.shape[0]
    mean = part[...] + jnp.dot(adj[:, tile:], received[...], preferred_element_type=jnp.float32)
    dims = (((1,), (1,)), ((), ()))
    got = lax.dot_general(mean.astype(jnp.bfloat16), w_neigh[...], dims, preferred_element_type=jnp.float32)
    out[...] = logits[...] + got


def logits_of(part, logits, received, adj, w_neigh):
    vmem = pl.BlockSpec(memory_space=pltpu.VMEM)
    return pl.pallas_call(
        logits_kernel,
        out_shape=jax.ShapeDtypeStruct(logits.shape, jnp.float32),
        in_specs=[vmem] * 5,
        out_specs=vmem,
        compiler_params=pltpu.CompilerParams(vmem_limit_bytes=32 * 1024 * 1024),
        name="logits",
    )(part, logits, received, adj, w_neigh.T)


def exchange(parts, stride, n, places):
    got = [parts[0]]
    for k in places:
        got.append(lax.ppermute(parts[k], "dom", [(i, i ^ (k * stride)) for i in range(n)]))
    return got


def body(
    features,
    tile_weight,
    tile_dst,
    tile_src,
    tile_rows,
    w_self1,
    neighbour_weight_first,
    send_list,
    send_count,
    adj_two,
    w_self2,
    w_neigh2,
):
    n = lax.axis_size("dom")
    tile = tile_weight.shape[1]
    groups = tile // UNIT
    per = groups // 2 // CHUNKS
    bits = n.bit_length() - 1
    assert n == 1 << bits and bits >= 2
    radices = [2] * (bits // 2) + [1] * (bits % 2)
    ids = jnp.stack([lax.axis_index("feat"), lax.axis_index("dom")]).astype(jnp.int32)
    swap = [(0, 1), (1, 0)]
    xp = lax.ppermute(features, "feat", swap)
    wp = lax.ppermute(neighbour_weight_first, "feat", swap)
    sp = lax.ppermute(w_self1, "feat", swap)
    tw = tile_weight.reshape(tile_weight.shape[0], groups, UNIT, tile)
    planned = plan(
        CHUNKS, per, n, 4, ids, tile_src, tile_rows, tile_dst, send_list, send_count, tw, features,
        neighbour_weight_first, w_self1,
    )
    tables, tbufs, (sel, xo, wo, so) = planned[:CHUNKS], planned[CHUNKS:2 * CHUNKS], planned[2 * CHUNKS:]
    done = []
    for chunk in range(CHUNKS):
        accs = gathered_sums(per, n, tables[chunk], tbufs[chunk], xo, xp)
        slots, rows = n // 4, per * UNIT
        parts = {k: sent_terms(k, slots, rows, accs, wo, wp) for k in (1, 2, 3)}
        parts[0] = own_terms(chunk, per, groups, slots, ids, accs, wo, wp, xo, xp, so, sp)
        got = exchange(parts, 1, n, (1, 2, 3))
        stride = 4
        for radix in radices[1:]:
            ways = 1 << radix
            parts = combine(n // stride, per * UNIT, ways, got[0], got[1:])
            got = exchange(parts, stride, n, range(ways - 1, 0, -1))
            stride *= ways
        done.append(got)
    own = hidden_rows(done, per * UNIT)
    other = lax.ppermute(own, "feat", swap)
    send = rows_to_send(own, other, sel)
    received = lax.all_to_all(send, "dom", 0, 0, tiled=True)
    part, logits = local_terms(groups, ids, own, other, adj_two, w_self2)
    return logits_of(part, logits, received, adj_two, w_neigh2)


def solution(mesh):
    in_specs = (
        P("dom", "feat"),
        P("dom", None, None),
        P("dom"),
        P("dom"),
        P("dom"),
        P("feat", None),
        P("feat", None),
        P(),
        P(),
        P("dom", None),
        P(),
        P(),
    )
    out_specs = P("dom", None)
    return jax.shard_map(body, mesh=mesh, in_specs=in_specs, out_specs=out_specs, check_vma=False)
```

```python
import functools

import jax
import jax.numpy as jnp
from jax import lax
from jax.experimental import pallas as pl
from jax.experimental.pallas import tpu as pltpu
from jax.sharding import PartitionSpec as P

UNIT = 16
BLOCK = 8
STEP = 8
PART = 256
CHUNKS = 1


def group_of(core, place, groups):
    pair = 2 * (place // 2) + core
    return pair if place % 2 == 0 else groups - 1 - pair


LN2 = 0.6931471805599453


def tail_rows(slots):
    return -(-slots // 16) * 16


def encode(x):
    top = jnp.max(jnp.abs(x), axis=0, keepdims=True)
    power = jnp.ceil(jnp.log(jnp.maximum(top, 1e-30)) * (1.0 / LN2) + 1e-3) - 15.0
    return jnp.floor(x * jnp.exp(power * -LN2) + 0.5), power


def to_int16(x):
    return x.astype(jnp.int32).astype(jnp.int16)


def write_coded(out, tail, slots, rows, value_of):
    tail[...] = jnp.zeros_like(tail)
    for s in range(slots):
        whole, power = encode(value_of(s))
        out[s * rows:(s + 1) * rows, :] = to_int16(whole)
        tail[s:s + 1, :] = power
    out[slots * rows:, :] = to_int16(tail[...])


def read_coded(ref, slots, rows):
    powers = ref[slots * rows:, :].astype(jnp.int32).astype(jnp.float32)

    def value_of(s):
        whole = ref[s * rows:(s + 1) * rows, :].astype(jnp.int32).astype(jnp.float32)
        return whole * jnp.exp(powers[s:s + 1, :] * LN2)

    return value_of


def plan_kernel(chunks, per, n, radix, n_src, ids, src_h, rows_h, dst_h, lists_h, counts_h, tw, xo, wo, so, *rest):
    tables, rest = rest[:chunks], rest[chunks:]
    tbufs, rest = rest[:chunks], rest[chunks:]
    sel, xo_out, wo_out, so_out = rest[:4]
    src_v, rows_v, dst_v, lists, counts, sems = rest[4:]
    core, me = ids[0], ids[1]
    tiles = src_v.shape[1]
    n_pos = tables[0].shape[1]
    units = per * tiles
    groups = 2 * per * chunks
    half = groups // 2
    gs = [group_of(core, i, groups) for i in range(half)]
    small = [(src_h, src_v), (rows_h, rows_v), (dst_h, dst_v), (lists_h, lists), (counts_h, counts)]
    large = [(tw.at[:, g], tbufs[i // per].at[pl.ds(i % per * tiles, tiles)]) for i, g in enumerate(gs)]
    large += [(xo, xo_out), (wo, wo_out), (so, so_out)]
    copies = [pltpu.make_async_copy(a, b, sems.at[i]) for i, (a, b) in enumerate(small + large)]
    for c in copies:
        c.start()
    lane = lax.broadcasted_iota(jnp.int32, (1, tiles), 1)
    block_i = lax.broadcasted_iota(jnp.int32, (n_src, tiles), 0)
    before = lax.broadcasted_iota(jnp.int32, (units, units), 0) < lax.broadcasted_iota(jnp.int32, (units, units), 1)
    before = jnp.where(before, 1.0, 0.0).astype(jnp.bfloat16)
    pos_i = lax.broadcasted_iota(jnp.int32, (tiles, n_pos), 1).astype(jnp.float32)
    place_i = lax.broadcasted_iota(jnp.int32, (1, n_pos), 1)
    trash = float(n * per << 14)
    for c in copies[:5]:
        c.wait()
    src, rows = src_v[...], rows_v[...]
    slot = jnp.bitwise_xor(dst_v[...], me)
    slot = jnp.bitwise_and(slot, radix - 1) * (n // radix) + lax.div(slot, radix)
    for c in range(chunks):
        hot, words, valid = [], [], []
        for j in range(per):
            limit = jnp.clip(rows - UNIT * gs[c * per + j], 0, UNIT)
            ok = limit > 0
            valid.append(ok)
            words.append(((slot * per + j) * 512 + (j * tiles + lane)) * 32 + limit)
            hot.append(jnp.where(jnp.logical_and(block_i == src, ok), 1.0, 0.0))
        hot = jnp.concatenate(hot, axis=1)
        earlier = jnp.dot(hot.astype(jnp.bfloat16), before, preferred_element_type=jnp.float32)
        blocks = jnp.floor((jnp.sum(hot, axis=1, keepdims=True) + (BLOCK - 1)) * (1.0 / BLOCK))
        run = jnp.zeros((1, 1), jnp.float32)
        pos = jnp.zeros((1, units), jnp.float32)
        owner = jnp.zeros((1, n_pos), jnp.float32)
        for s in range(n_src):
            pos = pos + hot[s:s + 1, :] * (earlier[s:s + 1, :] + run * BLOCK)
            run = run + blocks[s:s + 1, :]
            owner = owner + jnp.where(place_i.astype(jnp.float32) >= run, 1.0, 0.0)
        stack = [jnp.where(valid[j], pos[:, j * tiles:(j + 1) * tiles], -1.0) for j in range(per)]
        stack += [w.astype(jnp.float32) - trash for w in words]
        stack += [jnp.zeros((1, tiles), jnp.float32)] * (-len(stack) % 8)
        cols = jnp.concatenate(stack, axis=0).T
        found = jnp.zeros((tiles, n_pos), jnp.float32)
        for j in range(per):
            found = found + jnp.where(cols[:, j:j + 1] == pos_i, cols[:, per + j:per + j + 1], 0.0)
        word = jnp.sum(found, axis=0, keepdims=True) + trash
        owner = jnp.where(place_i == n_pos - 1, run, jnp.minimum(owner, n_src - 1.0))
        tables[c][0:1, :] = word.astype(jnp.int32)
        tables[c][1:2, :] = owner.astype(jnp.int32)

    slots = lists.shape[1]
    total = n * slots
    q_n = lax.broadcasted_iota(jnp.int32, (total, n), 0)
    r_n = lax.broadcasted_iota(jnp.int32, (total, n), 1)
    mine = lists[me].astype(jnp.float32)
    cnt = counts[pl.ds(me, 1), :]
    picked = jnp.zeros((total, n), jnp.float32)
    k_n = jnp.bitwise_and(q_n, slots - 1)
    for k in range(slots):
        picked = jnp.where(k_n == k, mine[k:k + 1, :], picked)
    good = jnp.logical_and(n - 1 - lax.div(q_n, slots) == r_n, k_n < cnt)
    row = jnp.sum(jnp.where(good, picked + 1.0, 0.0), axis=1, keepdims=True) - 1.0
    lane = lax.broadcasted_iota(jnp.int32, (1, sel.shape[1]), 1)
    name = jnp.zeros(lane.shape, jnp.int32)
    for i, g in enumerate(gs + [group_of(1 - core, i, groups) for i in range(half)]):
        name = jnp.where(lax.div(lane, UNIT) == i, g * UNIT + jnp.bitwise_and(lane, UNIT - 1), name)
    sel[...] = jnp.where(row == name.astype(jnp.float32), 1.0, 0.0).astype(jnp.bfloat16)

    for c in copies[5:]:
        c.wait()


def plan(chunks, per, n, radix, ids, src, rows, dst, send_list, send_count, tw, xo, wo, so):
    tiles, _, _, tile = tw.shape
    slots = send_list.shape[2]
    n_src = xo.shape[0] // tile
    blocks = -(-(per * tiles // BLOCK + n_src) // STEP) * STEP
    n_pos = -(-(blocks * BLOCK + 1) // 128) * 128
    smem = pl.BlockSpec(memory_space=pltpu.SMEM)
    vmem = pl.BlockSpec(memory_space=pltpu.VMEM)
    hbm = pl.BlockSpec(memory_space=pltpu.HBM)
    lists = jnp.swapaxes(send_list, 1, 2)
    half = chunks * per
    return pl.pallas_call(
        functools.partial(plan_kernel, chunks, per, n, radix, n_src),
        out_shape=[jax.ShapeDtypeStruct((2, n_pos), jnp.int32)] * chunks
        + [jax.ShapeDtypeStruct((per * tiles, UNIT, tile), tw.dtype)] * chunks
        + [
            jax.ShapeDtypeStruct((n * slots, 2 * half * UNIT), jnp.bfloat16),
            jax.ShapeDtypeStruct(xo.shape, xo.dtype),
            jax.ShapeDtypeStruct(wo.shape, wo.dtype),
            jax.ShapeDtypeStruct(so.shape, so.dtype),
        ],
        in_specs=[smem] + [hbm] * 9,
        out_specs=[vmem] * (2 * chunks + 4),
        scratch_shapes=[
            pltpu.VMEM((1, tiles), jnp.int32),
            pltpu.VMEM((1, tiles), jnp.int32),
            pltpu.VMEM((1, tiles), jnp.int32),
            pltpu.VMEM(lists.shape, jnp.int32),
            pltpu.VMEM(send_count.shape, jnp.int32),
            pltpu.SemaphoreType.DMA((5 + half + 3,)),
        ],
        compiler_params=pltpu.CompilerParams(vmem_limit_bytes=32 * 1024 * 1024),
        name="plan",
    )(ids, *[
        pltpu.with_memory_space_constraint(a, pltpu.HBM)
        for a in (src.reshape(1, tiles), rows.reshape(1, tiles), dst.reshape(1, tiles), lists, send_count, tw, xo, wo, so)
    ])


def tiles_kernel(table_v, tbuf, xo, xp, *rest):
    parts = len(rest) - 3
    accs, (masks, table, sem) = rest[:parts], rest[parts:]
    tile = tbuf.shape[2]
    width = xo.shape[1]
    to_scalar = pltpu.make_async_copy(table_v, table, sem)
    to_scalar.start()
    for acc in accs:
        acc[...] = jnp.zeros_like(acc)
    row_i = lax.broadcasted_iota(jnp.int32, (UNIT, tile), 0)
    for m in range(UNIT + 1):
        masks[m] = jnp.where(row_i < m, 1.0, 0.0).astype(jnp.bfloat16)
    columns = [(x, h) for x in (xo, xp) for h in range(0, width, PART)]
    to_scalar.wait()

    def step(i, carry):
        for m in range(STEP):
            b = i * STEP + m
            base = pl.multiple_of(table[1, b] * tile, tile)
            rows, places = [], []
            for k in range(BLOCK):
                word = table[0, b * BLOCK + k]
                u = jnp.bitwise_and(lax.shift_right_logical(word, 5), 511)
                rows.append(tbuf[u] * masks[jnp.bitwise_and(word, 31)])
                places.append(pl.multiple_of(lax.shift_right_logical(word, 14) * UNIT, UNIT))
            lhs = jnp.concatenate(rows, axis=0)
            for acc, (x, h) in zip(accs, columns):
                got = jnp.dot(lhs, x[pl.ds(base, tile), h:h + PART], preferred_element_type=jnp.float32)
                got = got.astype(jnp.bfloat16).astype(jnp.float32)
                for k in range(BLOCK):
                    acc[pl.ds(places[k], UNIT), :] += got[k * UNIT:(k + 1) * UNIT, :]
        return carry

    steps = lax.div(table[1, table.shape[1] - 1] + STEP - 1, STEP)
    lax.fori_loop(0, steps, step, 0)


def gathered_sums(per, n, table, tbuf, xo, xp):
    width = xo.shape[1]
    tile = tbuf.shape[2]
    vmem = pl.BlockSpec(memory_space=pltpu.VMEM)
    flops = 2 * tbuf.shape[0] * UNIT * tile * 2 * width
    parts = 2 * width // PART
    sums = jax.ShapeDtypeStruct(((n * per + 1) * UNIT, PART), jnp.float32)
    return pl.pallas_call(
        tiles_kernel,
        out_shape=[sums] * parts,
        in_specs=[vmem] * 4,
        out_specs=[vmem] * parts,
        scratch_shapes=[
            pltpu.VMEM((UNIT + 1, UNIT, tile), jnp.bfloat16),
            pltpu.SMEM(table.shape, jnp.int32),
            pltpu.SemaphoreType.DMA,
        ],
        compiler_params=pltpu.CompilerParams(vmem_limit_bytes=(12 << 20) + sums.size * 4 * parts),
        cost_estimate=pl.CostEstimate(flops=flops, bytes_accessed=8 << 20, transcendentals=0),
        name="gathered_sums",
    )(table, tbuf, xo, xp)


def weigh(accs, weights, first, count, out):
    size = min(256, count)

    def piece(r, carry):
        at = pl.multiple_of(r * size, size)
        got = jnp.zeros((size, out.shape[1]), jnp.float32)
        for i, acc in enumerate(accs):
            w, h = weights[i * PART // weights[0].shape[0]], i * PART % weights[0].shape[0]
            value = acc[pl.ds(first + at, size), :]
            high = value.astype(jnp.bfloat16)
            low = (value - high.astype(jnp.float32)).astype(jnp.bfloat16)
            got = got + jnp.dot(high, w[h:h + PART, :], preferred_element_type=jnp.float32)
            got = got + jnp.dot(low, w[h:h + PART, :], preferred_element_type=jnp.float32)
        out[pl.ds(at, size), :] = got
        return carry

    lax.fori_loop(0, count // size, piece, 0)


def sent_kernel(k, slots, rows, parts, wo, wp, *refs):
    accs, (out, sums, tail) = refs[:parts], refs[parts:]
    weigh(accs, (wo, wp), k * slots * rows, slots * rows, sums)
    write_coded(out, tail, slots, rows, lambda s: sums[s * rows:(s + 1) * rows, :])


def sent_terms(k, slots, rows, accs, wo, wp):
    hidden = wo.shape[1]
    vmem = pl.BlockSpec(memory_space=pltpu.VMEM)
    return pl.pallas_call(
        functools.partial(sent_kernel, k, slots, rows, len(accs)),
        out_shape=jax.ShapeDtypeStruct((slots * rows + tail_rows(slots), hidden), jnp.int16),
        in_specs=[vmem] * (2 + len(accs)),
        out_specs=vmem,
        scratch_shapes=[
            pltpu.VMEM((slots * rows, hidden), jnp.float32),
            pltpu.VMEM((tail_rows(slots), hidden), jnp.float32),
        ],
        compiler_params=pltpu.CompilerParams(vmem_limit_bytes=(12 << 20) + accs[0].size * 4 * len(accs)),
        cost_estimate=pl.CostEstimate(
            flops=4 * slots * rows * PART * len(accs) * hidden, bytes_accessed=2 << 20, transcendentals=0),
        name="sent_terms",
    )(wo, wp, *accs)


def own_kernel(chunk, per, groups, parts, ids, wo, wp, xo, xp, so, sp, *refs):
    accs, out = refs[:parts], refs[parts]
    weigh(accs, (wo, wp), 0, out.shape[0], out)
    for j in range(per):
        at = pl.multiple_of(group_of(ids[0], chunk * per + j, groups) * UNIT, UNIT)
        self = jnp.dot(xo[pl.ds(at, UNIT), :], so[...], preferred_element_type=jnp.float32)
        self = self + jnp.dot(xp[pl.ds(at, UNIT), :], sp[...], preferred_element_type=jnp.float32)
        out[j * UNIT:(j + 1) * UNIT, :] += self


def own_terms(chunk, per, groups, slots, ids, accs, wo, wp, xo, xp, so, sp):
    hidden = wo.shape[1]
    rows = per * UNIT
    smem = pl.BlockSpec(memory_space=pltpu.SMEM)
    vmem = pl.BlockSpec(memory_space=pltpu.VMEM)
    return pl.pallas_call(
        functools.partial(own_kernel, chunk, per, groups, len(accs)),
        out_shape=jax.ShapeDtypeStruct((slots * rows, hidden), jnp.float32),
        in_specs=[smem] + [vmem] * (6 + len(accs)),
        out_specs=vmem,
        compiler_params=pltpu.CompilerParams(vmem_limit_bytes=(12 << 20) + accs[0].size * 4 * len(accs)),
        cost_estimate=pl.CostEstimate(
            flops=4 * slots * rows * PART * len(accs) * hidden, bytes_accessed=2 << 20, transcendentals=0),
        name="own_terms",
    )(ids, wo, wp, xo, xp, so, sp, *accs)


def combine_kernel(slots, rows, ways, own, *refs):
    parts = len(refs) - ways - 1
    coded, outs, tail = refs[:parts], refs[parts:parts + ways], refs[parts + ways]
    values = [read_coded(a, slots, rows) for a in coded]

    def total(s):
        got = own[s * rows:(s + 1) * rows, :]
        for value in values:
            got = got + value(s)
        return got

    for i in range(slots // ways):
        outs[0][i * rows:(i + 1) * rows, :] = total(i * ways)
    for k in range(1, ways):
        write_coded(outs[k], tail, slots // ways, rows, lambda s: total(s * ways + k))


def combine(slots, rows, ways, own, coded):
    width = own.shape[1]
    left = slots // ways
    vmem = pl.BlockSpec(memory_space=pltpu.VMEM)
    out = jax.ShapeDtypeStruct((left * rows + tail_rows(left), width), jnp.int16)
    return pl.pallas_call(
        functools.partial(combine_kernel, slots, rows, ways),
        out_shape=[jax.ShapeDtypeStruct((left * rows, width), jnp.float32)] + [out] * (ways - 1),
        in_specs=[vmem] * (1 + len(coded)),
        out_specs=[vmem] * ways,
        scratch_shapes=[pltpu.VMEM((tail_rows(left), width), jnp.float32)],
        compiler_params=pltpu.CompilerParams(vmem_limit_bytes=32 * 1024 * 1024),
        name="combine",
    )(own, *coded)


def hidden_kernel(chunks, parts, rows, *refs):
    out = refs[chunks * parts]
    for c in range(chunks):
        own, coded = refs[c * parts], refs[c * parts + 1:(c + 1) * parts]
        total = own[:rows, :]
        for a in coded:
            total = total + read_coded(a, 1, rows)(0)
        out[c * rows:(c + 1) * rows, :] = jnp.maximum(total, 0.0).astype(jnp.bfloat16)


def hidden_rows(chunk_parts, rows):
    chunks, parts = len(chunk_parts), len(chunk_parts[0])
    width = chunk_parts[0][0].shape[1]
    vmem = pl.BlockSpec(memory_space=pltpu.VMEM)
    flat = [a for part in chunk_parts for a in part]
    return pl.pallas_call(
        functools.partial(hidden_kernel, chunks, parts, rows),
        out_shape=jax.ShapeDtypeStruct((chunks * rows, width), jnp.bfloat16),
        in_specs=[vmem] * len(flat),
        out_specs=vmem,
        compiler_params=pltpu.CompilerParams(vmem_limit_bytes=32 * 1024 * 1024),
        name="hidden_rows",
    )(*flat)


def send_kernel(own, other, sel, send):
    both = jnp.concatenate([own[...], other[...]], axis=0)
    send[...] = jnp.dot(sel[...], both, preferred_element_type=jnp.float32).astype(jnp.bfloat16)


def rows_to_send(own, other, sel):
    vmem = pl.BlockSpec(memory_space=pltpu.VMEM)
    return pl.pallas_call(
        send_kernel,
        out_shape=jax.ShapeDtypeStruct((sel.shape[0], own.shape[1]), jnp.bfloat16),
        in_specs=[vmem] * 3,
        out_specs=vmem,
        compiler_params=pltpu.CompilerParams(vmem_limit_bytes=32 * 1024 * 1024),
        name="rows_to_send",
    )(own, other, sel)


def local_kernel(groups, ids, own, other, adj, w_self, part, logits, hidden):
    core = ids[0]
    for i in range(groups // 2):
        mine = group_of(core, i, groups)
        theirs = group_of(1 - core, i, groups)
        hidden[pl.ds(pl.multiple_of(mine * UNIT, UNIT), UNIT), :] = own[i * UNIT:(i + 1) * UNIT, :]
        hidden[pl.ds(pl.multiple_of(theirs * UNIT, UNIT), UNIT), :] = other[i * UNIT:(i + 1) * UNIT, :]
    tile, rows = hidden.shape[0], adj.shape[0]
    part[...] = jnp.dot(adj[:, :tile], hidden[...], preferred_element_type=jnp.float32)
    dims = (((1,), (1,)), ((), ()))
    logits[...] = lax.dot_general(hidden[:rows, :], w_self[...], dims, preferred_element_type=jnp.float32)


def local_terms(groups, ids, own, other, adj, w_self):
    smem = pl.BlockSpec(memory_space=pltpu.SMEM)
    vmem = pl.BlockSpec(memory_space=pltpu.VMEM)
    width = own.shape[1]
    return pl.pallas_call(
        functools.partial(local_kernel, groups),
        out_shape=[
            jax.ShapeDtypeStruct((adj.shape[0], width), jnp.float32),
            jax.ShapeDtypeStruct((adj.shape[0], w_self.shape[1]), jnp.float32),
        ],
        in_specs=[smem] + [vmem] * 4,
        out_specs=[vmem] * 2,
        scratch_shapes=[pltpu.VMEM((groups * UNIT, width), jnp.bfloat16)],
        compiler_params=pltpu.CompilerParams(vmem_limit_bytes=32 * 1024 * 1024),
        name="local_terms",
    )(ids, own, other, adj, w_self.T)


def logits_kernel(slots, part, logits, received, adj, w_neigh, out):
    count = received.shape[0]
    tile = adj.shape[1] - count
    value = received[...].astype(jnp.float32)
    rows = [value[at:at + slots, :] for at in range(count - slots, -1, -slots)]
    rows = jnp.concatenate(rows, axis=0).astype(jnp.bfloat16)
    mean = part[...] + jnp.dot(adj[:, tile:], rows, preferred_element_type=jnp.float32)
    dims = (((1,), (1,)), ((), ()))
    got = lax.dot_general(mean.astype(jnp.bfloat16), w_neigh[...], dims, preferred_element_type=jnp.float32)
    out[...] = logits[...] + got


def logits_of(slots, part, logits, received, adj, w_neigh):
    vmem = pl.BlockSpec(memory_space=pltpu.VMEM)
    return pl.pallas_call(
        functools.partial(logits_kernel, slots),
        out_shape=jax.ShapeDtypeStruct(logits.shape, jnp.float32),
        in_specs=[vmem] * 5,
        out_specs=vmem,
        compiler_params=pltpu.CompilerParams(vmem_limit_bytes=32 * 1024 * 1024),
        name="logits",
    )(part, logits, received, adj, w_neigh.T)


def exchange(parts, stride, n, places):
    got = [parts[0]]
    for k in places:
        got.append(lax.ppermute(parts[k], "dom", [(i, i ^ (k * stride)) for i in range(n)]))
    return got


def body(
    features,
    tile_weight,
    tile_dst,
    tile_src,
    tile_rows,
    w_self1,
    neighbour_weight_first,
    send_list,
    send_count,
    adj_two,
    w_self2,
    w_neigh2,
):
    n = lax.axis_size("dom")
    tile = tile_weight.shape[1]
    groups = tile // UNIT
    per = groups // 2 // CHUNKS
    bits = n.bit_length() - 1
    assert n == 1 << bits and bits >= 2
    radices = [2] * (bits // 2) + [1] * (bits % 2)
    ids = jnp.stack([lax.axis_index("feat"), lax.axis_index("dom")]).astype(jnp.int32)
    swap = [(0, 1), (1, 0)]
    xp = lax.ppermute(features, "feat", swap)
    wp = lax.ppermute(neighbour_weight_first, "feat", swap)
    sp = lax.ppermute(w_self1, "feat", swap)
    tw = tile_weight.reshape(tile_weight.shape[0], groups, UNIT, tile)
    planned = plan(
        CHUNKS, per, n, 4, ids, tile_src, tile_rows, tile_dst, send_list, send_count, tw, features,
        neighbour_weight_first, w_self1,
    )
    tables, tbufs, (sel, xo, wo, so) = planned[:CHUNKS], planned[CHUNKS:2 * CHUNKS], planned[2 * CHUNKS:]
    done = []
    for chunk in range(CHUNKS):
        accs = gathered_sums(per, n, tables[chunk], tbufs[chunk], xo, xp)
        slots, rows = n // 4, per * UNIT
        parts = {k: sent_terms(k, slots, rows, accs, wo, wp) for k in (1, 2, 3)}
        parts[0] = own_terms(chunk, per, groups, slots, ids, accs, wo, wp, xo, xp, so, sp)
        got = exchange(parts, 1, n, (1, 2, 3))
        stride = 4
        for radix in radices[1:]:
            ways = 1 << radix
            parts = combine(n // stride, per * UNIT, ways, got[0], got[1:])
            got = exchange(parts, stride, n, range(ways - 1, 0, -1))
            stride *= ways
        done.append(got)
    own = hidden_rows(done, per * UNIT)
    other = lax.ppermute(own, "feat", swap)
    send = rows_to_send(own, other, sel)
    backwards = [list(range(n - 1, -1, -1))]
    received = lax.all_to_all(send, "dom", 0, 0, axis_index_groups=backwards, tiled=True)
    part, logits = local_terms(groups, ids, own, other, adj_two, w_self2)
    return logits_of(send_list.shape[2], part, logits, received, adj_two, w_neigh2)


def solution(mesh):
    in_specs = (
        P("dom", "feat"),
        P("dom", None, None),
        P("dom"),
        P("dom"),
        P("dom"),
        P("feat", None),
        P("feat", None),
        P(),
        P(),
        P("dom", None),
        P(),
        P(),
    )
    out_specs = P("dom", None)
    return jax.shard_map(body, mesh=mesh, in_specs=in_specs, out_specs=out_specs, check_vma=False)
```

```python
import functools

import jax
import jax.numpy as jnp
from jax import lax
from jax.experimental import pallas as pl
from jax.experimental.pallas import tpu as pltpu
from jax.sharding import PartitionSpec as P

UNIT = 16
BLOCK = 8
STEP = 8
PART = 256
CHUNKS = 1


def group_of(core, place, groups):
    return 2 * place + 1 - core


def group_order(n):
    first = n * 9 // 16
    return [first] + [i for i in range(n - 1, -1, -1) if i != first]


def ordered(block, n):
    first = n * 9 // 16
    down = n - block
    return jnp.where(block == 0, first, jnp.where(down > first, down, down - 1))


LN2 = 0.6931471805599453


def tail_rows(slots):
    return -(-slots // 16) * 16


def encode(x):
    top = jnp.max(jnp.abs(x), axis=0, keepdims=True)
    power = jnp.ceil(jnp.log(jnp.maximum(top, 1e-30)) * (1.0 / LN2) + 1e-3) - 15.0
    return jnp.floor(x * jnp.exp(power * -LN2) + 0.5), power


def to_int16(x):
    return x.astype(jnp.int32).astype(jnp.int16)


def write_coded(out, tail, slots, rows, value_of):
    tail[...] = jnp.zeros_like(tail)
    for s in range(slots):
        whole, power = encode(value_of(s))
        out[s * rows:(s + 1) * rows, :] = to_int16(whole)
        tail[s:s + 1, :] = power
    out[slots * rows:, :] = to_int16(tail[...])


def read_coded(ref, slots, rows):
    powers = ref[slots * rows:, :].astype(jnp.int32).astype(jnp.float32)

    def value_of(s):
        whole = ref[s * rows:(s + 1) * rows, :].astype(jnp.int32).astype(jnp.float32)
        return whole * jnp.exp(powers[s:s + 1, :] * LN2)

    return value_of


def plan_kernel(chunks, per, n, radix, n_src, ids, src_h, rows_h, dst_h, tw, xo, wo, so, *rest):
    tables, rest = rest[:chunks], rest[chunks:]
    tbufs, rest = rest[:chunks], rest[chunks:]
    xo_out, wo_out, so_out = rest[:3]
    src_v, rows_v, dst_v, sems = rest[3:]
    core, me = ids[0], ids[1]
    tiles = src_v.shape[1]
    n_pos = tables[0].shape[1]
    units = per * tiles
    groups = 2 * per * chunks
    half = groups // 2
    gs = [group_of(core, i, groups) for i in range(half)]
    small = [(src_h, src_v), (rows_h, rows_v), (dst_h, dst_v)]
    large = [(tw.at[:, g], tbufs[i // per].at[pl.ds(i % per * tiles, tiles)]) for i, g in enumerate(gs)]
    large += [(xo, xo_out), (wo, wo_out), (so, so_out)]
    copies = [pltpu.make_async_copy(a, b, sems.at[i]) for i, (a, b) in enumerate(small + large)]
    for c in copies:
        c.start()
    lane = lax.broadcasted_iota(jnp.int32, (1, tiles), 1)
    block_i = lax.broadcasted_iota(jnp.int32, (n_src, tiles), 0)
    before = lax.broadcasted_iota(jnp.int32, (units, units), 0) < lax.broadcasted_iota(jnp.int32, (units, units), 1)
    before = jnp.where(before, 1.0, 0.0).astype(jnp.bfloat16)
    pos_i = lax.broadcasted_iota(jnp.int32, (tiles, n_pos), 1).astype(jnp.float32)
    place_i = lax.broadcasted_iota(jnp.int32, (1, n_pos), 1)
    trash = float(n * per << 14)
    for c in copies[:3]:
        c.wait()
    src, rows = src_v[...], rows_v[...]
    slot = jnp.bitwise_xor(dst_v[...], me)
    slot = jnp.bitwise_and(slot, radix - 1) * (n // radix) + lax.div(slot, radix)
    for c in range(chunks):
        hot, words, valid = [], [], []
        for j in range(per):
            limit = jnp.clip(rows - UNIT * gs[c * per + j], 0, UNIT)
            ok = limit > 0
            valid.append(ok)
            words.append(((slot * per + j) * 512 + (j * tiles + lane)) * 32 + limit)
            hot.append(jnp.where(jnp.logical_and(block_i == src, ok), 1.0, 0.0))
        hot = jnp.concatenate(hot, axis=1)
        earlier = jnp.dot(hot.astype(jnp.bfloat16), before, preferred_element_type=jnp.float32)
        blocks = jnp.floor((jnp.sum(hot, axis=1, keepdims=True) + (BLOCK - 1)) * (1.0 / BLOCK))
        run = jnp.zeros((1, 1), jnp.float32)
        pos = jnp.zeros((1, units), jnp.float32)
        owner = jnp.zeros((1, n_pos), jnp.float32)
        for s in range(n_src):
            pos = pos + hot[s:s + 1, :] * (earlier[s:s + 1, :] + run * BLOCK)
            run = run + blocks[s:s + 1, :]
            owner = owner + jnp.where(place_i.astype(jnp.float32) >= run, 1.0, 0.0)
        stack = [jnp.where(valid[j], pos[:, j * tiles:(j + 1) * tiles], -1.0) for j in range(per)]
        stack += [w.astype(jnp.float32) - trash for w in words]
        stack += [jnp.zeros((1, tiles), jnp.float32)] * (-len(stack) % 8)
        cols = jnp.concatenate(stack, axis=0).T
        found = jnp.zeros((tiles, n_pos), jnp.float32)
        for j in range(per):
            found = found + jnp.where(cols[:, j:j + 1] == pos_i, cols[:, per + j:per + j + 1], 0.0)
        word = jnp.sum(found, axis=0, keepdims=True) + trash
        owner = jnp.where(place_i == n_pos - 1, run, jnp.minimum(owner, n_src - 1.0))
        tables[c][0:1, :] = word.astype(jnp.int32)
        tables[c][1:2, :] = owner.astype(jnp.int32)

    for c in copies[3:]:
        c.wait()


def plan(chunks, per, n, radix, ids, src, rows, dst, tw, xo, wo, so):
    tiles, _, _, tile = tw.shape
    n_src = xo.shape[0] // tile
    blocks = -(-(per * tiles // BLOCK + n_src) // STEP) * STEP
    n_pos = -(-(blocks * BLOCK + 1) // 128) * 128
    smem = pl.BlockSpec(memory_space=pltpu.SMEM)
    vmem = pl.BlockSpec(memory_space=pltpu.VMEM)
    hbm = pl.BlockSpec(memory_space=pltpu.HBM)
    half = chunks * per
    return pl.pallas_call(
        functools.partial(plan_kernel, chunks, per, n, radix, n_src),
        out_shape=[jax.ShapeDtypeStruct((2, n_pos), jnp.int32)] * chunks
        + [jax.ShapeDtypeStruct((per * tiles, UNIT, tile), tw.dtype)] * chunks
        + [
            jax.ShapeDtypeStruct(xo.shape, xo.dtype),
            jax.ShapeDtypeStruct(wo.shape, wo.dtype),
            jax.ShapeDtypeStruct(so.shape, so.dtype),
        ],
        in_specs=[smem] + [hbm] * 7,
        out_specs=[vmem] * (2 * chunks + 3),
        scratch_shapes=[
            pltpu.VMEM((1, tiles), jnp.int32),
            pltpu.VMEM((1, tiles), jnp.int32),
            pltpu.VMEM((1, tiles), jnp.int32),
            pltpu.SemaphoreType.DMA((3 + half + 3,)),
        ],
        compiler_params=pltpu.CompilerParams(vmem_limit_bytes=32 * 1024 * 1024),
        name="plan",
    )(ids, *[
        pltpu.with_memory_space_constraint(a, pltpu.HBM)
        for a in (src.reshape(1, tiles), rows.reshape(1, tiles), dst.reshape(1, tiles), tw, xo, wo, so)
    ])


def select_kernel(groups, ids, lists, counts, sel):
    core, me = ids[0], ids[1]
    n = lists.shape[0]
    slots = lists.shape[1]
    total = n * slots
    q_n = lax.broadcasted_iota(jnp.int32, (total, n), 0)
    r_n = lax.broadcasted_iota(jnp.int32, (total, n), 1)
    mine = lists[me].astype(jnp.float32)
    cnt = counts[pl.ds(me, 1), :]
    picked = jnp.zeros((total, n), jnp.float32)
    k_n = jnp.bitwise_and(q_n, slots - 1)
    for k in range(slots):
        picked = jnp.where(k_n == k, mine[k:k + 1, :], picked)
    good = jnp.logical_and(ordered(lax.div(q_n, slots), n) == r_n, k_n < cnt)
    row = jnp.sum(jnp.where(good, picked + 1.0, 0.0), axis=1, keepdims=True) - 1.0
    lane = lax.broadcasted_iota(jnp.int32, (1, sel.shape[1]), 1)
    name = jnp.zeros(lane.shape, jnp.int32)
    names = [group_of(c, i, groups) for c in (core, 1 - core) for i in range(groups // 2)]
    for i, g in enumerate(names):
        name = jnp.where(lax.div(lane, UNIT) == i, g * UNIT + jnp.bitwise_and(lane, UNIT - 1), name)
    sel[...] = jnp.where(row == name.astype(jnp.float32), 1.0, 0.0).astype(jnp.bfloat16)


def selection(groups, ids, send_list, send_count):
    n, _, slots = send_list.shape
    smem = pl.BlockSpec(memory_space=pltpu.SMEM)
    vmem = pl.BlockSpec(memory_space=pltpu.VMEM)
    return pl.pallas_call(
        functools.partial(select_kernel, groups),
        out_shape=jax.ShapeDtypeStruct((n * slots, groups * UNIT), jnp.bfloat16),
        in_specs=[smem, vmem, vmem],
        out_specs=vmem,
        compiler_params=pltpu.CompilerParams(vmem_limit_bytes=32 * 1024 * 1024),
        name="selection",
    )(ids, jnp.swapaxes(send_list, 1, 2), send_count)


def tiles_kernel(table_v, tbuf, xo, xp, *rest):
    parts = len(rest) - 3
    accs, (masks, table, sem) = rest[:parts], rest[parts:]
    tile = tbuf.shape[2]
    width = xo.shape[1]
    to_scalar = pltpu.make_async_copy(table_v, table, sem)
    to_scalar.start()
    for acc in accs:
        acc[...] = jnp.zeros_like(acc)
    row_i = lax.broadcasted_iota(jnp.int32, (UNIT, tile), 0)
    for m in range(UNIT + 1):
        masks[m] = jnp.where(row_i < m, 1.0, 0.0).astype(jnp.bfloat16)
    columns = [(x, h) for x in (xo, xp) for h in range(0, width, PART)]
    to_scalar.wait()

    def step(i, carry):
        for m in range(STEP):
            b = i * STEP + m
            base = pl.multiple_of(table[1, b] * tile, tile)
            rows, places = [], []
            for k in range(BLOCK):
                word = table[0, b * BLOCK + k]
                u = jnp.bitwise_and(lax.shift_right_logical(word, 5), 511)
                rows.append(tbuf[u] * masks[jnp.bitwise_and(word, 31)])
                places.append(pl.multiple_of(lax.shift_right_logical(word, 14) * UNIT, UNIT))
            lhs = jnp.concatenate(rows, axis=0)
            for acc, (x, h) in zip(accs, columns):
                got = jnp.dot(lhs, x[pl.ds(base, tile), h:h + PART], preferred_element_type=jnp.float32)
                got = got.astype(jnp.bfloat16).astype(jnp.float32)
                for k in range(BLOCK):
                    acc[pl.ds(places[k], UNIT), :] += got[k * UNIT:(k + 1) * UNIT, :]
        return carry

    steps = lax.div(table[1, table.shape[1] - 1] + STEP - 1, STEP)
    lax.fori_loop(0, steps, step, 0)


def gathered_sums(per, n, table, tbuf, xo, xp):
    width = xo.shape[1]
    tile = tbuf.shape[2]
    vmem = pl.BlockSpec(memory_space=pltpu.VMEM)
    flops = 2 * tbuf.shape[0] * UNIT * tile * 2 * width
    parts = 2 * width // PART
    sums = jax.ShapeDtypeStruct(((n * per + 1) * UNIT, PART), jnp.float32)
    return pl.pallas_call(
        tiles_kernel,
        out_shape=[sums] * parts,
        in_specs=[vmem] * 4,
        out_specs=[vmem] * parts,
        scratch_shapes=[
            pltpu.VMEM((UNIT + 1, UNIT, tile), jnp.bfloat16),
            pltpu.SMEM(table.shape, jnp.int32),
            pltpu.SemaphoreType.DMA,
        ],
        compiler_params=pltpu.CompilerParams(vmem_limit_bytes=(12 << 20) + sums.size * 4 * parts),
        cost_estimate=pl.CostEstimate(flops=flops, bytes_accessed=8 << 20, transcendentals=0),
        name="gathered_sums",
    )(table, tbuf, xo, xp)


def weigh(accs, weights, first, count, out):
    size = min(256, count)

    def piece(r, carry):
        at = pl.multiple_of(r * size, size)
        got = jnp.zeros((size, out.shape[1]), jnp.float32)
        for i, acc in enumerate(accs):
            w, h = weights[i * PART // weights[0].shape[0]], i * PART % weights[0].shape[0]
            value = acc[pl.ds(first + at, size), :]
            high = value.astype(jnp.bfloat16)
            low = (value - high.astype(jnp.float32)).astype(jnp.bfloat16)
            got = got + jnp.dot(high, w[h:h + PART, :], preferred_element_type=jnp.float32)
            got = got + jnp.dot(low, w[h:h + PART, :], preferred_element_type=jnp.float32)
        out[pl.ds(at, size), :] = got
        return carry

    lax.fori_loop(0, count // size, piece, 0)


def sent_kernel(k, slots, rows, parts, wo, wp, *refs):
    accs, (out, sums, tail) = refs[:parts], refs[parts:]
    weigh(accs, (wo, wp), k * slots * rows, slots * rows, sums)
    write_coded(out, tail, slots, rows, lambda s: sums[s * rows:(s + 1) * rows, :])


def sent_terms(k, slots, rows, accs, wo, wp):
    hidden = wo.shape[1]
    vmem = pl.BlockSpec(memory_space=pltpu.VMEM)
    return pl.pallas_call(
        functools.partial(sent_kernel, k, slots, rows, len(accs)),
        out_shape=jax.ShapeDtypeStruct((slots * rows + tail_rows(slots), hidden), jnp.int16),
        in_specs=[vmem] * (2 + len(accs)),
        out_specs=vmem,
        scratch_shapes=[
            pltpu.VMEM((slots * rows, hidden), jnp.float32),
            pltpu.VMEM((tail_rows(slots), hidden), jnp.float32),
        ],
        compiler_params=pltpu.CompilerParams(vmem_limit_bytes=(12 << 20) + accs[0].size * 4 * len(accs)),
        cost_estimate=pl.CostEstimate(
            flops=4 * slots * rows * PART * len(accs) * hidden, bytes_accessed=2 << 20, transcendentals=0),
        name="sent_terms",
    )(wo, wp, *accs)


def own_kernel(chunk, per, groups, parts, ids, wo, wp, xo, xp, so, sp, *refs):
    accs, out = refs[:parts], refs[parts]
    weigh(accs, (wo, wp), 0, out.shape[0], out)
    for j in range(per):
        at = pl.multiple_of(group_of(ids[0], chunk * per + j, groups) * UNIT, UNIT)
        self = jnp.dot(xo[pl.ds(at, UNIT), :], so[...], preferred_element_type=jnp.float32)
        self = self + jnp.dot(xp[pl.ds(at, UNIT), :], sp[...], preferred_element_type=jnp.float32)
        out[j * UNIT:(j + 1) * UNIT, :] += self


def own_terms(chunk, per, groups, slots, ids, accs, wo, wp, xo, xp, so, sp):
    hidden = wo.shape[1]
    rows = per * UNIT
    smem = pl.BlockSpec(memory_space=pltpu.SMEM)
    vmem = pl.BlockSpec(memory_space=pltpu.VMEM)
    return pl.pallas_call(
        functools.partial(own_kernel, chunk, per, groups, len(accs)),
        out_shape=jax.ShapeDtypeStruct((slots * rows, hidden), jnp.float32),
        in_specs=[smem] + [vmem] * (6 + len(accs)),
        out_specs=vmem,
        compiler_params=pltpu.CompilerParams(vmem_limit_bytes=(12 << 20) + accs[0].size * 4 * len(accs)),
        cost_estimate=pl.CostEstimate(
            flops=4 * slots * rows * PART * len(accs) * hidden, bytes_accessed=2 << 20, transcendentals=0),
        name="own_terms",
    )(ids, wo, wp, xo, xp, so, sp, *accs)


def combine_kernel(slots, rows, ways, own, *refs):
    parts = len(refs) - ways - 1
    coded, outs, tail = refs[:parts], refs[parts:parts + ways], refs[parts + ways]
    values = [read_coded(a, slots, rows) for a in coded]

    def total(s):
        got = own[s * rows:(s + 1) * rows, :]
        for value in values:
            got = got + value(s)
        return got

    for i in range(slots // ways):
        outs[0][i * rows:(i + 1) * rows, :] = total(i * ways)
    for k in range(1, ways):
        write_coded(outs[k], tail, slots // ways, rows, lambda s: total(s * ways + k))


def combine(slots, rows, ways, own, coded):
    width = own.shape[1]
    left = slots // ways
    vmem = pl.BlockSpec(memory_space=pltpu.VMEM)
    out = jax.ShapeDtypeStruct((left * rows + tail_rows(left), width), jnp.int16)
    return pl.pallas_call(
        functools.partial(combine_kernel, slots, rows, ways),
        out_shape=[jax.ShapeDtypeStruct((left * rows, width), jnp.float32)] + [out] * (ways - 1),
        in_specs=[vmem] * (1 + len(coded)),
        out_specs=[vmem] * ways,
        scratch_shapes=[pltpu.VMEM((tail_rows(left), width), jnp.float32)],
        compiler_params=pltpu.CompilerParams(vmem_limit_bytes=32 * 1024 * 1024),
        name="combine",
    )(own, *coded)


def hidden_kernel(chunks, parts, rows, *refs):
    out = refs[chunks * parts]
    for c in range(chunks):
        own, coded = refs[c * parts], refs[c * parts + 1:(c + 1) * parts]
        total = own[:rows, :]
        for a in coded:
            total = total + read_coded(a, 1, rows)(0)
        out[c * rows:(c + 1) * rows, :] = jnp.maximum(total, 0.0).astype(jnp.bfloat16)


def hidden_rows(chunk_parts, rows):
    chunks, parts = len(chunk_parts), len(chunk_parts[0])
    width = chunk_parts[0][0].shape[1]
    vmem = pl.BlockSpec(memory_space=pltpu.VMEM)
    flat = [a for part in chunk_parts for a in part]
    return pl.pallas_call(
        functools.partial(hidden_kernel, chunks, parts, rows),
        out_shape=jax.ShapeDtypeStruct((chunks * rows, width), jnp.bfloat16),
        in_specs=[vmem] * len(flat),
        out_specs=vmem,
        compiler_params=pltpu.CompilerParams(vmem_limit_bytes=32 * 1024 * 1024),
        name="hidden_rows",
    )(*flat)


def send_kernel(own, other, sel, send):
    both = jnp.concatenate([own[...], other[...]], axis=0)
    send[...] = jnp.dot(sel[...], both, preferred_element_type=jnp.float32).astype(jnp.bfloat16)


def rows_to_send(own, other, sel):
    vmem = pl.BlockSpec(memory_space=pltpu.VMEM)
    return pl.pallas_call(
        send_kernel,
        out_shape=pltpu.VMEM((sel.shape[0], own.shape[1]), jnp.bfloat16),
        in_specs=[vmem] * 3,
        out_specs=vmem,
        compiler_params=pltpu.CompilerParams(vmem_limit_bytes=32 * 1024 * 1024),
        name="rows_to_send",
    )(own, other, sel)


def local_kernel(n, groups, ids, own, other, adj, w_self, part, logits, adj_out, hidden):
    core = ids[0]
    for i in range(groups // 2):
        mine = group_of(core, i, groups)
        theirs = group_of(1 - core, i, groups)
        hidden[pl.ds(pl.multiple_of(mine * UNIT, UNIT), UNIT), :] = own[i * UNIT:(i + 1) * UNIT, :]
        hidden[pl.ds(pl.multiple_of(theirs * UNIT, UNIT), UNIT), :] = other[i * UNIT:(i + 1) * UNIT, :]
    tile, rows = hidden.shape[0], adj.shape[0]
    part[...] = jnp.dot(adj[:, :tile], hidden[...], preferred_element_type=jnp.float32)
    dims = (((1,), (1,)), ((), ()))
    logits[...] = lax.dot_general(hidden[:rows, :], w_self[...], dims, preferred_element_type=jnp.float32)
    count = adj.shape[1] - tile
    slots = count // n
    column = lax.broadcasted_iota(jnp.int32, (1, count), 1)
    source = ordered(lax.div(column, slots), n) * slots + lax.rem(column, slots)
    moved = jnp.where(lax.broadcasted_iota(jnp.int32, (count, count), 0) == source, 1.0, 0.0).astype(jnp.bfloat16)
    adj_out[...] = jnp.dot(adj[:, tile:], moved, preferred_element_type=jnp.float32).astype(jnp.bfloat16)


def local_terms(n, groups, ids, own, other, adj, w_self):
    smem = pl.BlockSpec(memory_space=pltpu.SMEM)
    vmem = pl.BlockSpec(memory_space=pltpu.VMEM)
    width = own.shape[1]
    return pl.pallas_call(
        functools.partial(local_kernel, n, groups),
        out_shape=[
            jax.ShapeDtypeStruct((adj.shape[0], width), jnp.float32),
            jax.ShapeDtypeStruct((adj.shape[0], w_self.shape[1]), jnp.float32),
            jax.ShapeDtypeStruct((adj.shape[0], adj.shape[1] - groups * UNIT), jnp.bfloat16),
        ],
        in_specs=[smem] + [vmem] * 4,
        out_specs=[vmem] * 3,
        scratch_shapes=[pltpu.VMEM((groups * UNIT, width), jnp.bfloat16)],
        compiler_params=pltpu.CompilerParams(vmem_limit_bytes=32 * 1024 * 1024),
        name="local_terms",
    )(ids, own, other, adj, w_self.T)


def logits_kernel(part, logits, received, adj, w_neigh, out):
    mean = part[...] + jnp.dot(adj[...], received[...], preferred_element_type=jnp.float32)
    dims = (((1,), (1,)), ((), ()))
    got = lax.dot_general(mean.astype(jnp.bfloat16), w_neigh[...], dims, preferred_element_type=jnp.float32)
    out[...] = logits[...] + got


def logits_of(part, logits, received, adj, w_neigh):
    vmem = pl.BlockSpec(memory_space=pltpu.VMEM)
    return pl.pallas_call(
        logits_kernel,
        out_shape=jax.ShapeDtypeStruct(logits.shape, jnp.float32),
        in_specs=[vmem] * 5,
        out_specs=vmem,
        compiler_params=pltpu.CompilerParams(vmem_limit_bytes=32 * 1024 * 1024),
        name="logits",
    )(part, logits, received, adj, w_neigh.T)


def exchange(parts, stride, n, places):
    got = [parts[0]]
    for k in places:
        got.append(lax.ppermute(parts[k], "dom", [(i, i ^ (k * stride)) for i in range(n)]))
    return got


def body(
    features,
    tile_weight,
    tile_dst,
    tile_src,
    tile_rows,
    w_self1,
    neighbour_weight_first,
    send_list,
    send_count,
    adj_two,
    w_self2,
    w_neigh2,
):
    n = lax.axis_size("dom")
    tile = tile_weight.shape[1]
    groups = tile // UNIT
    per = groups // 2 // CHUNKS
    bits = n.bit_length() - 1
    assert n == 1 << bits and bits >= 2
    radices = [2] * (bits // 2) + [1] * (bits % 2)
    ids = jnp.stack([lax.axis_index("feat"), lax.axis_index("dom")]).astype(jnp.int32)
    swap = [(0, 1), (1, 0)]
    xp = lax.ppermute(features, "feat", swap)
    wp = lax.ppermute(neighbour_weight_first, "feat", swap)
    sp = lax.ppermute(w_self1, "feat", swap)
    tw = tile_weight.reshape(tile_weight.shape[0], groups, UNIT, tile)
    planned = plan(
        CHUNKS, per, n, 4, ids, tile_src, tile_rows, tile_dst, tw, features, neighbour_weight_first, w_self1,
    )
    tables, tbufs, (xo, wo, so) = planned[:CHUNKS], planned[CHUNKS:2 * CHUNKS], planned[2 * CHUNKS:]
    done = []
    for chunk in range(CHUNKS):
        accs = gathered_sums(per, n, tables[chunk], tbufs[chunk], xo, xp)
        slots, rows = n // 4, per * UNIT
        parts = {k: sent_terms(k, slots, rows, accs, wo, wp) for k in (1, 2, 3)}
        parts[0] = own_terms(chunk, per, groups, slots, ids, accs, wo, wp, xo, xp, so, sp)
        got = exchange(parts, 1, n, (1, 2, 3))
        stride = 4
        for radix in radices[1:]:
            ways = 1 << radix
            parts = combine(n // stride, per * UNIT, ways, got[0], got[1:])
            got = exchange(parts, stride, n, range(ways - 1, 0, -1))
            stride *= ways
        done.append(got)
    sel = selection(groups, ids, send_list, send_count)
    own = hidden_rows(done, per * UNIT)
    other = lax.ppermute(own, "feat", swap)
    send = rows_to_send(own, other, sel)
    received = lax.all_to_all(send, "dom", 0, 0, axis_index_groups=[group_order(n)], tiled=True)
    part, logits, adj = local_terms(n, groups, ids, own, other, adj_two, w_self2)
    return logits_of(part, logits, received, adj, w_neigh2)


def solution(mesh):
    in_specs = (
        P("dom", "feat"),
        P("dom", None, None),
        P("dom"),
        P("dom"),
        P("dom"),
        P("feat", None),
        P("feat", None),
        P(),
        P(),
        P("dom", None),
        P(),
        P(),
    )
    out_specs = P("dom", None)
    return jax.shard_map(body, mesh=mesh, in_specs=in_specs, out_specs=out_specs, check_vma=False)
```

```python
import functools

import jax
import jax.numpy as jnp
from jax import lax
from jax.experimental import pallas as pl
from jax.experimental.pallas import tpu as pltpu
from jax.sharding import PartitionSpec as P

UNIT = 16
BLOCK = 8
STEP = 8
PART = 256
CHUNKS = 1


def group_of(core, place, groups):
    pair = 2 * (place // 2) + core
    return pair if place % 2 == 0 else groups - 1 - pair


LN2 = 0.6931471805599453


def tail_rows(slots):
    return -(-slots // 16) * 16


def encode(x):
    top = jnp.max(jnp.abs(x), axis=0, keepdims=True)
    power = jnp.ceil(jnp.log(jnp.maximum(top, 1e-30)) * (1.0 / LN2) + 1e-3) - 15.0
    return jnp.floor(x * jnp.exp(power * -LN2) + 0.5), power


def to_int16(x):
    return x.astype(jnp.int32).astype(jnp.int16)


def write_coded(out, tail, slots, rows, value_of):
    tail[...] = jnp.zeros_like(tail)
    for s in range(slots):
        whole, power = encode(value_of(s))
        out[s * rows:(s + 1) * rows, :] = to_int16(whole)
        tail[s:s + 1, :] = power
    out[slots * rows:, :] = to_int16(tail[...])


def read_coded(ref, slots, rows):
    powers = ref[slots * rows:, :].astype(jnp.int32).astype(jnp.float32)

    def value_of(s):
        whole = ref[s * rows:(s + 1) * rows, :].astype(jnp.int32).astype(jnp.float32)
        return whole * jnp.exp(powers[s:s + 1, :] * LN2)

    return value_of


def plan_kernel(chunks, per, n, radix, n_src, ids, src_h, rows_h, dst_h, tw, xo, wo, so, *rest):
    tables, rest = rest[:chunks], rest[chunks:]
    tbufs, rest = rest[:chunks], rest[chunks:]
    xo_out, wo_out, so_out = rest[:3]
    src_v, rows_v, dst_v, sems = rest[3:]
    core, me = ids[0], ids[1]
    tiles = src_v.shape[1]
    n_pos = tables[0].shape[1]
    units = per * tiles
    groups = 2 * per * chunks
    half = groups // 2
    gs = [group_of(core, i, groups) for i in range(half)]
    small = [(src_h, src_v), (rows_h, rows_v), (dst_h, dst_v)]
    large = [(tw.at[:, g], tbufs[i // per].at[pl.ds(i % per * tiles, tiles)]) for i, g in enumerate(gs)]
    large += [(xo, xo_out), (wo, wo_out), (so, so_out)]
    copies = [pltpu.make_async_copy(a, b, sems.at[i]) for i, (a, b) in enumerate(small + large)]
    for c in copies:
        c.start()
    lane = lax.broadcasted_iota(jnp.int32, (1, tiles), 1)
    block_i = lax.broadcasted_iota(jnp.int32, (n_src, tiles), 0)
    before = lax.broadcasted_iota(jnp.int32, (units, units), 0) < lax.broadcasted_iota(jnp.int32, (units, units), 1)
    before = jnp.where(before, 1.0, 0.0).astype(jnp.bfloat16)
    pos_i = lax.broadcasted_iota(jnp.int32, (tiles, n_pos), 1).astype(jnp.float32)
    place_i = lax.broadcasted_iota(jnp.int32, (1, n_pos), 1)
    trash = float(n * per << 14)
    for c in copies[:3]:
        c.wait()
    src, rows = src_v[...], rows_v[...]
    slot = jnp.bitwise_xor(dst_v[...], me)
    slot = jnp.bitwise_and(slot, radix - 1) * (n // radix) + lax.div(slot, radix)
    for c in range(chunks):
        hot, words, valid = [], [], []
        for j in range(per):
            limit = jnp.clip(rows - UNIT * gs[c * per + j], 0, UNIT)
            ok = limit > 0
            valid.append(ok)
            words.append(((slot * per + j) * 512 + (j * tiles + lane)) * 32 + limit)
            hot.append(jnp.where(jnp.logical_and(block_i == src, ok), 1.0, 0.0))
        hot = jnp.concatenate(hot, axis=1)
        earlier = jnp.dot(hot.astype(jnp.bfloat16), before, preferred_element_type=jnp.float32)
        blocks = jnp.floor((jnp.sum(hot, axis=1, keepdims=True) + (BLOCK - 1)) * (1.0 / BLOCK))
        run = jnp.zeros((1, 1), jnp.float32)
        pos = jnp.zeros((1, units), jnp.float32)
        owner = jnp.zeros((1, n_pos), jnp.float32)
        for s in range(n_src):
            pos = pos + hot[s:s + 1, :] * (earlier[s:s + 1, :] + run * BLOCK)
            run = run + blocks[s:s + 1, :]
            owner = owner + jnp.where(place_i.astype(jnp.float32) >= run, 1.0, 0.0)
        stack = [jnp.where(valid[j], pos[:, j * tiles:(j + 1) * tiles], -1.0) for j in range(per)]
        stack += [w.astype(jnp.float32) - trash for w in words]
        stack += [jnp.zeros((1, tiles), jnp.float32)] * (-len(stack) % 8)
        cols = jnp.concatenate(stack, axis=0).T
        found = jnp.zeros((tiles, n_pos), jnp.float32)
        for j in range(per):
            found = found + jnp.where(cols[:, j:j + 1] == pos_i, cols[:, per + j:per + j + 1], 0.0)
        word = jnp.sum(found, axis=0, keepdims=True) + trash
        owner = jnp.where(place_i == n_pos - 1, run, jnp.minimum(owner, n_src - 1.0))
        tables[c][0:1, :] = word.astype(jnp.int32)
        tables[c][1:2, :] = owner.astype(jnp.int32)

    for c in copies[3:]:
        c.wait()


def plan(chunks, per, n, radix, ids, src, rows, dst, tw, xo, wo, so):
    tiles, _, _, tile = tw.shape
    n_src = xo.shape[0] // tile
    blocks = -(-(per * tiles // BLOCK + n_src) // STEP) * STEP
    n_pos = -(-(blocks * BLOCK + 1) // 128) * 128
    smem = pl.BlockSpec(memory_space=pltpu.SMEM)
    vmem = pl.BlockSpec(memory_space=pltpu.VMEM)
    hbm = pl.BlockSpec(memory_space=pltpu.HBM)
    half = chunks * per
    return pl.pallas_call(
        functools.partial(plan_kernel, chunks, per, n, radix, n_src),
        out_shape=[jax.ShapeDtypeStruct((2, n_pos), jnp.int32)] * chunks
        + [jax.ShapeDtypeStruct((per * tiles, UNIT, tile), tw.dtype)] * chunks
        + [
            jax.ShapeDtypeStruct(xo.shape, xo.dtype),
            jax.ShapeDtypeStruct(wo.shape, wo.dtype),
            jax.ShapeDtypeStruct(so.shape, so.dtype),
        ],
        in_specs=[smem] + [hbm] * 7,
        out_specs=[vmem] * (2 * chunks + 3),
        scratch_shapes=[
            pltpu.VMEM((1, tiles), jnp.int32),
            pltpu.VMEM((1, tiles), jnp.int32),
            pltpu.VMEM((1, tiles), jnp.int32),
            pltpu.SemaphoreType.DMA((3 + half + 3,)),
        ],
        compiler_params=pltpu.CompilerParams(vmem_limit_bytes=32 * 1024 * 1024),
        name="plan",
    )(ids, *[
        pltpu.with_memory_space_constraint(a, pltpu.HBM)
        for a in (src.reshape(1, tiles), rows.reshape(1, tiles), dst.reshape(1, tiles), tw, xo, wo, so)
    ])


def select_kernel(groups, ids, lists, counts, sel):
    core, me = ids[0], ids[1]
    n = lists.shape[0]
    slots = lists.shape[1]
    total = n * slots
    q_n = lax.broadcasted_iota(jnp.int32, (total, n), 0)
    r_n = lax.broadcasted_iota(jnp.int32, (total, n), 1)
    mine = lists[me].astype(jnp.float32)
    cnt = counts[pl.ds(me, 1), :]
    picked = jnp.zeros((total, n), jnp.float32)
    k_n = jnp.bitwise_and(q_n, slots - 1)
    for k in range(slots):
        picked = jnp.where(k_n == k, mine[k:k + 1, :], picked)
    good = jnp.logical_and(n - 1 - lax.div(q_n, slots) == r_n, k_n < cnt)
    row = jnp.sum(jnp.where(good, picked + 1.0, 0.0), axis=1, keepdims=True) - 1.0
    lane = lax.broadcasted_iota(jnp.int32, (1, sel.shape[1]), 1)
    name = jnp.zeros(lane.shape, jnp.int32)
    for i in range(groups // 2):
        g = group_of(core, i, groups)
        name = jnp.where(lax.div(lane, UNIT) == i, g * UNIT + jnp.bitwise_and(lane, UNIT - 1), name)
    sel[...] = jnp.where(row == name.astype(jnp.float32), 1.0, 0.0).astype(jnp.bfloat16)


def selection(groups, ids, send_list, send_count):
    n, _, slots = send_list.shape
    smem = pl.BlockSpec(memory_space=pltpu.SMEM)
    vmem = pl.BlockSpec(memory_space=pltpu.VMEM)
    return pl.pallas_call(
        functools.partial(select_kernel, groups),
        out_shape=jax.ShapeDtypeStruct((n * slots, groups // 2 * UNIT), jnp.bfloat16),
        in_specs=[smem, vmem, vmem],
        out_specs=vmem,
        compiler_params=pltpu.CompilerParams(vmem_limit_bytes=32 * 1024 * 1024),
        name="selection",
    )(ids, jnp.swapaxes(send_list, 1, 2), send_count)


def tiles_kernel(table_v, tbuf, xo, xp, *rest):
    parts = len(rest) - 3
    accs, (masks, table, sem) = rest[:parts], rest[parts:]
    tile = tbuf.shape[2]
    width = xo.shape[1]
    to_scalar = pltpu.make_async_copy(table_v, table, sem)
    to_scalar.start()
    for acc in accs:
        acc[...] = jnp.zeros_like(acc)
    row_i = lax.broadcasted_iota(jnp.int32, (UNIT, tile), 0)
    for m in range(UNIT + 1):
        masks[m] = jnp.where(row_i < m, 1.0, 0.0).astype(jnp.bfloat16)
    columns = [(x, h) for x in (xo, xp) for h in range(0, width, PART)]
    to_scalar.wait()

    def step(i, carry):
        for m in range(STEP):
            b = i * STEP + m
            base = pl.multiple_of(table[1, b] * tile, tile)
            rows, places = [], []
            for k in range(BLOCK):
                word = table[0, b * BLOCK + k]
                u = jnp.bitwise_and(lax.shift_right_logical(word, 5), 511)
                rows.append(tbuf[u] * masks[jnp.bitwise_and(word, 31)])
                places.append(pl.multiple_of(lax.shift_right_logical(word, 14) * UNIT, UNIT))
            lhs = jnp.concatenate(rows, axis=0)
            for acc, (x, h) in zip(accs, columns):
                got = jnp.dot(lhs, x[pl.ds(base, tile), h:h + PART], preferred_element_type=jnp.float32)
                got = got.astype(jnp.bfloat16).astype(jnp.float32)
                for k in range(BLOCK):
                    acc[pl.ds(places[k], UNIT), :] += got[k * UNIT:(k + 1) * UNIT, :]
        return carry

    steps = lax.div(table[1, table.shape[1] - 1] + STEP - 1, STEP)
    lax.fori_loop(0, steps, step, 0)


def gathered_sums(per, n, table, tbuf, xo, xp):
    width = xo.shape[1]
    tile = tbuf.shape[2]
    vmem = pl.BlockSpec(memory_space=pltpu.VMEM)
    flops = 2 * tbuf.shape[0] * UNIT * tile * 2 * width
    parts = 2 * width // PART
    sums = jax.ShapeDtypeStruct(((n * per + 1) * UNIT, PART), jnp.float32)
    return pl.pallas_call(
        tiles_kernel,
        out_shape=[sums] * parts,
        in_specs=[vmem] * 4,
        out_specs=[vmem] * parts,
        scratch_shapes=[
            pltpu.VMEM((UNIT + 1, UNIT, tile), jnp.bfloat16),
            pltpu.SMEM(table.shape, jnp.int32),
            pltpu.SemaphoreType.DMA,
        ],
        compiler_params=pltpu.CompilerParams(vmem_limit_bytes=(12 << 20) + sums.size * 4 * parts),
        cost_estimate=pl.CostEstimate(flops=flops, bytes_accessed=8 << 20, transcendentals=0),
        name="gathered_sums",
    )(table, tbuf, xo, xp)


def weigh(accs, weights, first, count, out):
    size = min(256, count)

    def piece(r, carry):
        at = pl.multiple_of(r * size, size)
        got = jnp.zeros((size, out.shape[1]), jnp.float32)
        for i, acc in enumerate(accs):
            w, h = weights[i * PART // weights[0].shape[0]], i * PART % weights[0].shape[0]
            value = acc[pl.ds(first + at, size), :]
            high = value.astype(jnp.bfloat16)
            low = (value - high.astype(jnp.float32)).astype(jnp.bfloat16)
            got = got + jnp.dot(high, w[h:h + PART, :], preferred_element_type=jnp.float32)
            got = got + jnp.dot(low, w[h:h + PART, :], preferred_element_type=jnp.float32)
        out[pl.ds(at, size), :] = got
        return carry

    lax.fori_loop(0, count // size, piece, 0)


def sent_kernel(k, slots, rows, parts, wo, wp, *refs):
    accs, (out, sums, tail) = refs[:parts], refs[parts:]
    weigh(accs, (wo, wp), k * slots * rows, slots * rows, sums)
    write_coded(out, tail, slots, rows, lambda s: sums[s * rows:(s + 1) * rows, :])


def sent_terms(k, slots, rows, accs, wo, wp):
    hidden = wo.shape[1]
    vmem = pl.BlockSpec(memory_space=pltpu.VMEM)
    return pl.pallas_call(
        functools.partial(sent_kernel, k, slots, rows, len(accs)),
        out_shape=jax.ShapeDtypeStruct((slots * rows + tail_rows(slots), hidden), jnp.int16),
        in_specs=[vmem] * (2 + len(accs)),
        out_specs=vmem,
        scratch_shapes=[
            pltpu.VMEM((slots * rows, hidden), jnp.float32),
            pltpu.VMEM((tail_rows(slots), hidden), jnp.float32),
        ],
        compiler_params=pltpu.CompilerParams(vmem_limit_bytes=(12 << 20) + accs[0].size * 4 * len(accs)),
        cost_estimate=pl.CostEstimate(
            flops=4 * slots * rows * PART * len(accs) * hidden, bytes_accessed=2 << 20, transcendentals=0),
        name="sent_terms",
    )(wo, wp, *accs)


def own_kernel(chunk, per, groups, parts, ids, wo, wp, xo, xp, so, sp, *refs):
    accs, out = refs[:parts], refs[parts]
    weigh(accs, (wo, wp), 0, out.shape[0], out)
    for j in range(per):
        at = pl.multiple_of(group_of(ids[0], chunk * per + j, groups) * UNIT, UNIT)
        self = jnp.dot(xo[pl.ds(at, UNIT), :], so[...], preferred_element_type=jnp.float32)
        self = self + jnp.dot(xp[pl.ds(at, UNIT), :], sp[...], preferred_element_type=jnp.float32)
        out[j * UNIT:(j + 1) * UNIT, :] += self


def own_terms(chunk, per, groups, slots, ids, accs, wo, wp, xo, xp, so, sp):
    hidden = wo.shape[1]
    rows = per * UNIT
    smem = pl.BlockSpec(memory_space=pltpu.SMEM)
    vmem = pl.BlockSpec(memory_space=pltpu.VMEM)
    return pl.pallas_call(
        functools.partial(own_kernel, chunk, per, groups, len(accs)),
        out_shape=jax.ShapeDtypeStruct((slots * rows, hidden), jnp.float32),
        in_specs=[smem] + [vmem] * (6 + len(accs)),
        out_specs=vmem,
        compiler_params=pltpu.CompilerParams(vmem_limit_bytes=(12 << 20) + accs[0].size * 4 * len(accs)),
        cost_estimate=pl.CostEstimate(
            flops=4 * slots * rows * PART * len(accs) * hidden, bytes_accessed=2 << 20, transcendentals=0),
        name="own_terms",
    )(ids, wo, wp, xo, xp, so, sp, *accs)


def combine_kernel(slots, rows, ways, own, *refs):
    parts = len(refs) - ways - 1
    coded, outs, tail = refs[:parts], refs[parts:parts + ways], refs[parts + ways]
    values = [read_coded(a, slots, rows) for a in coded]

    def total(s):
        got = own[s * rows:(s + 1) * rows, :]
        for value in values:
            got = got + value(s)
        return got

    for i in range(slots // ways):
        outs[0][i * rows:(i + 1) * rows, :] = total(i * ways)
    for k in range(1, ways):
        write_coded(outs[k], tail, slots // ways, rows, lambda s: total(s * ways + k))


def combine(slots, rows, ways, own, coded):
    width = own.shape[1]
    left = slots // ways
    vmem = pl.BlockSpec(memory_space=pltpu.VMEM)
    out = jax.ShapeDtypeStruct((left * rows + tail_rows(left), width), jnp.int16)
    return pl.pallas_call(
        functools.partial(combine_kernel, slots, rows, ways),
        out_shape=[jax.ShapeDtypeStruct((left * rows, width), jnp.float32)] + [out] * (ways - 1),
        in_specs=[vmem] * (1 + len(coded)),
        out_specs=[vmem] * ways,
        scratch_shapes=[pltpu.VMEM((tail_rows(left), width), jnp.float32)],
        compiler_params=pltpu.CompilerParams(vmem_limit_bytes=32 * 1024 * 1024),
        name="combine",
    )(own, *coded)


def hidden_kernel(chunks, parts, rows, *refs):
    sel, own, send = refs[chunks * parts:]
    for c in range(chunks):
        mine, coded = refs[c * parts], refs[c * parts + 1:(c + 1) * parts]
        total = mine[:rows, :]
        for a in coded:
            total = total + read_coded(a, 1, rows)(0)
        own[c * rows:(c + 1) * rows, :] = jnp.maximum(total, 0.0).astype(jnp.bfloat16)
    picked = jnp.dot(sel[...], own[...], preferred_element_type=jnp.float32).astype(jnp.bfloat16)
    half = picked.shape[0]
    send[:half, :] = picked
    send[half:, :] = picked


def hidden_rows(chunk_parts, rows, sel):
    chunks, parts = len(chunk_parts), len(chunk_parts[0])
    width = chunk_parts[0][0].shape[1]
    vmem = pl.BlockSpec(memory_space=pltpu.VMEM)
    flat = [a for part in chunk_parts for a in part]
    return pl.pallas_call(
        functools.partial(hidden_kernel, chunks, parts, rows),
        out_shape=[
            jax.ShapeDtypeStruct((chunks * rows, width), jnp.bfloat16),
            jax.ShapeDtypeStruct((2 * sel.shape[0], width), jnp.bfloat16),
        ],
        in_specs=[vmem] * (len(flat) + 1),
        out_specs=[vmem] * 2,
        compiler_params=pltpu.CompilerParams(vmem_limit_bytes=32 * 1024 * 1024),
        name="hidden_rows",
    )(*flat, sel)


def local_kernel(n, groups, ids, own, other, adj, w_self, part, logits, adj_out, hidden):
    core = ids[0]
    for i in range(groups // 2):
        mine = group_of(core, i, groups)
        theirs = group_of(1 - core, i, groups)
        hidden[pl.ds(pl.multiple_of(mine * UNIT, UNIT), UNIT), :] = own[i * UNIT:(i + 1) * UNIT, :]
        hidden[pl.ds(pl.multiple_of(theirs * UNIT, UNIT), UNIT), :] = other[i * UNIT:(i + 1) * UNIT, :]
    tile, rows = hidden.shape[0], adj.shape[0]
    part[...] = jnp.dot(adj[:, :tile], hidden[...], preferred_element_type=jnp.float32)
    dims = (((1,), (1,)), ((), ()))
    logits[...] = lax.dot_general(hidden[:rows, :], w_self[...], dims, preferred_element_type=jnp.float32)
    count = adj.shape[1] - tile
    slots = count // n
    column = lax.broadcasted_iota(jnp.int32, (1, count), 1)
    source = (n - 1 - lax.div(column, slots)) * slots + lax.rem(column, slots)
    moved = jnp.where(lax.broadcasted_iota(jnp.int32, (count, count), 0) == source, 1.0, 0.0).astype(jnp.bfloat16)
    adj_out[...] = jnp.dot(adj[:, tile:], moved, preferred_element_type=jnp.float32).astype(jnp.bfloat16)


def local_terms(n, groups, ids, own, other, adj, w_self):
    smem = pl.BlockSpec(memory_space=pltpu.SMEM)
    vmem = pl.BlockSpec(memory_space=pltpu.VMEM)
    width = own.shape[1]
    return pl.pallas_call(
        functools.partial(local_kernel, n, groups),
        out_shape=[
            jax.ShapeDtypeStruct((adj.shape[0], width), jnp.float32),
            jax.ShapeDtypeStruct((adj.shape[0], w_self.shape[1]), jnp.float32),
            jax.ShapeDtypeStruct((adj.shape[0], adj.shape[1] - groups * UNIT), jnp.bfloat16),
        ],
        in_specs=[smem] + [vmem] * 4,
        out_specs=[vmem] * 3,
        scratch_shapes=[pltpu.VMEM((groups * UNIT, width), jnp.bfloat16)],
        compiler_params=pltpu.CompilerParams(vmem_limit_bytes=32 * 1024 * 1024),
        name="local_terms",
    )(ids, own, other, adj, w_self.T)


def logits_kernel(part, logits, received, adj, w_neigh, out):
    half = received.shape[0] // 2
    rows = received[:half, :].astype(jnp.float32) + received[half:, :].astype(jnp.float32)
    mean = part[...] + jnp.dot(adj[...], rows.astype(jnp.bfloat16), preferred_element_type=jnp.float32)
    dims = (((1,), (1,)), ((), ()))
    got = lax.dot_general(mean.astype(jnp.bfloat16), w_neigh[...], dims, preferred_element_type=jnp.float32)
    out[...] = logits[...] + got


def logits_of(part, logits, received, adj, w_neigh):
    vmem = pl.BlockSpec(memory_space=pltpu.VMEM)
    return pl.pallas_call(
        logits_kernel,
        out_shape=jax.ShapeDtypeStruct(logits.shape, jnp.float32),
        in_specs=[vmem] * 5,
        out_specs=vmem,
        compiler_params=pltpu.CompilerParams(vmem_limit_bytes=32 * 1024 * 1024),
        name="logits",
    )(part, logits, received, adj, w_neigh.T)


def exchange(parts, stride, n, places):
    got = [parts[0]]
    for k in places:
        got.append(lax.ppermute(parts[k], "dom", [(i, i ^ (k * stride)) for i in range(n)]))
    return got


def body(
    features,
    tile_weight,
    tile_dst,
    tile_src,
    tile_rows,
    w_self1,
    neighbour_weight_first,
    send_list,
    send_count,
    adj_two,
    w_self2,
    w_neigh2,
):
    n = lax.axis_size("dom")
    tile = tile_weight.shape[1]
    groups = tile // UNIT
    per = groups // 2 // CHUNKS
    bits = n.bit_length() - 1
    assert n == 1 << bits and bits >= 2
    radices = [2] * (bits // 2) + [1] * (bits % 2)
    ids = jnp.stack([lax.axis_index("feat"), lax.axis_index("dom")]).astype(jnp.int32)
    swap = [(0, 1), (1, 0)]
    xp = lax.ppermute(features, "feat", swap)
    wp = lax.ppermute(neighbour_weight_first, "feat", swap)
    sp = lax.ppermute(w_self1, "feat", swap)
    tw = tile_weight.reshape(tile_weight.shape[0], groups, UNIT, tile)
    planned = plan(
        CHUNKS, per, n, 4, ids, tile_src, tile_rows, tile_dst, tw, features, neighbour_weight_first, w_self1,
    )
    tables, tbufs, (xo, wo, so) = planned[:CHUNKS], planned[CHUNKS:2 * CHUNKS], planned[2 * CHUNKS:]
    done = []
    for chunk in range(CHUNKS):
        accs = gathered_sums(per, n, tables[chunk], tbufs[chunk], xo, xp)
        slots, rows = n // 4, per * UNIT
        parts = {k: sent_terms(k, slots, rows, accs, wo, wp) for k in (1, 2, 3)}
        parts[0] = own_terms(chunk, per, groups, slots, ids, accs, wo, wp, xo, xp, so, sp)
        got = exchange(parts, 1, n, (1, 2, 3))
        stride = 4
        for radix in radices[1:]:
            ways = 1 << radix
            parts = combine(n // stride, per * UNIT, ways, got[0], got[1:])
            got = exchange(parts, stride, n, range(ways - 1, 0, -1))
            stride *= ways
        done.append(got)
    sel = selection(groups, ids, send_list, send_count)
    own, send = hidden_rows(done, per * UNIT, sel)
    other = lax.ppermute(own, "feat", swap)
    backwards = [list(range(2 * n - 1, -1, -1))]
    received = lax.all_to_all(send, ("feat", "dom"), 0, 0, axis_index_groups=backwards, tiled=True)
    part, logits, adj = local_terms(n, groups, ids, own, other, adj_two, w_self2)
    return logits_of(part, logits, received, adj, w_neigh2)


def solution(mesh):
    in_specs = (
        P("dom", "feat"),
        P("dom", None, None),
        P("dom"),
        P("dom"),
        P("dom"),
        P("feat", None),
        P("feat", None),
        P(),
        P(),
        P("dom", None),
        P(),
        P(),
    )
    out_specs = P("dom", None)
    return jax.shard_map(body, mesh=mesh, in_specs=in_specs, out_specs=out_specs, check_vma=False)
```

```python
import functools

import jax
import jax.numpy as jnp
from jax import lax
from jax.experimental import pallas as pl
from jax.experimental.pallas import tpu as pltpu
from jax.sharding import PartitionSpec as P

UNIT = 16
BLOCK = 8
STEP = 8
PART = 256
CHUNKS = 1


def group_of(core, place, groups):
    pair = 2 * (place // 2) + core
    return pair if place % 2 == 0 else groups - 1 - pair


def group_order(n):
    first = n * 9 // 16
    return [first] + [i for i in range(n) if i != first]


def ordered(block, n):
    first = n * 9 // 16
    return jnp.where(block == 0, first, jnp.where(block <= first, block - 1, block))


LN2 = 0.6931471805599453


def tail_rows(slots):
    return -(-slots // 16) * 16


def encode(x):
    top = jnp.max(jnp.abs(x), axis=0, keepdims=True)
    power = jnp.ceil(jnp.log(jnp.maximum(top, 1e-30)) * (1.0 / LN2) + 1e-3) - 15.0
    return jnp.floor(x * jnp.exp(power * -LN2) + 0.5), power


def to_int16(x):
    return x.astype(jnp.int32).astype(jnp.int16)


def write_coded(out, tail, slots, rows, value_of):
    tail[...] = jnp.zeros_like(tail)
    for s in range(slots):
        whole, power = encode(value_of(s))
        out[s * rows:(s + 1) * rows, :] = to_int16(whole)
        tail[s:s + 1, :] = power
    out[slots * rows:, :] = to_int16(tail[...])


def read_coded(ref, slots, rows):
    powers = ref[slots * rows:, :].astype(jnp.int32).astype(jnp.float32)

    def value_of(s):
        whole = ref[s * rows:(s + 1) * rows, :].astype(jnp.int32).astype(jnp.float32)
        return whole * jnp.exp(powers[s:s + 1, :] * LN2)

    return value_of


def plan_kernel(chunks, per, n, radix, n_src, ids, src_h, rows_h, dst_h, tw, xo, wo, so, *rest):
    tables, rest = rest[:chunks], rest[chunks:]
    tbufs, rest = rest[:chunks], rest[chunks:]
    xo_out, wo_out, so_out = rest[:3]
    src_v, rows_v, dst_v, sems = rest[3:]
    core, me = ids[0], ids[1]
    tiles = src_v.shape[1]
    n_pos = tables[0].shape[1]
    units = per * tiles
    groups = 2 * per * chunks
    half = groups // 2
    gs = [group_of(core, i, groups) for i in range(half)]
    small = [(src_h, src_v), (rows_h, rows_v), (dst_h, dst_v)]
    large = [(tw.at[:, g], tbufs[i // per].at[pl.ds(i % per * tiles, tiles)]) for i, g in enumerate(gs)]
    large += [(xo, xo_out), (wo, wo_out), (so, so_out)]
    copies = [pltpu.make_async_copy(a, b, sems.at[i]) for i, (a, b) in enumerate(small + large)]
    for c in copies:
        c.start()
    lane = lax.broadcasted_iota(jnp.int32, (1, tiles), 1)
    block_i = lax.broadcasted_iota(jnp.int32, (n_src, tiles), 0)
    before = lax.broadcasted_iota(jnp.int32, (units, units), 0) < lax.broadcasted_iota(jnp.int32, (units, units), 1)
    before = jnp.where(before, 1.0, 0.0).astype(jnp.bfloat16)
    pos_i = lax.broadcasted_iota(jnp.int32, (tiles, n_pos), 1).astype(jnp.float32)
    place_i = lax.broadcasted_iota(jnp.int32, (1, n_pos), 1)
    trash = float(n * per << 14)
    for c in copies[:3]:
        c.wait()
    src, rows = src_v[...], rows_v[...]
    slot = jnp.bitwise_xor(dst_v[...], me)
    slot = jnp.bitwise_and(slot, radix - 1) * (n // radix) + lax.div(slot, radix)
    for c in range(chunks):
        hot, words, valid = [], [], []
        for j in range(per):
            limit = jnp.clip(rows - UNIT * gs[c * per + j], 0, UNIT)
            ok = limit > 0
            valid.append(ok)
            words.append(((slot * per + j) * 512 + (j * tiles + lane)) * 32 + limit)
            hot.append(jnp.where(jnp.logical_and(block_i == src, ok), 1.0, 0.0))
        hot = jnp.concatenate(hot, axis=1)
        earlier = jnp.dot(hot.astype(jnp.bfloat16), before, preferred_element_type=jnp.float32)
        blocks = jnp.floor((jnp.sum(hot, axis=1, keepdims=True) + (BLOCK - 1)) * (1.0 / BLOCK))
        run = jnp.zeros((1, 1), jnp.float32)
        pos = jnp.zeros((1, units), jnp.float32)
        owner = jnp.zeros((1, n_pos), jnp.float32)
        for s in range(n_src):
            pos = pos + hot[s:s + 1, :] * (earlier[s:s + 1, :] + run * BLOCK)
            run = run + blocks[s:s + 1, :]
            owner = owner + jnp.where(place_i.astype(jnp.float32) >= run, 1.0, 0.0)
        stack = [jnp.where(valid[j], pos[:, j * tiles:(j + 1) * tiles], -1.0) for j in range(per)]
        stack += [w.astype(jnp.float32) - trash for w in words]
        stack += [jnp.zeros((1, tiles), jnp.float32)] * (-len(stack) % 8)
        cols = jnp.concatenate(stack, axis=0).T
        found = jnp.zeros((tiles, n_pos), jnp.float32)
        for j in range(per):
            found = found + jnp.where(cols[:, j:j + 1] == pos_i, cols[:, per + j:per + j + 1], 0.0)
        word = jnp.sum(found, axis=0, keepdims=True) + trash
        owner = jnp.where(place_i == n_pos - 1, run, jnp.minimum(owner, n_src - 1.0))
        tables[c][0:1, :] = word.astype(jnp.int32)
        tables[c][1:2, :] = owner.astype(jnp.int32)

    for c in copies[3:]:
        c.wait()


def plan(chunks, per, n, radix, ids, src, rows, dst, tw, xo, wo, so):
    tiles, _, _, tile = tw.shape
    n_src = xo.shape[0] // tile
    blocks = -(-(per * tiles // BLOCK + n_src) // STEP) * STEP
    n_pos = -(-(blocks * BLOCK + 1) // 128) * 128
    smem = pl.BlockSpec(memory_space=pltpu.SMEM)
    vmem = pl.BlockSpec(memory_space=pltpu.VMEM)
    hbm = pl.BlockSpec(memory_space=pltpu.HBM)
    half = chunks * per
    return pl.pallas_call(
        functools.partial(plan_kernel, chunks, per, n, radix, n_src),
        out_shape=[jax.ShapeDtypeStruct((2, n_pos), jnp.int32)] * chunks
        + [jax.ShapeDtypeStruct((per * tiles, UNIT, tile), tw.dtype)] * chunks
        + [
            jax.ShapeDtypeStruct(xo.shape, xo.dtype),
            jax.ShapeDtypeStruct(wo.shape, wo.dtype),
            jax.ShapeDtypeStruct(so.shape, so.dtype),
        ],
        in_specs=[smem] + [hbm] * 7,
        out_specs=[vmem] * (2 * chunks + 3),
        scratch_shapes=[
            pltpu.VMEM((1, tiles), jnp.int32),
            pltpu.VMEM((1, tiles), jnp.int32),
            pltpu.VMEM((1, tiles), jnp.int32),
            pltpu.SemaphoreType.DMA((3 + half + 3,)),
        ],
        compiler_params=pltpu.CompilerParams(vmem_limit_bytes=32 * 1024 * 1024),
        name="plan",
    )(ids, *[
        pltpu.with_memory_space_constraint(a, pltpu.HBM)
        for a in (src.reshape(1, tiles), rows.reshape(1, tiles), dst.reshape(1, tiles), tw, xo, wo, so)
    ])


def select_kernel(groups, ids, lists, counts, adj, sel, adj_out):
    core, me = ids[0], ids[1]
    n = lists.shape[0]
    slots = lists.shape[1]
    total = n * slots
    q_n = lax.broadcasted_iota(jnp.int32, (total, n), 0)
    r_n = lax.broadcasted_iota(jnp.int32, (total, n), 1)
    mine = lists[me].astype(jnp.float32)
    cnt = counts[pl.ds(me, 1), :]
    picked = jnp.zeros((total, n), jnp.float32)
    k_n = jnp.bitwise_and(q_n, slots - 1)
    for k in range(slots):
        picked = jnp.where(k_n == k, mine[k:k + 1, :], picked)
    good = jnp.logical_and(ordered(lax.div(q_n, slots), n) == r_n, k_n < cnt)
    row = jnp.sum(jnp.where(good, picked + 1.0, 0.0), axis=1, keepdims=True) - 1.0
    lane = lax.broadcasted_iota(jnp.int32, (1, sel.shape[1]), 1)
    name = jnp.zeros(lane.shape, jnp.int32)
    names = [group_of(c, i, groups) for c in (core, 1 - core) for i in range(groups // 2)]
    for i, g in enumerate(names):
        name = jnp.where(lax.div(lane, UNIT) == i, g * UNIT + jnp.bitwise_and(lane, UNIT - 1), name)
    sel[...] = jnp.where(row == name.astype(jnp.float32), 1.0, 0.0).astype(jnp.bfloat16)
    column = lax.broadcasted_iota(jnp.int32, (1, total), 1)
    source = ordered(lax.div(column, slots), n) * slots + lax.rem(column, slots)
    moved = jnp.where(lax.broadcasted_iota(jnp.int32, (total, total), 0) == source, 1.0, 0.0).astype(jnp.bfloat16)
    adj_out[...] = jnp.dot(adj[:, groups * UNIT:], moved, preferred_element_type=jnp.float32).astype(jnp.bfloat16)


def selection(groups, ids, send_list, send_count, adj):
    n, _, slots = send_list.shape
    smem = pl.BlockSpec(memory_space=pltpu.SMEM)
    vmem = pl.BlockSpec(memory_space=pltpu.VMEM)
    return pl.pallas_call(
        functools.partial(select_kernel, groups),
        out_shape=[
            jax.ShapeDtypeStruct((n * slots, groups * UNIT), jnp.bfloat16),
            jax.ShapeDtypeStruct((adj.shape[0], n * slots), jnp.bfloat16),
        ],
        in_specs=[smem, vmem, vmem, vmem],
        out_specs=[vmem] * 2,
        compiler_params=pltpu.CompilerParams(vmem_limit_bytes=32 * 1024 * 1024),
        name="selection",
    )(ids, jnp.swapaxes(send_list, 1, 2), send_count, adj)


def tiles_kernel(table_v, tbuf, xo, xp, *rest):
    parts = len(rest) - 3
    accs, (masks, table, sem) = rest[:parts], rest[parts:]
    tile = tbuf.shape[2]
    width = xo.shape[1]
    to_scalar = pltpu.make_async_copy(table_v, table, sem)
    to_scalar.start()
    for acc in accs:
        acc[...] = jnp.zeros_like(acc)
    row_i = lax.broadcasted_iota(jnp.int32, (UNIT, tile), 0)
    for m in range(UNIT + 1):
        masks[m] = jnp.where(row_i < m, 1.0, 0.0).astype(jnp.bfloat16)
    columns = [(x, h) for x in (xo, xp) for h in range(0, width, PART)]
    to_scalar.wait()

    def step(i, carry):
        for m in range(STEP):
            b = i * STEP + m
            base = pl.multiple_of(table[1, b] * tile, tile)
            rows, places = [], []
            for k in range(BLOCK):
                word = table[0, b * BLOCK + k]
                u = jnp.bitwise_and(lax.shift_right_logical(word, 5), 511)
                rows.append(tbuf[u] * masks[jnp.bitwise_and(word, 31)])
                places.append(pl.multiple_of(lax.shift_right_logical(word, 14) * UNIT, UNIT))
            lhs = jnp.concatenate(rows, axis=0)
            for acc, (x, h) in zip(accs, columns):
                got = jnp.dot(lhs, x[pl.ds(base, tile), h:h + PART], preferred_element_type=jnp.float32)
                got = got.astype(jnp.bfloat16).astype(jnp.float32)
                for k in range(BLOCK):
                    acc[pl.ds(places[k], UNIT), :] += got[k * UNIT:(k + 1) * UNIT, :]
        return carry

    steps = lax.div(table[1, table.shape[1] - 1] + STEP - 1, STEP)
    lax.fori_loop(0, steps, step, 0)


def gathered_sums(per, n, table, tbuf, xo, xp):
    width = xo.shape[1]
    tile = tbuf.shape[2]
    vmem = pl.BlockSpec(memory_space=pltpu.VMEM)
    flops = 2 * tbuf.shape[0] * UNIT * tile * 2 * width
    parts = 2 * width // PART
    sums = jax.ShapeDtypeStruct(((n * per + 1) * UNIT, PART), jnp.float32)
    return pl.pallas_call(
        tiles_kernel,
        out_shape=[sums] * parts,
        in_specs=[vmem] * 4,
        out_specs=[vmem] * parts,
        scratch_shapes=[
            pltpu.VMEM((UNIT + 1, UNIT, tile), jnp.bfloat16),
            pltpu.SMEM(table.shape, jnp.int32),
            pltpu.SemaphoreType.DMA,
        ],
        compiler_params=pltpu.CompilerParams(vmem_limit_bytes=(12 << 20) + sums.size * 4 * parts),
        cost_estimate=pl.CostEstimate(flops=flops, bytes_accessed=8 << 20, transcendentals=0),
        name="gathered_sums",
    )(table, tbuf, xo, xp)


def weigh(accs, weights, first, count, out):
    size = min(256, count)

    def piece(r, carry):
        at = pl.multiple_of(r * size, size)
        got = jnp.zeros((size, out.shape[1]), jnp.float32)
        for i, acc in enumerate(accs):
            w, h = weights[i * PART // weights[0].shape[0]], i * PART % weights[0].shape[0]
            value = acc[pl.ds(first + at, size), :]
            high = value.astype(jnp.bfloat16)
            low = (value - high.astype(jnp.float32)).astype(jnp.bfloat16)
            got = got + jnp.dot(high, w[h:h + PART, :], preferred_element_type=jnp.float32)
            got = got + jnp.dot(low, w[h:h + PART, :], preferred_element_type=jnp.float32)
        out[pl.ds(at, size), :] = got
        return carry

    lax.fori_loop(0, count // size, piece, 0)


def sent_kernel(k, slots, rows, parts, wo, wp, *refs):
    accs, (out, sums, tail) = refs[:parts], refs[parts:]
    weigh(accs, (wo, wp), k * slots * rows, slots * rows, sums)
    write_coded(out, tail, slots, rows, lambda s: sums[s * rows:(s + 1) * rows, :])


def sent_terms(k, slots, rows, accs, wo, wp):
    hidden = wo.shape[1]
    vmem = pl.BlockSpec(memory_space=pltpu.VMEM)
    return pl.pallas_call(
        functools.partial(sent_kernel, k, slots, rows, len(accs)),
        out_shape=jax.ShapeDtypeStruct((slots * rows + tail_rows(slots), hidden), jnp.int16),
        in_specs=[vmem] * (2 + len(accs)),
        out_specs=vmem,
        scratch_shapes=[
            pltpu.VMEM((slots * rows, hidden), jnp.float32),
            pltpu.VMEM((tail_rows(slots), hidden), jnp.float32),
        ],
        compiler_params=pltpu.CompilerParams(vmem_limit_bytes=(12 << 20) + accs[0].size * 4 * len(accs)),
        cost_estimate=pl.CostEstimate(
            flops=4 * slots * rows * PART * len(accs) * hidden, bytes_accessed=2 << 20, transcendentals=0),
        name="sent_terms",
    )(wo, wp, *accs)


def own_kernel(chunk, per, groups, parts, ids, wo, wp, xo, xp, so, sp, *refs):
    accs, out = refs[:parts], refs[parts]
    weigh(accs, (wo, wp), 0, out.shape[0], out)
    for j in range(per):
        at = pl.multiple_of(group_of(ids[0], chunk * per + j, groups) * UNIT, UNIT)
        self = jnp.dot(xo[pl.ds(at, UNIT), :], so[...], preferred_element_type=jnp.float32)
        self = self + jnp.dot(xp[pl.ds(at, UNIT), :], sp[...], preferred_element_type=jnp.float32)
        out[j * UNIT:(j + 1) * UNIT, :] += self


def own_terms(chunk, per, groups, slots, ids, accs, wo, wp, xo, xp, so, sp):
    hidden = wo.shape[1]
    rows = per * UNIT
    smem = pl.BlockSpec(memory_space=pltpu.SMEM)
    vmem = pl.BlockSpec(memory_space=pltpu.VMEM)
    return pl.pallas_call(
        functools.partial(own_kernel, chunk, per, groups, len(accs)),
        out_shape=jax.ShapeDtypeStruct((slots * rows, hidden), jnp.float32),
        in_specs=[smem] + [vmem] * (6 + len(accs)),
        out_specs=vmem,
        compiler_params=pltpu.CompilerParams(vmem_limit_bytes=(12 << 20) + accs[0].size * 4 * len(accs)),
        cost_estimate=pl.CostEstimate(
            flops=4 * slots * rows * PART * len(accs) * hidden, bytes_accessed=2 << 20, transcendentals=0),
        name="own_terms",
    )(ids, wo, wp, xo, xp, so, sp, *accs)


def combine_kernel(slots, rows, ways, own, *refs):
    parts = len(refs) - ways - 1
    coded, outs, tail = refs[:parts], refs[parts:parts + ways], refs[parts + ways]
    values = [read_coded(a, slots, rows) for a in coded]

    def total(s):
        got = own[s * rows:(s + 1) * rows, :]
        for value in values:
            got = got + value(s)
        return got

    for i in range(slots // ways):
        outs[0][i * rows:(i + 1) * rows, :] = total(i * ways)
    for k in range(1, ways):
        write_coded(outs[k], tail, slots // ways, rows, lambda s: total(s * ways + k))


def combine(slots, rows, ways, own, coded):
    width = own.shape[1]
    left = slots // ways
    vmem = pl.BlockSpec(memory_space=pltpu.VMEM)
    out = jax.ShapeDtypeStruct((left * rows + tail_rows(left), width), jnp.int16)
    return pl.pallas_call(
        functools.partial(combine_kernel, slots, rows, ways),
        out_shape=[jax.ShapeDtypeStruct((left * rows, width), jnp.float32)] + [out] * (ways - 1),
        in_specs=[vmem] * (1 + len(coded)),
        out_specs=[vmem] * ways,
        scratch_shapes=[pltpu.VMEM((tail_rows(left), width), jnp.float32)],
        compiler_params=pltpu.CompilerParams(vmem_limit_bytes=32 * 1024 * 1024),
        name="combine",
    )(own, *coded)


def hidden_kernel(chunks, parts, rows, *refs):
    out = refs[chunks * parts]
    for c in range(chunks):
        own, coded = refs[c * parts], refs[c * parts + 1:(c + 1) * parts]
        total = own[:rows, :]
        for a in coded:
            total = total + read_coded(a, 1, rows)(0)
        out[c * rows:(c + 1) * rows, :] = jnp.maximum(total, 0.0).astype(jnp.bfloat16)


def hidden_rows(chunk_parts, rows):
    chunks, parts = len(chunk_parts), len(chunk_parts[0])
    width = chunk_parts[0][0].shape[1]
    vmem = pl.BlockSpec(memory_space=pltpu.VMEM)
    flat = [a for part in chunk_parts for a in part]
    return pl.pallas_call(
        functools.partial(hidden_kernel, chunks, parts, rows),
        out_shape=jax.ShapeDtypeStruct((chunks * rows, width), jnp.bfloat16),
        in_specs=[vmem] * len(flat),
        out_specs=vmem,
        compiler_params=pltpu.CompilerParams(vmem_limit_bytes=32 * 1024 * 1024),
        name="hidden_rows",
    )(*flat)


def send_kernel(own, other, sel, send):
    both = jnp.concatenate([own[...], other[...]], axis=0)
    send[...] = jnp.dot(sel[...], both, preferred_element_type=jnp.float32).astype(jnp.bfloat16)


def rows_to_send(own, other, sel):
    vmem = pl.BlockSpec(memory_space=pltpu.VMEM)
    return pl.pallas_call(
        send_kernel,
        out_shape=jax.ShapeDtypeStruct((sel.shape[0], own.shape[1]), jnp.bfloat16),
        in_specs=[vmem] * 3,
        out_specs=vmem,
        compiler_params=pltpu.CompilerParams(vmem_limit_bytes=32 * 1024 * 1024),
        name="rows_to_send",
    )(own, other, sel)


def logits_kernel(groups, ids, own, other, received, adj, adj_received, w_self, w_neigh, out, hidden):
    core = ids[0]
    for i in range(groups // 2):
        mine = group_of(core, i, groups)
        theirs = group_of(1 - core, i, groups)
        hidden[pl.ds(pl.multiple_of(mine * UNIT, UNIT), UNIT), :] = own[i * UNIT:(i + 1) * UNIT, :]
        hidden[pl.ds(pl.multiple_of(theirs * UNIT, UNIT), UNIT), :] = other[i * UNIT:(i + 1) * UNIT, :]
    tile, rows = hidden.shape[0], adj.shape[0]
    mean = jnp.dot(adj_received[...], received[...], preferred_element_type=jnp.float32)
    mean = mean + jnp.dot(adj[:, :tile], hidden[...], preferred_element_type=jnp.float32)
    dims = (((1,), (1,)), ((), ()))
    got = lax.dot_general(hidden[:rows, :], w_self[...], dims, preferred_element_type=jnp.float32)
    got = got + lax.dot_general(mean.astype(jnp.bfloat16), w_neigh[...], dims, preferred_element_type=jnp.float32)
    out[...] = got


def logits_of(groups, ids, own, other, received, adj, adj_received, w_self, w_neigh):
    smem = pl.BlockSpec(memory_space=pltpu.SMEM)
    vmem = pl.BlockSpec(memory_space=pltpu.VMEM)
    return pl.pallas_call(
        functools.partial(logits_kernel, groups),
        out_shape=jax.ShapeDtypeStruct((adj.shape[0], w_self.shape[1]), jnp.float32),
        in_specs=[smem] + [vmem] * 7,
        out_specs=vmem,
        scratch_shapes=[pltpu.VMEM((groups * UNIT, own.shape[1]), jnp.bfloat16)],
        compiler_params=pltpu.CompilerParams(vmem_limit_bytes=32 * 1024 * 1024),
        name="logits",
    )(ids, own, other, received, adj, adj_received, w_self.T, w_neigh.T)


def exchange(parts, stride, n, places):
    got = [parts[0]]
    for k in places:
        got.append(lax.ppermute(parts[k], "dom", [(i, i ^ (k * stride)) for i in range(n)]))
    return got


def body(
    features,
    tile_weight,
    tile_dst,
    tile_src,
    tile_rows,
    w_self1,
    neighbour_weight_first,
    send_list,
    send_count,
    adj_two,
    w_self2,
    w_neigh2,
):
    n = lax.axis_size("dom")
    tile = tile_weight.shape[1]
    groups = tile // UNIT
    per = groups // 2 // CHUNKS
    bits = n.bit_length() - 1
    assert n == 1 << bits and bits >= 2
    radices = [2] * (bits // 2) + [1] * (bits % 2)
    ids = jnp.stack([lax.axis_index("feat"), lax.axis_index("dom")]).astype(jnp.int32)
    swap = [(0, 1), (1, 0)]
    xp = lax.ppermute(features, "feat", swap)
    wp = lax.ppermute(neighbour_weight_first, "feat", swap)
    sp = lax.ppermute(w_self1, "feat", swap)
    tw = tile_weight.reshape(tile_weight.shape[0], groups, UNIT, tile)
    planned = plan(
        CHUNKS, per, n, 4, ids, tile_src, tile_rows, tile_dst, tw, features, neighbour_weight_first, w_self1,
    )
    tables, tbufs, (xo, wo, so) = planned[:CHUNKS], planned[CHUNKS:2 * CHUNKS], planned[2 * CHUNKS:]
    done = []
    for chunk in range(CHUNKS):
        accs = gathered_sums(per, n, tables[chunk], tbufs[chunk], xo, xp)
        slots, rows = n // 4, per * UNIT
        parts = {k: sent_terms(k, slots, rows, accs, wo, wp) for k in (1, 2, 3)}
        parts[0] = own_terms(chunk, per, groups, slots, ids, accs, wo, wp, xo, xp, so, sp)
        got = exchange(parts, 1, n, (1, 2, 3))
        stride = 4
        for radix in radices[1:]:
            ways = 1 << radix
            parts = combine(n // stride, per * UNIT, ways, got[0], got[1:])
            got = exchange(parts, stride, n, (2, 3, 1) if ways == 4 else (1,))
            stride *= ways
        done.append(got)
    sel, adj_received = selection(groups, ids, send_list, send_count, adj_two)
    own = hidden_rows(done, per * UNIT)
    other = lax.ppermute(own, "feat", swap)
    send = rows_to_send(own, other, sel)
    received = lax.all_to_all(send, "dom", 0, 0, axis_index_groups=[group_order(n)], tiled=True)
    return logits_of(groups, ids, own, other, received, adj_two, adj_received, w_self2, w_neigh2)


def solution(mesh):
    in_specs = (
        P("dom", "feat"),
        P("dom", None, None),
        P("dom"),
        P("dom"),
        P("dom"),
        P("feat", None),
        P("feat", None),
        P(),
        P(),
        P("dom", None),
        P(),
        P(),
    )
    out_specs = P("dom", None)
    return jax.shard_map(body, mesh=mesh, in_specs=in_specs, out_specs=out_specs, check_vma=False)
```

```python
import functools

import jax
import jax.numpy as jnp
from jax import lax
from jax.experimental import pallas as pl
from jax.experimental.pallas import tpu as pltpu
from jax.sharding import PartitionSpec as P

UNIT = 16
BLOCK = 8
STEP = 8
PART = 256
CHUNKS = 1


def group_of(core, place, groups):
    pair = 2 * (place // 2) + core
    return pair if place % 2 == 0 else groups - 1 - pair


def group_order(n):
    return list(range(n - 1, -1, -1))


LN2 = 0.6931471805599453


def tail_rows(slots):
    return -(-slots // 16) * 16


def encode(x):
    top = jnp.max(jnp.abs(x), axis=0, keepdims=True)
    power = jnp.ceil(jnp.log(jnp.maximum(top, 1e-30)) * (1.0 / LN2) + 1e-3) - 15.0
    return jnp.floor(x * jnp.exp(power * -LN2) + 0.5), power


def to_int16(x):
    return x.astype(jnp.int32).astype(jnp.int16)


def write_coded(out, tail, slots, rows, value_of):
    tail[...] = jnp.zeros_like(tail)
    for s in range(slots):
        whole, power = encode(value_of(s))
        out[s * rows:(s + 1) * rows, :] = to_int16(whole)
        tail[s:s + 1, :] = power
    out[slots * rows:, :] = to_int16(tail[...])


def read_coded(ref, slots, rows):
    powers = ref[slots * rows:, :].astype(jnp.int32).astype(jnp.float32)

    def value_of(s):
        whole = ref[s * rows:(s + 1) * rows, :].astype(jnp.int32).astype(jnp.float32)
        return whole * jnp.exp(powers[s:s + 1, :] * LN2)

    return value_of


def plan_kernel(chunks, per, n, radix, n_src, ids, src_h, rows_h, dst_h, tw, xo, wo, so, *rest):
    tables, rest = rest[:chunks], rest[chunks:]
    tbufs, rest = rest[:chunks], rest[chunks:]
    xo_out, wo_out, so_out = rest[:3]
    src_v, rows_v, dst_v, sems = rest[3:]
    core, me = ids[0], ids[1]
    tiles = src_v.shape[1]
    n_pos = tables[0].shape[1]
    units = per * tiles
    groups = 2 * per * chunks
    half = groups // 2
    gs = [group_of(core, i, groups) for i in range(half)]
    small = [(src_h, src_v), (rows_h, rows_v), (dst_h, dst_v)]
    large = [(tw.at[:, g], tbufs[i // per].at[pl.ds(i % per * tiles, tiles)]) for i, g in enumerate(gs)]
    large += [(xo, xo_out), (wo, wo_out), (so, so_out)]
    copies = [pltpu.make_async_copy(a, b, sems.at[i]) for i, (a, b) in enumerate(small + large)]
    for c in copies:
        c.start()
    lane = lax.broadcasted_iota(jnp.int32, (1, tiles), 1)
    block_i = lax.broadcasted_iota(jnp.int32, (n_src, tiles), 0)
    before = lax.broadcasted_iota(jnp.int32, (units, units), 0) < lax.broadcasted_iota(jnp.int32, (units, units), 1)
    before = jnp.where(before, 1.0, 0.0).astype(jnp.bfloat16)
    pos_i = lax.broadcasted_iota(jnp.int32, (tiles, n_pos), 1).astype(jnp.float32)
    place_i = lax.broadcasted_iota(jnp.int32, (1, n_pos), 1)
    trash = float(n * per << 14)
    for c in copies[:3]:
        c.wait()
    src, rows = src_v[...], rows_v[...]
    slot = jnp.bitwise_xor(dst_v[...], me)
    slot = jnp.bitwise_and(slot, radix - 1) * (n // radix) + lax.div(slot, radix)
    for c in range(chunks):
        hot, words, valid = [], [], []
        for j in range(per):
            limit = jnp.clip(rows - UNIT * gs[c * per + j], 0, UNIT)
            ok = limit > 0
            valid.append(ok)
            words.append(((slot * per + j) * 512 + (j * tiles + lane)) * 32 + limit)
            hot.append(jnp.where(jnp.logical_and(block_i == src, ok), 1.0, 0.0))
        hot = jnp.concatenate(hot, axis=1)
        earlier = jnp.dot(hot.astype(jnp.bfloat16), before, preferred_element_type=jnp.float32)
        blocks = jnp.floor((jnp.sum(hot, axis=1, keepdims=True) + (BLOCK - 1)) * (1.0 / BLOCK))
        run = jnp.zeros((1, 1), jnp.float32)
        pos = jnp.zeros((1, units), jnp.float32)
        owner = jnp.zeros((1, n_pos), jnp.float32)
        for s in range(n_src):
            pos = pos + hot[s:s + 1, :] * (earlier[s:s + 1, :] + run * BLOCK)
            run = run + blocks[s:s + 1, :]
            owner = owner + jnp.where(place_i.astype(jnp.float32) >= run, 1.0, 0.0)
        stack = [jnp.where(valid[j], pos[:, j * tiles:(j + 1) * tiles], -1.0) for j in range(per)]
        stack += [w.astype(jnp.float32) - trash for w in words]
        stack += [jnp.zeros((1, tiles), jnp.float32)] * (-len(stack) % 8)
        cols = jnp.concatenate(stack, axis=0).T
        found = jnp.zeros((tiles, n_pos), jnp.float32)
        for j in range(per):
            found = found + jnp.where(cols[:, j:j + 1] == pos_i, cols[:, per + j:per + j + 1], 0.0)
        word = jnp.sum(found, axis=0, keepdims=True) + trash
        owner = jnp.where(place_i == n_pos - 1, run, jnp.minimum(owner, n_src - 1.0))
        tables[c][0:1, :] = word.astype(jnp.int32)
        tables[c][1:2, :] = owner.astype(jnp.int32)

    for c in copies[3:]:
        c.wait()


def plan(chunks, per, n, radix, ids, src, rows, dst, tw, xo, wo, so):
    tiles, _, _, tile = tw.shape
    n_src = xo.shape[0] // tile
    blocks = -(-(per * tiles // BLOCK + n_src) // STEP) * STEP
    n_pos = -(-(blocks * BLOCK + 1) // 128) * 128
    smem = pl.BlockSpec(memory_space=pltpu.SMEM)
    vmem = pl.BlockSpec(memory_space=pltpu.VMEM)
    hbm = pl.BlockSpec(memory_space=pltpu.HBM)
    half = chunks * per
    return pl.pallas_call(
        functools.partial(plan_kernel, chunks, per, n, radix, n_src),
        out_shape=[jax.ShapeDtypeStruct((2, n_pos), jnp.int32)] * chunks
        + [jax.ShapeDtypeStruct((per * tiles, UNIT, tile), tw.dtype)] * chunks
        + [
            jax.ShapeDtypeStruct(xo.shape, xo.dtype),
            jax.ShapeDtypeStruct(wo.shape, wo.dtype),
            jax.ShapeDtypeStruct(so.shape, so.dtype),
        ],
        in_specs=[smem] + [hbm] * 7,
        out_specs=[vmem] * (2 * chunks + 3),
        scratch_shapes=[
            pltpu.VMEM((1, tiles), jnp.int32),
            pltpu.VMEM((1, tiles), jnp.int32),
            pltpu.VMEM((1, tiles), jnp.int32),
            pltpu.SemaphoreType.DMA((3 + half + 3,)),
        ],
        compiler_params=pltpu.CompilerParams(vmem_limit_bytes=32 * 1024 * 1024),
        name="plan",
    )(ids, *[
        pltpu.with_memory_space_constraint(a, pltpu.HBM)
        for a in (src.reshape(1, tiles), rows.reshape(1, tiles), dst.reshape(1, tiles), tw, xo, wo, so)
    ])


def select_kernel(groups, ids, lists, counts, adj, sel, front, adj_out):
    core, me = ids[0], ids[1]
    n = lists.shape[0]
    slots = lists.shape[1]
    total = n * slots
    q_n = lax.broadcasted_iota(jnp.int32, (total, n), 0)
    r_n = lax.broadcasted_iota(jnp.int32, (total, n), 1)
    mine = lists[me].astype(jnp.float32)
    cnt = counts[pl.ds(me, 1), :]
    picked = jnp.zeros((total, n), jnp.float32)
    k_n = jnp.bitwise_and(q_n, slots - 1)
    for k in range(slots):
        picked = jnp.where(k_n == k, mine[k:k + 1, :], picked)
    good = jnp.logical_and(n - 1 - lax.div(q_n, slots) == r_n, k_n < cnt)
    row = jnp.sum(jnp.where(good, picked + 1.0, 0.0), axis=1, keepdims=True) - 1.0
    lane = lax.broadcasted_iota(jnp.int32, (1, sel.shape[1]), 1)
    name = jnp.zeros(lane.shape, jnp.int32)
    names = [group_of(c, i, groups) for c in (core, 1 - core) for i in range(groups // 2)]
    for i, g in enumerate(names):
        name = jnp.where(lax.div(lane, UNIT) == i, g * UNIT + jnp.bitwise_and(lane, UNIT - 1), name)
    sel[...] = jnp.where(row == name.astype(jnp.float32), 1.0, 0.0).astype(jnp.bfloat16)
    tile, out_rows = groups * UNIT, adj.shape[0]
    placed = jnp.where(lax.broadcasted_iota(jnp.int32, (tile, tile), 0) == name, 1.0, 0.0).astype(jnp.bfloat16)
    front[:out_rows, :] = jnp.dot(adj[:, :tile], placed, preferred_element_type=jnp.float32).astype(jnp.bfloat16)
    front[out_rows:, :] = placed[:out_rows, :]
    column = lax.broadcasted_iota(jnp.int32, (1, total), 1)
    source = (n - 1 - lax.div(column, slots)) * slots + lax.rem(column, slots)
    moved = jnp.where(lax.broadcasted_iota(jnp.int32, (total, total), 0) == source, 1.0, 0.0).astype(jnp.bfloat16)
    adj_out[...] = jnp.dot(adj[:, groups * UNIT:], moved, preferred_element_type=jnp.float32).astype(jnp.bfloat16)


def selection(groups, ids, send_list, send_count, adj):
    n, _, slots = send_list.shape
    smem = pl.BlockSpec(memory_space=pltpu.SMEM)
    vmem = pl.BlockSpec(memory_space=pltpu.VMEM)
    return pl.pallas_call(
        functools.partial(select_kernel, groups),
        out_shape=[
            jax.ShapeDtypeStruct((n * slots, groups * UNIT), jnp.bfloat16),
            jax.ShapeDtypeStruct((2 * adj.shape[0], groups * UNIT), jnp.bfloat16),
            jax.ShapeDtypeStruct((adj.shape[0], n * slots), jnp.bfloat16),
        ],
        in_specs=[smem, vmem, vmem, vmem],
        out_specs=[vmem] * 3,
        compiler_params=pltpu.CompilerParams(vmem_limit_bytes=32 * 1024 * 1024),
        name="selection",
    )(ids, jnp.swapaxes(send_list, 1, 2), send_count, adj)


def tiles_kernel(table_v, tbuf, xo, xp, *rest):
    parts = len(rest) - 3
    accs, (masks, table, sem) = rest[:parts], rest[parts:]
    tile = tbuf.shape[2]
    width = xo.shape[1]
    to_scalar = pltpu.make_async_copy(table_v, table, sem)
    to_scalar.start()
    for acc in accs:
        acc[...] = jnp.zeros_like(acc)
    row_i = lax.broadcasted_iota(jnp.int32, (UNIT, tile), 0)
    for m in range(UNIT + 1):
        masks[m] = jnp.where(row_i < m, 1.0, 0.0).astype(jnp.bfloat16)
    columns = [(x, h) for x in (xo, xp) for h in range(0, width, PART)]
    to_scalar.wait()

    def step(i, carry):
        for m in range(STEP):
            b = i * STEP + m
            base = pl.multiple_of(table[1, b] * tile, tile)
            rows, places = [], []
            for k in range(BLOCK):
                word = table[0, b * BLOCK + k]
                u = jnp.bitwise_and(lax.shift_right_logical(word, 5), 511)
                rows.append(tbuf[u] * masks[jnp.bitwise_and(word, 31)])
                places.append(pl.multiple_of(lax.shift_right_logical(word, 14) * UNIT, UNIT))
            lhs = jnp.concatenate(rows, axis=0)
            for acc, (x, h) in zip(accs, columns):
                got = jnp.dot(lhs, x[pl.ds(base, tile), h:h + PART], preferred_element_type=jnp.float32)
                got = got.astype(jnp.bfloat16).astype(jnp.float32)
                for k in range(BLOCK):
                    acc[pl.ds(places[k], UNIT), :] += got[k * UNIT:(k + 1) * UNIT, :]
        return carry

    steps = lax.div(table[1, table.shape[1] - 1] + STEP - 1, STEP)
    lax.fori_loop(0, steps, step, 0)


def gathered_sums(per, n, table, tbuf, xo, xp):
    width = xo.shape[1]
    tile = tbuf.shape[2]
    vmem = pl.BlockSpec(memory_space=pltpu.VMEM)
    flops = 2 * tbuf.shape[0] * UNIT * tile * 2 * width
    parts = 2 * width // PART
    sums = jax.ShapeDtypeStruct(((n * per + 1) * UNIT, PART), jnp.float32)
    return pl.pallas_call(
        tiles_kernel,
        out_shape=[sums] * parts,
        in_specs=[vmem] * 4,
        out_specs=[vmem] * parts,
        scratch_shapes=[
            pltpu.VMEM((UNIT + 1, UNIT, tile), jnp.bfloat16),
            pltpu.SMEM(table.shape, jnp.int32),
            pltpu.SemaphoreType.DMA,
        ],
        compiler_params=pltpu.CompilerParams(vmem_limit_bytes=(12 << 20) + sums.size * 4 * parts),
        cost_estimate=pl.CostEstimate(flops=flops, bytes_accessed=8 << 20, transcendentals=0),
        name="gathered_sums",
    )(table, tbuf, xo, xp)


def weigh(accs, weights, first, count, out):
    size = min(256, count)

    def piece(r, carry):
        at = pl.multiple_of(r * size, size)
        got = jnp.zeros((size, out.shape[1]), jnp.float32)
        for i, acc in enumerate(accs):
            w, h = weights[i * PART // weights[0].shape[0]], i * PART % weights[0].shape[0]
            value = acc[pl.ds(first + at, size), :]
            high = value.astype(jnp.bfloat16)
            low = (value - high.astype(jnp.float32)).astype(jnp.bfloat16)
            got = got + jnp.dot(high, w[h:h + PART, :], preferred_element_type=jnp.float32)
            got = got + jnp.dot(low, w[h:h + PART, :], preferred_element_type=jnp.float32)
        out[pl.ds(at, size), :] = got
        return carry

    lax.fori_loop(0, count // size, piece, 0)


def sent_kernel(k, slots, rows, parts, wo, wp, *refs):
    accs, (out, sums, tail) = refs[:parts], refs[parts:]
    weigh(accs, (wo, wp), k * slots * rows, slots * rows, sums)
    write_coded(out, tail, slots, rows, lambda s: sums[s * rows:(s + 1) * rows, :])


def sent_terms(k, slots, rows, accs, wo, wp):
    hidden = wo.shape[1]
    vmem = pl.BlockSpec(memory_space=pltpu.VMEM)
    return pl.pallas_call(
        functools.partial(sent_kernel, k, slots, rows, len(accs)),
        out_shape=jax.ShapeDtypeStruct((slots * rows + tail_rows(slots), hidden), jnp.int16),
        in_specs=[vmem] * (2 + len(accs)),
        out_specs=vmem,
        scratch_shapes=[
            pltpu.VMEM((slots * rows, hidden), jnp.float32),
            pltpu.VMEM((tail_rows(slots), hidden), jnp.float32),
        ],
        compiler_params=pltpu.CompilerParams(vmem_limit_bytes=(12 << 20) + accs[0].size * 4 * len(accs)),
        cost_estimate=pl.CostEstimate(
            flops=4 * slots * rows * PART * len(accs) * hidden, bytes_accessed=2 << 20, transcendentals=0),
        name="sent_terms",
    )(wo, wp, *accs)


def own_kernel(chunk, per, groups, parts, ids, wo, wp, xo, so, *refs):
    accs, (out, theirs, terms) = refs[:parts], refs[parts:]
    weigh(accs, (wo, wp), 0, out.shape[0], out)
    terms[...] = jnp.dot(xo[:groups * UNIT, :], so[...], preferred_element_type=jnp.float32)
    for j in range(per):
        here = slice(j * UNIT, (j + 1) * UNIT)
        at = pl.multiple_of(group_of(ids[0], chunk * per + j, groups) * UNIT, UNIT)
        out[here, :] += terms[pl.ds(at, UNIT), :]
        at = pl.multiple_of(group_of(1 - ids[0], chunk * per + j, groups) * UNIT, UNIT)
        theirs[here, :] = terms[pl.ds(at, UNIT), :]


def own_terms(chunk, per, groups, slots, ids, accs, wo, wp, xo, so):
    hidden = wo.shape[1]
    rows = per * UNIT
    smem = pl.BlockSpec(memory_space=pltpu.SMEM)
    vmem = pl.BlockSpec(memory_space=pltpu.VMEM)
    return pl.pallas_call(
        functools.partial(own_kernel, chunk, per, groups, len(accs)),
        out_shape=[
            jax.ShapeDtypeStruct((slots * rows, hidden), jnp.float32),
            jax.ShapeDtypeStruct((rows, hidden), jnp.float32),
        ],
        in_specs=[smem] + [vmem] * (4 + len(accs)),
        out_specs=[vmem] * 2,
        scratch_shapes=[pltpu.VMEM((groups * UNIT, hidden), jnp.float32)],
        compiler_params=pltpu.CompilerParams(vmem_limit_bytes=(12 << 20) + accs[0].size * 4 * len(accs)),
        cost_estimate=pl.CostEstimate(
            flops=4 * slots * rows * PART * len(accs) * hidden, bytes_accessed=2 << 20, transcendentals=0),
        name="own_terms",
    )(ids, wo, wp, xo, so, *accs)


def combine_kernel(slots, rows, ways, own, *refs):
    parts = len(refs) - ways - 1
    coded, outs, tail = refs[:parts], refs[parts:parts + ways], refs[parts + ways]
    values = [read_coded(a, slots, rows) for a in coded]

    def total(s):
        got = own[s * rows:(s + 1) * rows, :]
        for value in values:
            got = got + value(s)
        return got

    for i in range(slots // ways):
        outs[0][i * rows:(i + 1) * rows, :] = total(i * ways)
    for k in range(1, ways):
        write_coded(outs[k], tail, slots // ways, rows, lambda s: total(s * ways + k))


def combine(slots, rows, ways, own, coded):
    width = own.shape[1]
    left = slots // ways
    vmem = pl.BlockSpec(memory_space=pltpu.VMEM)
    out = jax.ShapeDtypeStruct((left * rows + tail_rows(left), width), jnp.int16)
    return pl.pallas_call(
        functools.partial(combine_kernel, slots, rows, ways),
        out_shape=[jax.ShapeDtypeStruct((left * rows, width), jnp.float32)] + [out] * (ways - 1),
        in_specs=[vmem] * (1 + len(coded)),
        out_specs=[vmem] * ways,
        scratch_shapes=[pltpu.VMEM((tail_rows(left), width), jnp.float32)],
        compiler_params=pltpu.CompilerParams(vmem_limit_bytes=32 * 1024 * 1024),
        name="combine",
    )(own, *coded)


def hidden_kernel(chunks, parts, rows, *refs):
    out = refs[chunks * parts + 1]
    for c in range(chunks):
        own, self, coded = refs[c * parts], refs[c * parts + 1], refs[c * parts + 2:(c + 1) * parts]
        total = own[:rows, :] + self[...]
        for a in coded:
            total = total + read_coded(a, 1, rows)(0)
        out[c * rows:(c + 1) * rows, :] = jnp.maximum(total, 0.0).astype(jnp.bfloat16)


def hidden_rows(chunk_parts, rows, sel):
    chunks, parts = len(chunk_parts), len(chunk_parts[0])
    width = chunk_parts[0][0].shape[1]
    vmem = pl.BlockSpec(memory_space=pltpu.VMEM)
    flat = [a for part in chunk_parts for a in part]
    return pl.pallas_call(
        functools.partial(hidden_kernel, chunks, parts, rows),
        out_shape=jax.ShapeDtypeStruct((chunks * rows, width), jnp.bfloat16),
        in_specs=[vmem] * (len(flat) + 1),
        out_specs=vmem,
        compiler_params=pltpu.CompilerParams(vmem_limit_bytes=32 * 1024 * 1024),
        name="hidden_rows",
    )(*flat, sel)


def send_kernel(own, other, sel, send):
    both = jnp.concatenate([own[...], other[...]], axis=0)
    send[...] = jnp.dot(sel[...], both, preferred_element_type=jnp.float32).astype(jnp.bfloat16)


def rows_to_send(own, other, sel):
    vmem = pl.BlockSpec(memory_space=pltpu.VMEM)
    return pl.pallas_call(
        send_kernel,
        out_shape=jax.ShapeDtypeStruct((sel.shape[0], own.shape[1]), jnp.bfloat16),
        in_specs=[vmem] * 3,
        out_specs=vmem,
        compiler_params=pltpu.CompilerParams(vmem_limit_bytes=32 * 1024 * 1024),
        name="rows_to_send",
    )(own, other, sel)


def logits_kernel(own, other, received, front, adj_received, w_self, w_neigh, out):
    rows = out.shape[0]
    both = jnp.concatenate([own[...], other[...]], axis=0)
    local = jnp.dot(front[...], both, preferred_element_type=jnp.float32)
    mean = local[:rows, :] + jnp.dot(adj_received[...], received[...], preferred_element_type=jnp.float32)
    dims = (((1,), (1,)), ((), ()))
    got = lax.dot_general(local[rows:, :].astype(jnp.bfloat16), w_self[...], dims, preferred_element_type=jnp.float32)
    got = got + lax.dot_general(mean.astype(jnp.bfloat16), w_neigh[...], dims, preferred_element_type=jnp.float32)
    out[...] = got


def logits_of(own, other, received, front, adj_received, w_self, w_neigh):
    vmem = pl.BlockSpec(memory_space=pltpu.VMEM)
    return pl.pallas_call(
        logits_kernel,
        out_shape=jax.ShapeDtypeStruct((adj_received.shape[0], w_self.shape[1]), jnp.float32),
        in_specs=[vmem] * 7,
        out_specs=vmem,
        compiler_params=pltpu.CompilerParams(vmem_limit_bytes=32 * 1024 * 1024),
        name="logits",
    )(own, other, received, front, adj_received, w_self.T, w_neigh.T)


def exchange(parts, stride, n, places):
    got = [parts[0]]
    for k in places:
        got.append(lax.ppermute(parts[k], "dom", [(i, i ^ (k * stride)) for i in range(n)]))
    return got


def body(
    features,
    tile_weight,
    tile_dst,
    tile_src,
    tile_rows,
    w_self1,
    neighbour_weight_first,
    send_list,
    send_count,
    adj_two,
    w_self2,
    w_neigh2,
):
    n = lax.axis_size("dom")
    tile = tile_weight.shape[1]
    groups = tile // UNIT
    per = groups // 2 // CHUNKS
    bits = n.bit_length() - 1
    assert n == 1 << bits and bits >= 2
    radices = [2] * (bits // 2) + [1] * (bits % 2)
    ids = jnp.stack([lax.axis_index("feat"), lax.axis_index("dom")]).astype(jnp.int32)
    swap = [(0, 1), (1, 0)]
    xp = lax.ppermute(features, "feat", swap)
    wp = lax.ppermute(neighbour_weight_first, "feat", swap)
    tw = tile_weight.reshape(tile_weight.shape[0], groups, UNIT, tile)
    planned = plan(
        CHUNKS, per, n, 4, ids, tile_src, tile_rows, tile_dst, tw, features, neighbour_weight_first, w_self1,
    )
    tables, tbufs, (xo, wo, so) = planned[:CHUNKS], planned[CHUNKS:2 * CHUNKS], planned[2 * CHUNKS:]
    done = []
    for chunk in range(CHUNKS):
        accs = gathered_sums(per, n, tables[chunk], tbufs[chunk], xo, xp)
        slots, rows = n // 4, per * UNIT
        parts = {k: sent_terms(k, slots, rows, accs, wo, wp) for k in (1, 2, 3)}
        parts[0], theirs = own_terms(chunk, per, groups, slots, ids, accs, wo, wp, xo, so)
        self = lax.ppermute(theirs, "feat", swap)
        got = exchange(parts, 1, n, (1, 2, 3))
        stride = 4
        for radix in radices[1:]:
            ways = 1 << radix
            parts = combine(n // stride, per * UNIT, ways, got[0], got[1:])
            got = exchange(parts, stride, n, (2, 3, 1) if ways == 4 else (1,))
            stride *= ways
        done.append([got[0], self] + got[1:])
    sel, front, adj_received = selection(groups, ids, send_list, send_count, adj_two)
    own = hidden_rows(done, per * UNIT, sel)
    other = lax.ppermute(own, "feat", swap)
    send = rows_to_send(own, other, sel)
    received = lax.all_to_all(send, "dom", 0, 0, axis_index_groups=[group_order(n)], tiled=True)
    return logits_of(own, other, received, front, adj_received, w_self2, w_neigh2)


def solution(mesh):
    in_specs = (
        P("dom", "feat"),
        P("dom", None, None),
        P("dom"),
        P("dom"),
        P("dom"),
        P("feat", None),
        P("feat", None),
        P(),
        P(),
        P("dom", None),
        P(),
        P(),
    )
    out_specs = P("dom", None)
    return jax.shard_map(body, mesh=mesh, in_specs=in_specs, out_specs=out_specs, check_vma=False)
```

```python
import functools

import jax
import jax.numpy as jnp
from jax import lax
from jax.experimental import pallas as pl
from jax.experimental.pallas import tpu as pltpu
from jax.sharding import PartitionSpec as P

UNIT = 16
BLOCK = 8
STEP = 8
PART = 256
CHUNKS = 1


def group_of(core, place, groups):
    pair = 2 * (place // 2) + core
    return pair if place % 2 == 0 else groups - 1 - pair


def group_order(n):
    return list(range(n - 1, -1, -1))


LN2 = 0.6931471805599453


def tail_rows(slots):
    return -(-slots // 8) * 8


def encode(x):
    top = jnp.max(jnp.abs(x), axis=0, keepdims=True)
    power = jnp.ceil(jnp.log(jnp.maximum(top, 1e-30)) * (1.0 / LN2) + 1e-3) - 15.0
    return jnp.floor(x * jnp.exp(power * -LN2) + 0.5), power


def to_int16(x):
    return x.astype(jnp.int32).astype(jnp.int16)


def write_coded(out, tail, slots, rows, value_of):
    tail[...] = jnp.zeros_like(tail)
    for s in range(slots):
        whole, power = encode(value_of(s))
        out[s * rows:(s + 1) * rows, :] = to_int16(whole)
        tail[s:s + 1, :] = power
    out[slots * rows:, :] = to_int16(tail[...])


def read_coded(ref, slots, rows):
    powers = ref[slots * rows:, :].astype(jnp.int32).astype(jnp.float32)

    def value_of(s):
        whole = ref[s * rows:(s + 1) * rows, :].astype(jnp.int32).astype(jnp.float32)
        return whole * jnp.exp(powers[s:s + 1, :] * LN2)

    return value_of


def plan_kernel(chunks, per, n, radix, n_src, ids, src_h, rows_h, dst_h, tw, xo, wo, so, *rest):
    tables, rest = rest[:chunks], rest[chunks:]
    tbufs, rest = rest[:chunks], rest[chunks:]
    xo_out, wo_out, so_out = rest[:3]
    src_v, rows_v, dst_v, sems = rest[3:]
    core, me = ids[0], ids[1]
    tiles = src_v.shape[1]
    n_pos = tables[0].shape[1]
    units = per * tiles
    groups = 2 * per * chunks
    half = groups // 2
    gs = [group_of(core, i, groups) for i in range(half)]
    small = [(src_h, src_v), (rows_h, rows_v), (dst_h, dst_v)]
    large = [(tw.at[:, g], tbufs[i // per].at[pl.ds(i % per * tiles, tiles)]) for i, g in enumerate(gs)]
    large += [(xo, xo_out), (wo, wo_out), (so, so_out)]
    copies = [pltpu.make_async_copy(a, b, sems.at[i]) for i, (a, b) in enumerate(small + large)]
    for c in copies:
        c.start()
    lane = lax.broadcasted_iota(jnp.int32, (1, tiles), 1)
    block_i = lax.broadcasted_iota(jnp.int32, (n_src, tiles), 0)
    before = lax.broadcasted_iota(jnp.int32, (units, units), 0) < lax.broadcasted_iota(jnp.int32, (units, units), 1)
    before = jnp.where(before, 1.0, 0.0).astype(jnp.bfloat16)
    pos_i = lax.broadcasted_iota(jnp.int32, (tiles, n_pos), 1).astype(jnp.float32)
    place_i = lax.broadcasted_iota(jnp.int32, (1, n_pos), 1)
    trash = float(n * per << 14)
    for c in copies[:3]:
        c.wait()
    src, rows = src_v[...], rows_v[...]
    slot = jnp.bitwise_xor(dst_v[...], me)
    slot = jnp.bitwise_and(slot, radix - 1) * (n // radix) + lax.div(slot, radix)
    for c in range(chunks):
        hot, words, valid = [], [], []
        for j in range(per):
            limit = jnp.clip(rows - UNIT * gs[c * per + j], 0, UNIT)
            ok = limit > 0
            valid.append(ok)
            words.append(((slot * per + j) * 512 + (j * tiles + lane)) * 32 + limit)
            hot.append(jnp.where(jnp.logical_and(block_i == src, ok), 1.0, 0.0))
        hot = jnp.concatenate(hot, axis=1)
        earlier = jnp.dot(hot.astype(jnp.bfloat16), before, preferred_element_type=jnp.float32)
        blocks = jnp.floor((jnp.sum(hot, axis=1, keepdims=True) + (BLOCK - 1)) * (1.0 / BLOCK))
        run = jnp.zeros((1, 1), jnp.float32)
        pos = jnp.zeros((1, units), jnp.float32)
        owner = jnp.zeros((1, n_pos), jnp.float32)
        for s in range(n_src):
            pos = pos + hot[s:s + 1, :] * (earlier[s:s + 1, :] + run * BLOCK)
            run = run + blocks[s:s + 1, :]
            owner = owner + jnp.where(place_i.astype(jnp.float32) >= run, 1.0, 0.0)
        stack = [jnp.where(valid[j], pos[:, j * tiles:(j + 1) * tiles], -1.0) for j in range(per)]
        stack += [w.astype(jnp.float32) - trash for w in words]
        stack += [jnp.zeros((1, tiles), jnp.float32)] * (-len(stack) % 8)
        cols = jnp.concatenate(stack, axis=0).T
        found = jnp.zeros((tiles, n_pos), jnp.float32)
        for j in range(per):
            found = found + jnp.where(cols[:, j:j + 1] == pos_i, cols[:, per + j:per + j + 1], 0.0)
        word = jnp.sum(found, axis=0, keepdims=True) + trash
        owner = jnp.where(place_i == n_pos - 1, run, jnp.minimum(owner, n_src - 1.0))
        tables[c][0:1, :] = word.astype(jnp.int32)
        tables[c][1:2, :] = owner.astype(jnp.int32)

    for c in copies[3:]:
        c.wait()


def plan(chunks, per, n, radix, ids, src, rows, dst, tw, xo, wo, so):
    tiles, _, _, tile = tw.shape
    n_src = xo.shape[0] // tile
    blocks = -(-(per * tiles // BLOCK + n_src) // STEP) * STEP
    n_pos = -(-(blocks * BLOCK + 1) // 128) * 128
    smem = pl.BlockSpec(memory_space=pltpu.SMEM)
    vmem = pl.BlockSpec(memory_space=pltpu.VMEM)
    hbm = pl.BlockSpec(memory_space=pltpu.HBM)
    half = chunks * per
    return pl.pallas_call(
        functools.partial(plan_kernel, chunks, per, n, radix, n_src),
        out_shape=[jax.ShapeDtypeStruct((2, n_pos), jnp.int32)] * chunks
        + [jax.ShapeDtypeStruct((per * tiles, UNIT, tile), tw.dtype)] * chunks
        + [
            jax.ShapeDtypeStruct(xo.shape, xo.dtype),
            jax.ShapeDtypeStruct(wo.shape, wo.dtype),
            jax.ShapeDtypeStruct(so.shape, so.dtype),
        ],
        in_specs=[smem] + [hbm] * 7,
        out_specs=[vmem] * (2 * chunks + 3),
        scratch_shapes=[
            pltpu.VMEM((1, tiles), jnp.int32),
            pltpu.VMEM((1, tiles), jnp.int32),
            pltpu.VMEM((1, tiles), jnp.int32),
            pltpu.SemaphoreType.DMA((3 + half + 3,)),
        ],
        compiler_params=pltpu.CompilerParams(vmem_limit_bytes=32 * 1024 * 1024),
        name="plan",
    )(ids, *[
        pltpu.with_memory_space_constraint(a, pltpu.HBM)
        for a in (src.reshape(1, tiles), rows.reshape(1, tiles), dst.reshape(1, tiles), tw, xo, wo, so)
    ])


def select_kernel(groups, ids, lists, counts, adj, sel, front, adj_out):
    core, me = ids[0], ids[1]
    n = lists.shape[0]
    slots = lists.shape[1]
    total = n * slots
    q_n = lax.broadcasted_iota(jnp.int32, (total, n), 0)
    r_n = lax.broadcasted_iota(jnp.int32, (total, n), 1)
    mine = lists[me].astype(jnp.float32)
    cnt = counts[pl.ds(me, 1), :]
    picked = jnp.zeros((total, n), jnp.float32)
    k_n = jnp.bitwise_and(q_n, slots - 1)
    for k in range(slots):
        picked = jnp.where(k_n == k, mine[k:k + 1, :], picked)
    good = jnp.logical_and(n - 1 - lax.div(q_n, slots) == r_n, k_n < cnt)
    row = jnp.sum(jnp.where(good, picked + 1.0, 0.0), axis=1, keepdims=True) - 1.0
    lane = lax.broadcasted_iota(jnp.int32, (1, sel.shape[1]), 1)
    name = jnp.zeros(lane.shape, jnp.int32)
    names = [group_of(c, i, groups) for c in (core, 1 - core) for i in range(groups // 2)]
    for i, g in enumerate(names):
        name = jnp.where(lax.div(lane, UNIT) == i, g * UNIT + jnp.bitwise_and(lane, UNIT - 1), name)
    sel[...] = jnp.where(row == name.astype(jnp.float32), 1.0, 0.0).astype(jnp.bfloat16)
    tile, out_rows = groups * UNIT, adj.shape[0]
    placed = jnp.where(lax.broadcasted_iota(jnp.int32, (tile, tile), 0) == name, 1.0, 0.0).astype(jnp.bfloat16)
    front[:out_rows, :] = jnp.dot(adj[:, :tile], placed, preferred_element_type=jnp.float32).astype(jnp.bfloat16)
    front[out_rows:, :] = placed[:out_rows, :]
    column = lax.broadcasted_iota(jnp.int32, (1, total), 1)
    source = (n - 1 - lax.div(column, slots)) * slots + lax.rem(column, slots)
    moved = jnp.where(lax.broadcasted_iota(jnp.int32, (total, total), 0) == source, 1.0, 0.0).astype(jnp.bfloat16)
    adj_out[...] = jnp.dot(adj[:, groups * UNIT:], moved, preferred_element_type=jnp.float32).astype(jnp.bfloat16)


def selection(groups, ids, send_list, send_count, adj):
    n, _, slots = send_list.shape
    smem = pl.BlockSpec(memory_space=pltpu.SMEM)
    vmem = pl.BlockSpec(memory_space=pltpu.VMEM)
    return pl.pallas_call(
        functools.partial(select_kernel, groups),
        out_shape=[
            jax.ShapeDtypeStruct((n * slots, groups * UNIT), jnp.bfloat16),
            jax.ShapeDtypeStruct((2 * adj.shape[0], groups * UNIT), jnp.bfloat16),
            jax.ShapeDtypeStruct((adj.shape[0], n * slots), jnp.bfloat16),
        ],
        in_specs=[smem, vmem, vmem, vmem],
        out_specs=[vmem] * 3,
        compiler_params=pltpu.CompilerParams(vmem_limit_bytes=32 * 1024 * 1024),
        name="selection",
    )(ids, jnp.swapaxes(send_list, 1, 2), send_count, adj)


def tiles_kernel(table_v, tbuf, xo, xp, *rest):
    parts = len(rest) - 3
    accs, (masks, table, sem) = rest[:parts], rest[parts:]
    tile = tbuf.shape[2]
    width = xo.shape[1]
    to_scalar = pltpu.make_async_copy(table_v, table, sem)
    to_scalar.start()
    for acc in accs:
        acc[...] = jnp.zeros_like(acc)
    row_i = lax.broadcasted_iota(jnp.int32, (UNIT, tile), 0)
    for m in range(UNIT + 1):
        masks[m] = jnp.where(row_i < m, 1.0, 0.0).astype(jnp.bfloat16)
    columns = [(x, h) for x in (xo, xp) for h in range(0, width, PART)]
    to_scalar.wait()

    def step(i, carry):
        for m in range(STEP):
            at = i * STEP + m
            base = pl.multiple_of(table[1, at] * tile, tile)
            rows, places = [], []
            for k in range(BLOCK):
                word = table[0, at * BLOCK + k]
                u = jnp.bitwise_and(lax.shift_right_logical(word, 5), 511)
                rows.append(tbuf[u] * masks[jnp.bitwise_and(word, 31)])
                places.append(pl.multiple_of(lax.shift_right_logical(word, 14) * UNIT, UNIT))
            lhs = jnp.concatenate(rows, axis=0)
            alike = [jnp.where(places[k] == places[k + 1], 1.0, 0.0) for k in range(0, BLOCK, 2)]
            for acc, (x, h) in zip(accs, columns):
                got = jnp.dot(lhs, x[pl.ds(base, tile), h:h + PART], preferred_element_type=jnp.float32)
                got = got.astype(jnp.bfloat16).astype(jnp.float32)
                for k in range(0, BLOCK, 2):
                    first, second = pl.ds(places[k], UNIT), pl.ds(places[k + 1], UNIT)
                    a, b = got[k * UNIT:(k + 1) * UNIT, :], got[(k + 1) * UNIT:(k + 2) * UNIT, :]
                    b = b + a * alike[k // 2]
                    a, b = acc[first, :] + a, acc[second, :] + b
                    acc[first, :] = a
                    acc[second, :] = b
        return carry

    steps = lax.div(table[1, table.shape[1] - 1] + STEP - 1, STEP)
    lax.fori_loop(0, steps, step, 0)


def gathered_sums(per, n, table, tbuf, xo, xp):
    width = xo.shape[1]
    tile = tbuf.shape[2]
    vmem = pl.BlockSpec(memory_space=pltpu.VMEM)
    flops = 2 * tbuf.shape[0] * UNIT * tile * 2 * width
    parts = 2 * width // PART
    sums = jax.ShapeDtypeStruct(((n * per + 1) * UNIT, PART), jnp.float32)
    return pl.pallas_call(
        tiles_kernel,
        out_shape=[sums] * parts,
        in_specs=[vmem] * 4,
        out_specs=[vmem] * parts,
        scratch_shapes=[
            pltpu.VMEM((UNIT + 1, UNIT, tile), jnp.bfloat16),
            pltpu.SMEM(table.shape, jnp.int32),
            pltpu.SemaphoreType.DMA,
        ],
        compiler_params=pltpu.CompilerParams(vmem_limit_bytes=(12 << 20) + sums.size * 4 * parts),
        cost_estimate=pl.CostEstimate(flops=flops, bytes_accessed=8 << 20, transcendentals=0),
        name="gathered_sums",
    )(table, tbuf, xo, xp)


def weigh(accs, weights, first, count, out):
    size = min(256, count)

    def piece(r, carry):
        at = pl.multiple_of(r * size, size)
        got = jnp.zeros((size, out.shape[1]), jnp.float32)
        for i, acc in enumerate(accs):
            w, h = weights[i * PART // weights[0].shape[0]], i * PART % weights[0].shape[0]
            value = acc[pl.ds(first + at, size), :]
            high = value.astype(jnp.bfloat16)
            low = (value - high.astype(jnp.float32)).astype(jnp.bfloat16)
            got = got + jnp.dot(high, w[h:h + PART, :], preferred_element_type=jnp.float32)
            got = got + jnp.dot(low, w[h:h + PART, :], preferred_element_type=jnp.float32)
        out[pl.ds(at, size), :] = got
        return carry

    lax.fori_loop(0, count // size, piece, 0)


def sent_kernel(k, slots, rows, parts, wo, wp, *refs):
    accs, (out, sums, tail) = refs[:parts], refs[parts:]
    weigh(accs, (wo, wp), k * slots * rows, slots * rows, sums)
    write_coded(out, tail, slots, rows, lambda s: sums[s * rows:(s + 1) * rows, :])


def sent_terms(k, slots, rows, accs, wo, wp):
    hidden = wo.shape[1]
    vmem = pl.BlockSpec(memory_space=pltpu.VMEM)
    return pl.pallas_call(
        functools.partial(sent_kernel, k, slots, rows, len(accs)),
        out_shape=jax.ShapeDtypeStruct((slots * rows + tail_rows(slots), hidden), jnp.int16),
        in_specs=[vmem] * (2 + len(accs)),
        out_specs=vmem,
        scratch_shapes=[
            pltpu.VMEM((slots * rows, hidden), jnp.float32),
            pltpu.VMEM((tail_rows(slots), hidden), jnp.float32),
        ],
        compiler_params=pltpu.CompilerParams(vmem_limit_bytes=(12 << 20) + accs[0].size * 4 * len(accs)),
        cost_estimate=pl.CostEstimate(
            flops=4 * slots * rows * PART * len(accs) * hidden, bytes_accessed=2 << 20, transcendentals=0),
        name="sent_terms",
    )(wo, wp, *accs)


def own_kernel(chunk, per, groups, parts, ids, wo, wp, xo, so, *refs):
    accs, (out, theirs, terms) = refs[:parts], refs[parts:]
    weigh(accs, (wo, wp), 0, out.shape[0], out)
    terms[...] = jnp.dot(xo[:groups * UNIT, :], so[...], preferred_element_type=jnp.float32)
    for j in range(per):
        here = slice(j * UNIT, (j + 1) * UNIT)
        at = pl.multiple_of(group_of(ids[0], chunk * per + j, groups) * UNIT, UNIT)
        out[here, :] += terms[pl.ds(at, UNIT), :]
        at = pl.multiple_of(group_of(1 - ids[0], chunk * per + j, groups) * UNIT, UNIT)
        theirs[here, :] = terms[pl.ds(at, UNIT), :]


def own_terms(chunk, per, groups, slots, ids, accs, wo, wp, xo, so):
    hidden = wo.shape[1]
    rows = per * UNIT
    smem = pl.BlockSpec(memory_space=pltpu.SMEM)
    vmem = pl.BlockSpec(memory_space=pltpu.VMEM)
    return pl.pallas_call(
        functools.partial(own_kernel, chunk, per, groups, len(accs)),
        out_shape=[
            jax.ShapeDtypeStruct((slots * rows, hidden), jnp.float32),
            jax.ShapeDtypeStruct((rows, hidden), jnp.float32),
        ],
        in_specs=[smem] + [vmem] * (4 + len(accs)),
        out_specs=[vmem] * 2,
        scratch_shapes=[pltpu.VMEM((groups * UNIT, hidden), jnp.float32)],
        compiler_params=pltpu.CompilerParams(vmem_limit_bytes=(12 << 20) + accs[0].size * 4 * len(accs)),
        cost_estimate=pl.CostEstimate(
            flops=4 * slots * rows * PART * len(accs) * hidden, bytes_accessed=2 << 20, transcendentals=0),
        name="own_terms",
    )(ids, wo, wp, xo, so, *accs)


def combine_kernel(slots, rows, ways, own, *refs):
    parts = len(refs) - ways - 1
    coded, outs, tail = refs[:parts], refs[parts:parts + ways], refs[parts + ways]
    values = [read_coded(a, slots, rows) for a in coded]

    def total(s):
        got = own[s * rows:(s + 1) * rows, :]
        for value in values:
            got = got + value(s)
        return got

    for i in range(slots // ways):
        outs[0][i * rows:(i + 1) * rows, :] = total(i * ways)
    for k in range(1, ways):
        write_coded(outs[k], tail, slots // ways, rows, lambda s: total(s * ways + k))


def combine(slots, rows, ways, own, coded):
    width = own.shape[1]
    left = slots // ways
    vmem = pl.BlockSpec(memory_space=pltpu.VMEM)
    out = jax.ShapeDtypeStruct((left * rows + tail_rows(left), width), jnp.int16)
    return pl.pallas_call(
        functools.partial(combine_kernel, slots, rows, ways),
        out_shape=[jax.ShapeDtypeStruct((left * rows, width), jnp.float32)] + [out] * (ways - 1),
        in_specs=[vmem] * (1 + len(coded)),
        out_specs=[vmem] * ways,
        scratch_shapes=[pltpu.VMEM((tail_rows(left), width), jnp.float32)],
        compiler_params=pltpu.CompilerParams(vmem_limit_bytes=32 * 1024 * 1024),
        name="combine",
    )(own, *coded)


def hidden_kernel(chunks, parts, rows, *refs):
    out = refs[chunks * parts + 1]
    for c in range(chunks):
        own, self, coded = refs[c * parts], refs[c * parts + 1], refs[c * parts + 2:(c + 1) * parts]
        total = own[:rows, :] + self[...]
        for a in coded:
            total = total + read_coded(a, 1, rows)(0)
        out[c * rows:(c + 1) * rows, :] = jnp.maximum(total, 0.0).astype(jnp.bfloat16)


def hidden_rows(chunk_parts, rows, sel):
    chunks, parts = len(chunk_parts), len(chunk_parts[0])
    width = chunk_parts[0][0].shape[1]
    vmem = pl.BlockSpec(memory_space=pltpu.VMEM)
    flat = [a for part in chunk_parts for a in part]
    return pl.pallas_call(
        functools.partial(hidden_kernel, chunks, parts, rows),
        out_shape=jax.ShapeDtypeStruct((chunks * rows, width), jnp.bfloat16),
        in_specs=[vmem] * (len(flat) + 1),
        out_specs=vmem,
        compiler_params=pltpu.CompilerParams(vmem_limit_bytes=32 * 1024 * 1024),
        name="hidden_rows",
    )(*flat, sel)


def send_kernel(own, other, sel, send):
    both = jnp.concatenate([own[...], other[...]], axis=0)
    send[...] = jnp.dot(sel[...], both, preferred_element_type=jnp.float32).astype(jnp.bfloat16)


def rows_to_send(own, other, sel):
    vmem = pl.BlockSpec(memory_space=pltpu.VMEM)
    return pl.pallas_call(
        send_kernel,
        out_shape=jax.ShapeDtypeStruct((sel.shape[0], own.shape[1]), jnp.bfloat16),
        in_specs=[vmem] * 3,
        out_specs=vmem,
        compiler_params=pltpu.CompilerParams(vmem_limit_bytes=32 * 1024 * 1024),
        name="rows_to_send",
    )(own, other, sel)


def logits_kernel(own, other, received, front, adj_received, w_self, w_neigh, out):
    rows = out.shape[0]
    both = jnp.concatenate([own[...], other[...]], axis=0)
    local = jnp.dot(front[...], both, preferred_element_type=jnp.float32)
    mean = local[:rows, :] + jnp.dot(adj_received[...], received[...], preferred_element_type=jnp.float32)
    dims = (((1,), (1,)), ((), ()))
    got = lax.dot_general(local[rows:, :].astype(jnp.bfloat16), w_self[...], dims, preferred_element_type=jnp.float32)
    got = got + lax.dot_general(mean.astype(jnp.bfloat16), w_neigh[...], dims, preferred_element_type=jnp.float32)
    out[...] = got


def logits_of(own, other, received, front, adj_received, w_self, w_neigh):
    vmem = pl.BlockSpec(memory_space=pltpu.VMEM)
    return pl.pallas_call(
        logits_kernel,
        out_shape=jax.ShapeDtypeStruct((adj_received.shape[0], w_self.shape[1]), jnp.float32),
        in_specs=[vmem] * 7,
        out_specs=vmem,
        compiler_params=pltpu.CompilerParams(vmem_limit_bytes=32 * 1024 * 1024),
        name="logits",
    )(own, other, received, front, adj_received, w_self.T, w_neigh.T)


def exchange(parts, stride, n, places):
    got = [parts[0]]
    for k in places:
        got.append(lax.ppermute(parts[k], "dom", [(i, i ^ (k * stride)) for i in range(n)]))
    return got


def body(
    features,
    tile_weight,
    tile_dst,
    tile_src,
    tile_rows,
    w_self1,
    neighbour_weight_first,
    send_list,
    send_count,
    adj_two,
    w_self2,
    w_neigh2,
):
    n = lax.axis_size("dom")
    tile = tile_weight.shape[1]
    groups = tile // UNIT
    per = groups // 2 // CHUNKS
    bits = n.bit_length() - 1
    assert n == 1 << bits and bits >= 2
    radices = [2] * (bits // 2) + [1] * (bits % 2)
    ids = jnp.stack([lax.axis_index("feat"), lax.axis_index("dom")]).astype(jnp.int32)
    swap = [(0, 1), (1, 0)]
    xp = lax.ppermute(features, "feat", swap)
    wp = lax.ppermute(neighbour_weight_first, "feat", swap)
    tw = tile_weight.reshape(tile_weight.shape[0], groups, UNIT, tile)
    planned = plan(
        CHUNKS, per, n, 4, ids, tile_src, tile_rows, tile_dst, tw, features, neighbour_weight_first, w_self1,
    )
    tables, tbufs, (xo, wo, so) = planned[:CHUNKS], planned[CHUNKS:2 * CHUNKS], planned[2 * CHUNKS:]
    done = []
    for chunk in range(CHUNKS):
        accs = gathered_sums(per, n, tables[chunk], tbufs[chunk], xo, xp)
        slots, rows = n // 4, per * UNIT
        parts = {k: sent_terms(k, slots, rows, accs, wo, wp) for k in (1, 2, 3)}
        parts[0], theirs = own_terms(chunk, per, groups, slots, ids, accs, wo, wp, xo, so)
        self = lax.ppermute(theirs, "feat", swap)
        got = exchange(parts, 1, n, (1, 2, 3))
        stride = 4
        for radix in radices[1:]:
            ways = 1 << radix
            parts = combine(n // stride, per * UNIT, ways, got[0], got[1:])
            got = exchange(parts, stride, n, (2, 3, 1) if ways == 4 else (1,))
            stride *= ways
        done.append([got[0], self] + got[1:])
    sel, front, adj_received = selection(groups, ids, send_list, send_count, adj_two)
    own = hidden_rows(done, per * UNIT, sel)
    other = lax.ppermute(own, "feat", swap)
    send = rows_to_send(own, other, sel)
    received = lax.all_to_all(send, "dom", 0, 0, axis_index_groups=[group_order(n)], tiled=True)
    return logits_of(own, other, received, front, adj_received, w_self2, w_neigh2)


def solution(mesh):
    in_specs = (
        P("dom", "feat"),
        P("dom", None, None),
        P("dom"),
        P("dom"),
        P("dom"),
        P("feat", None),
        P("feat", None),
        P(),
        P(),
        P("dom", None),
        P(),
        P(),
    )
    out_specs = P("dom", None)
    return jax.shard_map(body, mesh=mesh, in_specs=in_specs, out_specs=out_specs, check_vma=False)
```

```python
import functools

import jax
import jax.numpy as jnp
from jax import lax
from jax.experimental import pallas as pl
from jax.experimental.pallas import tpu as pltpu
from jax.sharding import PartitionSpec as P

UNIT = 16
BLOCK = 16
STEP = 4
PART = 256
CHUNKS = 1


def group_of(core, place, groups):
    pair = 2 * (place // 2) + core
    return pair if place % 2 == 0 else groups - 1 - pair


def group_order(n):
    return list(range(n - 1, -1, -1))


LN2 = 0.6931471805599453


def tail_rows(slots):
    return -(-slots // 8) * 8


def encode(x):
    top = jnp.max(jnp.abs(x), axis=0, keepdims=True)
    power = jnp.ceil(jnp.log(jnp.maximum(top, 1e-30)) * (1.0 / LN2) + 1e-3) - 15.0
    return jnp.floor(x * jnp.exp(power * -LN2) + 0.5), power


def to_int16(x):
    return x.astype(jnp.int32).astype(jnp.int16)


def write_coded(out, tail, slots, rows, value_of):
    tail[...] = jnp.zeros_like(tail)
    for s in range(slots):
        whole, power = encode(value_of(s))
        out[s * rows:(s + 1) * rows, :] = to_int16(whole)
        tail[s:s + 1, :] = power
    out[slots * rows:, :] = to_int16(tail[...])


def read_coded(ref, slots, rows):
    powers = ref[slots * rows:, :].astype(jnp.int32).astype(jnp.float32)

    def value_of(s):
        whole = ref[s * rows:(s + 1) * rows, :].astype(jnp.int32).astype(jnp.float32)
        return whole * jnp.exp(powers[s:s + 1, :] * LN2)

    return value_of


def plan_kernel(chunks, per, n, radix, n_src, ids, src_h, rows_h, dst_h, tw, xo, wo, so, *rest):
    tables, rest = rest[:chunks], rest[chunks:]
    tbufs, rest = rest[:chunks], rest[chunks:]
    xo_out, wo_out, so_out = rest[:3]
    src_v, rows_v, dst_v, sems = rest[3:]
    core, me = ids[0], ids[1]
    tiles = src_v.shape[1]
    n_pos = tables[0].shape[1]
    units = per * tiles
    groups = 2 * per * chunks
    half = groups // 2
    gs = [group_of(core, i, groups) for i in range(half)]
    small = [(src_h, src_v), (rows_h, rows_v), (dst_h, dst_v)]
    large = [(tw.at[:, g], tbufs[i // per].at[pl.ds(i % per * tiles, tiles)]) for i, g in enumerate(gs)]
    large += [(xo, xo_out), (wo, wo_out), (so, so_out)]
    copies = [pltpu.make_async_copy(a, b, sems.at[i]) for i, (a, b) in enumerate(small + large)]
    for c in copies:
        c.start()
    lane = lax.broadcasted_iota(jnp.int32, (1, tiles), 1)
    block_i = lax.broadcasted_iota(jnp.int32, (n_src, tiles), 0)
    before = lax.broadcasted_iota(jnp.int32, (units, units), 0) < lax.broadcasted_iota(jnp.int32, (units, units), 1)
    before = jnp.where(before, 1.0, 0.0).astype(jnp.bfloat16)
    pos_i = lax.broadcasted_iota(jnp.int32, (tiles, n_pos), 1).astype(jnp.float32)
    place_i = lax.broadcasted_iota(jnp.int32, (1, n_pos), 1)
    trash = float(n * per << 14)
    for c in copies[:3]:
        c.wait()
    src, rows = src_v[...], rows_v[...]
    slot = jnp.bitwise_xor(dst_v[...], me)
    slot = jnp.bitwise_and(slot, radix - 1) * (n // radix) + lax.div(slot, radix)
    for c in range(chunks):
        hot, words, valid = [], [], []
        for j in range(per):
            limit = jnp.clip(rows - UNIT * gs[c * per + j], 0, UNIT)
            ok = limit > 0
            valid.append(ok)
            words.append(((slot * per + j) * 512 + (j * tiles + lane)) * 32 + limit)
            hot.append(jnp.where(jnp.logical_and(block_i == src, ok), 1.0, 0.0))
        hot = jnp.concatenate(hot, axis=1)
        earlier = jnp.dot(hot.astype(jnp.bfloat16), before, preferred_element_type=jnp.float32)
        blocks = jnp.floor((jnp.sum(hot, axis=1, keepdims=True) + (BLOCK - 1)) * (1.0 / BLOCK))
        run = jnp.zeros((1, 1), jnp.float32)
        pos = jnp.zeros((1, units), jnp.float32)
        owner = jnp.zeros((1, n_pos), jnp.float32)
        for s in range(n_src):
            pos = pos + hot[s:s + 1, :] * (earlier[s:s + 1, :] + run * BLOCK)
            run = run + blocks[s:s + 1, :]
            owner = owner + jnp.where(place_i.astype(jnp.float32) >= run, 1.0, 0.0)
        stack = [jnp.where(valid[j], pos[:, j * tiles:(j + 1) * tiles], -1.0) for j in range(per)]
        stack += [w.astype(jnp.float32) - trash for w in words]
        stack += [jnp.zeros((1, tiles), jnp.float32)] * (-len(stack) % 8)
        cols = jnp.concatenate(stack, axis=0).T
        found = jnp.zeros((tiles, n_pos), jnp.float32)
        for j in range(per):
            found = found + jnp.where(cols[:, j:j + 1] == pos_i, cols[:, per + j:per + j + 1], 0.0)
        word = jnp.sum(found, axis=0, keepdims=True) + trash
        owner = jnp.where(place_i == n_pos - 1, run, jnp.minimum(owner, n_src - 1.0))
        tables[c][0:1, :] = word.astype(jnp.int32)
        tables[c][1:2, :] = owner.astype(jnp.int32)

    for c in copies[3:]:
        c.wait()


def plan(chunks, per, n, radix, ids, src, rows, dst, tw, xo, wo, so):
    tiles, _, _, tile = tw.shape
    n_src = xo.shape[0] // tile
    blocks = -(-(per * tiles // BLOCK + n_src) // STEP) * STEP
    n_pos = -(-(blocks * BLOCK + 1) // 128) * 128
    smem = pl.BlockSpec(memory_space=pltpu.SMEM)
    vmem = pl.BlockSpec(memory_space=pltpu.VMEM)
    hbm = pl.BlockSpec(memory_space=pltpu.HBM)
    half = chunks * per
    return pl.pallas_call(
        functools.partial(plan_kernel, chunks, per, n, radix, n_src),
        out_shape=[jax.ShapeDtypeStruct((2, n_pos), jnp.int32)] * chunks
        + [jax.ShapeDtypeStruct((per * tiles, UNIT, tile), tw.dtype)] * chunks
        + [
            jax.ShapeDtypeStruct(xo.shape, xo.dtype),
            jax.ShapeDtypeStruct(wo.shape, wo.dtype),
            jax.ShapeDtypeStruct(so.shape, so.dtype),
        ],
        in_specs=[smem] + [hbm] * 7,
        out_specs=[vmem] * (2 * chunks + 3),
        scratch_shapes=[
            pltpu.VMEM((1, tiles), jnp.int32),
            pltpu.VMEM((1, tiles), jnp.int32),
            pltpu.VMEM((1, tiles), jnp.int32),
            pltpu.SemaphoreType.DMA((3 + half + 3,)),
        ],
        compiler_params=pltpu.CompilerParams(vmem_limit_bytes=32 * 1024 * 1024),
        name="plan",
    )(ids, *[
        pltpu.with_memory_space_constraint(a, pltpu.HBM)
        for a in (src.reshape(1, tiles), rows.reshape(1, tiles), dst.reshape(1, tiles), tw, xo, wo, so)
    ])


def select_kernel(groups, ids, lists, counts, adj, sel, front, adj_out):
    core, me = ids[0], ids[1]
    n = lists.shape[0]
    slots = lists.shape[1]
    total = n * slots
    q_n = lax.broadcasted_iota(jnp.int32, (total, n), 0)
    r_n = lax.broadcasted_iota(jnp.int32, (total, n), 1)
    mine = lists[me].astype(jnp.float32)
    cnt = counts[pl.ds(me, 1), :]
    picked = jnp.zeros((total, n), jnp.float32)
    k_n = jnp.bitwise_and(q_n, slots - 1)
    for k in range(slots):
        picked = jnp.where(k_n == k, mine[k:k + 1, :], picked)
    good = jnp.logical_and(n - 1 - lax.div(q_n, slots) == r_n, k_n < cnt)
    row = jnp.sum(jnp.where(good, picked + 1.0, 0.0), axis=1, keepdims=True) - 1.0
    lane = lax.broadcasted_iota(jnp.int32, (1, sel.shape[1]), 1)
    name = jnp.zeros(lane.shape, jnp.int32)
    names = [group_of(c, i, groups) for c in (core, 1 - core) for i in range(groups // 2)]
    for i, g in enumerate(names):
        name = jnp.where(lax.div(lane, UNIT) == i, g * UNIT + jnp.bitwise_and(lane, UNIT - 1), name)
    sel[...] = jnp.where(row == name.astype(jnp.float32), 1.0, 0.0).astype(jnp.bfloat16)
    tile, out_rows = groups * UNIT, adj.shape[0]
    placed = jnp.where(lax.broadcasted_iota(jnp.int32, (tile, tile), 0) == name, 1.0, 0.0).astype(jnp.bfloat16)
    front[:out_rows, :] = jnp.dot(adj[:, :tile], placed, preferred_element_type=jnp.float32).astype(jnp.bfloat16)
    front[out_rows:, :] = placed[:out_rows, :]
    column = lax.broadcasted_iota(jnp.int32, (1, total), 1)
    source = (n - 1 - lax.div(column, slots)) * slots + lax.rem(column, slots)
    moved = jnp.where(lax.broadcasted_iota(jnp.int32, (total, total), 0) == source, 1.0, 0.0).astype(jnp.bfloat16)
    adj_out[...] = jnp.dot(adj[:, groups * UNIT:], moved, preferred_element_type=jnp.float32).astype(jnp.bfloat16)


def selection(groups, ids, send_list, send_count, adj):
    n, _, slots = send_list.shape
    smem = pl.BlockSpec(memory_space=pltpu.SMEM)
    vmem = pl.BlockSpec(memory_space=pltpu.VMEM)
    return pl.pallas_call(
        functools.partial(select_kernel, groups),
        out_shape=[
            jax.ShapeDtypeStruct((n * slots, groups * UNIT), jnp.bfloat16),
            jax.ShapeDtypeStruct((2 * adj.shape[0], groups * UNIT), jnp.bfloat16),
            jax.ShapeDtypeStruct((adj.shape[0], n * slots), jnp.bfloat16),
        ],
        in_specs=[smem, vmem, vmem, vmem],
        out_specs=[vmem] * 3,
        compiler_params=pltpu.CompilerParams(vmem_limit_bytes=32 * 1024 * 1024),
        name="selection",
    )(ids, jnp.swapaxes(send_list, 1, 2), send_count, adj)


def tiles_kernel(table_v, tbuf, xo, xp, *rest):
    parts = len(rest) - 3
    accs, (masks, table, sem) = rest[:parts], rest[parts:]
    tile = tbuf.shape[2]
    width = xo.shape[1]
    to_scalar = pltpu.make_async_copy(table_v, table, sem)
    to_scalar.start()
    for acc in accs:
        acc[...] = jnp.zeros_like(acc)
    row_i = lax.broadcasted_iota(jnp.int32, (UNIT, tile), 0)
    for m in range(UNIT + 1):
        masks[m] = jnp.where(row_i < m, 1.0, 0.0).astype(jnp.bfloat16)
    columns = [(x, h) for x in (xo, xp) for h in range(0, width, PART)]
    to_scalar.wait()

    def step(i, carry):
        for m in range(STEP):
            at = i * STEP + m
            base = pl.multiple_of(table[1, at] * tile, tile)
            rows, places = [], []
            for k in range(BLOCK):
                word = table[0, at * BLOCK + k]
                u = jnp.bitwise_and(lax.shift_right_logical(word, 5), 511)
                rows.append(tbuf[u] * masks[jnp.bitwise_and(word, 31)])
                places.append(pl.multiple_of(lax.shift_right_logical(word, 14) * UNIT, UNIT))
            lhs = jnp.concatenate(rows, axis=0)
            for acc, (x, h) in zip(accs, columns):
                got = jnp.dot(lhs, x[pl.ds(base, tile), h:h + PART], preferred_element_type=jnp.float32)
                got = got.astype(jnp.bfloat16).astype(jnp.float32)
                for k in range(BLOCK):
                    acc[pl.ds(places[k], UNIT), :] += got[k * UNIT:(k + 1) * UNIT, :]
        return carry

    steps = lax.div(table[1, table.shape[1] - 1] + STEP - 1, STEP)
    lax.fori_loop(0, steps, step, 0)


def gathered_sums(per, n, table, tbuf, xo, xp):
    width = xo.shape[1]
    tile = tbuf.shape[2]
    vmem = pl.BlockSpec(memory_space=pltpu.VMEM)
    flops = 2 * tbuf.shape[0] * UNIT * tile * 2 * width
    parts = 2 * width // PART
    sums = jax.ShapeDtypeStruct(((n * per + 1) * UNIT, PART), jnp.float32)
    return pl.pallas_call(
        tiles_kernel,
        out_shape=[sums] * parts,
        in_specs=[vmem] * 4,
        out_specs=[vmem] * parts,
        scratch_shapes=[
            pltpu.VMEM((UNIT + 1, UNIT, tile), jnp.bfloat16),
            pltpu.SMEM(table.shape, jnp.int32),
            pltpu.SemaphoreType.DMA,
        ],
        compiler_params=pltpu.CompilerParams(vmem_limit_bytes=(12 << 20) + sums.size * 4 * parts),
        cost_estimate=pl.CostEstimate(flops=flops, bytes_accessed=8 << 20, transcendentals=0),
        name="gathered_sums",
    )(table, tbuf, xo, xp)


def weigh(accs, weights, first, count, out):
    size = min(256, count)

    def piece(r, carry):
        at = pl.multiple_of(r * size, size)
        got = jnp.zeros((size, out.shape[1]), jnp.float32)
        for i, acc in enumerate(accs):
            w, h = weights[i * PART // weights[0].shape[0]], i * PART % weights[0].shape[0]
            value = acc[pl.ds(first + at, size), :]
            high = value.astype(jnp.bfloat16)
            low = (value - high.astype(jnp.float32)).astype(jnp.bfloat16)
            both = jnp.dot(jnp.concatenate([high, low], axis=0), w[h:h + PART, :], preferred_element_type=jnp.float32)
            got = got + (both[:size, :] + both[size:, :])
        out[pl.ds(at, size), :] = got
        return carry

    lax.fori_loop(0, count // size, piece, 0)


def sent_kernel(k, slots, rows, parts, wo, wp, *refs):
    accs, (out, sums, tail) = refs[:parts], refs[parts:]
    weigh(accs, (wo, wp), k * slots * rows, slots * rows, sums)
    write_coded(out, tail, slots, rows, lambda s: sums[s * rows:(s + 1) * rows, :])


def sent_terms(k, slots, rows, accs, wo, wp):
    hidden = wo.shape[1]
    vmem = pl.BlockSpec(memory_space=pltpu.VMEM)
    return pl.pallas_call(
        functools.partial(sent_kernel, k, slots, rows, len(accs)),
        out_shape=jax.ShapeDtypeStruct((slots * rows + tail_rows(slots), hidden), jnp.int16),
        in_specs=[vmem] * (2 + len(accs)),
        out_specs=vmem,
        scratch_shapes=[
            pltpu.VMEM((slots * rows, hidden), jnp.float32),
            pltpu.VMEM((tail_rows(slots), hidden), jnp.float32),
        ],
        compiler_params=pltpu.CompilerParams(vmem_limit_bytes=(12 << 20) + accs[0].size * 4 * len(accs)),
        cost_estimate=pl.CostEstimate(
            flops=4 * slots * rows * PART * len(accs) * hidden, bytes_accessed=2 << 20, transcendentals=0),
        name="sent_terms",
    )(wo, wp, *accs)


def own_kernel(chunk, per, groups, parts, ids, wo, wp, xo, so, *refs):
    accs, (out, theirs, terms) = refs[:parts], refs[parts:]
    weigh(accs, (wo, wp), 0, out.shape[0], out)
    terms[...] = jnp.dot(xo[:groups * UNIT, :], so[...], preferred_element_type=jnp.float32)
    for j in range(per):
        here = slice(j * UNIT, (j + 1) * UNIT)
        at = pl.multiple_of(group_of(ids[0], chunk * per + j, groups) * UNIT, UNIT)
        out[here, :] += terms[pl.ds(at, UNIT), :]
        at = pl.multiple_of(group_of(1 - ids[0], chunk * per + j, groups) * UNIT, UNIT)
        theirs[here, :] = terms[pl.ds(at, UNIT), :]


def own_terms(chunk, per, groups, slots, ids, accs, wo, wp, xo, so):
    hidden = wo.shape[1]
    rows = per * UNIT
    smem = pl.BlockSpec(memory_space=pltpu.SMEM)
    vmem = pl.BlockSpec(memory_space=pltpu.VMEM)
    return pl.pallas_call(
        functools.partial(own_kernel, chunk, per, groups, len(accs)),
        out_shape=[
            jax.ShapeDtypeStruct((slots * rows, hidden), jnp.float32),
            jax.ShapeDtypeStruct((rows, hidden), jnp.float32),
        ],
        in_specs=[smem] + [vmem] * (4 + len(accs)),
        out_specs=[vmem] * 2,
        scratch_shapes=[pltpu.VMEM((groups * UNIT, hidden), jnp.float32)],
        compiler_params=pltpu.CompilerParams(vmem_limit_bytes=(12 << 20) + accs[0].size * 4 * len(accs)),
        cost_estimate=pl.CostEstimate(
            flops=4 * slots * rows * PART * len(accs) * hidden, bytes_accessed=2 << 20, transcendentals=0),
        name="own_terms",
    )(ids, wo, wp, xo, so, *accs)


def combine_kernel(slots, rows, ways, own, *refs):
    parts = len(refs) - ways - 1
    coded, outs, tail = refs[:parts], refs[parts:parts + ways], refs[parts + ways]
    values = [read_coded(a, slots, rows) for a in coded]

    def total(s):
        got = own[s * rows:(s + 1) * rows, :]
        for value in values:
            got = got + value(s)
        return got

    for i in range(slots // ways):
        outs[0][i * rows:(i + 1) * rows, :] = total(i * ways)
    for k in range(1, ways):
        write_coded(outs[k], tail, slots // ways, rows, lambda s: total(s * ways + k))


def combine(slots, rows, ways, own, coded):
    width = own.shape[1]
    left = slots // ways
    vmem = pl.BlockSpec(memory_space=pltpu.VMEM)
    out = jax.ShapeDtypeStruct((left * rows + tail_rows(left), width), jnp.int16)
    return pl.pallas_call(
        functools.partial(combine_kernel, slots, rows, ways),
        out_shape=[jax.ShapeDtypeStruct((left * rows, width), jnp.float32)] + [out] * (ways - 1),
        in_specs=[vmem] * (1 + len(coded)),
        out_specs=[vmem] * ways,
        scratch_shapes=[pltpu.VMEM((tail_rows(left), width), jnp.float32)],
        compiler_params=pltpu.CompilerParams(vmem_limit_bytes=32 * 1024 * 1024),
        name="combine",
    )(own, *coded)


def hidden_kernel(chunks, parts, rows, *refs):
    out = refs[chunks * parts + 1]
    for c in range(chunks):
        own, self, coded = refs[c * parts], refs[c * parts + 1], refs[c * parts + 2:(c + 1) * parts]
        total = own[:rows, :] + self[...]
        for a in coded:
            total = total + read_coded(a, 1, rows)(0)
        out[c * rows:(c + 1) * rows, :] = jnp.maximum(total, 0.0).astype(jnp.bfloat16)


def hidden_rows(chunk_parts, rows, sel):
    chunks, parts = len(chunk_parts), len(chunk_parts[0])
    width = chunk_parts[0][0].shape[1]
    vmem = pl.BlockSpec(memory_space=pltpu.VMEM)
    flat = [a for part in chunk_parts for a in part]
    return pl.pallas_call(
        functools.partial(hidden_kernel, chunks, parts, rows),
        out_shape=jax.ShapeDtypeStruct((chunks * rows, width), jnp.bfloat16),
        in_specs=[vmem] * (len(flat) + 1),
        out_specs=vmem,
        compiler_params=pltpu.CompilerParams(vmem_limit_bytes=32 * 1024 * 1024),
        name="hidden_rows",
    )(*flat, sel)


def send_kernel(own, other, sel, send):
    both = jnp.concatenate([own[...], other[...]], axis=0)
    send[...] = jnp.dot(sel[...], both, preferred_element_type=jnp.float32).astype(jnp.bfloat16)


def rows_to_send(own, other, sel):
    vmem = pl.BlockSpec(memory_space=pltpu.VMEM)
    return pl.pallas_call(
        send_kernel,
        out_shape=jax.ShapeDtypeStruct((sel.shape[0], own.shape[1]), jnp.bfloat16),
        in_specs=[vmem] * 3,
        out_specs=vmem,
        compiler_params=pltpu.CompilerParams(vmem_limit_bytes=32 * 1024 * 1024),
        name="rows_to_send",
    )(own, other, sel)


def logits_kernel(own, other, received, front, adj_received, w_self, w_neigh, out):
    rows = out.shape[0]
    both = jnp.concatenate([own[...], other[...]], axis=0)
    local = jnp.dot(front[...], both, preferred_element_type=jnp.float32)
    mean = local[:rows, :] + jnp.dot(adj_received[...], received[...], preferred_element_type=jnp.float32)
    dims = (((1,), (1,)), ((), ()))
    got = lax.dot_general(local[rows:, :].astype(jnp.bfloat16), w_self[...], dims, preferred_element_type=jnp.float32)
    got = got + lax.dot_general(mean.astype(jnp.bfloat16), w_neigh[...], dims, preferred_element_type=jnp.float32)
    out[...] = got


def logits_of(own, other, received, front, adj_received, w_self, w_neigh):
    vmem = pl.BlockSpec(memory_space=pltpu.VMEM)
    return pl.pallas_call(
        logits_kernel,
        out_shape=jax.ShapeDtypeStruct((adj_received.shape[0], w_self.shape[1]), jnp.float32),
        in_specs=[vmem] * 7,
        out_specs=vmem,
        compiler_params=pltpu.CompilerParams(vmem_limit_bytes=32 * 1024 * 1024),
        name="logits",
    )(own, other, received, front, adj_received, w_self.T, w_neigh.T)


def exchange(parts, stride, n, places):
    got = [parts[0]]
    for k in places:
        got.append(lax.ppermute(parts[k], "dom", [(i, i ^ (k * stride)) for i in range(n)]))
    return got


def body(
    features,
    tile_weight,
    tile_dst,
    tile_src,
    tile_rows,
    w_self1,
    neighbour_weight_first,
    send_list,
    send_count,
    adj_two,
    w_self2,
    w_neigh2,
):
    n = lax.axis_size("dom")
    tile = tile_weight.shape[1]
    groups = tile // UNIT
    per = groups // 2 // CHUNKS
    bits = n.bit_length() - 1
    assert n == 1 << bits and bits >= 2
    radices = [2] * (bits // 2) + [1] * (bits % 2)
    ids = jnp.stack([lax.axis_index("feat"), lax.axis_index("dom")]).astype(jnp.int32)
    swap = [(0, 1), (1, 0)]
    xp = lax.ppermute(features, "feat", swap)
    wp = lax.ppermute(neighbour_weight_first, "feat", swap)
    tw = tile_weight.reshape(tile_weight.shape[0], groups, UNIT, tile)
    planned = plan(
        CHUNKS, per, n, 4, ids, tile_src, tile_rows, tile_dst, tw, features, neighbour_weight_first, w_self1,
    )
    tables, tbufs, (xo, wo, so) = planned[:CHUNKS], planned[CHUNKS:2 * CHUNKS], planned[2 * CHUNKS:]
    done = []
    for chunk in range(CHUNKS):
        accs = gathered_sums(per, n, tables[chunk], tbufs[chunk], xo, xp)
        slots, rows = n // 4, per * UNIT
        parts = {k: sent_terms(k, slots, rows, accs, wo, wp) for k in (1, 2, 3)}
        parts[0], theirs = own_terms(chunk, per, groups, slots, ids, accs, wo, wp, xo, so)
        self = lax.ppermute(theirs, "feat", swap)
        got = exchange(parts, 1, n, (1, 2, 3))
        stride = 4
        for radix in radices[1:]:
            ways = 1 << radix
            parts = combine(n // stride, per * UNIT, ways, got[0], got[1:])
            got = exchange(parts, stride, n, (2, 3, 1) if ways == 4 else (1,))
            stride *= ways
        done.append([got[0], self] + got[1:])
    sel, front, adj_received = selection(groups, ids, send_list, send_count, adj_two)
    own = hidden_rows(done, per * UNIT, sel)
    other = lax.ppermute(own, "feat", swap)
    send = rows_to_send(own, other, sel)
    received = lax.all_to_all(send, "dom", 0, 0, axis_index_groups=[group_order(n)], tiled=True)
    return logits_of(own, other, received, front, adj_received, w_self2, w_neigh2)


def solution(mesh):
    in_specs = (
        P("dom", "feat"),
        P("dom", None, None),
        P("dom"),
        P("dom"),
        P("dom"),
        P("feat", None),
        P("feat", None),
        P(),
        P(),
        P("dom", None),
        P(),
        P(),
    )
    out_specs = P("dom", None)
    return jax.shard_map(body, mesh=mesh, in_specs=in_specs, out_specs=out_specs, check_vma=False)
```

```python
import functools

import jax
import jax.numpy as jnp
from jax import lax
from jax.experimental import pallas as pl
from jax.experimental.pallas import tpu as pltpu
from jax.sharding import PartitionSpec as P

UNIT = 16
BLOCK = 8
STEP = 8
PART = 256
CHUNKS = 1


def group_of(core, place, groups):
    pair = 2 * (place // 2) + core
    return pair if place % 2 == 0 else groups - 1 - pair


def group_order(n):
    return list(range(n - 1, -1, -1))


LN2 = 0.6931471805599453


def rounded(x):
    spread = x * 65537.0
    return spread - (spread - x)


def tail_rows(slots):
    return -(-slots // 8) * 8


def encode(x):
    top = jnp.max(jnp.abs(x), axis=0, keepdims=True)
    power = jnp.ceil(jnp.log(jnp.maximum(top, 1e-30)) * (1.0 / LN2) + 1e-3) - 15.0
    return jnp.floor(x * jnp.exp(power * -LN2) + 0.5), power


def to_int16(x):
    return x.astype(jnp.int32).astype(jnp.int16)


def write_coded(out, tail, slots, rows, value_of):
    tail[...] = jnp.zeros_like(tail)
    for s in range(slots):
        whole, power = encode(value_of(s))
        out[s * rows:(s + 1) * rows, :] = to_int16(whole)
        tail[s:s + 1, :] = power
    out[slots * rows:, :] = to_int16(tail[...])


def read_coded(ref, slots, rows):
    powers = ref[slots * rows:, :].astype(jnp.int32).astype(jnp.float32)

    def value_of(s):
        whole = ref[s * rows:(s + 1) * rows, :].astype(jnp.int32).astype(jnp.float32)
        return whole * jnp.exp(powers[s:s + 1, :] * LN2)

    return value_of


def plan_kernel(chunks, per, n, radix, n_src, ids, src_h, rows_h, dst_h, tw, xo, wo, so, *rest):
    tables, rest = rest[:chunks], rest[chunks:]
    tbufs, rest = rest[:chunks], rest[chunks:]
    xo_out, wo_out, so_out = rest[:3]
    src_v, rows_v, dst_v, sems = rest[3:]
    core, me = ids[0], ids[1]
    tiles = src_v.shape[1]
    n_pos = tables[0].shape[1]
    units = per * tiles
    groups = 2 * per * chunks
    half = groups // 2
    gs = [group_of(core, i, groups) for i in range(half)]
    small = [(src_h, src_v), (rows_h, rows_v), (dst_h, dst_v)]
    large = [(tw.at[:, g], tbufs[i // per].at[pl.ds(i % per * tiles, tiles)]) for i, g in enumerate(gs)]
    large += [(xo, xo_out), (wo, wo_out), (so, so_out)]
    copies = [pltpu.make_async_copy(a, b, sems.at[i]) for i, (a, b) in enumerate(small + large)]
    for c in copies:
        c.start()
    lane = lax.broadcasted_iota(jnp.int32, (1, tiles), 1)
    block_i = lax.broadcasted_iota(jnp.int32, (n_src, tiles), 0)
    before = lax.broadcasted_iota(jnp.int32, (units, units), 0) < lax.broadcasted_iota(jnp.int32, (units, units), 1)
    before = jnp.where(before, 1.0, 0.0).astype(jnp.bfloat16)
    pos_i = lax.broadcasted_iota(jnp.int32, (tiles, n_pos), 1).astype(jnp.float32)
    place_i = lax.broadcasted_iota(jnp.int32, (1, n_pos), 1)
    trash = float(n * per << 14)
    for c in copies[:3]:
        c.wait()
    src, rows = src_v[...], rows_v[...]
    slot = jnp.bitwise_xor(dst_v[...], me)
    slot = jnp.bitwise_and(slot, radix - 1) * (n // radix) + lax.div(slot, radix)
    for c in range(chunks):
        hot, words, valid = [], [], []
        for j in range(per):
            limit = jnp.clip(rows - UNIT * gs[c * per + j], 0, UNIT)
            ok = limit > 0
            valid.append(ok)
            words.append(((slot * per + j) * 512 + (j * tiles + lane)) * 32 + limit)
            hot.append(jnp.where(jnp.logical_and(block_i == src, ok), 1.0, 0.0))
        hot = jnp.concatenate(hot, axis=1)
        earlier = jnp.dot(hot.astype(jnp.bfloat16), before, preferred_element_type=jnp.float32)
        blocks = jnp.floor((jnp.sum(hot, axis=1, keepdims=True) + (BLOCK - 1)) * (1.0 / BLOCK))
        run = jnp.zeros((1, 1), jnp.float32)
        pos = jnp.zeros((1, units), jnp.float32)
        owner = jnp.zeros((1, n_pos), jnp.float32)
        for s in range(n_src):
            pos = pos + hot[s:s + 1, :] * (earlier[s:s + 1, :] + run * BLOCK)
            run = run + blocks[s:s + 1, :]
            owner = owner + jnp.where(place_i.astype(jnp.float32) >= run, 1.0, 0.0)
        stack = [jnp.where(valid[j], pos[:, j * tiles:(j + 1) * tiles], -1.0) for j in range(per)]
        stack += [w.astype(jnp.float32) - trash for w in words]
        stack += [jnp.zeros((1, tiles), jnp.float32)] * (-len(stack) % 8)
        cols = jnp.concatenate(stack, axis=0).T
        found = jnp.zeros((tiles, n_pos), jnp.float32)
        for j in range(per):
            found = found + jnp.where(cols[:, j:j + 1] == pos_i, cols[:, per + j:per + j + 1], 0.0)
        word = jnp.sum(found, axis=0, keepdims=True) + trash
        owner = jnp.where(place_i == n_pos - 1, run, jnp.minimum(owner, n_src - 1.0))
        tables[c][0:1, :] = word.astype(jnp.int32)
        tables[c][1:2, :] = owner.astype(jnp.int32)

    for c in copies[3:]:
        c.wait()


def plan(chunks, per, n, radix, ids, src, rows, dst, tw, xo, wo, so):
    tiles, _, _, tile = tw.shape
    n_src = xo.shape[0] // tile
    blocks = -(-(per * tiles // BLOCK + n_src) // STEP) * STEP
    n_pos = -(-(blocks * BLOCK + 1) // 128) * 128
    smem = pl.BlockSpec(memory_space=pltpu.SMEM)
    vmem = pl.BlockSpec(memory_space=pltpu.VMEM)
    hbm = pl.BlockSpec(memory_space=pltpu.HBM)
    half = chunks * per
    return pl.pallas_call(
        functools.partial(plan_kernel, chunks, per, n, radix, n_src),
        out_shape=[jax.ShapeDtypeStruct((2, n_pos), jnp.int32)] * chunks
        + [jax.ShapeDtypeStruct((per * tiles, UNIT, tile), tw.dtype)] * chunks
        + [
            jax.ShapeDtypeStruct(xo.shape, xo.dtype),
            jax.ShapeDtypeStruct(wo.shape, wo.dtype),
            jax.ShapeDtypeStruct(so.shape, so.dtype),
        ],
        in_specs=[smem] + [hbm] * 7,
        out_specs=[vmem] * (2 * chunks + 3),
        scratch_shapes=[
            pltpu.VMEM((1, tiles), jnp.int32),
            pltpu.VMEM((1, tiles), jnp.int32),
            pltpu.VMEM((1, tiles), jnp.int32),
            pltpu.SemaphoreType.DMA((3 + half + 3,)),
        ],
        compiler_params=pltpu.CompilerParams(vmem_limit_bytes=32 * 1024 * 1024),
        name="plan",
    )(ids, *[
        pltpu.with_memory_space_constraint(a, pltpu.HBM)
        for a in (src.reshape(1, tiles), rows.reshape(1, tiles), dst.reshape(1, tiles), tw, xo, wo, so)
    ])


def select_kernel(groups, ids, lists, counts, adj, sel, front, adj_out):
    core, me = ids[0], ids[1]
    n = lists.shape[0]
    slots = lists.shape[1]
    total = n * slots
    q_n = lax.broadcasted_iota(jnp.int32, (total, n), 0)
    r_n = lax.broadcasted_iota(jnp.int32, (total, n), 1)
    mine = lists[me].astype(jnp.float32)
    cnt = counts[pl.ds(me, 1), :]
    picked = jnp.zeros((total, n), jnp.float32)
    k_n = jnp.bitwise_and(q_n, slots - 1)
    for k in range(slots):
        picked = jnp.where(k_n == k, mine[k:k + 1, :], picked)
    good = jnp.logical_and(n - 1 - lax.div(q_n, slots) == r_n, k_n < cnt)
    row = jnp.sum(jnp.where(good, picked + 1.0, 0.0), axis=1, keepdims=True) - 1.0
    lane = lax.broadcasted_iota(jnp.int32, (1, sel.shape[1]), 1)
    name = jnp.zeros(lane.shape, jnp.int32)
    names = [group_of(c, i, groups) for c in (core, 1 - core) for i in range(groups // 2)]
    for i, g in enumerate(names):
        name = jnp.where(lax.div(lane, UNIT) == i, g * UNIT + jnp.bitwise_and(lane, UNIT - 1), name)
    sel[...] = jnp.where(row == name.astype(jnp.float32), 1.0, 0.0).astype(jnp.bfloat16)
    tile, out_rows = groups * UNIT, adj.shape[0]
    placed = jnp.where(lax.broadcasted_iota(jnp.int32, (tile, tile), 0) == name, 1.0, 0.0).astype(jnp.bfloat16)
    front[:out_rows, :] = jnp.dot(adj[:, :tile], placed, preferred_element_type=jnp.float32).astype(jnp.bfloat16)
    front[out_rows:, :] = placed[:out_rows, :]
    column = lax.broadcasted_iota(jnp.int32, (1, total), 1)
    source = (n - 1 - lax.div(column, slots)) * slots + lax.rem(column, slots)
    moved = jnp.where(lax.broadcasted_iota(jnp.int32, (total, total), 0) == source, 1.0, 0.0).astype(jnp.bfloat16)
    adj_out[...] = jnp.dot(adj[:, groups * UNIT:], moved, preferred_element_type=jnp.float32).astype(jnp.bfloat16)


def selection(groups, ids, send_list, send_count, adj):
    n, _, slots = send_list.shape
    smem = pl.BlockSpec(memory_space=pltpu.SMEM)
    vmem = pl.BlockSpec(memory_space=pltpu.VMEM)
    return pl.pallas_call(
        functools.partial(select_kernel, groups),
        out_shape=[
            jax.ShapeDtypeStruct((n * slots, groups * UNIT), jnp.bfloat16),
            jax.ShapeDtypeStruct((2 * adj.shape[0], groups * UNIT), jnp.bfloat16),
            jax.ShapeDtypeStruct((adj.shape[0], n * slots), jnp.bfloat16),
        ],
        in_specs=[smem, vmem, vmem, vmem],
        out_specs=[vmem] * 3,
        compiler_params=pltpu.CompilerParams(vmem_limit_bytes=32 * 1024 * 1024),
        name="selection",
    )(ids, jnp.swapaxes(send_list, 1, 2), send_count, adj)


def tiles_kernel(table_v, tbuf, xo, xp, *rest):
    parts = len(rest) - 3
    accs, (masks, table, sem) = rest[:parts], rest[parts:]
    tile = tbuf.shape[2]
    width = xo.shape[1]
    to_scalar = pltpu.make_async_copy(table_v, table, sem)
    to_scalar.start()
    for acc in accs:
        acc[...] = jnp.zeros_like(acc)
    row_i = lax.broadcasted_iota(jnp.int32, (UNIT, tile), 0)
    for m in range(UNIT + 1):
        masks[m] = jnp.where(row_i < m, 1.0, 0.0).astype(jnp.bfloat16)
    columns = [(x, h) for x in (xo, xp) for h in range(0, width, PART)]
    to_scalar.wait()

    def step(i, carry):
        for m in range(STEP):
            b = i * STEP + m
            base = pl.multiple_of(table[1, b] * tile, tile)
            rows, places = [], []
            for k in range(BLOCK):
                word = table[0, b * BLOCK + k]
                u = jnp.bitwise_and(lax.shift_right_logical(word, 5), 511)
                rows.append(tbuf[u] * masks[jnp.bitwise_and(word, 31)])
                places.append(pl.multiple_of(lax.shift_right_logical(word, 14) * UNIT, UNIT))
            lhs = jnp.concatenate(rows, axis=0)
            for acc, (x, h) in zip(accs, columns):
                got = jnp.dot(lhs, x[pl.ds(base, tile), h:h + PART], preferred_element_type=jnp.float32)
                got = rounded(got)
                for k in range(BLOCK):
                    acc[pl.ds(places[k], UNIT), :] += got[k * UNIT:(k + 1) * UNIT, :]
        return carry

    steps = lax.div(table[1, table.shape[1] - 1] + STEP - 1, STEP)
    lax.fori_loop(0, steps, step, 0)


def gathered_sums(per, n, table, tbuf, xo, xp):
    width = xo.shape[1]
    tile = tbuf.shape[2]
    vmem = pl.BlockSpec(memory_space=pltpu.VMEM)
    flops = 2 * tbuf.shape[0] * UNIT * tile * 2 * width
    parts = 2 * width // PART
    sums = jax.ShapeDtypeStruct(((n * per + 1) * UNIT, PART), jnp.float32)
    return pl.pallas_call(
        tiles_kernel,
        out_shape=[sums] * parts,
        in_specs=[vmem] * 4,
        out_specs=[vmem] * parts,
        scratch_shapes=[
            pltpu.VMEM((UNIT + 1, UNIT, tile), jnp.bfloat16),
            pltpu.SMEM(table.shape, jnp.int32),
            pltpu.SemaphoreType.DMA,
        ],
        compiler_params=pltpu.CompilerParams(vmem_limit_bytes=(12 << 20) + sums.size * 4 * parts),
        cost_estimate=pl.CostEstimate(flops=flops, bytes_accessed=8 << 20, transcendentals=0),
        name="gathered_sums",
    )(table, tbuf, xo, xp)


def weigh(accs, weights, first, count, out):
    size = min(256, count)

    def piece(r, carry):
        at = pl.multiple_of(r * size, size)
        got = jnp.zeros((size, out.shape[1]), jnp.float32)
        for i, acc in enumerate(accs):
            w, h = weights[i * PART // weights[0].shape[0]], i * PART % weights[0].shape[0]
            value = acc[pl.ds(first + at, size), :]
            high = rounded(value)
            both = jnp.concatenate([high.astype(jnp.bfloat16), (value - high).astype(jnp.bfloat16)], axis=0)
            both = jnp.dot(both, w[h:h + PART, :], preferred_element_type=jnp.float32)
            got = got + (both[:size, :] + both[size:, :])
        out[pl.ds(at, size), :] = got
        return carry

    lax.fori_loop(0, count // size, piece, 0)


def sent_kernel(k, slots, rows, parts, wo, wp, *refs):
    accs, (out, sums, tail) = refs[:parts], refs[parts:]
    weigh(accs, (wo, wp), k * slots * rows, slots * rows, sums)
    write_coded(out, tail, slots, rows, lambda s: sums[s * rows:(s + 1) * rows, :])


def sent_terms(k, slots, rows, accs, wo, wp):
    hidden = wo.shape[1]
    vmem = pl.BlockSpec(memory_space=pltpu.VMEM)
    return pl.pallas_call(
        functools.partial(sent_kernel, k, slots, rows, len(accs)),
        out_shape=jax.ShapeDtypeStruct((slots * rows + tail_rows(slots), hidden), jnp.int16),
        in_specs=[vmem] * (2 + len(accs)),
        out_specs=vmem,
        scratch_shapes=[
            pltpu.VMEM((slots * rows, hidden), jnp.float32),
            pltpu.VMEM((tail_rows(slots), hidden), jnp.float32),
        ],
        compiler_params=pltpu.CompilerParams(vmem_limit_bytes=(12 << 20) + accs[0].size * 4 * len(accs)),
        cost_estimate=pl.CostEstimate(
            flops=4 * slots * rows * PART * len(accs) * hidden, bytes_accessed=2 << 20, transcendentals=0),
        name="sent_terms",
    )(wo, wp, *accs)


def own_kernel(chunk, per, groups, parts, ids, wo, wp, xo, so, *refs):
    accs, (out, theirs, terms) = refs[:parts], refs[parts:]
    weigh(accs, (wo, wp), 0, out.shape[0], out)
    terms[...] = jnp.dot(xo[:groups * UNIT, :], so[...], preferred_element_type=jnp.float32)
    for j in range(per):
        here = slice(j * UNIT, (j + 1) * UNIT)
        at = pl.multiple_of(group_of(ids[0], chunk * per + j, groups) * UNIT, UNIT)
        out[here, :] += terms[pl.ds(at, UNIT), :]
        at = pl.multiple_of(group_of(1 - ids[0], chunk * per + j, groups) * UNIT, UNIT)
        theirs[here, :] = terms[pl.ds(at, UNIT), :]


def own_terms(chunk, per, groups, slots, ids, accs, wo, wp, xo, so):
    hidden = wo.shape[1]
    rows = per * UNIT
    smem = pl.BlockSpec(memory_space=pltpu.SMEM)
    vmem = pl.BlockSpec(memory_space=pltpu.VMEM)
    return pl.pallas_call(
        functools.partial(own_kernel, chunk, per, groups, len(accs)),
        out_shape=[
            jax.ShapeDtypeStruct((slots * rows, hidden), jnp.float32),
            jax.ShapeDtypeStruct((rows, hidden), jnp.float32),
        ],
        in_specs=[smem] + [vmem] * (4 + len(accs)),
        out_specs=[vmem] * 2,
        scratch_shapes=[pltpu.VMEM((groups * UNIT, hidden), jnp.float32)],
        compiler_params=pltpu.CompilerParams(vmem_limit_bytes=(12 << 20) + accs[0].size * 4 * len(accs)),
        cost_estimate=pl.CostEstimate(
            flops=4 * slots * rows * PART * len(accs) * hidden, bytes_accessed=2 << 20, transcendentals=0),
        name="own_terms",
    )(ids, wo, wp, xo, so, *accs)


def combine_kernel(slots, rows, ways, own, *refs):
    parts = len(refs) - ways - 1
    coded, outs, tail = refs[:parts], refs[parts:parts + ways], refs[parts + ways]
    values = [read_coded(a, slots, rows) for a in coded]

    def total(s):
        got = own[s * rows:(s + 1) * rows, :]
        for value in values:
            got = got + value(s)
        return got

    for i in range(slots // ways):
        outs[0][i * rows:(i + 1) * rows, :] = total(i * ways)
    for k in range(1, ways):
        write_coded(outs[k], tail, slots // ways, rows, lambda s: total(s * ways + k))


def combine(slots, rows, ways, own, coded):
    width = own.shape[1]
    left = slots // ways
    vmem = pl.BlockSpec(memory_space=pltpu.VMEM)
    out = jax.ShapeDtypeStruct((left * rows + tail_rows(left), width), jnp.int16)
    return pl.pallas_call(
        functools.partial(combine_kernel, slots, rows, ways),
        out_shape=[jax.ShapeDtypeStruct((left * rows, width), jnp.float32)] + [out] * (ways - 1),
        in_specs=[vmem] * (1 + len(coded)),
        out_specs=[vmem] * ways,
        scratch_shapes=[pltpu.VMEM((tail_rows(left), width), jnp.float32)],
        compiler_params=pltpu.CompilerParams(vmem_limit_bytes=32 * 1024 * 1024),
        name="combine",
    )(own, *coded)


def hidden_kernel(chunks, parts, rows, *refs):
    out = refs[chunks * parts + 1]
    for c in range(chunks):
        own, self, coded = refs[c * parts], refs[c * parts + 1], refs[c * parts + 2:(c + 1) * parts]
        total = own[:rows, :] + self[...]
        for a in coded:
            total = total + read_coded(a, 1, rows)(0)
        out[c * rows:(c + 1) * rows, :] = jnp.maximum(total, 0.0).astype(jnp.bfloat16)


def hidden_rows(chunk_parts, rows, sel):
    chunks, parts = len(chunk_parts), len(chunk_parts[0])
    width = chunk_parts[0][0].shape[1]
    vmem = pl.BlockSpec(memory_space=pltpu.VMEM)
    flat = [a for part in chunk_parts for a in part]
    return pl.pallas_call(
        functools.partial(hidden_kernel, chunks, parts, rows),
        out_shape=jax.ShapeDtypeStruct((chunks * rows, width), jnp.bfloat16),
        in_specs=[vmem] * (len(flat) + 1),
        out_specs=vmem,
        compiler_params=pltpu.CompilerParams(vmem_limit_bytes=32 * 1024 * 1024),
        name="hidden_rows",
    )(*flat, sel)


def send_kernel(own, other, sel, send):
    both = jnp.concatenate([own[...], other[...]], axis=0)
    send[...] = jnp.dot(sel[...], both, preferred_element_type=jnp.float32).astype(jnp.bfloat16)


def rows_to_send(own, other, sel):
    vmem = pl.BlockSpec(memory_space=pltpu.VMEM)
    return pl.pallas_call(
        send_kernel,
        out_shape=jax.ShapeDtypeStruct((sel.shape[0], own.shape[1]), jnp.bfloat16),
        in_specs=[vmem] * 3,
        out_specs=vmem,
        compiler_params=pltpu.CompilerParams(vmem_limit_bytes=32 * 1024 * 1024),
        name="rows_to_send",
    )(own, other, sel)


def logits_kernel(own, other, received, front, adj_received, w_self, w_neigh, out):
    rows = out.shape[0]
    both = jnp.concatenate([own[...], other[...]], axis=0)
    local = jnp.dot(front[...], both, preferred_element_type=jnp.float32)
    mean = local[:rows, :] + jnp.dot(adj_received[...], received[...], preferred_element_type=jnp.float32)
    dims = (((1,), (1,)), ((), ()))
    got = lax.dot_general(local[rows:, :].astype(jnp.bfloat16), w_self[...], dims, preferred_element_type=jnp.float32)
    got = got + lax.dot_general(mean.astype(jnp.bfloat16), w_neigh[...], dims, preferred_element_type=jnp.float32)
    out[...] = got


def logits_of(own, other, received, front, adj_received, w_self, w_neigh):
    vmem = pl.BlockSpec(memory_space=pltpu.VMEM)
    return pl.pallas_call(
        logits_kernel,
        out_shape=jax.ShapeDtypeStruct((adj_received.shape[0], w_self.shape[1]), jnp.float32),
        in_specs=[vmem] * 7,
        out_specs=vmem,
        compiler_params=pltpu.CompilerParams(vmem_limit_bytes=32 * 1024 * 1024),
        name="logits",
    )(own, other, received, front, adj_received, w_self.T, w_neigh.T)


def exchange(parts, stride, n, places):
    got = [parts[0]]
    for k in places:
        got.append(lax.ppermute(parts[k], "dom", [(i, i ^ (k * stride)) for i in range(n)]))
    return got


def body(
    features,
    tile_weight,
    tile_dst,
    tile_src,
    tile_rows,
    w_self1,
    neighbour_weight_first,
    send_list,
    send_count,
    adj_two,
    w_self2,
    w_neigh2,
):
    n = lax.axis_size("dom")
    tile = tile_weight.shape[1]
    groups = tile // UNIT
    per = groups // 2 // CHUNKS
    bits = n.bit_length() - 1
    assert n == 1 << bits and bits >= 2
    radices = [2] * (bits // 2) + [1] * (bits % 2)
    ids = jnp.stack([lax.axis_index("feat"), lax.axis_index("dom")]).astype(jnp.int32)
    swap = [(0, 1), (1, 0)]
    xp = lax.ppermute(features, "feat", swap)
    wp = lax.ppermute(neighbour_weight_first, "feat", swap)
    tw = tile_weight.reshape(tile_weight.shape[0], groups, UNIT, tile)
    planned = plan(
        CHUNKS, per, n, 4, ids, tile_src, tile_rows, tile_dst, tw, features, neighbour_weight_first, w_self1,
    )
    tables, tbufs, (xo, wo, so) = planned[:CHUNKS], planned[CHUNKS:2 * CHUNKS], planned[2 * CHUNKS:]
    done = []
    for chunk in range(CHUNKS):
        accs = gathered_sums(per, n, tables[chunk], tbufs[chunk], xo, xp)
        slots, rows = n // 4, per * UNIT
        parts = {k: sent_terms(k, slots, rows, accs, wo, wp) for k in (1, 2, 3)}
        parts[0], theirs = own_terms(chunk, per, groups, slots, ids, accs, wo, wp, xo, so)
        self = lax.ppermute(theirs, "feat", swap)
        got = exchange(parts, 1, n, (1, 2, 3))
        stride = 4
        for radix in radices[1:]:
            ways = 1 << radix
            parts = combine(n // stride, per * UNIT, ways, got[0], got[1:])
            got = exchange(parts, stride, n, (2, 3, 1) if ways == 4 else (1,))
            stride *= ways
        done.append([got[0], self] + got[1:])
    sel, front, adj_received = selection(groups, ids, send_list, send_count, adj_two)
    own = hidden_rows(done, per * UNIT, sel)
    other = lax.ppermute(own, "feat", swap)
    send = rows_to_send(own, other, sel)
    received = lax.all_to_all(send, "dom", 0, 0, axis_index_groups=[group_order(n)], tiled=True)
    return logits_of(own, other, received, front, adj_received, w_self2, w_neigh2)


def solution(mesh):
    in_specs = (
        P("dom", "feat"),
        P("dom", None, None),
        P("dom"),
        P("dom"),
        P("dom"),
        P("feat", None),
        P("feat", None),
        P(),
        P(),
        P("dom", None),
        P(),
        P(),
    )
    out_specs = P("dom", None)
    return jax.shard_map(body, mesh=mesh, in_specs=in_specs, out_specs=out_specs, check_vma=False)
```

```python
import functools

import jax
import jax.numpy as jnp
from jax import lax
from jax.experimental import pallas as pl
from jax.experimental.pallas import tpu as pltpu
from jax.sharding import PartitionSpec as P

UNIT = 16
BLOCK = 8
STEP = 4
PART = 256
CHUNKS = 1


def group_of(core, place, groups):
    pair = 2 * (place // 2) + core
    return pair if place % 2 == 0 else groups - 1 - pair


def group_order(n):
    return list(range(n - 1, -1, -1))


LN2 = 0.6931471805599453


def tail_rows(slots):
    return -(-slots // 8) * 8


def encode(x):
    top = jnp.max(jnp.abs(x), axis=0, keepdims=True)
    power = jnp.ceil(jnp.log(jnp.maximum(top, 1e-30)) * (1.0 / LN2) + 1e-3) - 15.0
    return jnp.floor(x * jnp.exp(power * -LN2) + 0.5), power


def to_int16(x):
    return x.astype(jnp.int32).astype(jnp.int16)


def write_coded(out, tail, slots, rows, value_of):
    tail[...] = jnp.zeros_like(tail)
    for s in range(slots):
        whole, power = encode(value_of(s))
        out[s * rows:(s + 1) * rows, :] = to_int16(whole)
        tail[s:s + 1, :] = power
    out[slots * rows:, :] = to_int16(tail[...])


def read_coded(ref, slots, rows):
    powers = ref[slots * rows:, :].astype(jnp.int32).astype(jnp.float32)

    def value_of(s):
        whole = ref[s * rows:(s + 1) * rows, :].astype(jnp.int32).astype(jnp.float32)
        return whole * jnp.exp(powers[s:s + 1, :] * LN2)

    return value_of


def plan_kernel(chunks, per, n, radix, n_src, ids, src_h, rows_h, dst_h, tw, xo, *rest):
    tables, rest = rest[:chunks], rest[chunks:]
    tbufs, rest = rest[:chunks], rest[chunks:]
    xo_out, src_v, rows_v, dst_v, sems = rest
    core, me = ids[0], ids[1]
    tiles = src_v.shape[1]
    n_pos = tables[0].shape[1]
    units = per * tiles
    groups = 2 * per * chunks
    half = groups // 2
    gs = [group_of(core, i, groups) for i in range(half)]
    small = [(src_h, src_v), (rows_h, rows_v), (dst_h, dst_v)]
    large = [(tw.at[:, g], tbufs[i // per].at[pl.ds(i % per * tiles, tiles)]) for i, g in enumerate(gs)]
    large += [(xo, xo_out)]
    copies = [pltpu.make_async_copy(a, b, sems.at[i]) for i, (a, b) in enumerate(small + large)]
    for c in copies:
        c.start()
    lane = lax.broadcasted_iota(jnp.int32, (1, tiles), 1)
    block_i = lax.broadcasted_iota(jnp.int32, (n_src, tiles), 0)
    before = lax.broadcasted_iota(jnp.int32, (units, units), 0) < lax.broadcasted_iota(jnp.int32, (units, units), 1)
    before = jnp.where(before, 1.0, 0.0).astype(jnp.bfloat16)
    pos_i = lax.broadcasted_iota(jnp.int32, (tiles, n_pos), 1).astype(jnp.float32)
    place_i = lax.broadcasted_iota(jnp.int32, (1, n_pos), 1)
    trash = float(n * per << 14)
    for c in copies[:3]:
        c.wait()
    src, rows = src_v[...], rows_v[...]
    slot = jnp.bitwise_xor(dst_v[...], me)
    slot = jnp.bitwise_and(slot, radix - 1) * (n // radix) + lax.div(slot, radix)
    for c in range(chunks):
        hot, words, valid = [], [], []
        for j in range(per):
            limit = jnp.clip(rows - UNIT * gs[c * per + j], 0, UNIT)
            ok = limit > 0
            valid.append(ok)
            words.append(((slot * per + j) * 512 + (j * tiles + lane)) * 32 + limit)
            hot.append(jnp.where(jnp.logical_and(block_i == src, ok), 1.0, 0.0))
        hot = jnp.concatenate(hot, axis=1)
        earlier = jnp.dot(hot.astype(jnp.bfloat16), before, preferred_element_type=jnp.float32)
        blocks = jnp.floor((jnp.sum(hot, axis=1, keepdims=True) + (BLOCK - 1)) * (1.0 / BLOCK))
        run = jnp.zeros((1, 1), jnp.float32)
        pos = jnp.zeros((1, units), jnp.float32)
        owner = jnp.zeros((1, n_pos), jnp.float32)
        for s in range(n_src):
            pos = pos + hot[s:s + 1, :] * (earlier[s:s + 1, :] + run * BLOCK)
            run = run + blocks[s:s + 1, :]
            owner = owner + jnp.where(place_i.astype(jnp.float32) >= run, 1.0, 0.0)
        stack = [jnp.where(valid[j], pos[:, j * tiles:(j + 1) * tiles], -1.0) for j in range(per)]
        stack += [w.astype(jnp.float32) - trash for w in words]
        stack += [jnp.zeros((1, tiles), jnp.float32)] * (-len(stack) % 8)
        cols = jnp.concatenate(stack, axis=0).T
        found = jnp.zeros((tiles, n_pos), jnp.float32)
        for j in range(per):
            found = found + jnp.where(cols[:, j:j + 1] == pos_i, cols[:, per + j:per + j + 1], 0.0)
        word = jnp.sum(found, axis=0, keepdims=True) + trash
        owner = jnp.where(place_i == n_pos - 1, run, jnp.minimum(owner, n_src - 1.0))
        tables[c][0:1, :] = word.astype(jnp.int32)
        tables[c][1:2, :] = owner.astype(jnp.int32)

    for c in copies[3:]:
        c.wait()


def plan(chunks, per, n, radix, ids, src, rows, dst, tw, xo):
    tiles, _, _, tile = tw.shape
    n_src = xo.shape[0] // tile
    blocks = -(-(per * tiles // BLOCK + n_src) // STEP) * STEP
    n_pos = -(-(blocks * BLOCK + 1) // 128) * 128
    smem = pl.BlockSpec(memory_space=pltpu.SMEM)
    vmem = pl.BlockSpec(memory_space=pltpu.VMEM)
    hbm = pl.BlockSpec(memory_space=pltpu.HBM)
    half = chunks * per
    return pl.pallas_call(
        functools.partial(plan_kernel, chunks, per, n, radix, n_src),
        out_shape=[jax.ShapeDtypeStruct((2, n_pos), jnp.int32)] * chunks
        + [jax.ShapeDtypeStruct((per * tiles, UNIT, tile), tw.dtype)] * chunks
        + [jax.ShapeDtypeStruct(xo.shape, xo.dtype)],
        in_specs=[smem] + [hbm] * 5,
        out_specs=[vmem] * (2 * chunks + 1),
        scratch_shapes=[
            pltpu.VMEM((1, tiles), jnp.int32),
            pltpu.VMEM((1, tiles), jnp.int32),
            pltpu.VMEM((1, tiles), jnp.int32),
            pltpu.SemaphoreType.DMA((3 + half + 1,)),
        ],
        compiler_params=pltpu.CompilerParams(vmem_limit_bytes=32 * 1024 * 1024),
        name="plan",
    )(ids, *[
        pltpu.with_memory_space_constraint(a, pltpu.HBM)
        for a in (src.reshape(1, tiles), rows.reshape(1, tiles), dst.reshape(1, tiles), tw, xo)
    ])


def select_kernel(groups, ids, lists, counts, adj, sel, front, adj_out):
    core, me = ids[0], ids[1]
    n = lists.shape[0]
    slots = lists.shape[1]
    total = n * slots
    q_n = lax.broadcasted_iota(jnp.int32, (total, n), 0)
    r_n = lax.broadcasted_iota(jnp.int32, (total, n), 1)
    mine = lists[me].astype(jnp.float32)
    cnt = counts[pl.ds(me, 1), :]
    picked = jnp.zeros((total, n), jnp.float32)
    k_n = jnp.bitwise_and(q_n, slots - 1)
    for k in range(slots):
        picked = jnp.where(k_n == k, mine[k:k + 1, :], picked)
    good = jnp.logical_and(n - 1 - lax.div(q_n, slots) == r_n, k_n < cnt)
    row = jnp.sum(jnp.where(good, picked + 1.0, 0.0), axis=1, keepdims=True) - 1.0
    lane = lax.broadcasted_iota(jnp.int32, (1, sel.shape[1]), 1)
    name = jnp.zeros(lane.shape, jnp.int32)
    names = [group_of(c, i, groups) for c in (core, 1 - core) for i in range(groups // 2)]
    for i, g in enumerate(names):
        name = jnp.where(lax.div(lane, UNIT) == i, g * UNIT + jnp.bitwise_and(lane, UNIT - 1), name)
    sel[...] = jnp.where(row == name.astype(jnp.float32), 1.0, 0.0).astype(jnp.bfloat16)
    tile, out_rows = groups * UNIT, adj.shape[0]
    placed = jnp.where(lax.broadcasted_iota(jnp.int32, (tile, tile), 0) == name, 1.0, 0.0).astype(jnp.bfloat16)
    front[:out_rows, :] = jnp.dot(adj[:, :tile], placed, preferred_element_type=jnp.float32).astype(jnp.bfloat16)
    front[out_rows:, :] = placed[:out_rows, :]
    column = lax.broadcasted_iota(jnp.int32, (1, total), 1)
    source = (n - 1 - lax.div(column, slots)) * slots + lax.rem(column, slots)
    moved = jnp.where(lax.broadcasted_iota(jnp.int32, (total, total), 0) == source, 1.0, 0.0).astype(jnp.bfloat16)
    adj_out[...] = jnp.dot(adj[:, groups * UNIT:], moved, preferred_element_type=jnp.float32).astype(jnp.bfloat16)


def selection(groups, ids, send_list, send_count, adj):
    n, _, slots = send_list.shape
    smem = pl.BlockSpec(memory_space=pltpu.SMEM)
    vmem = pl.BlockSpec(memory_space=pltpu.VMEM)
    return pl.pallas_call(
        functools.partial(select_kernel, groups),
        out_shape=[
            jax.ShapeDtypeStruct((n * slots, groups * UNIT), jnp.bfloat16),
            jax.ShapeDtypeStruct((2 * adj.shape[0], groups * UNIT), jnp.bfloat16),
            jax.ShapeDtypeStruct((adj.shape[0], n * slots), jnp.bfloat16),
        ],
        in_specs=[smem, vmem, vmem, vmem],
        out_specs=[vmem] * 3,
        compiler_params=pltpu.CompilerParams(vmem_limit_bytes=32 * 1024 * 1024),
        name="selection",
    )(ids, jnp.swapaxes(send_list, 1, 2), send_count, adj)


def tiles_kernel(table_v, tbuf, xo, xp, *rest):
    parts = len(rest) - 3
    accs, (masks, table, sem) = rest[:parts], rest[parts:]
    tile = tbuf.shape[2]
    width = xo.shape[1]
    to_scalar = pltpu.make_async_copy(table_v, table, sem)
    to_scalar.start()
    for acc in accs:
        acc[...] = jnp.zeros_like(acc)
    row_i = lax.broadcasted_iota(jnp.int32, (UNIT, tile), 0)
    for m in range(UNIT + 1):
        masks[m] = jnp.where(row_i < m, 1.0, 0.0).astype(jnp.bfloat16)
    columns = [(x, h) for x in (xo, xp) for h in range(0, width, PART)]
    to_scalar.wait()

    def step(i, carry):
        for m in range(STEP):
            b = i * STEP + m
            base = pl.multiple_of(table[1, b] * tile, tile)
            rows, places = [], []
            for k in range(BLOCK):
                word = table[0, b * BLOCK + k]
                u = jnp.bitwise_and(lax.shift_right_logical(word, 5), 511)
                rows.append(tbuf[u] * masks[jnp.bitwise_and(word, 31)])
                places.append(pl.multiple_of(lax.shift_right_logical(word, 14) * UNIT, UNIT))
            lhs = jnp.concatenate(rows, axis=0)
            for acc, (x, h) in zip(accs, columns):
                got = jnp.dot(lhs, x[pl.ds(base, tile), h:h + PART], preferred_element_type=jnp.float32)
                got = got.astype(jnp.bfloat16).astype(jnp.float32)
                for k in range(BLOCK):
                    acc[pl.ds(places[k], UNIT), :] += got[k * UNIT:(k + 1) * UNIT, :]
        return carry

    steps = lax.div(table[1, table.shape[1] - 1] + STEP - 1, STEP)
    lax.fori_loop(0, steps, step, 0)


def gathered_sums(per, n, table, tbuf, xo, xp):
    width = xo.shape[1]
    tile = tbuf.shape[2]
    vmem = pl.BlockSpec(memory_space=pltpu.VMEM)
    flops = 2 * tbuf.shape[0] * UNIT * tile * 2 * width
    parts = 2 * width // PART
    sums = jax.ShapeDtypeStruct(((n * per + 1) * UNIT, PART), jnp.float32)
    return pl.pallas_call(
        tiles_kernel,
        out_shape=[sums] * parts,
        in_specs=[vmem] * 4,
        out_specs=[vmem] * parts,
        scratch_shapes=[
            pltpu.VMEM((UNIT + 1, UNIT, tile), jnp.bfloat16),
            pltpu.SMEM(table.shape, jnp.int32),
            pltpu.SemaphoreType.DMA,
        ],
        compiler_params=pltpu.CompilerParams(vmem_limit_bytes=(12 << 20) + sums.size * 4 * parts),
        cost_estimate=pl.CostEstimate(flops=flops, bytes_accessed=8 << 20, transcendentals=0),
        name="gathered_sums",
    )(table, tbuf, xo, xp)


def weigh(accs, weights, first, count, out):
    size = min(256, count)

    def piece(r, carry):
        at = pl.multiple_of(r * size, size)
        got = jnp.zeros((size, out.shape[1]), jnp.float32)
        for i, acc in enumerate(accs):
            w, h = weights[i * PART // weights[0].shape[0]], i * PART % weights[0].shape[0]
            value = acc[pl.ds(first + at, size), :]
            high = value.astype(jnp.bfloat16)
            low = (value - high.astype(jnp.float32)).astype(jnp.bfloat16)
            got = got + jnp.dot(high, w[h:h + PART, :], preferred_element_type=jnp.float32)
            got = got + jnp.dot(low, w[h:h + PART, :], preferred_element_type=jnp.float32)
        out[pl.ds(at, size), :] = got
        return carry

    lax.fori_loop(0, count // size, piece, 0)


def sent_kernel(k, slots, rows, parts, wo, wp, *refs):
    accs, (out, sums, tail) = refs[:parts], refs[parts:]
    weigh(accs, (wo, wp), k * slots * rows, slots * rows, sums)
    write_coded(out, tail, slots, rows, lambda s: sums[s * rows:(s + 1) * rows, :])


def sent_terms(k, slots, rows, accs, wo, wp):
    hidden = wo.shape[1]
    vmem = pl.BlockSpec(memory_space=pltpu.VMEM)
    return pl.pallas_call(
        functools.partial(sent_kernel, k, slots, rows, len(accs)),
        out_shape=jax.ShapeDtypeStruct((slots * rows + tail_rows(slots), hidden), jnp.int16),
        in_specs=[vmem] * (2 + len(accs)),
        out_specs=vmem,
        scratch_shapes=[
            pltpu.VMEM((slots * rows, hidden), jnp.float32),
            pltpu.VMEM((tail_rows(slots), hidden), jnp.float32),
        ],
        compiler_params=pltpu.CompilerParams(vmem_limit_bytes=(12 << 20) + accs[0].size * 4 * len(accs)),
        cost_estimate=pl.CostEstimate(
            flops=4 * slots * rows * PART * len(accs) * hidden, bytes_accessed=2 << 20, transcendentals=0),
        name="sent_terms",
    )(wo, wp, *accs)


def own_kernel(chunk, per, groups, parts, ids, wo, wp, xo, so, *refs):
    accs, (out, theirs, terms) = refs[:parts], refs[parts:]
    weigh(accs, (wo, wp), 0, out.shape[0], out)
    terms[...] = jnp.dot(xo[:groups * UNIT, :], so[...], preferred_element_type=jnp.float32)
    for j in range(per):
        here = slice(j * UNIT, (j + 1) * UNIT)
        at = pl.multiple_of(group_of(ids[0], chunk * per + j, groups) * UNIT, UNIT)
        out[here, :] += terms[pl.ds(at, UNIT), :]
        at = pl.multiple_of(group_of(1 - ids[0], chunk * per + j, groups) * UNIT, UNIT)
        theirs[here, :] = terms[pl.ds(at, UNIT), :]


def own_terms(chunk, per, groups, slots, ids, accs, wo, wp, xo, so):
    hidden = wo.shape[1]
    rows = per * UNIT
    smem = pl.BlockSpec(memory_space=pltpu.SMEM)
    vmem = pl.BlockSpec(memory_space=pltpu.VMEM)
    return pl.pallas_call(
        functools.partial(own_kernel, chunk, per, groups, len(accs)),
        out_shape=[
            jax.ShapeDtypeStruct((slots * rows, hidden), jnp.float32),
            jax.ShapeDtypeStruct((rows, hidden), jnp.float32),
        ],
        in_specs=[smem] + [vmem] * (4 + len(accs)),
        out_specs=[vmem] * 2,
        scratch_shapes=[pltpu.VMEM((groups * UNIT, hidden), jnp.float32)],
        compiler_params=pltpu.CompilerParams(vmem_limit_bytes=(12 << 20) + accs[0].size * 4 * len(accs)),
        cost_estimate=pl.CostEstimate(
            flops=4 * slots * rows * PART * len(accs) * hidden, bytes_accessed=2 << 20, transcendentals=0),
        name="own_terms",
    )(ids, wo, wp, xo, so, *accs)


def combine_kernel(slots, rows, ways, own, *refs):
    parts = len(refs) - ways - 1
    coded, outs, tail = refs[:parts], refs[parts:parts + ways], refs[parts + ways]
    values = [read_coded(a, slots, rows) for a in coded]

    def total(s):
        got = own[s * rows:(s + 1) * rows, :]
        for value in values:
            got = got + value(s)
        return got

    for i in range(slots // ways):
        outs[0][i * rows:(i + 1) * rows, :] = total(i * ways)
    for k in range(1, ways):
        write_coded(outs[k], tail, slots // ways, rows, lambda s: total(s * ways + k))


def combine(slots, rows, ways, own, coded):
    width = own.shape[1]
    left = slots // ways
    vmem = pl.BlockSpec(memory_space=pltpu.VMEM)
    out = jax.ShapeDtypeStruct((left * rows + tail_rows(left), width), jnp.int16)
    return pl.pallas_call(
        functools.partial(combine_kernel, slots, rows, ways),
        out_shape=[jax.ShapeDtypeStruct((left * rows, width), jnp.float32)] + [out] * (ways - 1),
        in_specs=[vmem] * (1 + len(coded)),
        out_specs=[vmem] * ways,
        scratch_shapes=[pltpu.VMEM((tail_rows(left), width), jnp.float32)],
        compiler_params=pltpu.CompilerParams(vmem_limit_bytes=32 * 1024 * 1024),
        name="combine",
    )(own, *coded)


def hidden_kernel(chunks, parts, rows, *refs):
    out = refs[chunks * parts + 1]
    for c in range(chunks):
        own, self, coded = refs[c * parts], refs[c * parts + 1], refs[c * parts + 2:(c + 1) * parts]
        total = own[:rows, :] + self[...]
        for a in coded:
            total = total + read_coded(a, 1, rows)(0)
        out[c * rows:(c + 1) * rows, :] = jnp.maximum(total, 0.0).astype(jnp.bfloat16)


def hidden_rows(chunk_parts, rows, sel):
    chunks, parts = len(chunk_parts), len(chunk_parts[0])
    width = chunk_parts[0][0].shape[1]
    vmem = pl.BlockSpec(memory_space=pltpu.VMEM)
    flat = [a for part in chunk_parts for a in part]
    return pl.pallas_call(
        functools.partial(hidden_kernel, chunks, parts, rows),
        out_shape=jax.ShapeDtypeStruct((chunks * rows, width), jnp.bfloat16),
        in_specs=[vmem] * (len(flat) + 1),
        out_specs=vmem,
        compiler_params=pltpu.CompilerParams(vmem_limit_bytes=32 * 1024 * 1024),
        name="hidden_rows",
    )(*flat, sel)


def send_kernel(own, other, sel, send):
    both = jnp.concatenate([own[...], other[...]], axis=0)
    send[...] = jnp.dot(sel[...], both, preferred_element_type=jnp.float32).astype(jnp.bfloat16)


def rows_to_send(own, other, sel):
    vmem = pl.BlockSpec(memory_space=pltpu.VMEM)
    return pl.pallas_call(
        send_kernel,
        out_shape=jax.ShapeDtypeStruct((sel.shape[0], own.shape[1]), jnp.bfloat16),
        in_specs=[vmem] * 3,
        out_specs=vmem,
        compiler_params=pltpu.CompilerParams(vmem_limit_bytes=32 * 1024 * 1024),
        name="rows_to_send",
    )(own, other, sel)


def logits_kernel(own, other, received, front, adj_received, w_self, w_neigh, out):
    rows = out.shape[0]
    both = jnp.concatenate([own[...], other[...]], axis=0)
    local = jnp.dot(front[...], both, preferred_element_type=jnp.float32)
    mean = local[:rows, :] + jnp.dot(adj_received[...], received[...], preferred_element_type=jnp.float32)
    dims = (((1,), (1,)), ((), ()))
    got = lax.dot_general(local[rows:, :].astype(jnp.bfloat16), w_self[...], dims, preferred_element_type=jnp.float32)
    got = got + lax.dot_general(mean.astype(jnp.bfloat16), w_neigh[...], dims, preferred_element_type=jnp.float32)
    out[...] = got


def logits_of(own, other, received, front, adj_received, w_self, w_neigh):
    vmem = pl.BlockSpec(memory_space=pltpu.VMEM)
    return pl.pallas_call(
        logits_kernel,
        out_shape=jax.ShapeDtypeStruct((adj_received.shape[0], w_self.shape[1]), jnp.float32),
        in_specs=[vmem] * 7,
        out_specs=vmem,
        compiler_params=pltpu.CompilerParams(vmem_limit_bytes=32 * 1024 * 1024),
        name="logits",
    )(own, other, received, front, adj_received, w_self.T, w_neigh.T)


def exchange(parts, stride, n, places):
    got = [parts[0]]
    for k in places:
        got.append(lax.ppermute(parts[k], "dom", [(i, i ^ (k * stride)) for i in range(n)]))
    return got


def body(
    features,
    tile_weight,
    tile_dst,
    tile_src,
    tile_rows,
    w_self1,
    neighbour_weight_first,
    send_list,
    send_count,
    adj_two,
    w_self2,
    w_neigh2,
):
    n = lax.axis_size("dom")
    tile = tile_weight.shape[1]
    groups = tile // UNIT
    per = groups // 2 // CHUNKS
    bits = n.bit_length() - 1
    assert n == 1 << bits and bits >= 2
    radices = [2] * (bits // 2) + [1] * (bits % 2)
    ids = jnp.stack([lax.axis_index("feat"), lax.axis_index("dom")]).astype(jnp.int32)
    swap = [(0, 1), (1, 0)]
    xp = lax.ppermute(features, "feat", swap)
    wp = lax.ppermute(neighbour_weight_first, "feat", swap)
    tw = tile_weight.reshape(tile_weight.shape[0], groups, UNIT, tile)
    planned = plan(
        CHUNKS, per, n, 4, ids, tile_src, tile_rows, tile_dst, tw, features,
    )
    tables, tbufs, xo = planned[:CHUNKS], planned[CHUNKS:2 * CHUNKS], planned[2 * CHUNKS]
    wo, so = neighbour_weight_first, w_self1
    done = []
    for chunk in range(CHUNKS):
        accs = gathered_sums(per, n, tables[chunk], tbufs[chunk], xo, xp)
        slots, rows = n // 4, per * UNIT
        parts = {k: sent_terms(k, slots, rows, accs, wo, wp) for k in (1, 2, 3)}
        parts[0], theirs = own_terms(chunk, per, groups, slots, ids, accs, wo, wp, xo, so)
        self = lax.ppermute(theirs, "feat", swap)
        got = exchange(parts, 1, n, (1, 2, 3))
        stride = 4
        for radix in radices[1:]:
            ways = 1 << radix
            parts = combine(n // stride, per * UNIT, ways, got[0], got[1:])
            got = exchange(parts, stride, n, (2, 3, 1) if ways == 4 else (1,))
            stride *= ways
        done.append([got[0], self] + got[1:])
    sel, front, adj_received = selection(groups, ids, send_list, send_count, adj_two)
    own = hidden_rows(done, per * UNIT, sel)
    other = lax.ppermute(own, "feat", swap)
    send = rows_to_send(own, other, sel)
    received = lax.all_to_all(send, "dom", 0, 0, axis_index_groups=[group_order(n)], tiled=True)
    return logits_of(own, other, received, front, adj_received, w_self2, w_neigh2)


def solution(mesh):
    in_specs = (
        P("dom", "feat"),
        P("dom", None, None),
        P("dom"),
        P("dom"),
        P("dom"),
        P("feat", None),
        P("feat", None),
        P(),
        P(),
        P("dom", None),
        P(),
        P(),
    )
    out_specs = P("dom", None)
    return jax.shard_map(body, mesh=mesh, in_specs=in_specs, out_specs=out_specs, check_vma=False)
```

```python
import functools

import jax
import jax.numpy as jnp
from jax import lax
from jax.experimental import pallas as pl
from jax.experimental.pallas import tpu as pltpu
from jax.sharding import PartitionSpec as P

UNIT = 16
BLOCK = 8
STEP = 8
PART = 256
CHUNKS = 1


def group_of(core, place, groups):
    pair = 2 * (place // 2) + core
    return pair if place % 2 == 0 else groups - 1 - pair


def group_order(n):
    return list(range(n - 1, -1, -1))


LN2 = 0.6931471805599453


def tail_rows(slots):
    return -(-slots // 8) * 8


def encode(x):
    top = jnp.max(jnp.abs(x), axis=0, keepdims=True)
    power = jnp.ceil(jnp.log(jnp.maximum(top, 1e-30)) * (1.0 / LN2) + 1e-3) - 15.0
    return jnp.floor(x * jnp.exp(power * -LN2) + 0.5), power


def to_int16(x):
    return x.astype(jnp.int32).astype(jnp.int16)


def write_coded(out, tail, slots, rows, value_of):
    tail[...] = jnp.zeros_like(tail)
    for s in range(slots):
        whole, power = encode(value_of(s))
        out[s * rows:(s + 1) * rows, :] = to_int16(whole)
        tail[s:s + 1, :] = power
    out[slots * rows:, :] = to_int16(tail[...])


def read_coded(ref, slots, rows):
    powers = ref[slots * rows:, :].astype(jnp.int32).astype(jnp.float32)

    def value_of(s):
        whole = ref[s * rows:(s + 1) * rows, :].astype(jnp.int32).astype(jnp.float32)
        return whole * jnp.exp(powers[s:s + 1, :] * LN2)

    return value_of


def plan_kernel(chunks, per, n, radix, n_src, ids, src_h, rows_h, dst_h, tw, xo, *rest):
    tables, rest = rest[:chunks], rest[chunks:]
    tbufs, rest = rest[:chunks], rest[chunks:]
    xo_out, src_v, rows_v, dst_v, sems = rest
    core, me = ids[0], ids[1]
    tiles = src_v.shape[1]
    n_pos = tables[0].shape[1]
    units = per * tiles
    groups = 2 * per * chunks
    half = groups // 2
    gs = [group_of(core, i, groups) for i in range(half)]
    small = [(src_h, src_v), (rows_h, rows_v), (dst_h, dst_v)]
    large = [(tw.at[:, g], tbufs[i // per].at[pl.ds(i % per * tiles, tiles)]) for i, g in enumerate(gs)]
    large += [(xo, xo_out)]
    copies = [pltpu.make_async_copy(a, b, sems.at[i]) for i, (a, b) in enumerate(small + large)]
    for c in copies:
        c.start()
    lane = lax.broadcasted_iota(jnp.int32, (1, tiles), 1)
    block_i = lax.broadcasted_iota(jnp.int32, (n_src, tiles), 0)
    before = lax.broadcasted_iota(jnp.int32, (units, units), 0) < lax.broadcasted_iota(jnp.int32, (units, units), 1)
    before = jnp.where(before, 1.0, 0.0).astype(jnp.bfloat16)
    pos_i = lax.broadcasted_iota(jnp.int32, (tiles, n_pos), 1).astype(jnp.float32)
    place_i = lax.broadcasted_iota(jnp.int32, (1, n_pos), 1)
    trash = float(n * per << 14)
    for c in copies[:3]:
        c.wait()
    src, rows = src_v[...], rows_v[...]
    slot = jnp.bitwise_xor(dst_v[...], me)
    slot = jnp.bitwise_and(slot, radix - 1) * (n // radix) + lax.div(slot, radix)
    for c in range(chunks):
        hot, words, valid = [], [], []
        for j in range(per):
            limit = jnp.clip(rows - UNIT * gs[c * per + j], 0, UNIT)
            ok = limit > 0
            valid.append(ok)
            words.append(((slot * per + j) * 512 + (j * tiles + lane)) * 32 + limit)
            hot.append(jnp.where(jnp.logical_and(block_i == src, ok), 1.0, 0.0))
        hot = jnp.concatenate(hot, axis=1)
        earlier = jnp.dot(hot.astype(jnp.bfloat16), before, preferred_element_type=jnp.float32)
        blocks = jnp.floor((jnp.sum(hot, axis=1, keepdims=True) + (BLOCK - 1)) * (1.0 / BLOCK))
        ahead = jnp.zeros(blocks.shape, jnp.float32)
        source_i = lax.broadcasted_iota(jnp.int32, blocks.shape, 0)
        for s in range(n_src - 1):
            ahead = ahead + jnp.where(source_i > s, blocks[s:s + 1, :], 0.0)
        pos = jnp.sum(hot * (earlier + ahead * BLOCK), axis=0, keepdims=True)
        behind = jnp.where(place_i.astype(jnp.float32) >= ahead + blocks, 1.0, 0.0)
        owner = jnp.sum(behind, axis=0, keepdims=True)
        run = ahead[n_src - 1:, :] + blocks[n_src - 1:, :]
        stack = [jnp.where(valid[j], pos[:, j * tiles:(j + 1) * tiles], -1.0) for j in range(per)]
        stack += [w.astype(jnp.float32) - trash for w in words]
        stack += [jnp.zeros((1, tiles), jnp.float32)] * (-len(stack) % 8)
        cols = jnp.concatenate(stack, axis=0).T
        found = jnp.zeros((tiles, n_pos), jnp.float32)
        for j in range(per):
            found = found + jnp.where(cols[:, j:j + 1] == pos_i, cols[:, per + j:per + j + 1], 0.0)
        word = jnp.sum(found, axis=0, keepdims=True) + trash
        owner = jnp.where(place_i == n_pos - 1, run, jnp.minimum(owner, n_src - 1.0))
        tables[c][0:1, :] = word.astype(jnp.int32)
        tables[c][1:2, :] = owner.astype(jnp.int32)

    for c in copies[3:]:
        c.wait()


def plan(chunks, per, n, radix, ids, src, rows, dst, tw, xo):
    tiles, _, _, tile = tw.shape
    n_src = xo.shape[0] // tile
    blocks = -(-(per * tiles // BLOCK + n_src) // STEP) * STEP
    n_pos = -(-(blocks * BLOCK + 1) // 128) * 128
    smem = pl.BlockSpec(memory_space=pltpu.SMEM)
    vmem = pl.BlockSpec(memory_space=pltpu.VMEM)
    hbm = pl.BlockSpec(memory_space=pltpu.HBM)
    half = chunks * per
    return pl.pallas_call(
        functools.partial(plan_kernel, chunks, per, n, radix, n_src),
        out_shape=[jax.ShapeDtypeStruct((2, n_pos), jnp.int32)] * chunks
        + [jax.ShapeDtypeStruct((per * tiles, UNIT, tile), tw.dtype)] * chunks
        + [jax.ShapeDtypeStruct(xo.shape, xo.dtype)],
        in_specs=[smem] + [hbm] * 5,
        out_specs=[vmem] * (2 * chunks + 1),
        scratch_shapes=[
            pltpu.VMEM((1, tiles), jnp.int32),
            pltpu.VMEM((1, tiles), jnp.int32),
            pltpu.VMEM((1, tiles), jnp.int32),
            pltpu.SemaphoreType.DMA((3 + half + 1,)),
        ],
        compiler_params=pltpu.CompilerParams(vmem_limit_bytes=32 * 1024 * 1024),
        name="plan",
    )(ids, *[
        pltpu.with_memory_space_constraint(a, pltpu.HBM)
        for a in (src.reshape(1, tiles), rows.reshape(1, tiles), dst.reshape(1, tiles), tw, xo)
    ])


def select_kernel(groups, ids, lists, counts, adj, sel, front, adj_out):
    core, me = ids[0], ids[1]
    n = lists.shape[0]
    slots = lists.shape[1]
    total = n * slots
    q_n = lax.broadcasted_iota(jnp.int32, (total, n), 0)
    r_n = lax.broadcasted_iota(jnp.int32, (total, n), 1)
    mine = lists[me].astype(jnp.float32)
    cnt = counts[pl.ds(me, 1), :]
    picked = jnp.zeros((total, n), jnp.float32)
    k_n = jnp.bitwise_and(q_n, slots - 1)
    for k in range(slots):
        picked = jnp.where(k_n == k, mine[k:k + 1, :], picked)
    good = jnp.logical_and(n - 1 - lax.div(q_n, slots) == r_n, k_n < cnt)
    row = jnp.sum(jnp.where(good, picked + 1.0, 0.0), axis=1, keepdims=True) - 1.0
    lane = lax.broadcasted_iota(jnp.int32, (1, sel.shape[1]), 1)
    name = jnp.zeros(lane.shape, jnp.int32)
    names = [group_of(c, i, groups) for c in (core, 1 - core) for i in range(groups // 2)]
    for i, g in enumerate(names):
        name = jnp.where(lax.div(lane, UNIT) == i, g * UNIT + jnp.bitwise_and(lane, UNIT - 1), name)
    sel[...] = jnp.where(row == name.astype(jnp.float32), 1.0, 0.0).astype(jnp.bfloat16)
    tile, out_rows = groups * UNIT, adj.shape[0]
    placed = jnp.where(lax.broadcasted_iota(jnp.int32, (tile, tile), 0) == name, 1.0, 0.0).astype(jnp.bfloat16)
    front[:out_rows, :] = jnp.dot(adj[:, :tile], placed, preferred_element_type=jnp.float32).astype(jnp.bfloat16)
    front[out_rows:, :] = placed[:out_rows, :]
    column = lax.broadcasted_iota(jnp.int32, (1, total), 1)
    source = (n - 1 - lax.div(column, slots)) * slots + lax.rem(column, slots)
    moved = jnp.where(lax.broadcasted_iota(jnp.int32, (total, total), 0) == source, 1.0, 0.0).astype(jnp.bfloat16)
    adj_out[...] = jnp.dot(adj[:, groups * UNIT:], moved, preferred_element_type=jnp.float32).astype(jnp.bfloat16)


def selection(groups, ids, send_list, send_count, adj):
    n, _, slots = send_list.shape
    smem = pl.BlockSpec(memory_space=pltpu.SMEM)
    vmem = pl.BlockSpec(memory_space=pltpu.VMEM)
    return pl.pallas_call(
        functools.partial(select_kernel, groups),
        out_shape=[
            jax.ShapeDtypeStruct((n * slots, groups * UNIT), jnp.bfloat16),
            jax.ShapeDtypeStruct((2 * adj.shape[0], groups * UNIT), jnp.bfloat16),
            jax.ShapeDtypeStruct((adj.shape[0], n * slots), jnp.bfloat16),
        ],
        in_specs=[smem, vmem, vmem, vmem],
        out_specs=[vmem] * 3,
        compiler_params=pltpu.CompilerParams(vmem_limit_bytes=32 * 1024 * 1024),
        name="selection",
    )(ids, jnp.swapaxes(send_list, 1, 2), send_count, adj)


def tiles_kernel(table_v, tbuf, xo, xp, *rest):
    parts = len(rest) - 3
    accs, (masks, table, sem) = rest[:parts], rest[parts:]
    tile = tbuf.shape[2]
    width = xo.shape[1]
    to_scalar = pltpu.make_async_copy(table_v, table, sem)
    to_scalar.start()
    for acc in accs:
        acc[...] = jnp.zeros_like(acc)
    row_i = lax.broadcasted_iota(jnp.int32, (UNIT, tile), 0)
    for m in range(UNIT + 1):
        masks[m] = jnp.where(row_i < m, 1.0, 0.0).astype(jnp.bfloat16)
    columns = [(x, h) for x in (xo, xp) for h in range(0, width, PART)]
    to_scalar.wait()

    def blocks(first, count):
        for m in range(count):
            at = first + m
            base = pl.multiple_of(table[1, at] * tile, tile)
            rows, places = [], []
            for k in range(BLOCK):
                word = table[0, at * BLOCK + k]
                u = jnp.bitwise_and(lax.shift_right_logical(word, 5), 511)
                rows.append(tbuf[u] * masks[jnp.bitwise_and(word, 31)])
                places.append(pl.multiple_of(lax.shift_right_logical(word, 14) * UNIT, UNIT))
            lhs = jnp.concatenate(rows, axis=0)
            for acc, (x, h) in zip(accs, columns):
                got = jnp.dot(lhs, x[pl.ds(base, tile), h:h + PART], preferred_element_type=jnp.float32)
                got = got.astype(jnp.bfloat16).astype(jnp.float32)
                for k in range(BLOCK):
                    acc[pl.ds(places[k], UNIT), :] += got[k * UNIT:(k + 1) * UNIT, :]

    half = STEP // 2
    halves = lax.div(table[1, table.shape[1] - 1] + half - 1, half)
    steps = lax.div(halves, 2)

    def step(i, carry):
        blocks(i * STEP, STEP)
        return carry

    def last(i, carry):
        blocks(steps * STEP, half)
        return carry

    lax.fori_loop(0, steps, step, 0)
    lax.fori_loop(0, lax.rem(halves, 2), last, 0)


def gathered_sums(per, n, table, tbuf, xo, xp):
    width = xo.shape[1]
    tile = tbuf.shape[2]
    vmem = pl.BlockSpec(memory_space=pltpu.VMEM)
    flops = 2 * tbuf.shape[0] * UNIT * tile * 2 * width
    parts = 2 * width // PART
    sums = jax.ShapeDtypeStruct(((n * per + 1) * UNIT, PART), jnp.float32)
    return pl.pallas_call(
        tiles_kernel,
        out_shape=[sums] * parts,
        in_specs=[vmem] * 4,
        out_specs=[vmem] * parts,
        scratch_shapes=[
            pltpu.VMEM((UNIT + 1, UNIT, tile), jnp.bfloat16),
            pltpu.SMEM(table.shape, jnp.int32),
            pltpu.SemaphoreType.DMA,
        ],
        compiler_params=pltpu.CompilerParams(vmem_limit_bytes=(12 << 20) + sums.size * 4 * parts),
        cost_estimate=pl.CostEstimate(flops=flops, bytes_accessed=8 << 20, transcendentals=0),
        name="gathered_sums",
    )(table, tbuf, xo, xp)


def weigh(accs, weights, first, count, out):
    size = min(256, count)

    def piece(r, carry):
        at = pl.multiple_of(r * size, size)
        got = jnp.zeros((size, out.shape[1]), jnp.float32)
        for i, acc in enumerate(accs):
            w, h = weights[i * PART // weights[0].shape[0]], i * PART % weights[0].shape[0]
            value = acc[pl.ds(first + at, size), :]
            high = value.astype(jnp.bfloat16)
            low = (value - high.astype(jnp.float32)).astype(jnp.bfloat16)
            got = got + jnp.dot(high, w[h:h + PART, :], preferred_element_type=jnp.float32)
            got = got + jnp.dot(low, w[h:h + PART, :], preferred_element_type=jnp.float32)
        out[pl.ds(at, size), :] = got
        return carry

    lax.fori_loop(0, count // size, piece, 0)


def sent_kernel(k, slots, rows, parts, wo, wp, *refs):
    accs, (out, sums, tail) = refs[:parts], refs[parts:]
    weigh(accs, (wo, wp), k * slots * rows, slots * rows, sums)
    write_coded(out, tail, slots, rows, lambda s: sums[s * rows:(s + 1) * rows, :])


def sent_terms(k, slots, rows, accs, wo, wp):
    hidden = wo.shape[1]
    vmem = pl.BlockSpec(memory_space=pltpu.VMEM)
    return pl.pallas_call(
        functools.partial(sent_kernel, k, slots, rows, len(accs)),
        out_shape=jax.ShapeDtypeStruct((slots * rows + tail_rows(slots), hidden), jnp.int16),
        in_specs=[vmem] * (2 + len(accs)),
        out_specs=vmem,
        scratch_shapes=[
            pltpu.VMEM((slots * rows, hidden), jnp.float32),
            pltpu.VMEM((tail_rows(slots), hidden), jnp.float32),
        ],
        compiler_params=pltpu.CompilerParams(vmem_limit_bytes=(12 << 20) + accs[0].size * 4 * len(accs)),
        cost_estimate=pl.CostEstimate(
            flops=4 * slots * rows * PART * len(accs) * hidden, bytes_accessed=2 << 20, transcendentals=0),
        name="sent_terms",
    )(wo, wp, *accs)


def own_kernel(chunk, per, groups, parts, ids, wo, wp, xo, so, *refs):
    accs, (out, theirs, terms) = refs[:parts], refs[parts:]
    weigh(accs, (wo, wp), 0, out.shape[0], out)
    terms[...] = jnp.dot(xo[:groups * UNIT, :], so[...], preferred_element_type=jnp.float32)
    for j in range(per):
        here = slice(j * UNIT, (j + 1) * UNIT)
        at = pl.multiple_of(group_of(ids[0], chunk * per + j, groups) * UNIT, UNIT)
        out[here, :] += terms[pl.ds(at, UNIT), :]
        at = pl.multiple_of(group_of(1 - ids[0], chunk * per + j, groups) * UNIT, UNIT)
        theirs[here, :] = terms[pl.ds(at, UNIT), :]


def own_terms(chunk, per, groups, slots, ids, accs, wo, wp, xo, so):
    hidden = wo.shape[1]
    rows = per * UNIT
    smem = pl.BlockSpec(memory_space=pltpu.SMEM)
    vmem = pl.BlockSpec(memory_space=pltpu.VMEM)
    return pl.pallas_call(
        functools.partial(own_kernel, chunk, per, groups, len(accs)),
        out_shape=[
            jax.ShapeDtypeStruct((slots * rows, hidden), jnp.float32),
            jax.ShapeDtypeStruct((rows, hidden), jnp.float32),
        ],
        in_specs=[smem] + [vmem] * (4 + len(accs)),
        out_specs=[vmem] * 2,
        scratch_shapes=[pltpu.VMEM((groups * UNIT, hidden), jnp.float32)],
        compiler_params=pltpu.CompilerParams(vmem_limit_bytes=(12 << 20) + accs[0].size * 4 * len(accs)),
        cost_estimate=pl.CostEstimate(
            flops=4 * slots * rows * PART * len(accs) * hidden, bytes_accessed=2 << 20, transcendentals=0),
        name="own_terms",
    )(ids, wo, wp, xo, so, *accs)


def combine_kernel(slots, rows, ways, own, *refs):
    parts = len(refs) - ways - 1
    coded, outs, tail = refs[:parts], refs[parts:parts + ways], refs[parts + ways]
    values = [read_coded(a, slots, rows) for a in coded]

    def total(s):
        got = own[s * rows:(s + 1) * rows, :]
        for value in values:
            got = got + value(s)
        return got

    for i in range(slots // ways):
        outs[0][i * rows:(i + 1) * rows, :] = total(i * ways)
    for k in range(1, ways):
        write_coded(outs[k], tail, slots // ways, rows, lambda s: total(s * ways + k))


def combine(slots, rows, ways, own, coded):
    width = own.shape[1]
    left = slots // ways
    vmem = pl.BlockSpec(memory_space=pltpu.VMEM)
    out = jax.ShapeDtypeStruct((left * rows + tail_rows(left), width), jnp.int16)
    return pl.pallas_call(
        functools.partial(combine_kernel, slots, rows, ways),
        out_shape=[jax.ShapeDtypeStruct((left * rows, width), jnp.float32)] + [out] * (ways - 1),
        in_specs=[vmem] * (1 + len(coded)),
        out_specs=[vmem] * ways,
        scratch_shapes=[pltpu.VMEM((tail_rows(left), width), jnp.float32)],
        compiler_params=pltpu.CompilerParams(vmem_limit_bytes=32 * 1024 * 1024),
        name="combine",
    )(own, *coded)


def hidden_kernel(chunks, parts, rows, *refs):
    out = refs[chunks * parts + 1]
    for c in range(chunks):
        own, self, coded = refs[c * parts], refs[c * parts + 1], refs[c * parts + 2:(c + 1) * parts]
        total = own[:rows, :] + self[...]
        for a in coded:
            total = total + read_coded(a, 1, rows)(0)
        out[c * rows:(c + 1) * rows, :] = jnp.maximum(total, 0.0).astype(jnp.bfloat16)


def hidden_rows(chunk_parts, rows, sel):
    chunks, parts = len(chunk_parts), len(chunk_parts[0])
    width = chunk_parts[0][0].shape[1]
    vmem = pl.BlockSpec(memory_space=pltpu.VMEM)
    flat = [a for part in chunk_parts for a in part]
    return pl.pallas_call(
        functools.partial(hidden_kernel, chunks, parts, rows),
        out_shape=jax.ShapeDtypeStruct((chunks * rows, width), jnp.bfloat16),
        in_specs=[vmem] * (len(flat) + 1),
        out_specs=vmem,
        compiler_params=pltpu.CompilerParams(vmem_limit_bytes=32 * 1024 * 1024),
        name="hidden_rows",
    )(*flat, sel)


def send_kernel(own, other, sel, send):
    both = jnp.concatenate([own[...], other[...]], axis=0)
    send[...] = jnp.dot(sel[...], both, preferred_element_type=jnp.float32).astype(jnp.bfloat16)


def rows_to_send(own, other, sel):
    vmem = pl.BlockSpec(memory_space=pltpu.VMEM)
    return pl.pallas_call(
        send_kernel,
        out_shape=jax.ShapeDtypeStruct((sel.shape[0], own.shape[1]), jnp.bfloat16),
        in_specs=[vmem] * 3,
        out_specs=vmem,
        compiler_params=pltpu.CompilerParams(vmem_limit_bytes=32 * 1024 * 1024),
        name="rows_to_send",
    )(own, other, sel)


def logits_kernel(own, other, received, front, adj_received, w_self, w_neigh, out):
    rows = out.shape[0]
    both = jnp.concatenate([own[...], other[...]], axis=0)
    local = jnp.dot(front[...], both, preferred_element_type=jnp.float32)
    mean = local[:rows, :] + jnp.dot(adj_received[...], received[...], preferred_element_type=jnp.float32)
    dims = (((1,), (1,)), ((), ()))
    got = lax.dot_general(local[rows:, :].astype(jnp.bfloat16), w_self[...], dims, preferred_element_type=jnp.float32)
    got = got + lax.dot_general(mean.astype(jnp.bfloat16), w_neigh[...], dims, preferred_element_type=jnp.float32)
    out[...] = got


def logits_of(own, other, received, front, adj_received, w_self, w_neigh):
    vmem = pl.BlockSpec(memory_space=pltpu.VMEM)
    return pl.pallas_call(
        logits_kernel,
        out_shape=jax.ShapeDtypeStruct((adj_received.shape[0], w_self.shape[1]), jnp.float32),
        in_specs=[vmem] * 7,
        out_specs=vmem,
        compiler_params=pltpu.CompilerParams(vmem_limit_bytes=32 * 1024 * 1024),
        name="logits",
    )(own, other, received, front, adj_received, w_self.T, w_neigh.T)


def exchange(parts, stride, n, places):
    got = [parts[0]]
    for k in places:
        got.append(lax.ppermute(parts[k], "dom", [(i, i ^ (k * stride)) for i in range(n)]))
    return got


def body(
    features,
    tile_weight,
    tile_dst,
    tile_src,
    tile_rows,
    w_self1,
    neighbour_weight_first,
    send_list,
    send_count,
    adj_two,
    w_self2,
    w_neigh2,
):
    n = lax.axis_size("dom")
    tile = tile_weight.shape[1]
    groups = tile // UNIT
    per = groups // 2 // CHUNKS
    bits = n.bit_length() - 1
    assert n == 1 << bits and bits >= 2
    radices = [2] * (bits // 2) + [1] * (bits % 2)
    ids = jnp.stack([lax.axis_index("feat"), lax.axis_index("dom")]).astype(jnp.int32)
    swap = [(0, 1), (1, 0)]
    xp = lax.ppermute(features, "feat", swap)
    wp = lax.ppermute(neighbour_weight_first, "feat", swap)
    tw = tile_weight.reshape(tile_weight.shape[0], groups, UNIT, tile)
    planned = plan(
        CHUNKS, per, n, 4, ids, tile_src, tile_rows, tile_dst, tw, features,
    )
    tables, tbufs, xo = planned[:CHUNKS], planned[CHUNKS:2 * CHUNKS], planned[2 * CHUNKS]
    wo, so = neighbour_weight_first, w_self1
    done = []
    for chunk in range(CHUNKS):
        accs = gathered_sums(per, n, tables[chunk], tbufs[chunk], xo, xp)
        slots, rows = n // 4, per * UNIT
        parts = {k: sent_terms(k, slots, rows, accs, wo, wp) for k in (1, 2, 3)}
        parts[0], theirs = own_terms(chunk, per, groups, slots, ids, accs, wo, wp, xo, so)
        self = lax.ppermute(theirs, "feat", swap)
        got = exchange(parts, 1, n, (1, 2, 3))
        stride = 4
        for radix in radices[1:]:
            ways = 1 << radix
            parts = combine(n // stride, per * UNIT, ways, got[0], got[1:])
            got = exchange(parts, stride, n, (2, 3, 1) if ways == 4 else (1,))
            stride *= ways
        done.append([got[0], self] + got[1:])
    sel, front, adj_received = selection(groups, ids, send_list, send_count, adj_two)
    own = hidden_rows(done, per * UNIT, sel)
    other = lax.ppermute(own, "feat", swap)
    send = rows_to_send(own, other, sel)
    received = lax.all_to_all(send, "dom", 0, 0, axis_index_groups=[group_order(n)], tiled=True)
    return logits_of(own, other, received, front, adj_received, w_self2, w_neigh2)


def solution(mesh):
    in_specs = (
        P("dom", "feat"),
        P("dom", None, None),
        P("dom"),
        P("dom"),
        P("dom"),
        P("feat", None),
        P("feat", None),
        P(),
        P(),
        P("dom", None),
        P(),
        P(),
    )
    out_specs = P("dom", None)
    return jax.shard_map(body, mesh=mesh, in_specs=in_specs, out_specs=out_specs, check_vma=False)
```

```python
import functools

import jax
import jax.numpy as jnp
from jax import lax
from jax.experimental import pallas as pl
from jax.experimental.pallas import tpu as pltpu
from jax.sharding import PartitionSpec as P

UNIT = 16
BLOCK = 8
STEP = 8
PART = 256
CHUNKS = 1


def group_of(core, place, groups):
    pair = 2 * (place // 2) + core
    return pair if place % 2 == 0 else groups - 1 - pair


def group_order(n):
    return list(range(n - 1, -1, -1))


LN2 = 0.6931471805599453


def tail_rows(slots):
    return -(-slots // 8) * 8


def encode(x):
    top = jnp.max(jnp.abs(x), axis=0, keepdims=True)
    power = jnp.ceil(jnp.log(jnp.maximum(top, 1e-30)) * (1.0 / LN2) + 1e-3) - 15.0
    return jnp.floor(x * jnp.exp(power * -LN2) + 0.5), power


def to_int16(x):
    return x.astype(jnp.int32).astype(jnp.int16)


def write_coded(out, tail, slots, rows, value_of):
    tail[...] = jnp.zeros_like(tail)
    for s in range(slots):
        whole, power = encode(value_of(s))
        out[s * rows:(s + 1) * rows, :] = to_int16(whole)
        tail[s:s + 1, :] = power
    out[slots * rows:, :] = to_int16(tail[...])


def read_coded(ref, slots, rows):
    powers = ref[slots * rows:, :].astype(jnp.int32).astype(jnp.float32)

    def value_of(s):
        whole = ref[s * rows:(s + 1) * rows, :].astype(jnp.int32).astype(jnp.float32)
        return whole * jnp.exp(powers[s:s + 1, :] * LN2)

    return value_of


def plan_kernel(chunks, per, n, radix, n_src, ids, src_h, rows_h, dst_h, tw, xo, *rest):
    tables, rest = rest[:chunks], rest[chunks:]
    tbufs, rest = rest[:chunks], rest[chunks:]
    xo_out, src_v, rows_v, dst_v, sems = rest
    core, me = ids[0], ids[1]
    tiles = src_v.shape[1]
    n_pos = tables[0].shape[1]
    units = per * tiles
    groups = 2 * per * chunks
    half = groups // 2
    gs = [group_of(core, i, groups) for i in range(half)]
    small = [(src_h, src_v), (rows_h, rows_v), (dst_h, dst_v)]
    large = [(tw.at[:, g], tbufs[i // per].at[pl.ds(i % per * tiles, tiles)]) for i, g in enumerate(gs)]
    large += [(xo, xo_out)]
    copies = [pltpu.make_async_copy(a, b, sems.at[i]) for i, (a, b) in enumerate(small + large)]
    for c in copies:
        c.start()
    lane = lax.broadcasted_iota(jnp.int32, (1, tiles), 1)
    block_i = lax.broadcasted_iota(jnp.int32, (n_src, tiles), 0)
    before = lax.broadcasted_iota(jnp.int32, (units, units), 0) < lax.broadcasted_iota(jnp.int32, (units, units), 1)
    before = jnp.where(before, 1.0, 0.0).astype(jnp.bfloat16)
    pos_i = lax.broadcasted_iota(jnp.int32, (tiles, n_pos), 1).astype(jnp.float32)
    place_i = lax.broadcasted_iota(jnp.int32, (1, n_pos), 1)
    trash = float(n * per << 14)
    for c in copies[:3]:
        c.wait()
    src, rows = src_v[...], rows_v[...]
    slot = jnp.bitwise_xor(dst_v[...], me)
    slot = jnp.bitwise_and(slot, radix - 1) * (n // radix) + lax.div(slot, radix)
    for c in range(chunks):
        hot, words, valid = [], [], []
        for j in range(per):
            limit = jnp.clip(rows - UNIT * gs[c * per + j], 0, UNIT)
            ok = limit > 0
            valid.append(ok)
            words.append(((slot * per + j) * 512 + (j * tiles + lane)) * 32 + limit)
            hot.append(jnp.where(jnp.logical_and(block_i == src, ok), 1.0, 0.0))
        hot = jnp.concatenate(hot, axis=1)
        earlier = jnp.dot(hot.astype(jnp.bfloat16), before, preferred_element_type=jnp.float32)
        blocks = jnp.floor((jnp.sum(hot, axis=1, keepdims=True) + (BLOCK - 1)) * (1.0 / BLOCK))
        ahead = jnp.zeros(blocks.shape, jnp.float32)
        source_i = lax.broadcasted_iota(jnp.int32, blocks.shape, 0)
        for s in range(n_src - 1):
            ahead = ahead + jnp.where(source_i > s, blocks[s:s + 1, :], 0.0)
        pos = jnp.sum(hot * (earlier + ahead * BLOCK), axis=0, keepdims=True)
        behind = jnp.where(place_i.astype(jnp.float32) >= ahead + blocks, 1.0, 0.0)
        owner = jnp.sum(behind, axis=0, keepdims=True)
        run = ahead[n_src - 1:, :] + blocks[n_src - 1:, :]
        stack = [jnp.where(valid[j], pos[:, j * tiles:(j + 1) * tiles], -1.0) for j in range(per)]
        stack += [w.astype(jnp.float32) - trash for w in words]
        stack += [jnp.zeros((1, tiles), jnp.float32)] * (-len(stack) % 8)
        cols = jnp.concatenate(stack, axis=0).T
        found = jnp.zeros((tiles, n_pos), jnp.float32)
        for j in range(per):
            found = found + jnp.where(cols[:, j:j + 1] == pos_i, cols[:, per + j:per + j + 1], 0.0)
        word = jnp.sum(found, axis=0, keepdims=True) + trash
        owner = jnp.where(place_i == n_pos - 1, run, jnp.minimum(owner, n_src - 1.0))
        tables[c][0:1, :] = word.astype(jnp.int32)
        tables[c][1:2, :] = owner.astype(jnp.int32)

    for c in copies[3:]:
        c.wait()


def plan(chunks, per, n, radix, ids, src, rows, dst, tw, xo):
    tiles, _, _, tile = tw.shape
    n_src = xo.shape[0] // tile
    blocks = -(-(per * tiles // BLOCK + n_src) // STEP) * STEP
    n_pos = -(-(blocks * BLOCK + 1) // 128) * 128
    smem = pl.BlockSpec(memory_space=pltpu.SMEM)
    vmem = pl.BlockSpec(memory_space=pltpu.VMEM)
    hbm = pl.BlockSpec(memory_space=pltpu.HBM)
    half = chunks * per
    return pl.pallas_call(
        functools.partial(plan_kernel, chunks, per, n, radix, n_src),
        out_shape=[jax.ShapeDtypeStruct((2, n_pos), jnp.int32)] * chunks
        + [jax.ShapeDtypeStruct((per * tiles, UNIT, tile), tw.dtype)] * chunks
        + [jax.ShapeDtypeStruct(xo.shape, xo.dtype)],
        in_specs=[smem] + [hbm] * 5,
        out_specs=[vmem] * (2 * chunks + 1),
        scratch_shapes=[
            pltpu.VMEM((1, tiles), jnp.int32),
            pltpu.VMEM((1, tiles), jnp.int32),
            pltpu.VMEM((1, tiles), jnp.int32),
            pltpu.SemaphoreType.DMA((3 + half + 1,)),
        ],
        compiler_params=pltpu.CompilerParams(vmem_limit_bytes=32 * 1024 * 1024),
        name="plan",
    )(ids, *[
        pltpu.with_memory_space_constraint(a, pltpu.HBM)
        for a in (src.reshape(1, tiles), rows.reshape(1, tiles), dst.reshape(1, tiles), tw, xo)
    ])


def select_kernel(groups, ids, lists, counts, adj, sel, front, adj_out):
    core, me = ids[0], ids[1]
    n = lists.shape[0]
    slots = lists.shape[1]
    total = n * slots
    q_n = lax.broadcasted_iota(jnp.int32, (total, n), 0)
    r_n = lax.broadcasted_iota(jnp.int32, (total, n), 1)
    mine = lists[me].astype(jnp.float32)
    cnt = counts[pl.ds(me, 1), :]
    picked = jnp.zeros((total, n), jnp.float32)
    k_n = jnp.bitwise_and(q_n, slots - 1)
    for k in range(slots):
        picked = jnp.where(k_n == k, mine[k:k + 1, :], picked)
    good = jnp.logical_and(n - 1 - lax.div(q_n, slots) == r_n, k_n < cnt)
    row = jnp.sum(jnp.where(good, picked + 1.0, 0.0), axis=1, keepdims=True) - 1.0
    lane = lax.broadcasted_iota(jnp.int32, (1, sel.shape[1]), 1)
    name = jnp.zeros(lane.shape, jnp.int32)
    names = [group_of(c, i, groups) for c in (core, 1 - core) for i in range(groups // 2)]
    for i, g in enumerate(names):
        name = jnp.where(lax.div(lane, UNIT) == i, g * UNIT + jnp.bitwise_and(lane, UNIT - 1), name)
    sel[...] = jnp.where(row == name.astype(jnp.float32), 1.0, 0.0).astype(jnp.bfloat16)
    tile, out_rows = groups * UNIT, adj.shape[0]
    placed = jnp.where(lax.broadcasted_iota(jnp.int32, (tile, tile), 0) == name, 1.0, 0.0).astype(jnp.bfloat16)
    front[:out_rows, :] = jnp.dot(adj[:, :tile], placed, preferred_element_type=jnp.float32).astype(jnp.bfloat16)
    front[out_rows:, :] = placed[:out_rows, :]
    column = lax.broadcasted_iota(jnp.int32, (1, total), 1)
    source = (n - 1 - lax.div(column, slots)) * slots + lax.rem(column, slots)
    moved = jnp.where(lax.broadcasted_iota(jnp.int32, (total, total), 0) == source, 1.0, 0.0).astype(jnp.bfloat16)
    adj_out[...] = jnp.dot(adj[:, groups * UNIT:], moved, preferred_element_type=jnp.float32).astype(jnp.bfloat16)


def selection(groups, ids, send_list, send_count, adj):
    n, _, slots = send_list.shape
    smem = pl.BlockSpec(memory_space=pltpu.SMEM)
    vmem = pl.BlockSpec(memory_space=pltpu.VMEM)
    return pl.pallas_call(
        functools.partial(select_kernel, groups),
        out_shape=[
            jax.ShapeDtypeStruct((n * slots, groups * UNIT), jnp.bfloat16),
            jax.ShapeDtypeStruct((2 * adj.shape[0], groups * UNIT), jnp.bfloat16),
            jax.ShapeDtypeStruct((adj.shape[0], n * slots), jnp.bfloat16),
        ],
        in_specs=[smem, vmem, vmem, vmem],
        out_specs=[vmem] * 3,
        compiler_params=pltpu.CompilerParams(vmem_limit_bytes=32 * 1024 * 1024),
        name="selection",
    )(ids, jnp.swapaxes(send_list, 1, 2), send_count, adj)


def tiles_kernel(table_v, tbuf, xo, xp, *rest):
    parts = len(rest) - 3
    accs, (masks, table, sem) = rest[:parts], rest[parts:]
    tile = tbuf.shape[2]
    width = xo.shape[1]
    to_scalar = pltpu.make_async_copy(table_v, table, sem)
    to_scalar.start()
    for acc in accs:
        acc[...] = jnp.zeros_like(acc)
    row_i = lax.broadcasted_iota(jnp.int32, (UNIT, tile), 0)
    for m in range(UNIT + 1):
        masks[m] = jnp.where(row_i < m, 1.0, 0.0).astype(jnp.bfloat16)
    columns = [(x, h) for x in (xo, xp) for h in range(0, width, PART)]
    to_scalar.wait()

    def blocks(first, count):
        for m in range(count):
            at = first + m
            base = pl.multiple_of(table[1, at] * tile, tile)
            rows, places = [], []
            for k in range(BLOCK):
                word = table[0, at * BLOCK + k]
                u = jnp.bitwise_and(lax.shift_right_logical(word, 5), 511)
                rows.append(tbuf[u] * masks[jnp.bitwise_and(word, 31)])
                places.append(pl.multiple_of(lax.shift_right_logical(word, 14) * UNIT, UNIT))
            lhs = jnp.concatenate(rows, axis=0)
            for acc, (x, h) in zip(accs, columns):
                got = jnp.dot(lhs, x[pl.ds(base, tile), h:h + PART], preferred_element_type=jnp.float32)
                got = got.astype(jnp.bfloat16).astype(jnp.float32)
                for k in range(BLOCK):
                    acc[pl.ds(places[k], UNIT), :] += got[k * UNIT:(k + 1) * UNIT, :]

    half = STEP // 2
    halves = lax.div(table[1, table.shape[1] - 1] + half - 1, half)
    steps = lax.div(halves, 2)

    def step(i, carry):
        blocks(i * STEP, STEP)
        return carry

    def last(i, carry):
        blocks(steps * STEP, half)
        return carry

    lax.fori_loop(0, steps, step, 0)
    lax.fori_loop(0, lax.rem(halves, 2), last, 0)


def gathered_sums(per, n, table, tbuf, xo, xp):
    width = xo.shape[1]
    tile = tbuf.shape[2]
    vmem = pl.BlockSpec(memory_space=pltpu.VMEM)
    flops = 2 * tbuf.shape[0] * UNIT * tile * 2 * width
    parts = 2 * width // PART
    sums = jax.ShapeDtypeStruct(((n * per + 1) * UNIT, PART), jnp.float32)
    return pl.pallas_call(
        tiles_kernel,
        out_shape=[sums] * parts,
        in_specs=[vmem] * 4,
        out_specs=[vmem] * parts,
        scratch_shapes=[
            pltpu.VMEM((UNIT + 1, UNIT, tile), jnp.bfloat16),
            pltpu.SMEM(table.shape, jnp.int32),
            pltpu.SemaphoreType.DMA,
        ],
        compiler_params=pltpu.CompilerParams(vmem_limit_bytes=(12 << 20) + sums.size * 4 * parts),
        cost_estimate=pl.CostEstimate(flops=flops, bytes_accessed=8 << 20, transcendentals=0),
        name="gathered_sums",
    )(table, tbuf, xo, xp)


def weigh(accs, weights, first, count, out):
    size = min(256, count)

    def piece(at):
        got = jnp.zeros((size, out.shape[1]), jnp.float32)
        for i, acc in enumerate(accs):
            w, h = weights[i * PART // weights[0].shape[0]], i * PART % weights[0].shape[0]
            value = acc[pl.ds(first + at, size), :]
            high = value.astype(jnp.bfloat16)
            low = (value - high.astype(jnp.float32)).astype(jnp.bfloat16)
            got = got + jnp.dot(high, w[h:h + PART, :], preferred_element_type=jnp.float32)
            got = got + jnp.dot(low, w[h:h + PART, :], preferred_element_type=jnp.float32)
        out[pl.ds(at, size), :] = got

    if count == size:
        piece(0)
    else:
        lax.fori_loop(0, count // size, lambda r, carry: (piece(pl.multiple_of(r * size, size)), carry)[1], 0)


def sent_kernel(slots, rows, ways, parts, wo, wp, *refs):
    accs, outs, scratch = refs[:parts], refs[parts:parts + ways - 1], refs[parts + ways - 1:]
    for k in range(ways - 1, 0, -1):
        sums, tail = scratch[2 * k - 2:2 * k]
        weigh(accs, (wo, wp), k * slots * rows, slots * rows, sums)
        write_coded(outs[k - 1], tail, slots, rows, lambda s: sums[s * rows:(s + 1) * rows, :])


def sent_terms(ways, slots, rows, accs, wo, wp):
    hidden = wo.shape[1]
    vmem = pl.BlockSpec(memory_space=pltpu.VMEM)
    coded = jax.ShapeDtypeStruct((slots * rows + tail_rows(slots), hidden), jnp.int16)
    return pl.pallas_call(
        functools.partial(sent_kernel, slots, rows, ways, len(accs)),
        out_shape=[coded] * (ways - 1),
        in_specs=[vmem] * (2 + len(accs)),
        out_specs=[vmem] * (ways - 1),
        scratch_shapes=[
            pltpu.VMEM((slots * rows, hidden), jnp.float32),
            pltpu.VMEM((tail_rows(slots), hidden), jnp.float32),
        ] * (ways - 1),
        compiler_params=pltpu.CompilerParams(vmem_limit_bytes=(20 << 20) + accs[0].size * 4 * len(accs)),
        cost_estimate=pl.CostEstimate(
            flops=4 * (ways - 1) * slots * rows * PART * len(accs) * hidden, bytes_accessed=6 << 20, transcendentals=0),
        name="sent_terms",
    )(wo, wp, *accs)


def own_kernel(chunk, per, groups, parts, ids, wo, wp, xo, so, *refs):
    accs, (out, theirs, terms) = refs[:parts], refs[parts:]
    weigh(accs, (wo, wp), 0, out.shape[0], out)
    terms[...] = jnp.dot(xo[:groups * UNIT, :], so[...], preferred_element_type=jnp.float32)
    for j in range(per):
        here = slice(j * UNIT, (j + 1) * UNIT)
        at = pl.multiple_of(group_of(ids[0], chunk * per + j, groups) * UNIT, UNIT)
        out[here, :] += terms[pl.ds(at, UNIT), :]
        at = pl.multiple_of(group_of(1 - ids[0], chunk * per + j, groups) * UNIT, UNIT)
        theirs[here, :] = terms[pl.ds(at, UNIT), :]


def own_terms(chunk, per, groups, slots, ids, accs, wo, wp, xo, so):
    hidden = wo.shape[1]
    rows = per * UNIT
    smem = pl.BlockSpec(memory_space=pltpu.SMEM)
    vmem = pl.BlockSpec(memory_space=pltpu.VMEM)
    return pl.pallas_call(
        functools.partial(own_kernel, chunk, per, groups, len(accs)),
        out_shape=[
            jax.ShapeDtypeStruct((slots * rows, hidden), jnp.float32),
            jax.ShapeDtypeStruct((rows, hidden), jnp.float32),
        ],
        in_specs=[smem] + [vmem] * (4 + len(accs)),
        out_specs=[vmem] * 2,
        scratch_shapes=[pltpu.VMEM((groups * UNIT, hidden), jnp.float32)],
        compiler_params=pltpu.CompilerParams(vmem_limit_bytes=(12 << 20) + accs[0].size * 4 * len(accs)),
        cost_estimate=pl.CostEstimate(
            flops=4 * slots * rows * PART * len(accs) * hidden, bytes_accessed=2 << 20, transcendentals=0),
        name="own_terms",
    )(ids, wo, wp, xo, so, *accs)


def combine_kernel(slots, rows, ways, own, *refs):
    parts = len(refs) - ways - 1
    coded, outs, tail = refs[:parts], refs[parts:parts + ways], refs[parts + ways]
    values = [read_coded(a, slots, rows) for a in coded]

    def total(s):
        got = own[s * rows:(s + 1) * rows, :]
        for value in values:
            got = got + value(s)
        return got

    for i in range(slots // ways):
        outs[0][i * rows:(i + 1) * rows, :] = total(i * ways)
    for k in range(1, ways):
        write_coded(outs[k], tail, slots // ways, rows, lambda s: total(s * ways + k))


def combine(slots, rows, ways, own, coded):
    width = own.shape[1]
    left = slots // ways
    vmem = pl.BlockSpec(memory_space=pltpu.VMEM)
    out = jax.ShapeDtypeStruct((left * rows + tail_rows(left), width), jnp.int16)
    return pl.pallas_call(
        functools.partial(combine_kernel, slots, rows, ways),
        out_shape=[jax.ShapeDtypeStruct((left * rows, width), jnp.float32)] + [out] * (ways - 1),
        in_specs=[vmem] * (1 + len(coded)),
        out_specs=[vmem] * ways,
        scratch_shapes=[pltpu.VMEM((tail_rows(left), width), jnp.float32)],
        compiler_params=pltpu.CompilerParams(vmem_limit_bytes=32 * 1024 * 1024),
        name="combine",
    )(own, *coded)


def hidden_kernel(chunks, parts, rows, *refs):
    out = refs[chunks * parts + 1]
    for c in range(chunks):
        own, self, coded = refs[c * parts], refs[c * parts + 1], refs[c * parts + 2:(c + 1) * parts]
        total = own[:rows, :] + self[...]
        for a in coded:
            total = total + read_coded(a, 1, rows)(0)
        out[c * rows:(c + 1) * rows, :] = jnp.maximum(total, 0.0).astype(jnp.bfloat16)


def hidden_rows(chunk_parts, rows, sel):
    chunks, parts = len(chunk_parts), len(chunk_parts[0])
    width = chunk_parts[0][0].shape[1]
    vmem = pl.BlockSpec(memory_space=pltpu.VMEM)
    flat = [a for part in chunk_parts for a in part]
    return pl.pallas_call(
        functools.partial(hidden_kernel, chunks, parts, rows),
        out_shape=jax.ShapeDtypeStruct((chunks * rows, width), jnp.bfloat16),
        in_specs=[vmem] * (len(flat) + 1),
        out_specs=vmem,
        compiler_params=pltpu.CompilerParams(vmem_limit_bytes=32 * 1024 * 1024),
        name="hidden_rows",
    )(*flat, sel)


def send_kernel(own, other, sel, send):
    both = jnp.concatenate([own[...], other[...]], axis=0)
    send[...] = jnp.dot(sel[...], both, preferred_element_type=jnp.float32).astype(jnp.bfloat16)


def rows_to_send(own, other, sel):
    vmem = pl.BlockSpec(memory_space=pltpu.VMEM)
    return pl.pallas_call(
        send_kernel,
        out_shape=jax.ShapeDtypeStruct((sel.shape[0], own.shape[1]), jnp.bfloat16),
        in_specs=[vmem] * 3,
        out_specs=vmem,
        compiler_params=pltpu.CompilerParams(vmem_limit_bytes=32 * 1024 * 1024),
        name="rows_to_send",
    )(own, other, sel)


def logits_kernel(own, other, received, front, adj_received, w_self, w_neigh, out):
    rows = out.shape[0]
    both = jnp.concatenate([own[...], other[...]], axis=0)
    local = jnp.dot(front[...], both, preferred_element_type=jnp.float32)
    mean = local[:rows, :] + jnp.dot(adj_received[...], received[...], preferred_element_type=jnp.float32)
    dims = (((1,), (1,)), ((), ()))
    got = lax.dot_general(local[rows:, :].astype(jnp.bfloat16), w_self[...], dims, preferred_element_type=jnp.float32)
    got = got + lax.dot_general(mean.astype(jnp.bfloat16), w_neigh[...], dims, preferred_element_type=jnp.float32)
    out[...] = got


def logits_of(own, other, received, front, adj_received, w_self, w_neigh):
    vmem = pl.BlockSpec(memory_space=pltpu.VMEM)
    return pl.pallas_call(
        logits_kernel,
        out_shape=jax.ShapeDtypeStruct((adj_received.shape[0], w_self.shape[1]), jnp.float32),
        in_specs=[vmem] * 7,
        out_specs=vmem,
        compiler_params=pltpu.CompilerParams(vmem_limit_bytes=32 * 1024 * 1024),
        name="logits",
    )(own, other, received, front, adj_received, w_self.T, w_neigh.T)


def exchange(parts, stride, n, places):
    got = [parts[0]]
    for k in places:
        got.append(lax.ppermute(parts[k], "dom", [(i, i ^ (k * stride)) for i in range(n)]))
    return got


def body(
    features,
    tile_weight,
    tile_dst,
    tile_src,
    tile_rows,
    w_self1,
    neighbour_weight_first,
    send_list,
    send_count,
    adj_two,
    w_self2,
    w_neigh2,
):
    n = lax.axis_size("dom")
    tile = tile_weight.shape[1]
    groups = tile // UNIT
    per = groups // 2 // CHUNKS
    bits = n.bit_length() - 1
    assert n == 1 << bits and bits >= 2
    radices = [2] * (bits // 2) + [1] * (bits % 2)
    ids = jnp.stack([lax.axis_index("feat"), lax.axis_index("dom")]).astype(jnp.int32)
    swap = [(0, 1), (1, 0)]
    xp = lax.ppermute(features, "feat", swap)
    wp = lax.ppermute(neighbour_weight_first, "feat", swap)
    tw = tile_weight.reshape(tile_weight.shape[0], groups, UNIT, tile)
    planned = plan(
        CHUNKS, per, n, 4, ids, tile_src, tile_rows, tile_dst, tw, features,
    )
    tables, tbufs, xo = planned[:CHUNKS], planned[CHUNKS:2 * CHUNKS], planned[2 * CHUNKS]
    wo, so = neighbour_weight_first, w_self1
    done = []
    for chunk in range(CHUNKS):
        accs = gathered_sums(per, n, tables[chunk], tbufs[chunk], xo, xp)
        slots, rows = n // 4, per * UNIT
        parts = dict(enumerate(sent_terms(4, slots, rows, accs, wo, wp), 1))
        parts[0], theirs = own_terms(chunk, per, groups, slots, ids, accs, wo, wp, xo, so)
        self = lax.ppermute(theirs, "feat", swap)
        got = exchange(parts, 1, n, (3, 2, 1))
        stride = 4
        for radix in radices[1:]:
            ways = 1 << radix
            parts = combine(n // stride, per * UNIT, ways, got[0], got[1:])
            got = exchange(parts, stride, n, (2, 3, 1) if ways == 4 else (1,))
            stride *= ways
        done.append([got[0], self] + got[1:])
    sel, front, adj_received = selection(groups, ids, send_list, send_count, adj_two)
    own = hidden_rows(done, per * UNIT, sel)
    other = lax.ppermute(own, "feat", swap)
    send = rows_to_send(own, other, sel)
    received = lax.all_to_all(send, "dom", 0, 0, axis_index_groups=[group_order(n)], tiled=True)
    return logits_of(own, other, received, front, adj_received, w_self2, w_neigh2)


def solution(mesh):
    in_specs = (
        P("dom", "feat"),
        P("dom", None, None),
        P("dom"),
        P("dom"),
        P("dom"),
        P("feat", None),
        P("feat", None),
        P(),
        P(),
        P("dom", None),
        P(),
        P(),
    )
    out_specs = P("dom", None)
    return jax.shard_map(body, mesh=mesh, in_specs=in_specs, out_specs=out_specs, check_vma=False)
```

```python
import functools

import jax
import jax.numpy as jnp
from jax import lax
from jax.experimental import pallas as pl
from jax.experimental.pallas import tpu as pltpu
from jax.sharding import PartitionSpec as P

UNIT = 16
BLOCK = 8
STEP = 8
PART = 256
CHUNKS = 1


def group_of(core, place, groups):
    return 2 * place + 1 - core


def group_order(n):
    return list(range(n - 1, -1, -1))


LN2 = 0.6931471805599453


def tail_rows(slots):
    return -(-slots // 8) * 8


def encode(x):
    top = jnp.max(jnp.abs(x), axis=0, keepdims=True)
    power = jnp.ceil(jnp.log(jnp.maximum(top, 1e-30)) * (1.0 / LN2) + 1e-3) - 15.0
    return jnp.floor(x * jnp.exp(power * -LN2) + 0.5), power


def to_int16(x):
    return x.astype(jnp.int32).astype(jnp.int16)


def write_coded(out, tail, slots, rows, value_of):
    tail[...] = jnp.zeros_like(tail)
    for s in range(slots):
        whole, power = encode(value_of(s))
        out[s * rows:(s + 1) * rows, :] = to_int16(whole)
        tail[s:s + 1, :] = power
    out[slots * rows:, :] = to_int16(tail[...])


def read_coded(ref, slots, rows):
    powers = ref[slots * rows:, :].astype(jnp.int32).astype(jnp.float32)

    def value_of(s):
        whole = ref[s * rows:(s + 1) * rows, :].astype(jnp.int32).astype(jnp.float32)
        return whole * jnp.exp(powers[s:s + 1, :] * LN2)

    return value_of


def plan_kernel(chunks, per, n, radix, n_src, ids, src_h, rows_h, dst_h, tw, xo, *rest):
    tables, rest = rest[:chunks], rest[chunks:]
    tbufs, rest = rest[:chunks], rest[chunks:]
    xo_out, src_v, rows_v, dst_v, sems = rest
    core, me = ids[0], ids[1]
    tiles = src_v.shape[1]
    n_pos = tables[0].shape[1]
    units = per * tiles
    groups = 2 * per * chunks
    half = groups // 2
    gs = [group_of(core, i, groups) for i in range(half)]
    small = [(src_h, src_v), (rows_h, rows_v), (dst_h, dst_v)]
    large = [(tw.at[:, g], tbufs[i // per].at[pl.ds(i % per * tiles, tiles)]) for i, g in enumerate(gs)]
    large += [(xo, xo_out)]
    copies = [pltpu.make_async_copy(a, b, sems.at[i]) for i, (a, b) in enumerate(small + large)]
    for c in copies:
        c.start()
    lane = lax.broadcasted_iota(jnp.int32, (1, tiles), 1)
    block_i = lax.broadcasted_iota(jnp.int32, (n_src, tiles), 0)
    before = lax.broadcasted_iota(jnp.int32, (units, units), 0) < lax.broadcasted_iota(jnp.int32, (units, units), 1)
    before = jnp.where(before, 1.0, 0.0).astype(jnp.bfloat16)
    pos_i = lax.broadcasted_iota(jnp.int32, (tiles, n_pos), 1).astype(jnp.float32)
    place_i = lax.broadcasted_iota(jnp.int32, (1, n_pos), 1)
    trash = float(n * per << 14)
    for c in copies[:3]:
        c.wait()
    src, rows = src_v[...], rows_v[...]
    slot = jnp.bitwise_xor(dst_v[...], me)
    slot = jnp.bitwise_and(slot, radix - 1) * (n // radix) + lax.div(slot, radix)
    for c in range(chunks):
        hot, words, valid = [], [], []
        for j in range(per):
            limit = jnp.clip(rows - UNIT * gs[c * per + j], 0, UNIT)
            ok = limit > 0
            valid.append(ok)
            words.append(((slot * per + j) * 512 + (j * tiles + lane)) * 32 + limit)
            hot.append(jnp.where(jnp.logical_and(block_i == src, ok), 1.0, 0.0))
        hot = jnp.concatenate(hot, axis=1)
        earlier = jnp.dot(hot.astype(jnp.bfloat16), before, preferred_element_type=jnp.float32)
        blocks = jnp.floor((jnp.sum(hot, axis=1, keepdims=True) + (BLOCK - 1)) * (1.0 / BLOCK))
        ahead = jnp.zeros(blocks.shape, jnp.float32)
        source_i = lax.broadcasted_iota(jnp.int32, blocks.shape, 0)
        for s in range(n_src - 1):
            ahead = ahead + jnp.where(source_i > s, blocks[s:s + 1, :], 0.0)
        pos = jnp.sum(hot * (earlier + ahead * BLOCK), axis=0, keepdims=True)
        behind = jnp.where(place_i.astype(jnp.float32) >= ahead + blocks, 1.0, 0.0)
        owner = jnp.sum(behind, axis=0, keepdims=True)
        run = ahead[n_src - 1:, :] + blocks[n_src - 1:, :]
        stack = [jnp.where(valid[j], pos[:, j * tiles:(j + 1) * tiles], -1.0) for j in range(per)]
        stack += [w.astype(jnp.float32) - trash for w in words]
        stack += [jnp.zeros((1, tiles), jnp.float32)] * (-len(stack) % 8)
        cols = jnp.concatenate(stack, axis=0).T
        found = jnp.zeros((tiles, n_pos), jnp.float32)
        for j in range(per):
            found = found + jnp.where(cols[:, j:j + 1] == pos_i, cols[:, per + j:per + j + 1], 0.0)
        word = jnp.sum(found, axis=0, keepdims=True) + trash
        owner = jnp.where(place_i == n_pos - 1, run, jnp.minimum(owner, n_src - 1.0))
        tables[c][0:1, :] = word.astype(jnp.int32)
        tables[c][1:2, :] = owner.astype(jnp.int32)

    for c in copies[3:]:
        c.wait()


def plan(chunks, per, n, radix, ids, src, rows, dst, tw, xo):
    tiles, _, _, tile = tw.shape
    n_src = xo.shape[0] // tile
    blocks = -(-(per * tiles // BLOCK + n_src) // STEP) * STEP
    n_pos = -(-(blocks * BLOCK + 1) // 128) * 128
    smem = pl.BlockSpec(memory_space=pltpu.SMEM)
    vmem = pl.BlockSpec(memory_space=pltpu.VMEM)
    hbm = pl.BlockSpec(memory_space=pltpu.HBM)
    half = chunks * per
    return pl.pallas_call(
        functools.partial(plan_kernel, chunks, per, n, radix, n_src),
        out_shape=[jax.ShapeDtypeStruct((2, n_pos), jnp.int32)] * chunks
        + [jax.ShapeDtypeStruct((per * tiles, UNIT, tile), tw.dtype)] * chunks
        + [jax.ShapeDtypeStruct(xo.shape, xo.dtype)],
        in_specs=[smem] + [hbm] * 5,
        out_specs=[vmem] * (2 * chunks + 1),
        scratch_shapes=[
            pltpu.VMEM((1, tiles), jnp.int32),
            pltpu.VMEM((1, tiles), jnp.int32),
            pltpu.VMEM((1, tiles), jnp.int32),
            pltpu.SemaphoreType.DMA((3 + half + 1,)),
        ],
        compiler_params=pltpu.CompilerParams(vmem_limit_bytes=32 * 1024 * 1024),
        name="plan",
    )(ids, *[
        pltpu.with_memory_space_constraint(a, pltpu.HBM)
        for a in (src.reshape(1, tiles), rows.reshape(1, tiles), dst.reshape(1, tiles), tw, xo)
    ])


def select_kernel(groups, ids, lists, counts, adj, sel, front, adj_out):
    core, me = ids[0], ids[1]
    n = lists.shape[0]
    slots = lists.shape[1]
    total = n * slots
    q_n = lax.broadcasted_iota(jnp.int32, (total, n), 0)
    r_n = lax.broadcasted_iota(jnp.int32, (total, n), 1)
    mine = lists[me].astype(jnp.float32)
    cnt = counts[pl.ds(me, 1), :]
    picked = jnp.zeros((total, n), jnp.float32)
    k_n = jnp.bitwise_and(q_n, slots - 1)
    for k in range(slots):
        picked = jnp.where(k_n == k, mine[k:k + 1, :], picked)
    good = jnp.logical_and(n - 1 - lax.div(q_n, slots) == r_n, k_n < cnt)
    row = jnp.sum(jnp.where(good, picked + 1.0, 0.0), axis=1, keepdims=True) - 1.0
    lane = lax.broadcasted_iota(jnp.int32, (1, sel.shape[1]), 1)
    name = jnp.zeros(lane.shape, jnp.int32)
    names = [group_of(c, i, groups) for c in (core, 1 - core) for i in range(groups // 2)]
    for i, g in enumerate(names):
        name = jnp.where(lax.div(lane, UNIT) == i, g * UNIT + jnp.bitwise_and(lane, UNIT - 1), name)
    sel[...] = jnp.where(row == name.astype(jnp.float32), 1.0, 0.0).astype(jnp.bfloat16)
    tile, out_rows = groups * UNIT, adj.shape[0]
    placed = jnp.where(lax.broadcasted_iota(jnp.int32, (tile, tile), 0) == name, 1.0, 0.0).astype(jnp.bfloat16)
    front[:out_rows, :] = jnp.dot(adj[:, :tile], placed, preferred_element_type=jnp.float32).astype(jnp.bfloat16)
    front[out_rows:, :] = placed[:out_rows, :]
    column = lax.broadcasted_iota(jnp.int32, (1, total), 1)
    source = (n - 1 - lax.div(column, slots)) * slots + lax.rem(column, slots)
    moved = jnp.where(lax.broadcasted_iota(jnp.int32, (total, total), 0) == source, 1.0, 0.0).astype(jnp.bfloat16)
    adj_out[...] = jnp.dot(adj[:, groups * UNIT:], moved, preferred_element_type=jnp.float32).astype(jnp.bfloat16)


def selection(groups, ids, send_list, send_count, adj):
    n, _, slots = send_list.shape
    smem = pl.BlockSpec(memory_space=pltpu.SMEM)
    vmem = pl.BlockSpec(memory_space=pltpu.VMEM)
    return pl.pallas_call(
        functools.partial(select_kernel, groups),
        out_shape=[
            jax.ShapeDtypeStruct((n * slots, groups * UNIT), jnp.bfloat16),
            jax.ShapeDtypeStruct((2 * adj.shape[0], groups * UNIT), jnp.bfloat16),
            jax.ShapeDtypeStruct((adj.shape[0], n * slots), jnp.bfloat16),
        ],
        in_specs=[smem, vmem, vmem, vmem],
        out_specs=[vmem] * 3,
        compiler_params=pltpu.CompilerParams(vmem_limit_bytes=32 * 1024 * 1024),
        name="selection",
    )(ids, jnp.swapaxes(send_list, 1, 2), send_count, adj)


def tiles_kernel(table_v, tbuf, xo, xp, *rest):
    parts = len(rest) - 3
    accs, (masks, table, sem) = rest[:parts], rest[parts:]
    tile = tbuf.shape[2]
    width = xo.shape[1]
    to_scalar = pltpu.make_async_copy(table_v, table, sem)
    to_scalar.start()
    for acc in accs:
        acc[...] = jnp.zeros_like(acc)
    row_i = lax.broadcasted_iota(jnp.int32, (UNIT, tile), 0)
    for m in range(UNIT + 1):
        masks[m] = jnp.where(row_i < m, 1.0, 0.0).astype(jnp.bfloat16)
    columns = [(x, h) for x in (xo, xp) for h in range(0, width, PART)]
    to_scalar.wait()

    def blocks(first, count):
        for m in range(count):
            at = first + m
            base = pl.multiple_of(table[1, at] * tile, tile)
            rows, places = [], []
            for k in range(BLOCK):
                word = table[0, at * BLOCK + k]
                u = jnp.bitwise_and(lax.shift_right_logical(word, 5), 511)
                rows.append(tbuf[u] * masks[jnp.bitwise_and(word, 31)])
                places.append(pl.multiple_of(lax.shift_right_logical(word, 14) * UNIT, UNIT))
            lhs = jnp.concatenate(rows, axis=0)
            for acc, (x, h) in zip(accs, columns):
                got = jnp.dot(lhs, x[pl.ds(base, tile), h:h + PART], preferred_element_type=jnp.float32)
                got = got.astype(jnp.bfloat16).astype(jnp.float32)
                for k in range(BLOCK):
                    acc[pl.ds(places[k], UNIT), :] += got[k * UNIT:(k + 1) * UNIT, :]

    half = STEP // 2
    halves = lax.div(table[1, table.shape[1] - 1] + half - 1, half)
    steps = lax.div(halves, 2)

    def step(i, carry):
        blocks(i * STEP, STEP)
        return carry

    def last(i, carry):
        blocks(steps * STEP, half)
        return carry

    lax.fori_loop(0, steps, step, 0)
    lax.fori_loop(0, lax.rem(halves, 2), last, 0)


def gathered_sums(per, n, table, tbuf, xo, xp):
    width = xo.shape[1]
    tile = tbuf.shape[2]
    vmem = pl.BlockSpec(memory_space=pltpu.VMEM)
    flops = 2 * tbuf.shape[0] * UNIT * tile * 2 * width
    parts = 2 * width // PART
    sums = jax.ShapeDtypeStruct(((n * per + 1) * UNIT, PART), jnp.float32)
    return pl.pallas_call(
        tiles_kernel,
        out_shape=[sums] * parts,
        in_specs=[vmem] * 4,
        out_specs=[vmem] * parts,
        scratch_shapes=[
            pltpu.VMEM((UNIT + 1, UNIT, tile), jnp.bfloat16),
            pltpu.SMEM(table.shape, jnp.int32),
            pltpu.SemaphoreType.DMA,
        ],
        compiler_params=pltpu.CompilerParams(vmem_limit_bytes=(12 << 20) + sums.size * 4 * parts),
        cost_estimate=pl.CostEstimate(flops=flops, bytes_accessed=8 << 20, transcendentals=0),
        name="gathered_sums",
    )(table, tbuf, xo, xp)


def weigh(accs, weights, first, count, out):
    size = min(256, count)

    def piece(r, carry):
        at = pl.multiple_of(r * size, size)
        got = jnp.zeros((size, out.shape[1]), jnp.float32)
        for i, acc in enumerate(accs):
            w, h = weights[i * PART // weights[0].shape[0]], i * PART % weights[0].shape[0]
            value = acc[pl.ds(first + at, size), :]
            high = value.astype(jnp.bfloat16)
            low = (value - high.astype(jnp.float32)).astype(jnp.bfloat16)
            got = got + jnp.dot(high, w[h:h + PART, :], preferred_element_type=jnp.float32)
            got = got + jnp.dot(low, w[h:h + PART, :], preferred_element_type=jnp.float32)
        out[pl.ds(at, size), :] = got
        return carry

    lax.fori_loop(0, count // size, piece, 0)


def sent_kernel(k, slots, rows, parts, wo, wp, *refs):
    accs, (out, sums, tail) = refs[:parts], refs[parts:]
    weigh(accs, (wo, wp), k * slots * rows, slots * rows, sums)
    write_coded(out, tail, slots, rows, lambda s: sums[s * rows:(s + 1) * rows, :])


def sent_terms(k, slots, rows, accs, wo, wp):
    hidden = wo.shape[1]
    vmem = pl.BlockSpec(memory_space=pltpu.VMEM)
    return pl.pallas_call(
        functools.partial(sent_kernel, k, slots, rows, len(accs)),
        out_shape=jax.ShapeDtypeStruct((slots * rows + tail_rows(slots), hidden), jnp.int16),
        in_specs=[vmem] * (2 + len(accs)),
        out_specs=vmem,
        scratch_shapes=[
            pltpu.VMEM((slots * rows, hidden), jnp.float32),
            pltpu.VMEM((tail_rows(slots), hidden), jnp.float32),
        ],
        compiler_params=pltpu.CompilerParams(vmem_limit_bytes=(12 << 20) + accs[0].size * 4 * len(accs)),
        cost_estimate=pl.CostEstimate(
            flops=4 * slots * rows * PART * len(accs) * hidden, bytes_accessed=2 << 20, transcendentals=0),
        name="sent_terms",
    )(wo, wp, *accs)


def own_kernel(chunk, per, groups, parts, ids, wo, wp, xo, so, *refs):
    accs, (out, theirs, terms) = refs[:parts], refs[parts:]
    weigh(accs, (wo, wp), 0, out.shape[0], out)
    terms[...] = jnp.dot(xo[:groups * UNIT, :], so[...], preferred_element_type=jnp.float32)
    for j in range(per):
        here = slice(j * UNIT, (j + 1) * UNIT)
        at = pl.multiple_of(group_of(ids[0], chunk * per + j, groups) * UNIT, UNIT)
        out[here, :] += terms[pl.ds(at, UNIT), :]
        at = pl.multiple_of(group_of(1 - ids[0], chunk * per + j, groups) * UNIT, UNIT)
        theirs[here, :] = terms[pl.ds(at, UNIT), :]


def own_terms(chunk, per, groups, slots, ids, accs, wo, wp, xo, so):
    hidden = wo.shape[1]
    rows = per * UNIT
    smem = pl.BlockSpec(memory_space=pltpu.SMEM)
    vmem = pl.BlockSpec(memory_space=pltpu.VMEM)
    return pl.pallas_call(
        functools.partial(own_kernel, chunk, per, groups, len(accs)),
        out_shape=[
            jax.ShapeDtypeStruct((slots * rows, hidden), jnp.float32),
            jax.ShapeDtypeStruct((rows, hidden), jnp.float32),
        ],
        in_specs=[smem] + [vmem] * (4 + len(accs)),
        out_specs=[vmem] * 2,
        scratch_shapes=[pltpu.VMEM((groups * UNIT, hidden), jnp.float32)],
        compiler_params=pltpu.CompilerParams(vmem_limit_bytes=(12 << 20) + accs[0].size * 4 * len(accs)),
        cost_estimate=pl.CostEstimate(
            flops=4 * slots * rows * PART * len(accs) * hidden, bytes_accessed=2 << 20, transcendentals=0),
        name="own_terms",
    )(ids, wo, wp, xo, so, *accs)


def combine_kernel(slots, rows, ways, own, *refs):
    parts = len(refs) - ways - 1
    coded, outs, tail = refs[:parts], refs[parts:parts + ways], refs[parts + ways]
    values = [read_coded(a, slots, rows) for a in coded]

    def total(s):
        got = own[s * rows:(s + 1) * rows, :]
        for value in values:
            got = got + value(s)
        return got

    for i in range(slots // ways):
        outs[0][i * rows:(i + 1) * rows, :] = total(i * ways)
    for k in range(1, ways):
        write_coded(outs[k], tail, slots // ways, rows, lambda s: total(s * ways + k))


def combine(slots, rows, ways, own, coded):
    width = own.shape[1]
    left = slots // ways
    vmem = pl.BlockSpec(memory_space=pltpu.VMEM)
    out = jax.ShapeDtypeStruct((left * rows + tail_rows(left), width), jnp.int16)
    return pl.pallas_call(
        functools.partial(combine_kernel, slots, rows, ways),
        out_shape=[jax.ShapeDtypeStruct((left * rows, width), jnp.float32)] + [out] * (ways - 1),
        in_specs=[vmem] * (1 + len(coded)),
        out_specs=[vmem] * ways,
        scratch_shapes=[pltpu.VMEM((tail_rows(left), width), jnp.float32)],
        compiler_params=pltpu.CompilerParams(vmem_limit_bytes=32 * 1024 * 1024),
        name="combine",
    )(own, *coded)


def hidden_kernel(chunks, parts, rows, *refs):
    out = refs[chunks * parts + 1]
    for c in range(chunks):
        own, self, coded = refs[c * parts], refs[c * parts + 1], refs[c * parts + 2:(c + 1) * parts]
        total = own[:rows, :] + self[...]
        for a in coded:
            total = total + read_coded(a, 1, rows)(0)
        out[c * rows:(c + 1) * rows, :] = jnp.maximum(total, 0.0).astype(jnp.bfloat16)


def hidden_rows(chunk_parts, rows, sel):
    chunks, parts = len(chunk_parts), len(chunk_parts[0])
    width = chunk_parts[0][0].shape[1]
    vmem = pl.BlockSpec(memory_space=pltpu.VMEM)
    flat = [a for part in chunk_parts for a in part]
    return pl.pallas_call(
        functools.partial(hidden_kernel, chunks, parts, rows),
        out_shape=jax.ShapeDtypeStruct((chunks * rows, width), jnp.bfloat16),
        in_specs=[vmem] * (len(flat) + 1),
        out_specs=vmem,
        compiler_params=pltpu.CompilerParams(vmem_limit_bytes=32 * 1024 * 1024),
        name="hidden_rows",
    )(*flat, sel)


def send_kernel(own, other, sel, send):
    both = jnp.concatenate([own[...], other[...]], axis=0)
    send[...] = jnp.dot(sel[...], both, preferred_element_type=jnp.float32).astype(jnp.bfloat16)


def rows_to_send(own, other, sel):
    vmem = pl.BlockSpec(memory_space=pltpu.VMEM)
    return pl.pallas_call(
        send_kernel,
        out_shape=jax.ShapeDtypeStruct((sel.shape[0], own.shape[1]), jnp.bfloat16),
        in_specs=[vmem] * 3,
        out_specs=vmem,
        compiler_params=pltpu.CompilerParams(vmem_limit_bytes=32 * 1024 * 1024),
        name="rows_to_send",
    )(own, other, sel)


def logits_kernel(own, other, received, front, adj_received, w_self, w_neigh, out):
    rows = out.shape[0]
    both = jnp.concatenate([own[...], other[...]], axis=0)
    local = jnp.dot(front[...], both, preferred_element_type=jnp.float32)
    mean = local[:rows, :] + jnp.dot(adj_received[...], received[...], preferred_element_type=jnp.float32)
    dims = (((1,), (1,)), ((), ()))
    got = lax.dot_general(local[rows:, :].astype(jnp.bfloat16), w_self[...], dims, preferred_element_type=jnp.float32)
    got = got + lax.dot_general(mean.astype(jnp.bfloat16), w_neigh[...], dims, preferred_element_type=jnp.float32)
    out[...] = got


def logits_of(own, other, received, front, adj_received, w_self, w_neigh):
    vmem = pl.BlockSpec(memory_space=pltpu.VMEM)
    return pl.pallas_call(
        logits_kernel,
        out_shape=jax.ShapeDtypeStruct((adj_received.shape[0], w_self.shape[1]), jnp.float32),
        in_specs=[vmem] * 7,
        out_specs=vmem,
        compiler_params=pltpu.CompilerParams(vmem_limit_bytes=32 * 1024 * 1024),
        name="logits",
    )(own, other, received, front, adj_received, w_self.T, w_neigh.T)


def exchange(parts, stride, n, places):
    got = [parts[0]]
    for k in places:
        got.append(lax.ppermute(parts[k], "dom", [(i, i ^ (k * stride)) for i in range(n)]))
    return got


def body(
    features,
    tile_weight,
    tile_dst,
    tile_src,
    tile_rows,
    w_self1,
    neighbour_weight_first,
    send_list,
    send_count,
    adj_two,
    w_self2,
    w_neigh2,
):
    n = lax.axis_size("dom")
    tile = tile_weight.shape[1]
    groups = tile // UNIT
    per = groups // 2 // CHUNKS
    bits = n.bit_length() - 1
    assert n == 1 << bits and bits >= 2
    radices = [2] * (bits // 2) + [1] * (bits % 2)
    ids = jnp.stack([lax.axis_index("feat"), lax.axis_index("dom")]).astype(jnp.int32)
    swap = [(0, 1), (1, 0)]
    xp = lax.ppermute(features, "feat", swap)
    wp = lax.ppermute(neighbour_weight_first, "feat", swap)
    tw = tile_weight.reshape(tile_weight.shape[0], groups, UNIT, tile)
    planned = plan(
        CHUNKS, per, n, 4, ids, tile_src, tile_rows, tile_dst, tw, features,
    )
    tables, tbufs, xo = planned[:CHUNKS], planned[CHUNKS:2 * CHUNKS], planned[2 * CHUNKS]
    wo, so = neighbour_weight_first, w_self1
    done = []
    for chunk in range(CHUNKS):
        accs = gathered_sums(per, n, tables[chunk], tbufs[chunk], xo, xp)
        slots, rows = n // 4, per * UNIT
        parts = {k: sent_terms(k, slots, rows, accs, wo, wp) for k in (1, 2, 3)}
        parts[0], theirs = own_terms(chunk, per, groups, slots, ids, accs, wo, wp, xo, so)
        self = lax.ppermute(theirs, "feat", swap)
        got = exchange(parts, 1, n, (1, 2, 3))
        stride = 4
        for radix in radices[1:]:
            ways = 1 << radix
            parts = combine(n // stride, per * UNIT, ways, got[0], got[1:])
            got = exchange(parts, stride, n, (2, 3, 1) if ways == 4 else (1,))
            stride *= ways
        done.append([got[0], self] + got[1:])
    sel, front, adj_received = selection(groups, ids, send_list, send_count, adj_two)
    own = hidden_rows(done, per * UNIT, sel)
    other = lax.ppermute(own, "feat", swap)
    send = rows_to_send(own, other, sel)
    received = lax.all_to_all(send, "dom", 0, 0, axis_index_groups=[group_order(n)], tiled=True)
    return logits_of(own, other, received, front, adj_received, w_self2, w_neigh2)


def solution(mesh):
    in_specs = (
        P("dom", "feat"),
        P("dom", None, None),
        P("dom"),
        P("dom"),
        P("dom"),
        P("feat", None),
        P("feat", None),
        P(),
        P(),
        P("dom", None),
        P(),
        P(),
    )
    out_specs = P("dom", None)
    return jax.shard_map(body, mesh=mesh, in_specs=in_specs, out_specs=out_specs, check_vma=False)
```

```python
import functools

import jax
import jax.numpy as jnp
from jax import lax
from jax.experimental import pallas as pl
from jax.experimental.pallas import tpu as pltpu
from jax.sharding import PartitionSpec as P

UNIT = 16
BLOCK = 8
STEP = 8
PART = 256
CHUNKS = 1


def group_of(core, place, groups):
    pair = 2 * (place // 2) + core
    return pair if place % 2 == 0 else groups - 1 - pair


def group_order(n):
    return list(range(n - 1, -1, -1))


KINDS = 3
LN2 = 0.6931471805599453


def tail_rows(slots):
    return -(-slots // 8) * 8


def encode(x):
    top = jnp.max(jnp.abs(x), axis=0, keepdims=True)
    power = jnp.ceil(jnp.log(jnp.maximum(top, 1e-30)) * (1.0 / LN2) + 1e-3) - 15.0
    return jnp.floor(x * jnp.exp(power * -LN2) + 0.5), power


def to_int16(x):
    return x.astype(jnp.int32).astype(jnp.int16)


def write_coded(out, tail, slots, rows, value_of):
    tail[...] = jnp.zeros_like(tail)
    for s in range(slots):
        whole, power = encode(value_of(s))
        out[s * rows:(s + 1) * rows, :] = to_int16(whole)
        tail[s:s + 1, :] = power
    out[slots * rows:, :] = to_int16(tail[...])


def read_coded(ref, slots, rows):
    powers = ref[slots * rows:, :].astype(jnp.int32).astype(jnp.float32)

    def value_of(s):
        whole = ref[s * rows:(s + 1) * rows, :].astype(jnp.int32).astype(jnp.float32)
        return whole * jnp.exp(powers[s:s + 1, :] * LN2)

    return value_of


def trash_of(n, per, radix):
    return (radix - 2) * (n // radix) * per


def plan_kernel(chunks, per, n, radix, n_src, ids, src_h, rows_h, dst_h, tw, xo, *rest):
    tables, rest = rest[:chunks], rest[chunks:]
    tbufs, rest = rest[:chunks], rest[chunks:]
    xo_out, src_v, rows_v, dst_v, sems = rest
    core, me = ids[0], ids[1]
    tiles = src_v.shape[1]
    n_pos = tables[0].shape[1]
    units = per * tiles
    groups = 2 * per * chunks
    half = groups // 2
    gs = [group_of(core, i, groups) for i in range(half)]
    small = [(src_h, src_v), (rows_h, rows_v), (dst_h, dst_v)]
    large = [(tw.at[:, g], tbufs[i // per].at[pl.ds(i % per * tiles, tiles)]) for i, g in enumerate(gs)]
    large += [(xo, xo_out)]
    copies = [pltpu.make_async_copy(a, b, sems.at[i]) for i, (a, b) in enumerate(small + large)]
    for c in copies:
        c.start()
    lane = lax.broadcasted_iota(jnp.int32, (1, tiles), 1)
    block_i = lax.broadcasted_iota(jnp.int32, (KINDS * n_src, tiles), 0)
    before = lax.broadcasted_iota(jnp.int32, (units, units), 0) < lax.broadcasted_iota(jnp.int32, (units, units), 1)
    before = jnp.where(before, 1.0, 0.0).astype(jnp.bfloat16)
    pos_i = lax.broadcasted_iota(jnp.int32, (tiles, n_pos), 1).astype(jnp.float32)
    place_i = lax.broadcasted_iota(jnp.int32, (1, n_pos), 1)
    trash = float(trash_of(n, per, radix) << 14)
    for c in copies[:3]:
        c.wait()
    src, rows = src_v[...], rows_v[...]
    slot = jnp.bitwise_xor(dst_v[...], me)
    partner = jnp.bitwise_and(slot, radix - 1)
    kind = jnp.where(partner == radix - 1, 0, jnp.where(partner > 0, 1, 2))
    slot = lax.div(slot, radix) + jnp.where(kind == 1, partner - 1, 0) * (n // radix)
    cell = kind * n_src + src
    cells = KINDS * n_src
    for c in range(chunks):
        hot, words, valid = [], [], []
        for j in range(per):
            limit = jnp.clip(rows - UNIT * gs[c * per + j], 0, UNIT)
            ok = limit > 0
            valid.append(ok)
            words.append(((slot * per + j) * 512 + (j * tiles + lane)) * 32 + limit)
            hot.append(jnp.where(jnp.logical_and(block_i == cell, ok), 1.0, 0.0))
        hot = jnp.concatenate(hot, axis=1)
        earlier = jnp.dot(hot.astype(jnp.bfloat16), before, preferred_element_type=jnp.float32)
        blocks = jnp.floor((jnp.sum(hot, axis=1, keepdims=True) + (BLOCK - 1)) * (1.0 / BLOCK))
        half_step = STEP // 2
        ahead = jnp.zeros(blocks.shape, jnp.float32)
        cell_i = lax.broadcasted_iota(jnp.int32, blocks.shape, 0)
        starts = [jnp.zeros((1, 1), jnp.float32)]
        for k in range(KINDS):
            count = jnp.zeros((1, 1), jnp.float32)
            for s in range(k * n_src, (k + 1) * n_src):
                here = blocks[s:s + 1, :]
                ahead = ahead + jnp.where(jnp.logical_and(cell_i > s, cell_i < (k + 1) * n_src), here, 0.0)
                count = count + here
            ahead = ahead + jnp.where(lax.div(cell_i, n_src) == k, starts[k], 0.0)
            starts.append(starts[k] + jnp.floor((count + (half_step - 1)) * (1.0 / half_step)) * half_step)
        pos = jnp.sum(hot * (earlier + ahead * BLOCK), axis=0, keepdims=True)
        behind = jnp.where(place_i.astype(jnp.float32) >= ahead + blocks, 1.0, 0.0)
        owner = jnp.minimum(jnp.sum(behind, axis=0, keepdims=True), cells - 1.0)
        owner = owner - n_src * jnp.floor(owner * (1.0 / n_src))
        for k in range(KINDS + 1):
            owner = jnp.where(place_i == n_pos - 1 - k, starts[k], owner)
        stack = [jnp.where(valid[j], pos[:, j * tiles:(j + 1) * tiles], -1.0) for j in range(per)]
        stack += [w.astype(jnp.float32) - trash for w in words]
        stack += [jnp.zeros((1, tiles), jnp.float32)] * (-len(stack) % 8)
        cols = jnp.concatenate(stack, axis=0).T
        found = jnp.zeros((tiles, n_pos), jnp.float32)
        for j in range(per):
            found = found + jnp.where(cols[:, j:j + 1] == pos_i, cols[:, per + j:per + j + 1], 0.0)
        word = jnp.sum(found, axis=0, keepdims=True) + trash
        tables[c][0:1, :] = word.astype(jnp.int32)
        tables[c][1:2, :] = owner.astype(jnp.int32)

    for c in copies[3:]:
        c.wait()


def plan(chunks, per, n, radix, ids, src, rows, dst, tw, xo):
    tiles, _, _, tile = tw.shape
    n_src = xo.shape[0] // tile
    half_step = STEP // 2
    blocks = per * tiles // BLOCK + KINDS * n_src + KINDS * half_step
    n_pos = -(-(blocks * BLOCK) // 128) * 128
    smem = pl.BlockSpec(memory_space=pltpu.SMEM)
    vmem = pl.BlockSpec(memory_space=pltpu.VMEM)
    hbm = pl.BlockSpec(memory_space=pltpu.HBM)
    half = chunks * per
    return pl.pallas_call(
        functools.partial(plan_kernel, chunks, per, n, radix, n_src),
        out_shape=[jax.ShapeDtypeStruct((2, n_pos), jnp.int32)] * chunks
        + [jax.ShapeDtypeStruct((per * tiles, UNIT, tile), tw.dtype)] * chunks
        + [jax.ShapeDtypeStruct(xo.shape, xo.dtype)],
        in_specs=[smem] + [hbm] * 5,
        out_specs=[vmem] * (2 * chunks + 1),
        scratch_shapes=[
            pltpu.VMEM((1, tiles), jnp.int32),
            pltpu.VMEM((1, tiles), jnp.int32),
            pltpu.VMEM((1, tiles), jnp.int32),
            pltpu.SemaphoreType.DMA((3 + half + 1,)),
        ],
        compiler_params=pltpu.CompilerParams(vmem_limit_bytes=32 * 1024 * 1024),
        name="plan",
    )(ids, *[
        pltpu.with_memory_space_constraint(a, pltpu.HBM)
        for a in (src.reshape(1, tiles), rows.reshape(1, tiles), dst.reshape(1, tiles), tw, xo)
    ])


def select_kernel(groups, ids, lists, counts, adj, sel, front, adj_out):
    core, me = ids[0], ids[1]
    n = lists.shape[0]
    slots = lists.shape[1]
    total = n * slots
    q_n = lax.broadcasted_iota(jnp.int32, (total, n), 0)
    r_n = lax.broadcasted_iota(jnp.int32, (total, n), 1)
    mine = lists[me].astype(jnp.float32)
    cnt = counts[pl.ds(me, 1), :]
    picked = jnp.zeros((total, n), jnp.float32)
    k_n = jnp.bitwise_and(q_n, slots - 1)
    for k in range(slots):
        picked = jnp.where(k_n == k, mine[k:k + 1, :], picked)
    good = jnp.logical_and(n - 1 - lax.div(q_n, slots) == r_n, k_n < cnt)
    row = jnp.sum(jnp.where(good, picked + 1.0, 0.0), axis=1, keepdims=True) - 1.0
    lane = lax.broadcasted_iota(jnp.int32, (1, sel.shape[1]), 1)
    name = jnp.zeros(lane.shape, jnp.int32)
    names = [group_of(c, i, groups) for c in (core, 1 - core) for i in range(groups // 2)]
    for i, g in enumerate(names):
        name = jnp.where(lax.div(lane, UNIT) == i, g * UNIT + jnp.bitwise_and(lane, UNIT - 1), name)
    sel[...] = jnp.where(row == name.astype(jnp.float32), 1.0, 0.0).astype(jnp.bfloat16)
    tile, out_rows = groups * UNIT, adj.shape[0]
    placed = jnp.where(lax.broadcasted_iota(jnp.int32, (tile, tile), 0) == name, 1.0, 0.0).astype(jnp.bfloat16)
    front[:out_rows, :] = jnp.dot(adj[:, :tile], placed, preferred_element_type=jnp.float32).astype(jnp.bfloat16)
    front[out_rows:, :] = placed[:out_rows, :]
    column = lax.broadcasted_iota(jnp.int32, (1, total), 1)
    source = (n - 1 - lax.div(column, slots)) * slots + lax.rem(column, slots)
    moved = jnp.where(lax.broadcasted_iota(jnp.int32, (total, total), 0) == source, 1.0, 0.0).astype(jnp.bfloat16)
    adj_out[...] = jnp.dot(adj[:, groups * UNIT:], moved, preferred_element_type=jnp.float32).astype(jnp.bfloat16)


def selection(groups, ids, send_list, send_count, adj):
    n, _, slots = send_list.shape
    smem = pl.BlockSpec(memory_space=pltpu.SMEM)
    vmem = pl.BlockSpec(memory_space=pltpu.VMEM)
    return pl.pallas_call(
        functools.partial(select_kernel, groups),
        out_shape=[
            jax.ShapeDtypeStruct((n * slots, groups * UNIT), jnp.bfloat16),
            jax.ShapeDtypeStruct((2 * adj.shape[0], groups * UNIT), jnp.bfloat16),
            jax.ShapeDtypeStruct((adj.shape[0], n * slots), jnp.bfloat16),
        ],
        in_specs=[smem, vmem, vmem, vmem],
        out_specs=[vmem] * 3,
        compiler_params=pltpu.CompilerParams(vmem_limit_bytes=32 * 1024 * 1024),
        name="selection",
    )(ids, jnp.swapaxes(send_list, 1, 2), send_count, adj)


def tiles_kernel(kind, used, table_v, tbuf, xo, xp, *rest):
    parts = len(rest) - 3
    accs, (masks, table, sem) = rest[:parts], rest[parts:]
    tile = tbuf.shape[2]
    width = xo.shape[1]
    to_scalar = pltpu.make_async_copy(table_v, table, sem)
    to_scalar.start()
    for acc in accs:
        acc[:used, :] = jnp.zeros((used, acc.shape[1]), jnp.float32)
    row_i = lax.broadcasted_iota(jnp.int32, (UNIT, tile), 0)
    for m in range(UNIT + 1):
        masks[m] = jnp.where(row_i < m, 1.0, 0.0).astype(jnp.bfloat16)
    columns = [(x, h) for x in (xo, xp) for h in range(0, width, PART)]
    to_scalar.wait()

    def blocks(first, count):
        for m in range(count):
            at = first + m
            base = pl.multiple_of(table[1, at] * tile, tile)
            rows, places = [], []
            for k in range(BLOCK):
                word = table[0, at * BLOCK + k]
                u = jnp.bitwise_and(lax.shift_right_logical(word, 5), 511)
                rows.append(tbuf[u] * masks[jnp.bitwise_and(word, 31)])
                places.append(pl.multiple_of(lax.shift_right_logical(word, 14) * UNIT, UNIT))
            lhs = jnp.concatenate(rows, axis=0)
            for acc, (x, h) in zip(accs, columns):
                got = jnp.dot(lhs, x[pl.ds(base, tile), h:h + PART], preferred_element_type=jnp.float32)
                got = got.astype(jnp.bfloat16).astype(jnp.float32)
                for k in range(BLOCK):
                    acc[pl.ds(places[k], UNIT), :] += got[k * UNIT:(k + 1) * UNIT, :]

    half = STEP // 2
    begin = table[1, table.shape[1] - 1 - kind]
    halves = lax.div(table[1, table.shape[1] - 2 - kind] - begin, half)
    steps = lax.div(halves, 2)

    def step(i, carry):
        blocks(begin + i * STEP, STEP)
        return carry

    def last(i, carry):
        blocks(begin + steps * STEP, half)
        return carry

    lax.fori_loop(0, steps, step, 0)
    lax.fori_loop(0, lax.rem(halves, 2), last, 0)


def gathered_sums(kind, used, per, n, radix, table, tbuf, xo, xp):
    width = xo.shape[1]
    tile = tbuf.shape[2]
    vmem = pl.BlockSpec(memory_space=pltpu.VMEM)
    flops = 2 * tbuf.shape[0] * UNIT * tile * 2 * width // 3
    parts = 2 * width // PART
    sums = jax.ShapeDtypeStruct(((trash_of(n, per, radix) + 1) * UNIT, PART), jnp.float32)
    return pl.pallas_call(
        functools.partial(tiles_kernel, kind, used),
        out_shape=[sums] * parts,
        in_specs=[vmem] * 4,
        out_specs=[vmem] * parts,
        scratch_shapes=[
            pltpu.VMEM((UNIT + 1, UNIT, tile), jnp.bfloat16),
            pltpu.SMEM(table.shape, jnp.int32),
            pltpu.SemaphoreType.DMA,
        ],
        compiler_params=pltpu.CompilerParams(vmem_limit_bytes=(12 << 20) + sums.size * 4 * parts),
        cost_estimate=pl.CostEstimate(flops=flops, bytes_accessed=4 << 20, transcendentals=0),
        name="gathered_sums",
    )(table, tbuf, xo, xp)


def weigh(accs, weights, first, count, out):
    size = min(256, count)

    def piece(r, carry):
        at = pl.multiple_of(r * size, size)
        got = jnp.zeros((size, out.shape[1]), jnp.float32)
        for i, acc in enumerate(accs):
            w, h = weights[i * PART // weights[0].shape[0]], i * PART % weights[0].shape[0]
            value = acc[pl.ds(first + at, size), :]
            high = value.astype(jnp.bfloat16)
            low = (value - high.astype(jnp.float32)).astype(jnp.bfloat16)
            got = got + jnp.dot(high, w[h:h + PART, :], preferred_element_type=jnp.float32)
            got = got + jnp.dot(low, w[h:h + PART, :], preferred_element_type=jnp.float32)
        out[pl.ds(at, size), :] = got
        return carry

    lax.fori_loop(0, count // size, piece, 0)


def sent_kernel(first, slots, rows, parts, wo, wp, *refs):
    accs, (out, sums, tail) = refs[:parts], refs[parts:]
    weigh(accs, (wo, wp), first, slots * rows, sums)
    write_coded(out, tail, slots, rows, lambda s: sums[s * rows:(s + 1) * rows, :])


def sent_terms(first, slots, rows, accs, wo, wp):
    hidden = wo.shape[1]
    vmem = pl.BlockSpec(memory_space=pltpu.VMEM)
    return pl.pallas_call(
        functools.partial(sent_kernel, first, slots, rows, len(accs)),
        out_shape=jax.ShapeDtypeStruct((slots * rows + tail_rows(slots), hidden), jnp.int16),
        in_specs=[vmem] * (2 + len(accs)),
        out_specs=vmem,
        scratch_shapes=[
            pltpu.VMEM((slots * rows, hidden), jnp.float32),
            pltpu.VMEM((tail_rows(slots), hidden), jnp.float32),
        ],
        compiler_params=pltpu.CompilerParams(vmem_limit_bytes=(12 << 20) + accs[0].size * 4 * len(accs)),
        cost_estimate=pl.CostEstimate(
            flops=4 * slots * rows * PART * len(accs) * hidden, bytes_accessed=2 << 20, transcendentals=0),
        name="sent_terms",
    )(wo, wp, *accs)


def own_kernel(chunk, per, groups, parts, ids, wo, wp, xo, so, *refs):
    accs, (out, theirs, terms) = refs[:parts], refs[parts:]
    weigh(accs, (wo, wp), 0, out.shape[0], out)
    terms[...] = jnp.dot(xo[:groups * UNIT, :], so[...], preferred_element_type=jnp.float32)
    for j in range(per):
        here = slice(j * UNIT, (j + 1) * UNIT)
        at = pl.multiple_of(group_of(ids[0], chunk * per + j, groups) * UNIT, UNIT)
        out[here, :] += terms[pl.ds(at, UNIT), :]
        at = pl.multiple_of(group_of(1 - ids[0], chunk * per + j, groups) * UNIT, UNIT)
        theirs[here, :] = terms[pl.ds(at, UNIT), :]


def own_terms(chunk, per, groups, slots, ids, accs, wo, wp, xo, so):
    hidden = wo.shape[1]
    rows = per * UNIT
    smem = pl.BlockSpec(memory_space=pltpu.SMEM)
    vmem = pl.BlockSpec(memory_space=pltpu.VMEM)
    return pl.pallas_call(
        functools.partial(own_kernel, chunk, per, groups, len(accs)),
        out_shape=[
            jax.ShapeDtypeStruct((slots * rows, hidden), jnp.float32),
            jax.ShapeDtypeStruct((rows, hidden), jnp.float32),
        ],
        in_specs=[smem] + [vmem] * (4 + len(accs)),
        out_specs=[vmem] * 2,
        scratch_shapes=[pltpu.VMEM((groups * UNIT, hidden), jnp.float32)],
        compiler_params=pltpu.CompilerParams(vmem_limit_bytes=(12 << 20) + accs[0].size * 4 * len(accs)),
        cost_estimate=pl.CostEstimate(
            flops=4 * slots * rows * PART * len(accs) * hidden, bytes_accessed=2 << 20, transcendentals=0),
        name="own_terms",
    )(ids, wo, wp, xo, so, *accs)


def combine_kernel(slots, rows, ways, own, *refs):
    parts = len(refs) - ways - 1
    coded, outs, tail = refs[:parts], refs[parts:parts + ways], refs[parts + ways]
    values = [read_coded(a, slots, rows) for a in coded]

    def total(s):
        got = own[s * rows:(s + 1) * rows, :]
        for value in values:
            got = got + value(s)
        return got

    for i in range(slots // ways):
        outs[0][i * rows:(i + 1) * rows, :] = total(i * ways)
    for k in range(1, ways):
        write_coded(outs[k], tail, slots // ways, rows, lambda s: total(s * ways + k))


def combine(slots, rows, ways, own, coded):
    width = own.shape[1]
    left = slots // ways
    vmem = pl.BlockSpec(memory_space=pltpu.VMEM)
    out = jax.ShapeDtypeStruct((left * rows + tail_rows(left), width), jnp.int16)
    return pl.pallas_call(
        functools.partial(combine_kernel, slots, rows, ways),
        out_shape=[jax.ShapeDtypeStruct((left * rows, width), jnp.float32)] + [out] * (ways - 1),
        in_specs=[vmem] * (1 + len(coded)),
        out_specs=[vmem] * ways,
        scratch_shapes=[pltpu.VMEM((tail_rows(left), width), jnp.float32)],
        compiler_params=pltpu.CompilerParams(vmem_limit_bytes=32 * 1024 * 1024),
        name="combine",
    )(own, *coded)


def hidden_kernel(chunks, parts, rows, *refs):
    out = refs[chunks * parts + 1]
    for c in range(chunks):
        own, self, coded = refs[c * parts], refs[c * parts + 1], refs[c * parts + 2:(c + 1) * parts]
        total = own[:rows, :] + self[...]
        for a in coded:
            total = total + read_coded(a, 1, rows)(0)
        out[c * rows:(c + 1) * rows, :] = jnp.maximum(total, 0.0).astype(jnp.bfloat16)


def hidden_rows(chunk_parts, rows, sel):
    chunks, parts = len(chunk_parts), len(chunk_parts[0])
    width = chunk_parts[0][0].shape[1]
    vmem = pl.BlockSpec(memory_space=pltpu.VMEM)
    flat = [a for part in chunk_parts for a in part]
    return pl.pallas_call(
        functools.partial(hidden_kernel, chunks, parts, rows),
        out_shape=jax.ShapeDtypeStruct((chunks * rows, width), jnp.bfloat16),
        in_specs=[vmem] * (len(flat) + 1),
        out_specs=vmem,
        compiler_params=pltpu.CompilerParams(vmem_limit_bytes=32 * 1024 * 1024),
        name="hidden_rows",
    )(*flat, sel)


def send_kernel(own, other, sel, send):
    both = jnp.concatenate([own[...], other[...]], axis=0)
    send[...] = jnp.dot(sel[...], both, preferred_element_type=jnp.float32).astype(jnp.bfloat16)


def rows_to_send(own, other, sel):
    vmem = pl.BlockSpec(memory_space=pltpu.VMEM)
    return pl.pallas_call(
        send_kernel,
        out_shape=jax.ShapeDtypeStruct((sel.shape[0], own.shape[1]), jnp.bfloat16),
        in_specs=[vmem] * 3,
        out_specs=vmem,
        compiler_params=pltpu.CompilerParams(vmem_limit_bytes=32 * 1024 * 1024),
        name="rows_to_send",
    )(own, other, sel)


def logits_kernel(own, other, received, front, adj_received, w_self, w_neigh, out):
    rows = out.shape[0]
    both = jnp.concatenate([own[...], other[...]], axis=0)
    local = jnp.dot(front[...], both, preferred_element_type=jnp.float32)
    mean = local[:rows, :] + jnp.dot(adj_received[...], received[...], preferred_element_type=jnp.float32)
    dims = (((1,), (1,)), ((), ()))
    got = lax.dot_general(local[rows:, :].astype(jnp.bfloat16), w_self[...], dims, preferred_element_type=jnp.float32)
    got = got + lax.dot_general(mean.astype(jnp.bfloat16), w_neigh[...], dims, preferred_element_type=jnp.float32)
    out[...] = got


def logits_of(own, other, received, front, adj_received, w_self, w_neigh):
    vmem = pl.BlockSpec(memory_space=pltpu.VMEM)
    return pl.pallas_call(
        logits_kernel,
        out_shape=jax.ShapeDtypeStruct((adj_received.shape[0], w_self.shape[1]), jnp.float32),
        in_specs=[vmem] * 7,
        out_specs=vmem,
        compiler_params=pltpu.CompilerParams(vmem_limit_bytes=32 * 1024 * 1024),
        name="logits",
    )(own, other, received, front, adj_received, w_self.T, w_neigh.T)


def exchange(parts, stride, n, places):
    got = [parts[0]]
    for k in places:
        got.append(lax.ppermute(parts[k], "dom", [(i, i ^ (k * stride)) for i in range(n)]))
    return got


def body(
    features,
    tile_weight,
    tile_dst,
    tile_src,
    tile_rows,
    w_self1,
    neighbour_weight_first,
    send_list,
    send_count,
    adj_two,
    w_self2,
    w_neigh2,
):
    n = lax.axis_size("dom")
    tile = tile_weight.shape[1]
    groups = tile // UNIT
    per = groups // 2 // CHUNKS
    bits = n.bit_length() - 1
    assert n == 1 << bits and bits >= 2
    radices = [2] * (bits // 2) + [1] * (bits % 2)
    ids = jnp.stack([lax.axis_index("feat"), lax.axis_index("dom")]).astype(jnp.int32)
    swap = [(0, 1), (1, 0)]
    xp = lax.ppermute(features, "feat", swap)
    wp = lax.ppermute(neighbour_weight_first, "feat", swap)
    tw = tile_weight.reshape(tile_weight.shape[0], groups, UNIT, tile)
    planned = plan(
        CHUNKS, per, n, 4, ids, tile_src, tile_rows, tile_dst, tw, features,
    )
    tables, tbufs, xo = planned[:CHUNKS], planned[CHUNKS:2 * CHUNKS], planned[2 * CHUNKS]
    wo, so = neighbour_weight_first, w_self1
    done = []
    for chunk in range(CHUNKS):
        slots, rows = n // 4, per * UNIT
        size = slots * rows
        far, near, mine = (
            gathered_sums(kind, used, per, n, 4, tables[chunk], tbufs[chunk], xo, xp)
            for kind, used in enumerate((size, 2 * size, size))
        )
        parts = {
            1: sent_terms(0, slots, rows, near, wo, wp),
            2: sent_terms(size, slots, rows, near, wo, wp),
            3: sent_terms(0, slots, rows, far, wo, wp),
        }
        parts[0], theirs = own_terms(chunk, per, groups, slots, ids, mine, wo, wp, xo, so)
        self = lax.ppermute(theirs, "feat", swap)
        got = exchange(parts, 1, n, (1, 2, 3))
        stride = 4
        for radix in radices[1:]:
            ways = 1 << radix
            parts = combine(n // stride, per * UNIT, ways, got[0], got[1:])
            got = exchange(parts, stride, n, (2, 3, 1) if ways == 4 else (1,))
            stride *= ways
        done.append([got[0], self] + got[1:])
    sel, front, adj_received = selection(groups, ids, send_list, send_count, adj_two)
    own = hidden_rows(done, per * UNIT, sel)
    other = lax.ppermute(own, "feat", swap)
    send = rows_to_send(own, other, sel)
    received = lax.all_to_all(send, "dom", 0, 0, axis_index_groups=[group_order(n)], tiled=True)
    return logits_of(own, other, received, front, adj_received, w_self2, w_neigh2)


def solution(mesh):
    in_specs = (
        P("dom", "feat"),
        P("dom", None, None),
        P("dom"),
        P("dom"),
        P("dom"),
        P("feat", None),
        P("feat", None),
        P(),
        P(),
        P("dom", None),
        P(),
        P(),
    )
    out_specs = P("dom", None)
    return jax.shard_map(body, mesh=mesh, in_specs=in_specs, out_specs=out_specs, check_vma=False)
```

```python
import functools

import jax
import jax.numpy as jnp
from jax import lax
from jax.experimental import pallas as pl
from jax.experimental.pallas import tpu as pltpu
from jax.sharding import PartitionSpec as P

UNIT = 16
BLOCK = 4
STEP = 16
PART = 256
CHUNKS = 1


def group_of(core, place, groups):
    pair = 2 * (place // 2) + core
    return pair if place % 2 == 0 else groups - 1 - pair


def group_order(n):
    return list(range(n - 1, -1, -1))


KINDS = 3
LN2 = 0.6931471805599453


def tail_rows(slots):
    return -(-slots // 8) * 8


def encode(x):
    top = jnp.max(jnp.abs(x), axis=0, keepdims=True)
    power = jnp.ceil(jnp.log(jnp.maximum(top, 1e-30)) * (1.0 / LN2) + 1e-3) - 15.0
    return jnp.floor(x * jnp.exp(power * -LN2) + 0.5), power


def to_int16(x):
    return x.astype(jnp.int32).astype(jnp.int16)


def write_coded(out, tail, slots, rows, value_of):
    tail[...] = jnp.zeros_like(tail)
    for s in range(slots):
        whole, power = encode(value_of(s))
        out[s * rows:(s + 1) * rows, :] = to_int16(whole)
        tail[s:s + 1, :] = power
    out[slots * rows:, :] = to_int16(tail[...])


def read_coded(ref, slots, rows):
    powers = ref[slots * rows:, :].astype(jnp.int32).astype(jnp.float32)

    def value_of(s):
        whole = ref[s * rows:(s + 1) * rows, :].astype(jnp.int32).astype(jnp.float32)
        return whole * jnp.exp(powers[s:s + 1, :] * LN2)

    return value_of


def trash_of(n, per, radix):
    return (radix - 2) * (n // radix) * per


def plan_kernel(chunks, per, n, radix, n_src, ids, src_h, rows_h, dst_h, tw, xo, *rest):
    tables, rest = rest[:chunks], rest[chunks:]
    tbufs, rest = rest[:chunks], rest[chunks:]
    xo_out, src_v, rows_v, dst_v, sems = rest
    core, me = ids[0], ids[1]
    tiles = src_v.shape[1]
    n_pos = tables[0].shape[1]
    units = per * tiles
    groups = 2 * per * chunks
    half = groups // 2
    gs = [group_of(core, i, groups) for i in range(half)]
    small = [(src_h, src_v), (rows_h, rows_v), (dst_h, dst_v)]
    large = [(tw.at[:, g], tbufs[i // per].at[pl.ds(i % per * tiles, tiles)]) for i, g in enumerate(gs)]
    large += [(xo, xo_out)]
    copies = [pltpu.make_async_copy(a, b, sems.at[i]) for i, (a, b) in enumerate(small + large)]
    for c in copies:
        c.start()
    lane = lax.broadcasted_iota(jnp.int32, (1, tiles), 1)
    block_i = lax.broadcasted_iota(jnp.int32, (KINDS * n_src, tiles), 0)
    before = lax.broadcasted_iota(jnp.int32, (units, units), 0) < lax.broadcasted_iota(jnp.int32, (units, units), 1)
    before = jnp.where(before, 1.0, 0.0).astype(jnp.bfloat16)
    pos_i = lax.broadcasted_iota(jnp.int32, (tiles, n_pos), 1).astype(jnp.float32)
    place_i = lax.broadcasted_iota(jnp.int32, (1, n_pos), 1)
    trash = float(trash_of(n, per, radix) << 14)
    for c in copies[:3]:
        c.wait()
    src, rows = src_v[...], rows_v[...]
    slot = jnp.bitwise_xor(dst_v[...], me)
    partner = jnp.bitwise_and(slot, radix - 1)
    kind = jnp.where(partner == radix - 1, 0, jnp.where(partner > 0, 1, 2))
    slot = lax.div(slot, radix) + jnp.where(kind == 1, partner - 1, 0) * (n // radix)
    cell = kind * n_src + src
    cells = KINDS * n_src
    for c in range(chunks):
        hot, words, valid = [], [], []
        for j in range(per):
            limit = jnp.clip(rows - UNIT * gs[c * per + j], 0, UNIT)
            ok = limit > 0
            valid.append(ok)
            words.append(((slot * per + j) * 512 + (j * tiles + lane)) * 32 + limit)
            hot.append(jnp.where(jnp.logical_and(block_i == cell, ok), 1.0, 0.0))
        hot = jnp.concatenate(hot, axis=1)
        earlier = jnp.dot(hot.astype(jnp.bfloat16), before, preferred_element_type=jnp.float32)
        blocks = jnp.floor((jnp.sum(hot, axis=1, keepdims=True) + (BLOCK - 1)) * (1.0 / BLOCK))
        half_step = STEP // 2
        ahead = jnp.zeros(blocks.shape, jnp.float32)
        cell_i = lax.broadcasted_iota(jnp.int32, blocks.shape, 0)
        starts = [jnp.zeros((1, 1), jnp.float32)]
        for k in range(KINDS):
            count = jnp.zeros((1, 1), jnp.float32)
            for s in range(k * n_src, (k + 1) * n_src):
                here = blocks[s:s + 1, :]
                ahead = ahead + jnp.where(jnp.logical_and(cell_i > s, cell_i < (k + 1) * n_src), here, 0.0)
                count = count + here
            ahead = ahead + jnp.where(lax.div(cell_i, n_src) == k, starts[k], 0.0)
            starts.append(starts[k] + jnp.floor((count + (half_step - 1)) * (1.0 / half_step)) * half_step)
        pos = jnp.sum(hot * (earlier + ahead * BLOCK), axis=0, keepdims=True)
        behind = jnp.where(place_i.astype(jnp.float32) >= ahead + blocks, 1.0, 0.0)
        owner = jnp.minimum(jnp.sum(behind, axis=0, keepdims=True), cells - 1.0)
        owner = owner - n_src * jnp.floor(owner * (1.0 / n_src))
        for k in range(KINDS + 1):
            owner = jnp.where(place_i == n_pos - 1 - k, starts[k], owner)
        stack = [jnp.where(valid[j], pos[:, j * tiles:(j + 1) * tiles], -1.0) for j in range(per)]
        stack += [w.astype(jnp.float32) - trash for w in words]
        stack += [jnp.zeros((1, tiles), jnp.float32)] * (-len(stack) % 8)
        cols = jnp.concatenate(stack, axis=0).T
        found = jnp.zeros((tiles, n_pos), jnp.float32)
        for j in range(per):
            found = found + jnp.where(cols[:, j:j + 1] == pos_i, cols[:, per + j:per + j + 1], 0.0)
        word = jnp.sum(found, axis=0, keepdims=True) + trash
        tables[c][0:1, :] = word.astype(jnp.int32)
        tables[c][1:2, :] = owner.astype(jnp.int32)

    for c in copies[3:]:
        c.wait()


def plan(chunks, per, n, radix, ids, src, rows, dst, tw, xo):
    tiles, _, _, tile = tw.shape
    n_src = xo.shape[0] // tile
    half_step = STEP // 2
    blocks = per * tiles // BLOCK + KINDS * n_src + KINDS * half_step
    n_pos = -(-(blocks * BLOCK) // 128) * 128
    smem = pl.BlockSpec(memory_space=pltpu.SMEM)
    vmem = pl.BlockSpec(memory_space=pltpu.VMEM)
    hbm = pl.BlockSpec(memory_space=pltpu.HBM)
    half = chunks * per
    return pl.pallas_call(
        functools.partial(plan_kernel, chunks, per, n, radix, n_src),
        out_shape=[jax.ShapeDtypeStruct((2, n_pos), jnp.int32)] * chunks
        + [jax.ShapeDtypeStruct((per * tiles, UNIT, tile), tw.dtype)] * chunks
        + [jax.ShapeDtypeStruct(xo.shape, xo.dtype)],
        in_specs=[smem] + [hbm] * 5,
        out_specs=[vmem] * (2 * chunks + 1),
        scratch_shapes=[
            pltpu.VMEM((1, tiles), jnp.int32),
            pltpu.VMEM((1, tiles), jnp.int32),
            pltpu.VMEM((1, tiles), jnp.int32),
            pltpu.SemaphoreType.DMA((3 + half + 1,)),
        ],
        compiler_params=pltpu.CompilerParams(vmem_limit_bytes=32 * 1024 * 1024),
        name="plan",
    )(ids, *[
        pltpu.with_memory_space_constraint(a, pltpu.HBM)
        for a in (src.reshape(1, tiles), rows.reshape(1, tiles), dst.reshape(1, tiles), tw, xo)
    ])


def select_kernel(groups, ids, lists, counts, adj, sel, front, adj_out):
    core, me = ids[0], ids[1]
    n = lists.shape[0]
    slots = lists.shape[1]
    total = n * slots
    q_n = lax.broadcasted_iota(jnp.int32, (total, n), 0)
    r_n = lax.broadcasted_iota(jnp.int32, (total, n), 1)
    mine = lists[me].astype(jnp.float32)
    cnt = counts[pl.ds(me, 1), :]
    picked = jnp.zeros((total, n), jnp.float32)
    k_n = jnp.bitwise_and(q_n, slots - 1)
    for k in range(slots):
        picked = jnp.where(k_n == k, mine[k:k + 1, :], picked)
    good = jnp.logical_and(n - 1 - lax.div(q_n, slots) == r_n, k_n < cnt)
    row = jnp.sum(jnp.where(good, picked + 1.0, 0.0), axis=1, keepdims=True) - 1.0
    lane = lax.broadcasted_iota(jnp.int32, (1, sel.shape[1]), 1)
    name = jnp.zeros(lane.shape, jnp.int32)
    names = [group_of(c, i, groups) for c in (core, 1 - core) for i in range(groups // 2)]
    for i, g in enumerate(names):
        name = jnp.where(lax.div(lane, UNIT) == i, g * UNIT + jnp.bitwise_and(lane, UNIT - 1), name)
    sel[...] = jnp.where(row == name.astype(jnp.float32), 1.0, 0.0).astype(jnp.bfloat16)
    tile, out_rows = groups * UNIT, adj.shape[0]
    placed = jnp.where(lax.broadcasted_iota(jnp.int32, (tile, tile), 0) == name, 1.0, 0.0).astype(jnp.bfloat16)
    front[:out_rows, :] = jnp.dot(adj[:, :tile], placed, preferred_element_type=jnp.float32).astype(jnp.bfloat16)
    front[out_rows:, :] = placed[:out_rows, :]
    column = lax.broadcasted_iota(jnp.int32, (1, total), 1)
    source = (n - 1 - lax.div(column, slots)) * slots + lax.rem(column, slots)
    moved = jnp.where(lax.broadcasted_iota(jnp.int32, (total, total), 0) == source, 1.0, 0.0).astype(jnp.bfloat16)
    adj_out[...] = jnp.dot(adj[:, groups * UNIT:], moved, preferred_element_type=jnp.float32).astype(jnp.bfloat16)


def selection(groups, ids, send_list, send_count, adj):
    n, _, slots = send_list.shape
    smem = pl.BlockSpec(memory_space=pltpu.SMEM)
    vmem = pl.BlockSpec(memory_space=pltpu.VMEM)
    return pl.pallas_call(
        functools.partial(select_kernel, groups),
        out_shape=[
            jax.ShapeDtypeStruct((n * slots, groups * UNIT), jnp.bfloat16),
            jax.ShapeDtypeStruct((2 * adj.shape[0], groups * UNIT), jnp.bfloat16),
            jax.ShapeDtypeStruct((adj.shape[0], n * slots), jnp.bfloat16),
        ],
        in_specs=[smem, vmem, vmem, vmem],
        out_specs=[vmem] * 3,
        compiler_params=pltpu.CompilerParams(vmem_limit_bytes=32 * 1024 * 1024),
        name="selection",
    )(ids, jnp.swapaxes(send_list, 1, 2), send_count, adj)


def tiles_kernel(kind, used, table_v, tbuf, xo, xp, *rest):
    parts = len(rest) - 3
    accs, (masks, table, sem) = rest[:parts], rest[parts:]
    tile = tbuf.shape[2]
    width = xo.shape[1]
    to_scalar = pltpu.make_async_copy(table_v, table, sem)
    to_scalar.start()
    for acc in accs:
        acc[:used, :] = jnp.zeros((used, acc.shape[1]), jnp.float32)
    row_i = lax.broadcasted_iota(jnp.int32, (UNIT, tile), 0)
    for m in range(UNIT + 1):
        masks[m] = jnp.where(row_i < m, 1.0, 0.0).astype(jnp.bfloat16)
    columns = [(x, h) for x in (xo, xp) for h in range(0, width, PART)]
    to_scalar.wait()

    def blocks(first, count):
        for m in range(count):
            at = first + m
            base = pl.multiple_of(table[1, at] * tile, tile)
            rows, places = [], []
            for k in range(BLOCK):
                word = table[0, at * BLOCK + k]
                u = jnp.bitwise_and(lax.shift_right_logical(word, 5), 511)
                rows.append(tbuf[u] * masks[jnp.bitwise_and(word, 31)])
                places.append(pl.multiple_of(lax.shift_right_logical(word, 14) * UNIT, UNIT))
            lhs = jnp.concatenate(rows, axis=0)
            for acc, (x, h) in zip(accs, columns):
                got = jnp.dot(lhs, x[pl.ds(base, tile), h:h + PART], preferred_element_type=jnp.float32)
                got = got.astype(jnp.bfloat16).astype(jnp.float32)
                for k in range(BLOCK):
                    acc[pl.ds(places[k], UNIT), :] += got[k * UNIT:(k + 1) * UNIT, :]

    half = STEP // 2
    begin = table[1, table.shape[1] - 1 - kind]
    halves = lax.div(table[1, table.shape[1] - 2 - kind] - begin, half)
    steps = lax.div(halves, 2)

    def step(i, carry):
        blocks(begin + i * STEP, STEP)
        return carry

    def last(i, carry):
        blocks(begin + steps * STEP, half)
        return carry

    lax.fori_loop(0, steps, step, 0)
    lax.fori_loop(0, lax.rem(halves, 2), last, 0)


def gathered_sums(kind, used, per, n, radix, table, tbuf, xo, xp):
    width = xo.shape[1]
    tile = tbuf.shape[2]
    vmem = pl.BlockSpec(memory_space=pltpu.VMEM)
    flops = 2 * tbuf.shape[0] * UNIT * tile * 2 * width // 3
    parts = 2 * width // PART
    sums = jax.ShapeDtypeStruct(((trash_of(n, per, radix) + 1) * UNIT, PART), jnp.float32)
    return pl.pallas_call(
        functools.partial(tiles_kernel, kind, used),
        out_shape=[sums] * parts,
        in_specs=[vmem] * 4,
        out_specs=[vmem] * parts,
        scratch_shapes=[
            pltpu.VMEM((UNIT + 1, UNIT, tile), jnp.bfloat16),
            pltpu.SMEM(table.shape, jnp.int32),
            pltpu.SemaphoreType.DMA,
        ],
        compiler_params=pltpu.CompilerParams(vmem_limit_bytes=(12 << 20) + sums.size * 4 * parts),
        cost_estimate=pl.CostEstimate(flops=flops, bytes_accessed=4 << 20, transcendentals=0),
        name="gathered_sums",
    )(table, tbuf, xo, xp)


def weigh(accs, weights, first, count, out):
    size = min(256, count)

    def piece(r, carry):
        at = pl.multiple_of(r * size, size)
        got = jnp.zeros((size, out.shape[1]), jnp.float32)
        for i, acc in enumerate(accs):
            w, h = weights[i * PART // weights[0].shape[0]], i * PART % weights[0].shape[0]
            value = acc[pl.ds(first + at, size), :]
            high = value.astype(jnp.bfloat16)
            low = (value - high.astype(jnp.float32)).astype(jnp.bfloat16)
            got = got + jnp.dot(high, w[h:h + PART, :], preferred_element_type=jnp.float32)
            got = got + jnp.dot(low, w[h:h + PART, :], preferred_element_type=jnp.float32)
        out[pl.ds(at, size), :] = got
        return carry

    lax.fori_loop(0, count // size, piece, 0)


def sent_kernel(first, slots, rows, parts, wo, wp, *refs):
    accs, (out, sums, tail) = refs[:parts], refs[parts:]
    weigh(accs, (wo, wp), first, slots * rows, sums)
    write_coded(out, tail, slots, rows, lambda s: sums[s * rows:(s + 1) * rows, :])


def sent_terms(first, slots, rows, accs, wo, wp):
    hidden = wo.shape[1]
    vmem = pl.BlockSpec(memory_space=pltpu.VMEM)
    return pl.pallas_call(
        functools.partial(sent_kernel, first, slots, rows, len(accs)),
        out_shape=jax.ShapeDtypeStruct((slots * rows + tail_rows(slots), hidden), jnp.int16),
        in_specs=[vmem] * (2 + len(accs)),
        out_specs=vmem,
        scratch_shapes=[
            pltpu.VMEM((slots * rows, hidden), jnp.float32),
            pltpu.VMEM((tail_rows(slots), hidden), jnp.float32),
        ],
        compiler_params=pltpu.CompilerParams(vmem_limit_bytes=(12 << 20) + accs[0].size * 4 * len(accs)),
        cost_estimate=pl.CostEstimate(
            flops=4 * slots * rows * PART * len(accs) * hidden, bytes_accessed=2 << 20, transcendentals=0),
        name="sent_terms",
    )(wo, wp, *accs)


def own_kernel(parts, wo, wp, *refs):
    accs, out = refs[:parts], refs[parts]
    weigh(accs, (wo, wp), 0, out.shape[0], out)


def own_terms(count, accs, wo, wp):
    hidden = wo.shape[1]
    vmem = pl.BlockSpec(memory_space=pltpu.VMEM)
    return pl.pallas_call(
        functools.partial(own_kernel, len(accs)),
        out_shape=jax.ShapeDtypeStruct((count, hidden), jnp.float32),
        in_specs=[vmem] * (2 + len(accs)),
        out_specs=vmem,
        compiler_params=pltpu.CompilerParams(vmem_limit_bytes=(12 << 20) + accs[0].size * 4 * len(accs)),
        cost_estimate=pl.CostEstimate(
            flops=4 * count * PART * len(accs) * hidden, bytes_accessed=2 << 20, transcendentals=0),
        name="own_terms",
    )(wo, wp, *accs)


def self_kernel(chunk, per, groups, ids, xo, so, unused, mine, theirs, terms):
    terms[...] = jnp.dot(xo[:groups * UNIT, :], so[...], preferred_element_type=jnp.float32)
    for j in range(per):
        here = slice(j * UNIT, (j + 1) * UNIT)
        at = pl.multiple_of(group_of(ids[0], chunk * per + j, groups) * UNIT, UNIT)
        mine[here, :] = terms[pl.ds(at, UNIT), :]
        at = pl.multiple_of(group_of(1 - ids[0], chunk * per + j, groups) * UNIT, UNIT)
        theirs[here, :] = terms[pl.ds(at, UNIT), :]


def self_terms(chunk, per, groups, ids, xo, so, after):
    rows, hidden = per * UNIT, so.shape[1]
    smem = pl.BlockSpec(memory_space=pltpu.SMEM)
    vmem = pl.BlockSpec(memory_space=pltpu.VMEM)
    return pl.pallas_call(
        functools.partial(self_kernel, chunk, per, groups),
        out_shape=[jax.ShapeDtypeStruct((rows, hidden), jnp.float32)] * 2,
        in_specs=[smem, vmem, vmem, vmem],
        out_specs=[vmem] * 2,
        scratch_shapes=[pltpu.VMEM((groups * UNIT, hidden), jnp.float32)],
        compiler_params=pltpu.CompilerParams(vmem_limit_bytes=32 * 1024 * 1024),
        name="self_terms",
    )(ids, xo, so, after)


def combine_kernel(slots, rows, ways, own, *refs):
    parts = len(refs) - ways - 1
    coded, outs, tail = refs[:parts], refs[parts:parts + ways], refs[parts + ways]
    values = [read_coded(a, slots, rows) for a in coded]

    def total(s):
        got = own[s * rows:(s + 1) * rows, :]
        for value in values:
            got = got + value(s)
        return got

    for i in range(slots // ways):
        outs[0][i * rows:(i + 1) * rows, :] = total(i * ways)
    for k in range(1, ways):
        write_coded(outs[k], tail, slots // ways, rows, lambda s: total(s * ways + k))


def combine(slots, rows, ways, own, coded):
    width = own.shape[1]
    left = slots // ways
    vmem = pl.BlockSpec(memory_space=pltpu.VMEM)
    out = jax.ShapeDtypeStruct((left * rows + tail_rows(left), width), jnp.int16)
    return pl.pallas_call(
        functools.partial(combine_kernel, slots, rows, ways),
        out_shape=[jax.ShapeDtypeStruct((left * rows, width), jnp.float32)] + [out] * (ways - 1),
        in_specs=[vmem] * (1 + len(coded)),
        out_specs=[vmem] * ways,
        scratch_shapes=[pltpu.VMEM((tail_rows(left), width), jnp.float32)],
        compiler_params=pltpu.CompilerParams(vmem_limit_bytes=32 * 1024 * 1024),
        name="combine",
    )(own, *coded)


def hidden_kernel(chunks, parts, rows, *refs):
    out = refs[chunks * parts + 1]
    for c in range(chunks):
        own, mine, theirs, coded = *refs[c * parts:c * parts + 3], refs[c * parts + 3:(c + 1) * parts]
        total = own[:rows, :] + (mine[...] + theirs[...])
        for a in coded:
            total = total + read_coded(a, 1, rows)(0)
        out[c * rows:(c + 1) * rows, :] = jnp.maximum(total, 0.0).astype(jnp.bfloat16)


def hidden_rows(chunk_parts, rows, sel):
    chunks, parts = len(chunk_parts), len(chunk_parts[0])
    width = chunk_parts[0][0].shape[1]
    vmem = pl.BlockSpec(memory_space=pltpu.VMEM)
    flat = [a for part in chunk_parts for a in part]
    return pl.pallas_call(
        functools.partial(hidden_kernel, chunks, parts, rows),
        out_shape=jax.ShapeDtypeStruct((chunks * rows, width), jnp.bfloat16),
        in_specs=[vmem] * (len(flat) + 1),
        out_specs=vmem,
        compiler_params=pltpu.CompilerParams(vmem_limit_bytes=32 * 1024 * 1024),
        name="hidden_rows",
    )(*flat, sel)


def send_kernel(own, other, sel, send):
    both = jnp.concatenate([own[...], other[...]], axis=0)
    send[...] = jnp.dot(sel[...], both, preferred_element_type=jnp.float32).astype(jnp.bfloat16)


def rows_to_send(own, other, sel):
    vmem = pl.BlockSpec(memory_space=pltpu.VMEM)
    return pl.pallas_call(
        send_kernel,
        out_shape=jax.ShapeDtypeStruct((sel.shape[0], own.shape[1]), jnp.bfloat16),
        in_specs=[vmem] * 3,
        out_specs=vmem,
        compiler_params=pltpu.CompilerParams(vmem_limit_bytes=32 * 1024 * 1024),
        name="rows_to_send",
    )(own, other, sel)


def logits_kernel(own, other, received, front, adj_received, w_self, w_neigh, out):
    rows = out.shape[0]
    both = jnp.concatenate([own[...], other[...]], axis=0)
    local = jnp.dot(front[...], both, preferred_element_type=jnp.float32)
    mean = local[:rows, :] + jnp.dot(adj_received[...], received[...], preferred_element_type=jnp.float32)
    dims = (((1,), (1,)), ((), ()))
    got = lax.dot_general(local[rows:, :].astype(jnp.bfloat16), w_self[...], dims, preferred_element_type=jnp.float32)
    got = got + lax.dot_general(mean.astype(jnp.bfloat16), w_neigh[...], dims, preferred_element_type=jnp.float32)
    out[...] = got


def logits_of(own, other, received, front, adj_received, w_self, w_neigh):
    vmem = pl.BlockSpec(memory_space=pltpu.VMEM)
    return pl.pallas_call(
        logits_kernel,
        out_shape=jax.ShapeDtypeStruct((adj_received.shape[0], w_self.shape[1]), jnp.float32),
        in_specs=[vmem] * 7,
        out_specs=vmem,
        compiler_params=pltpu.CompilerParams(vmem_limit_bytes=32 * 1024 * 1024),
        name="logits",
    )(own, other, received, front, adj_received, w_self.T, w_neigh.T)


def exchange(parts, stride, n, places):
    got = [parts[0]]
    for k in places:
        got.append(lax.ppermute(parts[k], "dom", [(i, i ^ (k * stride)) for i in range(n)]))
    return got


def body(
    features,
    tile_weight,
    tile_dst,
    tile_src,
    tile_rows,
    w_self1,
    neighbour_weight_first,
    send_list,
    send_count,
    adj_two,
    w_self2,
    w_neigh2,
):
    n = lax.axis_size("dom")
    tile = tile_weight.shape[1]
    groups = tile // UNIT
    per = groups // 2 // CHUNKS
    bits = n.bit_length() - 1
    assert n == 1 << bits and bits >= 2
    radices = [2] * (bits // 2) + [1] * (bits % 2)
    ids = jnp.stack([lax.axis_index("feat"), lax.axis_index("dom")]).astype(jnp.int32)
    swap = [(0, 1), (1, 0)]
    xp = lax.ppermute(features, "feat", swap)
    wp = lax.ppermute(neighbour_weight_first, "feat", swap)
    tw = tile_weight.reshape(tile_weight.shape[0], groups, UNIT, tile)
    planned = plan(
        CHUNKS, per, n, 4, ids, tile_src, tile_rows, tile_dst, tw, features,
    )
    tables, tbufs, xo = planned[:CHUNKS], planned[CHUNKS:2 * CHUNKS], planned[2 * CHUNKS]
    wo, so = neighbour_weight_first, w_self1
    done = []
    for chunk in range(CHUNKS):
        slots, rows = n // 4, per * UNIT
        size = slots * rows
        far, near, mine = (
            gathered_sums(kind, used, per, n, 4, tables[chunk], tbufs[chunk], xo, xp)
            for kind, used in enumerate((size, 2 * size, size))
        )
        parts = {
            1: sent_terms(0, slots, rows, near, wo, wp),
            2: sent_terms(size, slots, rows, near, wo, wp),
            3: sent_terms(0, slots, rows, far, wo, wp),
        }
        parts[0] = own_terms(size, mine, wo, wp)
        got = exchange(parts, 1, n, (1, 2, 3))
        stride = 4
        for radix in radices[1:]:
            ways = 1 << radix
            parts = combine(n // stride, per * UNIT, ways, got[0], got[1:])
            got = exchange(parts, stride, n, (2, 3, 1) if ways == 4 else (1,))
            stride *= ways
        self_here, self_there = self_terms(chunk, per, groups, ids, xo, so, parts[0])
        self_other = lax.ppermute(self_there, "feat", swap)
        done.append([got[0], self_here, self_other] + got[1:])
    sel, front, adj_received = selection(groups, ids, send_list, send_count, adj_two)
    own = hidden_rows(done, per * UNIT, sel)
    other = lax.ppermute(own, "feat", swap)
    send = rows_to_send(own, other, sel)
    received = lax.all_to_all(send, "dom", 0, 0, axis_index_groups=[group_order(n)], tiled=True)
    return logits_of(own, other, received, front, adj_received, w_self2, w_neigh2)


def solution(mesh):
    in_specs = (
        P("dom", "feat"),
        P("dom", None, None),
        P("dom"),
        P("dom"),
        P("dom"),
        P("feat", None),
        P("feat", None),
        P(),
        P(),
        P("dom", None),
        P(),
        P(),
    )
    out_specs = P("dom", None)
    return jax.shard_map(body, mesh=mesh, in_specs=in_specs, out_specs=out_specs, check_vma=False)
```

```python
import functools

import jax
import jax.numpy as jnp
from jax import lax
from jax.experimental import pallas as pl
from jax.experimental.pallas import tpu as pltpu
from jax.sharding import PartitionSpec as P

UNIT = 16
BLOCK = 4
STEP = 16
PART = 256
CHUNKS = 1


def group_of(core, place, groups):
    pair = 2 * (place // 2) + core
    return pair if place % 2 == 0 else groups - 1 - pair


def group_order(n):
    return list(range(n - 1, -1, -1))


LN2 = 0.6931471805599453


def tail_rows(slots):
    return -(-slots // 8) * 8


def encode(x):
    top = jnp.max(jnp.abs(x), axis=0, keepdims=True)
    power = jnp.ceil(jnp.log(jnp.maximum(top, 1e-30)) * (1.0 / LN2) + 1e-3) - 15.0
    return jnp.floor(x * jnp.exp(power * -LN2) + 0.5), power


def to_int16(x):
    return x.astype(jnp.int32).astype(jnp.int16)


def write_coded(out, tail, slots, rows, value_of):
    tail[...] = jnp.zeros_like(tail)
    for s in range(slots):
        whole, power = encode(value_of(s))
        out[s * rows:(s + 1) * rows, :] = to_int16(whole)
        tail[s:s + 1, :] = power
    out[slots * rows:, :] = to_int16(tail[...])


def read_coded(ref, slots, rows):
    powers = ref[slots * rows:, :].astype(jnp.int32).astype(jnp.float32)

    def value_of(s):
        whole = ref[s * rows:(s + 1) * rows, :].astype(jnp.int32).astype(jnp.float32)
        return whole * jnp.exp(powers[s:s + 1, :] * LN2)

    return value_of


def plan_kernel(chunks, per, n, radix, n_src, ids, src_h, rows_h, dst_h, tw, xo, *rest):
    tables, rest = rest[:chunks], rest[chunks:]
    tbufs, rest = rest[:chunks], rest[chunks:]
    xo_out, src_v, rows_v, dst_v, sems = rest
    core, me = ids[0], ids[1]
    tiles = src_v.shape[1]
    n_pos = tables[0].shape[1]
    units = per * tiles
    groups = 2 * per * chunks
    half = groups // 2
    gs = [group_of(core, i, groups) for i in range(half)]
    small = [(src_h, src_v), (rows_h, rows_v), (dst_h, dst_v)]
    large = [(tw.at[:, g], tbufs[i // per].at[pl.ds(i % per * tiles, tiles)]) for i, g in enumerate(gs)]
    large += [(xo, xo_out)]
    copies = [pltpu.make_async_copy(a, b, sems.at[i]) for i, (a, b) in enumerate(small + large)]
    for c in copies:
        c.start()
    lane = lax.broadcasted_iota(jnp.int32, (1, tiles), 1)
    block_i = lax.broadcasted_iota(jnp.int32, (n_src, tiles), 0)
    before = lax.broadcasted_iota(jnp.int32, (units, units), 0) < lax.broadcasted_iota(jnp.int32, (units, units), 1)
    before = jnp.where(before, 1.0, 0.0).astype(jnp.bfloat16)
    pos_i = lax.broadcasted_iota(jnp.int32, (tiles, n_pos), 1).astype(jnp.float32)
    place_i = lax.broadcasted_iota(jnp.int32, (1, n_pos), 1)
    trash = float(n * per << 14)
    for c in copies[:3]:
        c.wait()
    src, rows = src_v[...], rows_v[...]
    slot = jnp.bitwise_xor(dst_v[...], me)
    slot = jnp.bitwise_and(slot, radix - 1) * (n // radix) + lax.div(slot, radix)
    for c in range(chunks):
        hot, words, valid = [], [], []
        for j in range(per):
            limit = jnp.clip(rows - UNIT * gs[c * per + j], 0, UNIT)
            ok = limit > 0
            valid.append(ok)
            words.append(((slot * per + j) * 512 + (j * tiles + lane)) * 32 + limit)
            hot.append(jnp.where(jnp.logical_and(block_i == src, ok), 1.0, 0.0))
        hot = jnp.concatenate(hot, axis=1)
        earlier = jnp.dot(hot.astype(jnp.bfloat16), before, preferred_element_type=jnp.float32)
        blocks = jnp.floor((jnp.sum(hot, axis=1, keepdims=True) + (BLOCK - 1)) * (1.0 / BLOCK))
        ahead = jnp.zeros(blocks.shape, jnp.float32)
        source_i = lax.broadcasted_iota(jnp.int32, blocks.shape, 0)
        for s in range(n_src - 1):
            ahead = ahead + jnp.where(source_i > s, blocks[s:s + 1, :], 0.0)
        pos = jnp.sum(hot * (earlier + ahead * BLOCK), axis=0, keepdims=True)
        behind = jnp.where(place_i.astype(jnp.float32) >= ahead + blocks, 1.0, 0.0)
        owner = jnp.sum(behind, axis=0, keepdims=True)
        run = ahead[n_src - 1:, :] + blocks[n_src - 1:, :]
        stack = [jnp.where(valid[j], pos[:, j * tiles:(j + 1) * tiles], -1.0) for j in range(per)]
        stack += [w.astype(jnp.float32) - trash for w in words]
        stack += [jnp.zeros((1, tiles), jnp.float32)] * (-len(stack) % 8)
        cols = jnp.concatenate(stack, axis=0).T
        found = jnp.zeros((tiles, n_pos), jnp.float32)
        for j in range(per):
            found = found + jnp.where(cols[:, j:j + 1] == pos_i, cols[:, per + j:per + j + 1], 0.0)
        word = jnp.sum(found, axis=0, keepdims=True) + trash
        owner = jnp.where(place_i == n_pos - 1, run, jnp.minimum(owner, n_src - 1.0))
        tables[c][0:1, :] = word.astype(jnp.int32)
        tables[c][1:2, :] = owner.astype(jnp.int32)

    for c in copies[3:]:
        c.wait()


def plan(chunks, per, n, radix, ids, src, rows, dst, tw, xo):
    tiles, _, _, tile = tw.shape
    n_src = xo.shape[0] // tile
    blocks = -(-(per * tiles // BLOCK + n_src) // STEP) * STEP
    n_pos = -(-(blocks * BLOCK + 1) // 128) * 128
    smem = pl.BlockSpec(memory_space=pltpu.SMEM)
    vmem = pl.BlockSpec(memory_space=pltpu.VMEM)
    hbm = pl.BlockSpec(memory_space=pltpu.HBM)
    half = chunks * per
    return pl.pallas_call(
        functools.partial(plan_kernel, chunks, per, n, radix, n_src),
        out_shape=[jax.ShapeDtypeStruct((2, n_pos), jnp.int32)] * chunks
        + [jax.ShapeDtypeStruct((per * tiles, UNIT, tile), tw.dtype)] * chunks
        + [jax.ShapeDtypeStruct(xo.shape, xo.dtype)],
        in_specs=[smem] + [hbm] * 5,
        out_specs=[vmem] * (2 * chunks + 1),
        scratch_shapes=[
            pltpu.VMEM((1, tiles), jnp.int32),
            pltpu.VMEM((1, tiles), jnp.int32),
            pltpu.VMEM((1, tiles), jnp.int32),
            pltpu.SemaphoreType.DMA((3 + half + 1,)),
        ],
        compiler_params=pltpu.CompilerParams(vmem_limit_bytes=32 * 1024 * 1024),
        name="plan",
    )(ids, *[
        pltpu.with_memory_space_constraint(a, pltpu.HBM)
        for a in (src.reshape(1, tiles), rows.reshape(1, tiles), dst.reshape(1, tiles), tw, xo)
    ])


def select_kernel(groups, ids, lists, counts, adj, sel, front, adj_out):
    core, me = ids[0], ids[1]
    n = lists.shape[0]
    slots = lists.shape[1]
    total = n * slots
    q_n = lax.broadcasted_iota(jnp.int32, (total, n), 0)
    r_n = lax.broadcasted_iota(jnp.int32, (total, n), 1)
    mine = lists[me].astype(jnp.float32)
    cnt = counts[pl.ds(me, 1), :]
    picked = jnp.zeros((total, n), jnp.float32)
    k_n = jnp.bitwise_and(q_n, slots - 1)
    for k in range(slots):
        picked = jnp.where(k_n == k, mine[k:k + 1, :], picked)
    good = jnp.logical_and(n - 1 - lax.div(q_n, slots) == r_n, k_n < cnt)
    row = jnp.sum(jnp.where(good, picked + 1.0, 0.0), axis=1, keepdims=True) - 1.0
    lane = lax.broadcasted_iota(jnp.int32, (1, sel.shape[1]), 1)
    name = jnp.zeros(lane.shape, jnp.int32)
    names = [group_of(c, i, groups) for c in (core, 1 - core) for i in range(groups // 2)]
    for i, g in enumerate(names):
        name = jnp.where(lax.div(lane, UNIT) == i, g * UNIT + jnp.bitwise_and(lane, UNIT - 1), name)
    sel[...] = jnp.where(row == name.astype(jnp.float32), 1.0, 0.0).astype(jnp.bfloat16)
    tile, out_rows = groups * UNIT, adj.shape[0]
    placed = jnp.where(lax.broadcasted_iota(jnp.int32, (tile, tile), 0) == name, 1.0, 0.0).astype(jnp.bfloat16)
    front[:out_rows, :] = jnp.dot(adj[:, :tile], placed, preferred_element_type=jnp.float32).astype(jnp.bfloat16)
    front[out_rows:, :] = placed[:out_rows, :]
    column = lax.broadcasted_iota(jnp.int32, (1, total), 1)
    source = (n - 1 - lax.div(column, slots)) * slots + lax.rem(column, slots)
    moved = jnp.where(lax.broadcasted_iota(jnp.int32, (total, total), 0) == source, 1.0, 0.0).astype(jnp.bfloat16)
    adj_out[...] = jnp.dot(adj[:, groups * UNIT:], moved, preferred_element_type=jnp.float32).astype(jnp.bfloat16)


def selection(groups, ids, send_list, send_count, adj):
    n, _, slots = send_list.shape
    smem = pl.BlockSpec(memory_space=pltpu.SMEM)
    vmem = pl.BlockSpec(memory_space=pltpu.VMEM)
    return pl.pallas_call(
        functools.partial(select_kernel, groups),
        out_shape=[
            jax.ShapeDtypeStruct((n * slots, groups * UNIT), jnp.bfloat16),
            jax.ShapeDtypeStruct((2 * adj.shape[0], groups * UNIT), jnp.bfloat16),
            jax.ShapeDtypeStruct((adj.shape[0], n * slots), jnp.bfloat16),
        ],
        in_specs=[smem, vmem, vmem, vmem],
        out_specs=[vmem] * 3,
        compiler_params=pltpu.CompilerParams(vmem_limit_bytes=32 * 1024 * 1024),
        name="selection",
    )(ids, jnp.swapaxes(send_list, 1, 2), send_count, adj)


def tiles_kernel(table_v, tbuf, xo, xp, *rest):
    parts = len(rest) - 3
    accs, (masks, table, sem) = rest[:parts], rest[parts:]
    tile = tbuf.shape[2]
    width = xo.shape[1]
    to_scalar = pltpu.make_async_copy(table_v, table, sem)
    to_scalar.start()
    for acc in accs:
        acc[...] = jnp.zeros_like(acc)
    row_i = lax.broadcasted_iota(jnp.int32, (UNIT, tile), 0)
    for m in range(UNIT + 1):
        masks[m] = jnp.where(row_i < m, 1.0, 0.0).astype(jnp.bfloat16)
    columns = [(x, h) for x in (xo, xp) for h in range(0, width, PART)]
    to_scalar.wait()

    def blocks(first, count):
        for m in range(count):
            at = first + m
            base = pl.multiple_of(table[1, at] * tile, tile)
            rows, places = [], []
            for k in range(BLOCK):
                word = table[0, at * BLOCK + k]
                u = jnp.bitwise_and(lax.shift_right_logical(word, 5), 511)
                rows.append(tbuf[u] * masks[jnp.bitwise_and(word, 31)])
                places.append(pl.multiple_of(lax.shift_right_logical(word, 14) * UNIT, UNIT))
            lhs = jnp.concatenate(rows, axis=0)
            for acc, (x, h) in zip(accs, columns):
                got = jnp.dot(lhs, x[pl.ds(base, tile), h:h + PART], preferred_element_type=jnp.float32)
                got = got.astype(jnp.bfloat16).astype(jnp.float32)
                for k in range(BLOCK):
                    acc[pl.ds(places[k], UNIT), :] += got[k * UNIT:(k + 1) * UNIT, :]

    half = STEP // 2
    halves = lax.div(table[1, table.shape[1] - 1] + half - 1, half)
    steps = lax.div(halves, 2)

    def step(i, carry):
        blocks(i * STEP, STEP)
        return carry

    def last(i, carry):
        blocks(steps * STEP, half)
        return carry

    lax.fori_loop(0, steps, step, 0)
    lax.fori_loop(0, lax.rem(halves, 2), last, 0)


def gathered_sums(per, n, table, tbuf, xo, xp):
    width = xo.shape[1]
    tile = tbuf.shape[2]
    vmem = pl.BlockSpec(memory_space=pltpu.VMEM)
    flops = 2 * tbuf.shape[0] * UNIT * tile * 2 * width
    parts = 2 * width // PART
    sums = jax.ShapeDtypeStruct(((n * per + 1) * UNIT, PART), jnp.float32)
    return pl.pallas_call(
        tiles_kernel,
        out_shape=[sums] * parts,
        in_specs=[vmem] * 4,
        out_specs=[vmem] * parts,
        scratch_shapes=[
            pltpu.VMEM((UNIT + 1, UNIT, tile), jnp.bfloat16),
            pltpu.SMEM(table.shape, jnp.int32),
            pltpu.SemaphoreType.DMA,
        ],
        compiler_params=pltpu.CompilerParams(vmem_limit_bytes=(12 << 20) + sums.size * 4 * parts),
        cost_estimate=pl.CostEstimate(flops=flops, bytes_accessed=8 << 20, transcendentals=0),
        name="gathered_sums",
    )(table, tbuf, xo, xp)


def weigh(accs, weights, first, count, out):
    size = min(256, count)

    def piece(r, carry):
        at = r * size if isinstance(r, int) else pl.multiple_of(r * size, size)
        got = jnp.zeros((size, out.shape[1]), jnp.float32)
        for i, acc in enumerate(accs):
            w, h = weights[i * PART // weights[0].shape[0]], i * PART % weights[0].shape[0]
            value = acc[pl.ds(first + at, size), :]
            high = value.astype(jnp.bfloat16)
            low = (value - high.astype(jnp.float32)).astype(jnp.bfloat16)
            got = got + jnp.dot(high, w[h:h + PART, :], preferred_element_type=jnp.float32)
            got = got + jnp.dot(low, w[h:h + PART, :], preferred_element_type=jnp.float32)
        out[pl.ds(at, size), :] = got
        return carry

    if count == size:
        piece(0, 0)
    else:
        lax.fori_loop(0, count // size, piece, 0)


def sent_kernel(ks, slots, rows, parts, wo, wp, *refs):
    accs, outs, scratch = refs[:parts], refs[parts:parts + len(ks)], refs[parts + len(ks):]
    for i, k in enumerate(ks):
        sums, tail = scratch[2 * i:2 * i + 2]
        weigh(accs, (wo, wp), k * slots * rows, slots * rows, sums)
        write_coded(outs[i], tail, slots, rows, lambda s: sums[s * rows:(s + 1) * rows, :])


def sent_terms(ks, slots, rows, accs, wo, wp):
    hidden = wo.shape[1]
    vmem = pl.BlockSpec(memory_space=pltpu.VMEM)
    coded = jax.ShapeDtypeStruct((slots * rows + tail_rows(slots), hidden), jnp.int16)
    return pl.pallas_call(
        functools.partial(sent_kernel, ks, slots, rows, len(accs)),
        out_shape=[coded] * len(ks),
        in_specs=[vmem] * (2 + len(accs)),
        out_specs=[vmem] * len(ks),
        scratch_shapes=[
            pltpu.VMEM((slots * rows, hidden), jnp.float32),
            pltpu.VMEM((tail_rows(slots), hidden), jnp.float32),
        ] * len(ks),
        compiler_params=pltpu.CompilerParams(vmem_limit_bytes=(20 << 20) + accs[0].size * 4 * len(accs)),
        cost_estimate=pl.CostEstimate(
            flops=4 * len(ks) * slots * rows * PART * len(accs) * hidden, bytes_accessed=2 << 20, transcendentals=0),
        name="sent_terms",
    )(wo, wp, *accs)


def own_kernel(chunk, per, groups, parts, ids, wo, wp, xo, so, *refs):
    accs, (out, theirs, terms) = refs[:parts], refs[parts:]
    weigh(accs, (wo, wp), 0, out.shape[0], out)
    terms[...] = jnp.dot(xo[:groups * UNIT, :], so[...], preferred_element_type=jnp.float32)
    for j in range(per):
        here = slice(j * UNIT, (j + 1) * UNIT)
        at = pl.multiple_of(group_of(ids[0], chunk * per + j, groups) * UNIT, UNIT)
        out[here, :] += terms[pl.ds(at, UNIT), :]
        at = pl.multiple_of(group_of(1 - ids[0], chunk * per + j, groups) * UNIT, UNIT)
        theirs[here, :] = terms[pl.ds(at, UNIT), :]


def own_terms(chunk, per, groups, slots, ids, accs, wo, wp, xo, so):
    hidden = wo.shape[1]
    rows = per * UNIT
    smem = pl.BlockSpec(memory_space=pltpu.SMEM)
    vmem = pl.BlockSpec(memory_space=pltpu.VMEM)
    return pl.pallas_call(
        functools.partial(own_kernel, chunk, per, groups, len(accs)),
        out_shape=[
            jax.ShapeDtypeStruct((slots * rows, hidden), jnp.float32),
            jax.ShapeDtypeStruct((rows, hidden), jnp.float32),
        ],
        in_specs=[smem] + [vmem] * (4 + len(accs)),
        out_specs=[vmem] * 2,
        scratch_shapes=[pltpu.VMEM((groups * UNIT, hidden), jnp.float32)],
        compiler_params=pltpu.CompilerParams(vmem_limit_bytes=(12 << 20) + accs[0].size * 4 * len(accs)),
        cost_estimate=pl.CostEstimate(
            flops=4 * slots * rows * PART * len(accs) * hidden, bytes_accessed=2 << 20, transcendentals=0),
        name="own_terms",
    )(ids, wo, wp, xo, so, *accs)


def combine_kernel(slots, rows, ways, own, *refs):
    parts = len(refs) - ways - 1
    coded, outs, tail = refs[:parts], refs[parts:parts + ways], refs[parts + ways]
    values = [read_coded(a, slots, rows) for a in coded]

    def total(s):
        got = own[s * rows:(s + 1) * rows, :]
        for value in values:
            got = got + value(s)
        return got

    for i in range(slots // ways):
        outs[0][i * rows:(i + 1) * rows, :] = total(i * ways)
    for k in range(1, ways):
        write_coded(outs[k], tail, slots // ways, rows, lambda s: total(s * ways + k))


def combine(slots, rows, ways, own, coded):
    width = own.shape[1]
    left = slots // ways
    vmem = pl.BlockSpec(memory_space=pltpu.VMEM)
    out = jax.ShapeDtypeStruct((left * rows + tail_rows(left), width), jnp.int16)
    return pl.pallas_call(
        functools.partial(combine_kernel, slots, rows, ways),
        out_shape=[jax.ShapeDtypeStruct((left * rows, width), jnp.float32)] + [out] * (ways - 1),
        in_specs=[vmem] * (1 + len(coded)),
        out_specs=[vmem] * ways,
        scratch_shapes=[pltpu.VMEM((tail_rows(left), width), jnp.float32)],
        compiler_params=pltpu.CompilerParams(vmem_limit_bytes=32 * 1024 * 1024),
        name="combine",
    )(own, *coded)


def hidden_kernel(chunks, parts, rows, *refs):
    out = refs[chunks * parts + 1]
    for c in range(chunks):
        own, self, coded = refs[c * parts], refs[c * parts + 1], refs[c * parts + 2:(c + 1) * parts]
        total = own[:rows, :] + self[...]
        for a in coded:
            total = total + read_coded(a, 1, rows)(0)
        out[c * rows:(c + 1) * rows, :] = jnp.maximum(total, 0.0).astype(jnp.bfloat16)


def hidden_rows(chunk_parts, rows, sel):
    chunks, parts = len(chunk_parts), len(chunk_parts[0])
    width = chunk_parts[0][0].shape[1]
    vmem = pl.BlockSpec(memory_space=pltpu.VMEM)
    flat = [a for part in chunk_parts for a in part]
    return pl.pallas_call(
        functools.partial(hidden_kernel, chunks, parts, rows),
        out_shape=jax.ShapeDtypeStruct((chunks * rows, width), jnp.bfloat16),
        in_specs=[vmem] * (len(flat) + 1),
        out_specs=vmem,
        compiler_params=pltpu.CompilerParams(vmem_limit_bytes=32 * 1024 * 1024),
        name="hidden_rows",
    )(*flat, sel)


def send_kernel(own, other, sel, send):
    both = jnp.concatenate([own[...], other[...]], axis=0)
    send[...] = jnp.dot(sel[...], both, preferred_element_type=jnp.float32).astype(jnp.bfloat16)


def rows_to_send(own, other, sel):
    vmem = pl.BlockSpec(memory_space=pltpu.VMEM)
    return pl.pallas_call(
        send_kernel,
        out_shape=jax.ShapeDtypeStruct((sel.shape[0], own.shape[1]), jnp.bfloat16),
        in_specs=[vmem] * 3,
        out_specs=vmem,
        compiler_params=pltpu.CompilerParams(vmem_limit_bytes=32 * 1024 * 1024),
        name="rows_to_send",
    )(own, other, sel)


def logits_kernel(own, other, received, front, adj_received, w_self, w_neigh, out):
    rows = out.shape[0]
    both = jnp.concatenate([own[...], other[...]], axis=0)
    local = jnp.dot(front[...], both, preferred_element_type=jnp.float32)
    mean = local[:rows, :] + jnp.dot(adj_received[...], received[...], preferred_element_type=jnp.float32)
    dims = (((1,), (1,)), ((), ()))
    got = lax.dot_general(local[rows:, :].astype(jnp.bfloat16), w_self[...], dims, preferred_element_type=jnp.float32)
    got = got + lax.dot_general(mean.astype(jnp.bfloat16), w_neigh[...], dims, preferred_element_type=jnp.float32)
    out[...] = got


def logits_of(own, other, received, front, adj_received, w_self, w_neigh):
    vmem = pl.BlockSpec(memory_space=pltpu.VMEM)
    return pl.pallas_call(
        logits_kernel,
        out_shape=jax.ShapeDtypeStruct((adj_received.shape[0], w_self.shape[1]), jnp.float32),
        in_specs=[vmem] * 7,
        out_specs=vmem,
        compiler_params=pltpu.CompilerParams(vmem_limit_bytes=32 * 1024 * 1024),
        name="logits",
    )(own, other, received, front, adj_received, w_self.T, w_neigh.T)


def exchange(parts, stride, n, places):
    got = [parts[0]]
    for k in places:
        got.append(lax.ppermute(parts[k], "dom", [(i, i ^ (k * stride)) for i in range(n)]))
    return got


def body(
    features,
    tile_weight,
    tile_dst,
    tile_src,
    tile_rows,
    w_self1,
    neighbour_weight_first,
    send_list,
    send_count,
    adj_two,
    w_self2,
    w_neigh2,
):
    n = lax.axis_size("dom")
    tile = tile_weight.shape[1]
    groups = tile // UNIT
    per = groups // 2 // CHUNKS
    bits = n.bit_length() - 1
    assert n == 1 << bits and bits >= 2
    radices = [2] * (bits // 2) + [1] * (bits % 2)
    ids = jnp.stack([lax.axis_index("feat"), lax.axis_index("dom")]).astype(jnp.int32)
    swap = [(0, 1), (1, 0)]
    xp = lax.ppermute(features, "feat", swap)
    wp = lax.ppermute(neighbour_weight_first, "feat", swap)
    tw = tile_weight.reshape(tile_weight.shape[0], groups, UNIT, tile)
    planned = plan(
        CHUNKS, per, n, 4, ids, tile_src, tile_rows, tile_dst, tw, features,
    )
    tables, tbufs, xo = planned[:CHUNKS], planned[CHUNKS:2 * CHUNKS], planned[2 * CHUNKS]
    wo, so = neighbour_weight_first, w_self1
    done = []
    for chunk in range(CHUNKS):
        accs = gathered_sums(per, n, tables[chunk], tbufs[chunk], xo, xp)
        slots, rows = n // 4, per * UNIT
        parts = {}
        (parts[3],) = sent_terms((3,), slots, rows, accs, wo, wp)
        parts[2], parts[1] = sent_terms((2, 1), slots, rows, accs, wo, wp)
        parts[0], theirs = own_terms(chunk, per, groups, slots, ids, accs, wo, wp, xo, so)
        self = lax.ppermute(theirs, "feat", swap)
        got = exchange(parts, 1, n, (1, 2, 3))
        stride = 4
        for radix in radices[1:]:
            ways = 1 << radix
            parts = combine(n // stride, per * UNIT, ways, got[0], got[1:])
            got = exchange(parts, stride, n, (2, 3, 1) if ways == 4 else (1,))
            stride *= ways
        done.append([got[0], self] + got[1:])
    sel, front, adj_received = selection(groups, ids, send_list, send_count, adj_two)
    own = hidden_rows(done, per * UNIT, sel)
    other = lax.ppermute(own, "feat", swap)
    send = rows_to_send(own, other, sel)
    received = lax.all_to_all(send, "dom", 0, 0, axis_index_groups=[group_order(n)], tiled=True)
    return logits_of(own, other, received, front, adj_received, w_self2, w_neigh2)


def solution(mesh):
    in_specs = (
        P("dom", "feat"),
        P("dom", None, None),
        P("dom"),
        P("dom"),
        P("dom"),
        P("feat", None),
        P("feat", None),
        P(),
        P(),
        P("dom", None),
        P(),
        P(),
    )
    out_specs = P("dom", None)
    return jax.shard_map(body, mesh=mesh, in_specs=in_specs, out_specs=out_specs, check_vma=False)
```

```python
import functools

import jax
import jax.numpy as jnp
from jax import lax
from jax.experimental import pallas as pl
from jax.experimental.pallas import tpu as pltpu
from jax.sharding import PartitionSpec as P

UNIT = 16
BLOCK = 4
STEP = 16
PIECES = 4
PART = 256
CHUNKS = 1


def group_of(core, place, groups):
    pair = 2 * (place // 2) + core
    return pair if place % 2 == 0 else groups - 1 - pair


def group_order(n):
    return list(range(n - 1, -1, -1))


LN2 = 0.6931471805599453


def tail_rows(slots):
    return -(-slots // 8) * 8


def encode(x):
    top = jnp.max(jnp.abs(x), axis=0, keepdims=True)
    power = jnp.ceil(jnp.log(jnp.maximum(top, 1e-30)) * (1.0 / LN2) + 1e-3) - 15.0
    return jnp.floor(x * jnp.exp(power * -LN2) + 0.5), power


def to_int16(x):
    return x.astype(jnp.int32).astype(jnp.int16)


def write_coded(out, tail, slots, rows, value_of):
    tail[...] = jnp.zeros_like(tail)
    for s in range(slots):
        whole, power = encode(value_of(s))
        out[s * rows:(s + 1) * rows, :] = to_int16(whole)
        tail[s:s + 1, :] = power
    out[slots * rows:, :] = to_int16(tail[...])


def read_coded(ref, slots, rows):
    powers = ref[slots * rows:, :].astype(jnp.int32).astype(jnp.float32)

    def value_of(s):
        whole = ref[s * rows:(s + 1) * rows, :].astype(jnp.int32).astype(jnp.float32)
        return whole * jnp.exp(powers[s:s + 1, :] * LN2)

    return value_of


def plan_kernel(chunks, per, n, radix, n_src, ids, src_h, rows_h, dst_h, tw, xo, *rest):
    tables, rest = rest[:chunks], rest[chunks:]
    tbufs, rest = rest[:chunks], rest[chunks:]
    xo_out, src_v, rows_v, dst_v, sems = rest
    core, me = ids[0], ids[1]
    tiles = src_v.shape[1]
    n_pos = tables[0].shape[1]
    units = per * tiles
    groups = 2 * per * chunks
    half = groups // 2
    gs = [group_of(core, i, groups) for i in range(half)]
    small = [(src_h, src_v), (rows_h, rows_v), (dst_h, dst_v)]
    some, rows = tiles // PIECES, xo.shape[0] // PIECES
    large = [
        (tw.at[pl.ds(q * some, some), g], tbufs[i // per].at[pl.ds(i % per * tiles + q * some, some)])
        for i, g in enumerate(gs)
        for q in range(PIECES)
    ]
    large += [(xo.at[pl.ds(q * rows, rows)], xo_out.at[pl.ds(q * rows, rows)]) for q in range(PIECES)]
    copies = [pltpu.make_async_copy(a, b, sems.at[i]) for i, (a, b) in enumerate(small + large)]
    for c in copies:
        c.start()
    lane = lax.broadcasted_iota(jnp.int32, (1, tiles), 1)
    block_i = lax.broadcasted_iota(jnp.int32, (n_src, tiles), 0)
    before = lax.broadcasted_iota(jnp.int32, (units, units), 0) < lax.broadcasted_iota(jnp.int32, (units, units), 1)
    before = jnp.where(before, 1.0, 0.0).astype(jnp.bfloat16)
    pos_i = lax.broadcasted_iota(jnp.int32, (tiles, n_pos), 1).astype(jnp.float32)
    place_i = lax.broadcasted_iota(jnp.int32, (1, n_pos), 1)
    trash = float(n * per << 14)
    for c in copies[:3]:
        c.wait()
    src, rows = src_v[...], rows_v[...]
    slot = jnp.bitwise_xor(dst_v[...], me)
    slot = jnp.bitwise_and(slot, radix - 1) * (n // radix) + lax.div(slot, radix)
    for c in range(chunks):
        hot, words, valid = [], [], []
        for j in range(per):
            limit = jnp.clip(rows - UNIT * gs[c * per + j], 0, UNIT)
            ok = limit > 0
            valid.append(ok)
            words.append(((slot * per + j) * 512 + (j * tiles + lane)) * 32 + limit)
            hot.append(jnp.where(jnp.logical_and(block_i == src, ok), 1.0, 0.0))
        hot = jnp.concatenate(hot, axis=1)
        earlier = jnp.dot(hot.astype(jnp.bfloat16), before, preferred_element_type=jnp.float32)
        blocks = jnp.floor((jnp.sum(hot, axis=1, keepdims=True) + (BLOCK - 1)) * (1.0 / BLOCK))
        ahead = jnp.zeros(blocks.shape, jnp.float32)
        source_i = lax.broadcasted_iota(jnp.int32, blocks.shape, 0)
        for s in range(n_src - 1):
            ahead = ahead + jnp.where(source_i > s, blocks[s:s + 1, :], 0.0)
        pos = jnp.sum(hot * (earlier + ahead * BLOCK), axis=0, keepdims=True)
        behind = jnp.where(place_i.astype(jnp.float32) >= ahead + blocks, 1.0, 0.0)
        owner = jnp.sum(behind, axis=0, keepdims=True)
        run = ahead[n_src - 1:, :] + blocks[n_src - 1:, :]
        stack = [jnp.where(valid[j], pos[:, j * tiles:(j + 1) * tiles], -1.0) for j in range(per)]
        stack += [w.astype(jnp.float32) - trash for w in words]
        stack += [jnp.zeros((1, tiles), jnp.float32)] * (-len(stack) % 8)
        cols = jnp.concatenate(stack, axis=0).T
        found = jnp.zeros((tiles, n_pos), jnp.float32)
        for j in range(per):
            found = found + jnp.where(cols[:, j:j + 1] == pos_i, cols[:, per + j:per + j + 1], 0.0)
        word = jnp.sum(found, axis=0, keepdims=True) + trash
        owner = jnp.where(place_i == n_pos - 1, run, jnp.minimum(owner, n_src - 1.0))
        tables[c][0:1, :] = word.astype(jnp.int32)
        tables[c][1:2, :] = owner.astype(jnp.int32)

    for c in copies[3:]:
        c.wait()


def plan(chunks, per, n, radix, ids, src, rows, dst, tw, xo):
    tiles, _, _, tile = tw.shape
    n_src = xo.shape[0] // tile
    blocks = -(-(per * tiles // BLOCK + n_src) // STEP) * STEP
    n_pos = -(-(blocks * BLOCK + 1) // 128) * 128
    smem = pl.BlockSpec(memory_space=pltpu.SMEM)
    vmem = pl.BlockSpec(memory_space=pltpu.VMEM)
    hbm = pl.BlockSpec(memory_space=pltpu.HBM)
    half = chunks * per
    return pl.pallas_call(
        functools.partial(plan_kernel, chunks, per, n, radix, n_src),
        out_shape=[jax.ShapeDtypeStruct((2, n_pos), jnp.int32)] * chunks
        + [jax.ShapeDtypeStruct((per * tiles, UNIT, tile), tw.dtype)] * chunks
        + [jax.ShapeDtypeStruct(xo.shape, xo.dtype)],
        in_specs=[smem] + [hbm] * 5,
        out_specs=[vmem] * (2 * chunks + 1),
        scratch_shapes=[
            pltpu.VMEM((1, tiles), jnp.int32),
            pltpu.VMEM((1, tiles), jnp.int32),
            pltpu.VMEM((1, tiles), jnp.int32),
            pltpu.SemaphoreType.DMA((3 + (half + 1) * PIECES,)),
        ],
        compiler_params=pltpu.CompilerParams(vmem_limit_bytes=32 * 1024 * 1024),
        name="plan",
    )(ids, *[
        pltpu.with_memory_space_constraint(a, pltpu.HBM)
        for a in (src.reshape(1, tiles), rows.reshape(1, tiles), dst.reshape(1, tiles), tw, xo)
    ])


def select_kernel(groups, ids, lists, counts, adj, sel, front, adj_out):
    core, me = ids[0], ids[1]
    n = lists.shape[0]
    slots = lists.shape[1]
    total = n * slots
    q_n = lax.broadcasted_iota(jnp.int32, (total, n), 0)
    r_n = lax.broadcasted_iota(jnp.int32, (total, n), 1)
    mine = lists[me].astype(jnp.float32)
    cnt = counts[pl.ds(me, 1), :]
    picked = jnp.zeros((total, n), jnp.float32)
    k_n = jnp.bitwise_and(q_n, slots - 1)
    for k in range(slots):
        picked = jnp.where(k_n == k, mine[k:k + 1, :], picked)
    good = jnp.logical_and(n - 1 - lax.div(q_n, slots) == r_n, k_n < cnt)
    row = jnp.sum(jnp.where(good, picked + 1.0, 0.0), axis=1, keepdims=True) - 1.0
    lane = lax.broadcasted_iota(jnp.int32, (1, sel.shape[1]), 1)
    name = jnp.zeros(lane.shape, jnp.int32)
    names = [group_of(c, i, groups) for c in (core, 1 - core) for i in range(groups // 2)]
    for i, g in enumerate(names):
        name = jnp.where(lax.div(lane, UNIT) == i, g * UNIT + jnp.bitwise_and(lane, UNIT - 1), name)
    sel[...] = jnp.where(row == name.astype(jnp.float32), 1.0, 0.0).astype(jnp.bfloat16)
    tile, out_rows = groups * UNIT, adj.shape[0]
    placed = jnp.where(lax.broadcasted_iota(jnp.int32, (tile, tile), 0) == name, 1.0, 0.0).astype(jnp.bfloat16)
    front[:out_rows, :] = jnp.dot(adj[:, :tile], placed, preferred_element_type=jnp.float32).astype(jnp.bfloat16)
    front[out_rows:, :] = placed[:out_rows, :]
    column = lax.broadcasted_iota(jnp.int32, (1, total), 1)
    source = (n - 1 - lax.div(column, slots)) * slots + lax.rem(column, slots)
    moved = jnp.where(lax.broadcasted_iota(jnp.int32, (total, total), 0) == source, 1.0, 0.0).astype(jnp.bfloat16)
    adj_out[...] = jnp.dot(adj[:, groups * UNIT:], moved, preferred_element_type=jnp.float32).astype(jnp.bfloat16)


def selection(groups, ids, send_list, send_count, adj):
    n, _, slots = send_list.shape
    smem = pl.BlockSpec(memory_space=pltpu.SMEM)
    vmem = pl.BlockSpec(memory_space=pltpu.VMEM)
    return pl.pallas_call(
        functools.partial(select_kernel, groups),
        out_shape=[
            jax.ShapeDtypeStruct((n * slots, groups * UNIT), jnp.bfloat16),
            jax.ShapeDtypeStruct((2 * adj.shape[0], groups * UNIT), jnp.bfloat16),
            jax.ShapeDtypeStruct((adj.shape[0], n * slots), jnp.bfloat16),
        ],
        in_specs=[smem, vmem, vmem, vmem],
        out_specs=[vmem] * 3,
        compiler_params=pltpu.CompilerParams(vmem_limit_bytes=32 * 1024 * 1024),
        name="selection",
    )(ids, jnp.swapaxes(send_list, 1, 2), send_count, adj)


def tiles_kernel(table_v, tbuf, xo, xp, *rest):
    parts = len(rest) - 3
    accs, (masks, table, sem) = rest[:parts], rest[parts:]
    tile = tbuf.shape[2]
    width = xo.shape[1]
    to_scalar = pltpu.make_async_copy(table_v, table, sem)
    to_scalar.start()
    for acc in accs:
        acc[...] = jnp.zeros_like(acc)
    row_i = lax.broadcasted_iota(jnp.int32, (UNIT, tile), 0)
    for m in range(UNIT + 1):
        masks[m] = jnp.where(row_i < m, 1.0, 0.0).astype(jnp.bfloat16)
    columns = [(x, h) for x in (xo, xp) for h in range(0, width, PART)]
    to_scalar.wait()

    def blocks(first, count):
        for m in range(count):
            at = first + m
            base = pl.multiple_of(table[1, at] * tile, tile)
            rows, places = [], []
            for k in range(BLOCK):
                word = table[0, at * BLOCK + k]
                u = jnp.bitwise_and(lax.shift_right_logical(word, 5), 511)
                rows.append(tbuf[u] * masks[jnp.bitwise_and(word, 31)])
                places.append(pl.multiple_of(lax.shift_right_logical(word, 14) * UNIT, UNIT))
            lhs = jnp.concatenate(rows, axis=0)
            for acc, (x, h) in zip(accs, columns):
                got = jnp.dot(lhs, x[pl.ds(base, tile), h:h + PART], preferred_element_type=jnp.float32)
                got = got.astype(jnp.bfloat16).astype(jnp.float32)
                for k in range(BLOCK):
                    acc[pl.ds(places[k], UNIT), :] += got[k * UNIT:(k + 1) * UNIT, :]

    half = STEP // 2
    halves = lax.div(table[1, table.shape[1] - 1] + half - 1, half)
    steps = lax.div(halves, 2)

    def step(i, carry):
        blocks(i * STEP, STEP)
        return carry

    def last(i, carry):
        blocks(steps * STEP, half)
        return carry

    lax.fori_loop(0, steps, step, 0)
    lax.fori_loop(0, lax.rem(halves, 2), last, 0)


def gathered_sums(per, n, table, tbuf, xo, xp):
    width = xo.shape[1]
    tile = tbuf.shape[2]
    vmem = pl.BlockSpec(memory_space=pltpu.VMEM)
    flops = 2 * tbuf.shape[0] * UNIT * tile * 2 * width
    parts = 2 * width // PART
    sums = jax.ShapeDtypeStruct(((n * per + 1) * UNIT, PART), jnp.float32)
    return pl.pallas_call(
        tiles_kernel,
        out_shape=[sums] * parts,
        in_specs=[vmem] * 4,
        out_specs=[vmem] * parts,
        scratch_shapes=[
            pltpu.VMEM((UNIT + 1, UNIT, tile), jnp.bfloat16),
            pltpu.SMEM(table.shape, jnp.int32),
            pltpu.SemaphoreType.DMA,
        ],
        compiler_params=pltpu.CompilerParams(vmem_limit_bytes=(12 << 20) + sums.size * 4 * parts),
        cost_estimate=pl.CostEstimate(flops=flops, bytes_accessed=8 << 20, transcendentals=0),
        name="gathered_sums",
    )(table, tbuf, xo, xp)


def weigh(accs, weights, first, count, out):
    size = min(256, count)

    def piece(r, carry):
        at = r * size if isinstance(r, int) else pl.multiple_of(r * size, size)
        got = jnp.zeros((size, out.shape[1]), jnp.float32)
        for i, acc in enumerate(accs):
            w, h = weights[i * PART // weights[0].shape[0]], i * PART % weights[0].shape[0]
            value = acc[pl.ds(first + at, size), :]
            high = value.astype(jnp.bfloat16)
            low = (value - high.astype(jnp.float32)).astype(jnp.bfloat16)
            got = got + jnp.dot(high, w[h:h + PART, :], preferred_element_type=jnp.float32)
            got = got + jnp.dot(low, w[h:h + PART, :], preferred_element_type=jnp.float32)
        out[pl.ds(at, size), :] = got
        return carry

    if count == size:
        piece(0, 0)
    else:
        lax.fori_loop(0, count // size, piece, 0)


def sent_kernel(ks, slots, rows, parts, wo, wp, *refs):
    accs, outs, scratch = refs[:parts], refs[parts:parts + len(ks)], refs[parts + len(ks):]
    for i, k in enumerate(ks):
        sums, tail = scratch[2 * i:2 * i + 2]
        weigh(accs, (wo, wp), k * slots * rows, slots * rows, sums)
        write_coded(outs[i], tail, slots, rows, lambda s: sums[s * rows:(s + 1) * rows, :])


def sent_terms(ks, slots, rows, accs, wo, wp):
    hidden = wo.shape[1]
    vmem = pl.BlockSpec(memory_space=pltpu.VMEM)
    coded = jax.ShapeDtypeStruct((slots * rows + tail_rows(slots), hidden), jnp.int16)
    return pl.pallas_call(
        functools.partial(sent_kernel, ks, slots, rows, len(accs)),
        out_shape=[coded] * len(ks),
        in_specs=[vmem] * (2 + len(accs)),
        out_specs=[vmem] * len(ks),
        scratch_shapes=[
            pltpu.VMEM((slots * rows, hidden), jnp.float32),
            pltpu.VMEM((tail_rows(slots), hidden), jnp.float32),
        ] * len(ks),
        compiler_params=pltpu.CompilerParams(vmem_limit_bytes=(20 << 20) + accs[0].size * 4 * len(accs)),
        cost_estimate=pl.CostEstimate(
            flops=4 * len(ks) * slots * rows * PART * len(accs) * hidden, bytes_accessed=2 << 20, transcendentals=0),
        name="sent_terms",
    )(wo, wp, *accs)


def own_kernel(chunk, per, groups, parts, ids, wo, wp, xo, so, *refs):
    accs, (out, theirs, terms) = refs[:parts], refs[parts:]
    weigh(accs, (wo, wp), 0, out.shape[0], out)
    terms[...] = jnp.dot(xo[:groups * UNIT, :], so[...], preferred_element_type=jnp.float32)
    for j in range(per):
        here = slice(j * UNIT, (j + 1) * UNIT)
        at = pl.multiple_of(group_of(ids[0], chunk * per + j, groups) * UNIT, UNIT)
        out[here, :] += terms[pl.ds(at, UNIT), :]
        at = pl.multiple_of(group_of(1 - ids[0], chunk * per + j, groups) * UNIT, UNIT)
        theirs[here, :] = terms[pl.ds(at, UNIT), :]


def own_terms(chunk, per, groups, slots, ids, accs, wo, wp, xo, so):
    hidden = wo.shape[1]
    rows = per * UNIT
    smem = pl.BlockSpec(memory_space=pltpu.SMEM)
    vmem = pl.BlockSpec(memory_space=pltpu.VMEM)
    return pl.pallas_call(
        functools.partial(own_kernel, chunk, per, groups, len(accs)),
        out_shape=[
            jax.ShapeDtypeStruct((slots * rows, hidden), jnp.float32),
            jax.ShapeDtypeStruct((rows, hidden), jnp.float32),
        ],
        in_specs=[smem] + [vmem] * (4 + len(accs)),
        out_specs=[vmem] * 2,
        scratch_shapes=[pltpu.VMEM((groups * UNIT, hidden), jnp.float32)],
        compiler_params=pltpu.CompilerParams(vmem_limit_bytes=(12 << 20) + accs[0].size * 4 * len(accs)),
        cost_estimate=pl.CostEstimate(
            flops=4 * slots * rows * PART * len(accs) * hidden, bytes_accessed=2 << 20, transcendentals=0),
        name="own_terms",
    )(ids, wo, wp, xo, so, *accs)


def combine_kernel(slots, rows, ways, own, *refs):
    parts = len(refs) - ways - 1
    coded, outs, tail = refs[:parts], refs[parts:parts + ways], refs[parts + ways]
    values = [read_coded(a, slots, rows) for a in coded]

    def total(s):
        got = own[s * rows:(s + 1) * rows, :]
        for value in values:
            got = got + value(s)
        return got

    for i in range(slots // ways):
        outs[0][i * rows:(i + 1) * rows, :] = total(i * ways)
    for k in range(1, ways):
        write_coded(outs[k], tail, slots // ways, rows, lambda s: total(s * ways + k))


def combine(slots, rows, ways, own, coded):
    width = own.shape[1]
    left = slots // ways
    vmem = pl.BlockSpec(memory_space=pltpu.VMEM)
    out = jax.ShapeDtypeStruct((left * rows + tail_rows(left), width), jnp.int16)
    return pl.pallas_call(
        functools.partial(combine_kernel, slots, rows, ways),
        out_shape=[jax.ShapeDtypeStruct((left * rows, width), jnp.float32)] + [out] * (ways - 1),
        in_specs=[vmem] * (1 + len(coded)),
        out_specs=[vmem] * ways,
        scratch_shapes=[pltpu.VMEM((tail_rows(left), width), jnp.float32)],
        compiler_params=pltpu.CompilerParams(vmem_limit_bytes=32 * 1024 * 1024),
        name="combine",
    )(own, *coded)


def hidden_kernel(chunks, parts, rows, *refs):
    out = refs[chunks * parts + 1]
    for c in range(chunks):
        own, self, coded = refs[c * parts], refs[c * parts + 1], refs[c * parts + 2:(c + 1) * parts]
        total = own[:rows, :] + self[...]
        for a in coded:
            total = total + read_coded(a, 1, rows)(0)
        out[c * rows:(c + 1) * rows, :] = jnp.maximum(total, 0.0).astype(jnp.bfloat16)


def hidden_rows(chunk_parts, rows, sel):
    chunks, parts = len(chunk_parts), len(chunk_parts[0])
    width = chunk_parts[0][0].shape[1]
    vmem = pl.BlockSpec(memory_space=pltpu.VMEM)
    flat = [a for part in chunk_parts for a in part]
    return pl.pallas_call(
        functools.partial(hidden_kernel, chunks, parts, rows),
        out_shape=jax.ShapeDtypeStruct((chunks * rows, width), jnp.bfloat16),
        in_specs=[vmem] * (len(flat) + 1),
        out_specs=vmem,
        compiler_params=pltpu.CompilerParams(vmem_limit_bytes=32 * 1024 * 1024),
        name="hidden_rows",
    )(*flat, sel)


def send_kernel(own, other, sel, send):
    both = jnp.concatenate([own[...], other[...]], axis=0)
    send[...] = jnp.dot(sel[...], both, preferred_element_type=jnp.float32).astype(jnp.bfloat16)


def rows_to_send(own, other, sel):
    vmem = pl.BlockSpec(memory_space=pltpu.VMEM)
    return pl.pallas_call(
        send_kernel,
        out_shape=jax.ShapeDtypeStruct((sel.shape[0], own.shape[1]), jnp.bfloat16),
        in_specs=[vmem] * 3,
        out_specs=vmem,
        compiler_params=pltpu.CompilerParams(vmem_limit_bytes=32 * 1024 * 1024),
        name="rows_to_send",
    )(own, other, sel)


def logits_kernel(own, other, received, front, adj_received, w_self, w_neigh, out):
    rows = out.shape[0]
    both = jnp.concatenate([own[...], other[...]], axis=0)
    local = jnp.dot(front[...], both, preferred_element_type=jnp.float32)
    mean = local[:rows, :] + jnp.dot(adj_received[...], received[...], preferred_element_type=jnp.float32)
    dims = (((1,), (1,)), ((), ()))
    got = lax.dot_general(local[rows:, :].astype(jnp.bfloat16), w_self[...], dims, preferred_element_type=jnp.float32)
    got = got + lax.dot_general(mean.astype(jnp.bfloat16), w_neigh[...], dims, preferred_element_type=jnp.float32)
    out[...] = got


def logits_of(own, other, received, front, adj_received, w_self, w_neigh):
    vmem = pl.BlockSpec(memory_space=pltpu.VMEM)
    return pl.pallas_call(
        logits_kernel,
        out_shape=jax.ShapeDtypeStruct((adj_received.shape[0], w_self.shape[1]), jnp.float32),
        in_specs=[vmem] * 7,
        out_specs=vmem,
        compiler_params=pltpu.CompilerParams(vmem_limit_bytes=32 * 1024 * 1024),
        name="logits",
    )(own, other, received, front, adj_received, w_self.T, w_neigh.T)


def exchange(parts, stride, n, places):
    got = [parts[0]]
    for k in places:
        got.append(lax.ppermute(parts[k], "dom", [(i, i ^ (k * stride)) for i in range(n)]))
    return got


def body(
    features,
    tile_weight,
    tile_dst,
    tile_src,
    tile_rows,
    w_self1,
    neighbour_weight_first,
    send_list,
    send_count,
    adj_two,
    w_self2,
    w_neigh2,
):
    n = lax.axis_size("dom")
    tile = tile_weight.shape[1]
    groups = tile // UNIT
    per = groups // 2 // CHUNKS
    bits = n.bit_length() - 1
    assert n == 1 << bits and bits >= 2
    radices = [2] * (bits // 2) + [1] * (bits % 2)
    ids = jnp.stack([lax.axis_index("feat"), lax.axis_index("dom")]).astype(jnp.int32)
    swap = [(0, 1), (1, 0)]
    xp = lax.ppermute(features, "feat", swap)
    wp = lax.ppermute(neighbour_weight_first, "feat", swap)
    tw = tile_weight.reshape(tile_weight.shape[0], groups, UNIT, tile)
    planned = plan(
        CHUNKS, per, n, 4, ids, tile_src, tile_rows, tile_dst, tw, features,
    )
    tables, tbufs, xo = planned[:CHUNKS], planned[CHUNKS:2 * CHUNKS], planned[2 * CHUNKS]
    wo, so = neighbour_weight_first, w_self1
    done = []
    for chunk in range(CHUNKS):
        accs = gathered_sums(per, n, tables[chunk], tbufs[chunk], xo, xp)
        slots, rows = n // 4, per * UNIT
        parts = {}
        (parts[3],) = sent_terms((3,), slots, rows, accs, wo, wp)
        parts[2], parts[1] = sent_terms((2, 1), slots, rows, accs, wo, wp)
        parts[0], theirs = own_terms(chunk, per, groups, slots, ids, accs, wo, wp, xo, so)
        self = lax.ppermute(theirs, "feat", swap)
        got = exchange(parts, 1, n, (1, 2, 3))
        stride = 4
        for radix in radices[1:]:
            ways = 1 << radix
            parts = combine(n // stride, per * UNIT, ways, got[0], got[1:])
            got = exchange(parts, stride, n, (2, 3, 1) if ways == 4 else (1,))
            stride *= ways
        done.append([got[0], self] + got[1:])
    sel, front, adj_received = selection(groups, ids, send_list, send_count, adj_two)
    own = hidden_rows(done, per * UNIT, sel)
    other = lax.ppermute(own, "feat", swap)
    send = rows_to_send(own, other, sel)
    received = lax.all_to_all(send, "dom", 0, 0, axis_index_groups=[group_order(n)], tiled=True)
    return logits_of(own, other, received, front, adj_received, w_self2, w_neigh2)


def solution(mesh):
    in_specs = (
        P("dom", "feat"),
        P("dom", None, None),
        P("dom"),
        P("dom"),
        P("dom"),
        P("feat", None),
        P("feat", None),
        P(),
        P(),
        P("dom", None),
        P(),
        P(),
    )
    out_specs = P("dom", None)
    return jax.shard_map(body, mesh=mesh, in_specs=in_specs, out_specs=out_specs, check_vma=False)
```

```python
import functools

import jax
import jax.numpy as jnp
from jax import lax
from jax.experimental import pallas as pl
from jax.experimental.pallas import tpu as pltpu
from jax.sharding import PartitionSpec as P

UNIT = 16
BLOCK = 4
STEP = 16
PART = 256
CHUNKS = 1


def group_of(core, place, groups):
    pair = 2 * (place // 2) + core
    return pair if place % 2 == 0 else groups - 1 - pair


def group_order(n):
    return list(range(n - 1, -1, -1))


LN2 = 0.6931471805599453


def tail_rows(slots):
    return -(-slots // 8) * 8


def encode(x):
    top = jnp.max(jnp.abs(x), axis=0, keepdims=True)
    power = jnp.ceil(jnp.log(jnp.maximum(top, 1e-30)) * (1.0 / LN2) + 1e-3) - 15.0
    return jnp.floor(x * jnp.exp(power * -LN2) + 0.5), power


def to_int16(x):
    return x.astype(jnp.int32).astype(jnp.int16)


def write_coded(out, tail, slots, rows, value_of):
    tail[...] = jnp.zeros_like(tail)
    for s in range(slots):
        whole, power = encode(value_of(s))
        out[s * rows:(s + 1) * rows, :] = to_int16(whole)
        tail[s:s + 1, :] = power
    out[slots * rows:, :] = to_int16(tail[...])


def read_coded(ref, slots, rows):
    powers = ref[slots * rows:, :].astype(jnp.int32).astype(jnp.float32)

    def value_of(s):
        whole = ref[s * rows:(s + 1) * rows, :].astype(jnp.int32).astype(jnp.float32)
        return whole * jnp.exp(powers[s:s + 1, :] * LN2)

    return value_of


def plan_kernel(chunks, per, n, radix, n_src, ids, src_h, rows_h, dst_h, tw, xo, *rest):
    tables, rest = rest[:chunks], rest[chunks:]
    tbufs, rest = rest[:chunks], rest[chunks:]
    xo_out, src_v, rows_v, dst_v, sems = rest
    core, me = ids[0], ids[1]
    tiles = src_v.shape[1]
    n_pos = tables[0].shape[1]
    units = per * tiles
    groups = 2 * per * chunks
    half = groups // 2
    gs = [group_of(core, i, groups) for i in range(half)]
    small = [(src_h, src_v), (rows_h, rows_v), (dst_h, dst_v)]
    large = [(tw.at[:, g], tbufs[i // per].at[pl.ds(i % per * tiles, tiles)]) for i, g in enumerate(gs)]
    large += [(xo, xo_out)]
    copies = [pltpu.make_async_copy(a, b, sems.at[i]) for i, (a, b) in enumerate(small + large)]
    for c in copies:
        c.start()
    lane = lax.broadcasted_iota(jnp.int32, (1, tiles), 1)
    block_i = lax.broadcasted_iota(jnp.int32, (n_src, tiles), 0)
    before = lax.broadcasted_iota(jnp.int32, (tiles, tiles), 0) < lax.broadcasted_iota(jnp.int32, (tiles, tiles), 1)
    before = jnp.where(before, 1.0, 0.0).astype(jnp.bfloat16)
    pos_i = lax.broadcasted_iota(jnp.int32, (tiles, n_pos), 1).astype(jnp.float32)
    place_i = lax.broadcasted_iota(jnp.int32, (1, n_pos), 1)
    trash = float(n * per << 14)
    for c in copies[:3]:
        c.wait()
    src, rows = src_v[...], rows_v[...]
    slot = jnp.bitwise_xor(dst_v[...], me)
    slot = jnp.bitwise_and(slot, radix - 1) * (n // radix) + lax.div(slot, radix)
    for c in range(chunks):
        hot, words, valid = [], [], []
        for j in range(per):
            limit = jnp.clip(rows - UNIT * gs[c * per + j], 0, UNIT)
            ok = limit > 0
            valid.append(ok)
            words.append(((slot * per + j) * 512 + (j * tiles + lane)) * 32 + limit)
            hot.append(jnp.where(jnp.logical_and(block_i == src, ok), 1.0, 0.0))
        stacked = jnp.concatenate(hot, axis=0)
        earlier = jnp.dot(stacked.astype(jnp.bfloat16), before, preferred_element_type=jnp.float32)
        counts = jnp.sum(stacked, axis=1, keepdims=True)
        counts = [counts[j * n_src:(j + 1) * n_src, :] for j in range(per)]
        blocks = jnp.floor((sum(counts) + (BLOCK - 1)) * (1.0 / BLOCK))
        ahead = jnp.zeros(blocks.shape, jnp.float32)
        source_i = lax.broadcasted_iota(jnp.int32, blocks.shape, 0)
        for s in range(n_src - 1):
            ahead = ahead + jnp.where(source_i > s, blocks[s:s + 1, :], 0.0)
        first, pos = ahead * BLOCK, []
        for j in range(per):
            place = hot[j] * (earlier[j * n_src:(j + 1) * n_src, :] + first)
            pos.append(jnp.sum(place, axis=0, keepdims=True))
            first = first + counts[j]
        behind = jnp.where(place_i.astype(jnp.float32) >= ahead + blocks, 1.0, 0.0)
        owner = jnp.sum(behind, axis=0, keepdims=True)
        run = ahead[n_src - 1:, :] + blocks[n_src - 1:, :]
        stack = [jnp.where(valid[j], pos[j], -1.0) for j in range(per)]
        stack += [w.astype(jnp.float32) - trash for w in words]
        stack += [jnp.zeros((1, tiles), jnp.float32)] * (-len(stack) % 8)
        cols = jnp.concatenate(stack, axis=0).T
        found = jnp.zeros((tiles, n_pos), jnp.float32)
        for j in range(per):
            found = found + jnp.where(cols[:, j:j + 1] == pos_i, cols[:, per + j:per + j + 1], 0.0)
        word = jnp.sum(found, axis=0, keepdims=True) + trash
        owner = jnp.where(place_i == n_pos - 1, run, jnp.minimum(owner, n_src - 1.0))
        tables[c][0:1, :] = word.astype(jnp.int32)
        tables[c][1:2, :] = owner.astype(jnp.int32)

    for c in copies[3:]:
        c.wait()


def plan(chunks, per, n, radix, ids, src, rows, dst, tw, xo):
    tiles, _, _, tile = tw.shape
    n_src = xo.shape[0] // tile
    blocks = -(-(per * tiles // BLOCK + n_src) // STEP) * STEP
    n_pos = -(-(blocks * BLOCK + 1) // 128) * 128
    smem = pl.BlockSpec(memory_space=pltpu.SMEM)
    vmem = pl.BlockSpec(memory_space=pltpu.VMEM)
    hbm = pl.BlockSpec(memory_space=pltpu.HBM)
    half = chunks * per
    return pl.pallas_call(
        functools.partial(plan_kernel, chunks, per, n, radix, n_src),
        out_shape=[jax.ShapeDtypeStruct((2, n_pos), jnp.int32)] * chunks
        + [jax.ShapeDtypeStruct((per * tiles, UNIT, tile), tw.dtype)] * chunks
        + [jax.ShapeDtypeStruct(xo.shape, xo.dtype)],
        in_specs=[smem] + [hbm] * 5,
        out_specs=[vmem] * (2 * chunks + 1),
        scratch_shapes=[
            pltpu.VMEM((1, tiles), jnp.int32),
            pltpu.VMEM((1, tiles), jnp.int32),
            pltpu.VMEM((1, tiles), jnp.int32),
            pltpu.SemaphoreType.DMA((3 + half + 1,)),
        ],
        compiler_params=pltpu.CompilerParams(vmem_limit_bytes=32 * 1024 * 1024),
        name="plan",
    )(ids, *[
        pltpu.with_memory_space_constraint(a, pltpu.HBM)
        for a in (src.reshape(1, tiles), rows.reshape(1, tiles), dst.reshape(1, tiles), tw, xo)
    ])


def select_kernel(groups, ids, lists, counts, adj, sel, front, adj_out):
    core, me = ids[0], ids[1]
    n = lists.shape[0]
    slots = lists.shape[1]
    total = n * slots
    q_n = lax.broadcasted_iota(jnp.int32, (total, n), 0)
    r_n = lax.broadcasted_iota(jnp.int32, (total, n), 1)
    mine = lists[me].astype(jnp.float32)
    cnt = counts[pl.ds(me, 1), :]
    picked = jnp.zeros((total, n), jnp.float32)
    k_n = jnp.bitwise_and(q_n, slots - 1)
    for k in range(slots):
        picked = jnp.where(k_n == k, mine[k:k + 1, :], picked)
    good = jnp.logical_and(n - 1 - lax.div(q_n, slots) == r_n, k_n < cnt)
    row = jnp.sum(jnp.where(good, picked + 1.0, 0.0), axis=1, keepdims=True) - 1.0
    lane = lax.broadcasted_iota(jnp.int32, (1, sel.shape[1]), 1)
    name = jnp.zeros(lane.shape, jnp.int32)
    names = [group_of(c, i, groups) for c in (core, 1 - core) for i in range(groups // 2)]
    for i, g in enumerate(names):
        name = jnp.where(lax.div(lane, UNIT) == i, g * UNIT + jnp.bitwise_and(lane, UNIT - 1), name)
    sel[...] = jnp.where(row == name.astype(jnp.float32), 1.0, 0.0).astype(jnp.bfloat16)
    tile, out_rows = groups * UNIT, adj.shape[0]
    placed = jnp.where(lax.broadcasted_iota(jnp.int32, (tile, tile), 0) == name, 1.0, 0.0).astype(jnp.bfloat16)
    front[:out_rows, :] = jnp.dot(adj[:, :tile], placed, preferred_element_type=jnp.float32).astype(jnp.bfloat16)
    front[out_rows:, :] = placed[:out_rows, :]
    column = lax.broadcasted_iota(jnp.int32, (1, total), 1)
    source = (n - 1 - lax.div(column, slots)) * slots + lax.rem(column, slots)
    moved = jnp.where(lax.broadcasted_iota(jnp.int32, (total, total), 0) == source, 1.0, 0.0).astype(jnp.bfloat16)
    adj_out[...] = jnp.dot(adj[:, groups * UNIT:], moved, preferred_element_type=jnp.float32).astype(jnp.bfloat16)


def selection(groups, ids, send_list, send_count, adj):
    n, _, slots = send_list.shape
    smem = pl.BlockSpec(memory_space=pltpu.SMEM)
    vmem = pl.BlockSpec(memory_space=pltpu.VMEM)
    return pl.pallas_call(
        functools.partial(select_kernel, groups),
        out_shape=[
            jax.ShapeDtypeStruct((n * slots, groups * UNIT), jnp.bfloat16),
            jax.ShapeDtypeStruct((2 * adj.shape[0], groups * UNIT), jnp.bfloat16),
            jax.ShapeDtypeStruct((adj.shape[0], n * slots), jnp.bfloat16),
        ],
        in_specs=[smem, vmem, vmem, vmem],
        out_specs=[vmem] * 3,
        compiler_params=pltpu.CompilerParams(vmem_limit_bytes=32 * 1024 * 1024),
        name="selection",
    )(ids, jnp.swapaxes(send_list, 1, 2), send_count, adj)


def tiles_kernel(table_v, tbuf, xo, xp, *rest):
    parts = len(rest) - 3
    accs, (masks, table, sem) = rest[:parts], rest[parts:]
    tile = tbuf.shape[2]
    width = xo.shape[1]
    to_scalar = pltpu.make_async_copy(table_v, table, sem)
    to_scalar.start()
    for acc in accs:
        acc[...] = jnp.zeros_like(acc)
    row_i = lax.broadcasted_iota(jnp.int32, (UNIT, tile), 0)
    for m in range(UNIT + 1):
        masks[m] = jnp.where(row_i < m, 1.0, 0.0).astype(jnp.bfloat16)
    columns = [(x, h) for x in (xo, xp) for h in range(0, width, PART)]
    to_scalar.wait()

    def blocks(first, count):
        for m in range(count):
            at = first + m
            base = pl.multiple_of(table[1, at] * tile, tile)
            rows, places = [], []
            for k in range(BLOCK):
                word = table[0, at * BLOCK + k]
                u = jnp.bitwise_and(lax.shift_right_logical(word, 5), 511)
                rows.append(tbuf[u] * masks[jnp.bitwise_and(word, 31)])
                places.append(pl.multiple_of(lax.shift_right_logical(word, 14) * UNIT, UNIT))
            lhs = jnp.concatenate(rows, axis=0)
            for acc, (x, h) in zip(accs, columns):
                got = jnp.dot(lhs, x[pl.ds(base, tile), h:h + PART], preferred_element_type=jnp.float32)
                got = got.astype(jnp.bfloat16).astype(jnp.float32)
                for k in range(BLOCK):
                    acc[pl.ds(places[k], UNIT), :] += got[k * UNIT:(k + 1) * UNIT, :]

    half = STEP // 2
    halves = lax.div(table[1, table.shape[1] - 1] + half - 1, half)
    steps = lax.div(halves, 2)

    def step(i, carry):
        blocks(i * STEP, STEP)
        return carry

    def last(i, carry):
        blocks(steps * STEP, half)
        return carry

    lax.fori_loop(0, steps, step, 0)
    lax.fori_loop(0, lax.rem(halves, 2), last, 0)


def gathered_sums(per, n, table, tbuf, xo, xp):
    width = xo.shape[1]
    tile = tbuf.shape[2]
    vmem = pl.BlockSpec(memory_space=pltpu.VMEM)
    flops = 2 * tbuf.shape[0] * UNIT * tile * 2 * width
    parts = 2 * width // PART
    sums = jax.ShapeDtypeStruct(((n * per + 1) * UNIT, PART), jnp.float32)
    return pl.pallas_call(
        tiles_kernel,
        out_shape=[sums] * parts,
        in_specs=[vmem] * 4,
        out_specs=[vmem] * parts,
        scratch_shapes=[
            pltpu.VMEM((UNIT + 1, UNIT, tile), jnp.bfloat16),
            pltpu.SMEM(table.shape, jnp.int32),
            pltpu.SemaphoreType.DMA,
        ],
        compiler_params=pltpu.CompilerParams(vmem_limit_bytes=(12 << 20) + sums.size * 4 * parts),
        cost_estimate=pl.CostEstimate(flops=flops, bytes_accessed=8 << 20, transcendentals=0),
        name="gathered_sums",
    )(table, tbuf, xo, xp)


def weigh(accs, weights, first, count, out):
    size = min(256, count)

    def piece(r, carry):
        at = r * size if isinstance(r, int) else pl.multiple_of(r * size, size)
        got = jnp.zeros((size, out.shape[1]), jnp.float32)
        for i, acc in enumerate(accs):
            w, h = weights[i * PART // weights[0].shape[0]], i * PART % weights[0].shape[0]
            value = acc[pl.ds(first + at, size), :]
            high = value.astype(jnp.bfloat16)
            low = (value - high.astype(jnp.float32)).astype(jnp.bfloat16)
            got = got + jnp.dot(high, w[h:h + PART, :], preferred_element_type=jnp.float32)
            got = got + jnp.dot(low, w[h:h + PART, :], preferred_element_type=jnp.float32)
        out[pl.ds(at, size), :] = got
        return carry

    if count == size:
        piece(0, 0)
    else:
        lax.fori_loop(0, count // size, piece, 0)


def sent_kernel(ks, slots, rows, parts, wo, wp, *refs):
    accs, outs, scratch = refs[:parts], refs[parts:parts + len(ks)], refs[parts + len(ks):]
    for i, k in enumerate(ks):
        sums, tail = scratch[2 * i:2 * i + 2]
        weigh(accs, (wo, wp), k * slots * rows, slots * rows, sums)
        write_coded(outs[i], tail, slots, rows, lambda s: sums[s * rows:(s + 1) * rows, :])


def sent_terms(ks, slots, rows, accs, wo, wp):
    hidden = wo.shape[1]
    vmem = pl.BlockSpec(memory_space=pltpu.VMEM)
    coded = jax.ShapeDtypeStruct((slots * rows + tail_rows(slots), hidden), jnp.int16)
    return pl.pallas_call(
        functools.partial(sent_kernel, ks, slots, rows, len(accs)),
        out_shape=[coded] * len(ks),
        in_specs=[vmem] * (2 + len(accs)),
        out_specs=[vmem] * len(ks),
        scratch_shapes=[
            pltpu.VMEM((slots * rows, hidden), jnp.float32),
            pltpu.VMEM((tail_rows(slots), hidden), jnp.float32),
        ] * len(ks),
        compiler_params=pltpu.CompilerParams(vmem_limit_bytes=(20 << 20) + accs[0].size * 4 * len(accs)),
        cost_estimate=pl.CostEstimate(
            flops=4 * len(ks) * slots * rows * PART * len(accs) * hidden, bytes_accessed=2 << 20, transcendentals=0),
        name="sent_terms",
    )(wo, wp, *accs)


def own_kernel(chunk, per, groups, parts, ids, wo, wp, xo, so, *refs):
    accs, (out, theirs, terms) = refs[:parts], refs[parts:]
    weigh(accs, (wo, wp), 0, out.shape[0], out)
    terms[...] = jnp.dot(xo[:groups * UNIT, :], so[...], preferred_element_type=jnp.float32)
    for j in range(per):
        here = slice(j * UNIT, (j + 1) * UNIT)
        at = pl.multiple_of(group_of(ids[0], chunk * per + j, groups) * UNIT, UNIT)
        out[here, :] += terms[pl.ds(at, UNIT), :]
        at = pl.multiple_of(group_of(1 - ids[0], chunk * per + j, groups) * UNIT, UNIT)
        theirs[here, :] = terms[pl.ds(at, UNIT), :]


def own_terms(chunk, per, groups, slots, ids, accs, wo, wp, xo, so):
    hidden = wo.shape[1]
    rows = per * UNIT
    smem = pl.BlockSpec(memory_space=pltpu.SMEM)
    vmem = pl.BlockSpec(memory_space=pltpu.VMEM)
    return pl.pallas_call(
        functools.partial(own_kernel, chunk, per, groups, len(accs)),
        out_shape=[
            jax.ShapeDtypeStruct((slots * rows, hidden), jnp.float32),
            jax.ShapeDtypeStruct((rows, hidden), jnp.float32),
        ],
        in_specs=[smem] + [vmem] * (4 + len(accs)),
        out_specs=[vmem] * 2,
        scratch_shapes=[pltpu.VMEM((groups * UNIT, hidden), jnp.float32)],
        compiler_params=pltpu.CompilerParams(vmem_limit_bytes=(12 << 20) + accs[0].size * 4 * len(accs)),
        cost_estimate=pl.CostEstimate(
            flops=4 * slots * rows * PART * len(accs) * hidden, bytes_accessed=2 << 20, transcendentals=0),
        name="own_terms",
    )(ids, wo, wp, xo, so, *accs)


def combine_kernel(slots, rows, ways, own, *refs):
    parts = len(refs) - ways - 1
    coded, outs, tail = refs[:parts], refs[parts:parts + ways], refs[parts + ways]
    values = [read_coded(a, slots, rows) for a in coded]

    def total(s):
        got = own[s * rows:(s + 1) * rows, :]
        for value in values:
            got = got + value(s)
        return got

    for i in range(slots // ways):
        outs[0][i * rows:(i + 1) * rows, :] = total(i * ways)
    for k in range(1, ways):
        write_coded(outs[k], tail, slots // ways, rows, lambda s: total(s * ways + k))


def combine(slots, rows, ways, own, coded):
    width = own.shape[1]
    left = slots // ways
    vmem = pl.BlockSpec(memory_space=pltpu.VMEM)
    out = jax.ShapeDtypeStruct((left * rows + tail_rows(left), width), jnp.int16)
    return pl.pallas_call(
        functools.partial(combine_kernel, slots, rows, ways),
        out_shape=[jax.ShapeDtypeStruct((left * rows, width), jnp.float32)] + [out] * (ways - 1),
        in_specs=[vmem] * (1 + len(coded)),
        out_specs=[vmem] * ways,
        scratch_shapes=[pltpu.VMEM((tail_rows(left), width), jnp.float32)],
        compiler_params=pltpu.CompilerParams(vmem_limit_bytes=32 * 1024 * 1024),
        name="combine",
    )(own, *coded)


def hidden_kernel(chunks, parts, rows, *refs):
    out = refs[chunks * parts + 1]
    for c in range(chunks):
        own, self, coded = refs[c * parts], refs[c * parts + 1], refs[c * parts + 2:(c + 1) * parts]
        total = own[:rows, :] + self[...]
        for a in coded:
            total = total + read_coded(a, 1, rows)(0)
        out[c * rows:(c + 1) * rows, :] = jnp.maximum(total, 0.0).astype(jnp.bfloat16)


def hidden_rows(chunk_parts, rows, sel):
    chunks, parts = len(chunk_parts), len(chunk_parts[0])
    width = chunk_parts[0][0].shape[1]
    vmem = pl.BlockSpec(memory_space=pltpu.VMEM)
    flat = [a for part in chunk_parts for a in part]
    return pl.pallas_call(
        functools.partial(hidden_kernel, chunks, parts, rows),
        out_shape=jax.ShapeDtypeStruct((chunks * rows, width), jnp.bfloat16),
        in_specs=[vmem] * (len(flat) + 1),
        out_specs=vmem,
        compiler_params=pltpu.CompilerParams(vmem_limit_bytes=32 * 1024 * 1024),
        name="hidden_rows",
    )(*flat, sel)


def send_kernel(own, other, sel, send):
    both = jnp.concatenate([own[...], other[...]], axis=0)
    send[...] = jnp.dot(sel[...], both, preferred_element_type=jnp.float32).astype(jnp.bfloat16)


def rows_to_send(own, other, sel):
    vmem = pl.BlockSpec(memory_space=pltpu.VMEM)
    return pl.pallas_call(
        send_kernel,
        out_shape=jax.ShapeDtypeStruct((sel.shape[0], own.shape[1]), jnp.bfloat16),
        in_specs=[vmem] * 3,
        out_specs=vmem,
        compiler_params=pltpu.CompilerParams(vmem_limit_bytes=32 * 1024 * 1024),
        name="rows_to_send",
    )(own, other, sel)


def logits_kernel(own, other, received, front, adj_received, w_self, w_neigh, out):
    rows = out.shape[0]
    both = jnp.concatenate([own[...], other[...]], axis=0)
    local = jnp.dot(front[...], both, preferred_element_type=jnp.float32)
    mean = local[:rows, :] + jnp.dot(adj_received[...], received[...], preferred_element_type=jnp.float32)
    dims = (((1,), (1,)), ((), ()))
    got = lax.dot_general(local[rows:, :].astype(jnp.bfloat16), w_self[...], dims, preferred_element_type=jnp.float32)
    got = got + lax.dot_general(mean.astype(jnp.bfloat16), w_neigh[...], dims, preferred_element_type=jnp.float32)
    out[...] = got


def logits_of(own, other, received, front, adj_received, w_self, w_neigh):
    vmem = pl.BlockSpec(memory_space=pltpu.VMEM)
    return pl.pallas_call(
        logits_kernel,
        out_shape=jax.ShapeDtypeStruct((adj_received.shape[0], w_self.shape[1]), jnp.float32),
        in_specs=[vmem] * 7,
        out_specs=vmem,
        compiler_params=pltpu.CompilerParams(vmem_limit_bytes=32 * 1024 * 1024),
        name="logits",
    )(own, other, received, front, adj_received, w_self.T, w_neigh.T)


def exchange(parts, stride, n, places):
    got = [parts[0]]
    for k in places:
        got.append(lax.ppermute(parts[k], "dom", [(i, i ^ (k * stride)) for i in range(n)]))
    return got


def body(
    features,
    tile_weight,
    tile_dst,
    tile_src,
    tile_rows,
    w_self1,
    neighbour_weight_first,
    send_list,
    send_count,
    adj_two,
    w_self2,
    w_neigh2,
):
    n = lax.axis_size("dom")
    tile = tile_weight.shape[1]
    groups = tile // UNIT
    per = groups // 2 // CHUNKS
    bits = n.bit_length() - 1
    assert n == 1 << bits and bits >= 2
    radices = [2] * (bits // 2) + [1] * (bits % 2)
    ids = jnp.stack([lax.axis_index("feat"), lax.axis_index("dom")]).astype(jnp.int32)
    swap = [(0, 1), (1, 0)]
    xp = lax.ppermute(features, "feat", swap)
    wp = lax.ppermute(neighbour_weight_first, "feat", swap)
    tw = tile_weight.reshape(tile_weight.shape[0], groups, UNIT, tile)
    planned = plan(
        CHUNKS, per, n, 4, ids, tile_src, tile_rows, tile_dst, tw, features,
    )
    tables, tbufs, xo = planned[:CHUNKS], planned[CHUNKS:2 * CHUNKS], planned[2 * CHUNKS]
    wo, so = neighbour_weight_first, w_self1
    done = []
    for chunk in range(CHUNKS):
        accs = gathered_sums(per, n, tables[chunk], tbufs[chunk], xo, xp)
        slots, rows = n // 4, per * UNIT
        parts = {}
        (parts[3],) = sent_terms((3,), slots, rows, accs, wo, wp)
        parts[2], parts[1] = sent_terms((2, 1), slots, rows, accs, wo, wp)
        parts[0], theirs = own_terms(chunk, per, groups, slots, ids, accs, wo, wp, xo, so)
        self = lax.ppermute(theirs, "feat", swap)
        got = exchange(parts, 1, n, (1, 2, 3))
        stride = 4
        for radix in radices[1:]:
            ways = 1 << radix
            parts = combine(n // stride, per * UNIT, ways, got[0], got[1:])
            got = exchange(parts, stride, n, (2, 3, 1) if ways == 4 else (1,))
            stride *= ways
        done.append([got[0], self] + got[1:])
    sel, front, adj_received = selection(groups, ids, send_list, send_count, adj_two)
    own = hidden_rows(done, per * UNIT, sel)
    other = lax.ppermute(own, "feat", swap)
    send = rows_to_send(own, other, sel)
    received = lax.all_to_all(send, "dom", 0, 0, axis_index_groups=[group_order(n)], tiled=True)
    return logits_of(own, other, received, front, adj_received, w_self2, w_neigh2)


def solution(mesh):
    in_specs = (
        P("dom", "feat"),
        P("dom", None, None),
        P("dom"),
        P("dom"),
        P("dom"),
        P("feat", None),
        P("feat", None),
        P(),
        P(),
        P("dom", None),
        P(),
        P(),
    )
    out_specs = P("dom", None)
    return jax.shard_map(body, mesh=mesh, in_specs=in_specs, out_specs=out_specs, check_vma=False)
```

```python
import functools

import jax
import jax.numpy as jnp
from jax import lax
from jax.experimental import pallas as pl
from jax.experimental.pallas import tpu as pltpu
from jax.sharding import PartitionSpec as P

UNIT = 16
BLOCK = 4
STEP = 16
PART = 256
CHUNKS = 1


def group_of(core, place, groups):
    pair = 2 * (place // 2) + core
    return pair if place % 2 == 0 else groups - 1 - pair


def group_order(n):
    return list(range(n - 1, -1, -1))


LN2 = 0.6931471805599453


def tail_rows(slots):
    return -(-slots // 8) * 8


def encode(x):
    top = jnp.max(jnp.abs(x), axis=0, keepdims=True)
    power = jnp.ceil(jnp.log(jnp.maximum(top, 1e-30)) * (1.0 / LN2) + 1e-3) - 15.0
    return jnp.floor(x * jnp.exp(power * -LN2) + 0.5), power


def to_int16(x):
    return x.astype(jnp.int32).astype(jnp.int16)


def write_coded(out, tail, slots, rows, value_of):
    tail[...] = jnp.zeros_like(tail)
    for s in range(slots):
        whole, power = encode(value_of(s))
        out[s * rows:(s + 1) * rows, :] = to_int16(whole)
        tail[s:s + 1, :] = power
    out[slots * rows:, :] = to_int16(tail[...])


def read_coded(ref, slots, rows):
    powers = ref[slots * rows:, :].astype(jnp.int32).astype(jnp.float32)

    def value_of(s):
        whole = ref[s * rows:(s + 1) * rows, :].astype(jnp.int32).astype(jnp.float32)
        return whole * jnp.exp(powers[s:s + 1, :] * LN2)

    return value_of


def plan_kernel(chunks, per, n, radix, n_src, ids, src_h, rows_h, dst_h, tw, xo, *rest):
    tables, (tbuf, xo_out, src_v, rows_v, dst_v, sems) = rest[:chunks], rest[chunks:]
    core, me = ids[0], ids[1]
    tiles = src_v.shape[1]
    n_pos = tables[0].shape[1]
    units = per * tiles
    groups = 2 * per * chunks
    half = groups // 2
    gs = [group_of(core, i, groups) for i in range(half)]
    small = [(src_h, src_v), (rows_h, rows_v), (dst_h, dst_v)]
    large = [(tw, tbuf), (xo, xo_out)]
    copies = [pltpu.make_async_copy(a, b, sems.at[i]) for i, (a, b) in enumerate(small + large)]
    for c in copies:
        c.start()
    lane = lax.broadcasted_iota(jnp.int32, (1, tiles), 1)
    block_i = lax.broadcasted_iota(jnp.int32, (n_src, tiles), 0)
    before = lax.broadcasted_iota(jnp.int32, (tiles, tiles), 0) < lax.broadcasted_iota(jnp.int32, (tiles, tiles), 1)
    before = jnp.where(before, 1.0, 0.0).astype(jnp.bfloat16)
    pos_i = lax.broadcasted_iota(jnp.int32, (tiles, n_pos), 1).astype(jnp.float32)
    place_i = lax.broadcasted_iota(jnp.int32, (1, n_pos), 1)
    trash = float(n * per << 14)
    for c in copies[:3]:
        c.wait()
    src, rows = src_v[...], rows_v[...]
    slot = jnp.bitwise_xor(dst_v[...], me)
    slot = jnp.bitwise_and(slot, radix - 1) * (n // radix) + lax.div(slot, radix)
    for c in range(chunks):
        hot, words, valid = [], [], []
        for j in range(per):
            limit = jnp.clip(rows - UNIT * gs[c * per + j], 0, UNIT)
            ok = limit > 0
            valid.append(ok)
            words.append(((slot * per + j) * 512 + (j * tiles + lane)) * 32 + limit)
            hot.append(jnp.where(jnp.logical_and(block_i == src, ok), 1.0, 0.0))
        stacked = jnp.concatenate(hot, axis=0)
        earlier = jnp.dot(stacked.astype(jnp.bfloat16), before, preferred_element_type=jnp.float32)
        counts = jnp.sum(stacked, axis=1, keepdims=True)
        counts = [counts[j * n_src:(j + 1) * n_src, :] for j in range(per)]
        blocks = jnp.floor((sum(counts) + (BLOCK - 1)) * (1.0 / BLOCK))
        ahead = jnp.zeros(blocks.shape, jnp.float32)
        source_i = lax.broadcasted_iota(jnp.int32, blocks.shape, 0)
        for s in range(n_src - 1):
            ahead = ahead + jnp.where(source_i > s, blocks[s:s + 1, :], 0.0)
        first, pos = ahead * BLOCK, []
        for j in range(per):
            place = hot[j] * (earlier[j * n_src:(j + 1) * n_src, :] + first)
            pos.append(jnp.sum(place, axis=0, keepdims=True))
            first = first + counts[j]
        behind = jnp.where(place_i.astype(jnp.float32) >= ahead + blocks, 1.0, 0.0)
        owner = jnp.sum(behind, axis=0, keepdims=True)
        run = ahead[n_src - 1:, :] + blocks[n_src - 1:, :]
        stack = [jnp.where(valid[j], pos[j], -1.0) for j in range(per)]
        stack += [w.astype(jnp.float32) - trash for w in words]
        stack += [jnp.zeros((1, tiles), jnp.float32)] * (-len(stack) % 8)
        cols = jnp.concatenate(stack, axis=0).T
        found = jnp.zeros((tiles, n_pos), jnp.float32)
        for j in range(per):
            found = found + jnp.where(cols[:, j:j + 1] == pos_i, cols[:, per + j:per + j + 1], 0.0)
        word = jnp.sum(found, axis=0, keepdims=True) + trash
        owner = jnp.where(place_i == n_pos - 1, run, jnp.minimum(owner, n_src - 1.0))
        tables[c][0:1, :] = word.astype(jnp.int32)
        tables[c][1:2, :] = owner.astype(jnp.int32)

    for c in copies[3:]:
        c.wait()


def plan(chunks, per, n, radix, ids, src, rows, dst, tw, xo):
    tiles, _, _, tile = tw.shape
    n_src = xo.shape[0] // tile
    blocks = -(-(per * tiles // BLOCK + n_src) // STEP) * STEP
    n_pos = -(-(blocks * BLOCK + 1) // 128) * 128
    smem = pl.BlockSpec(memory_space=pltpu.SMEM)
    vmem = pl.BlockSpec(memory_space=pltpu.VMEM)
    hbm = pl.BlockSpec(memory_space=pltpu.HBM)
    return pl.pallas_call(
        functools.partial(plan_kernel, chunks, per, n, radix, n_src),
        out_shape=[jax.ShapeDtypeStruct((2, n_pos), jnp.int32)] * chunks
        + [jax.ShapeDtypeStruct(tw.shape, tw.dtype), jax.ShapeDtypeStruct(xo.shape, xo.dtype)],
        in_specs=[smem] + [hbm] * 5,
        out_specs=[vmem] * (chunks + 2),
        scratch_shapes=[
            pltpu.VMEM((1, tiles), jnp.int32),
            pltpu.VMEM((1, tiles), jnp.int32),
            pltpu.VMEM((1, tiles), jnp.int32),
            pltpu.SemaphoreType.DMA((3 + 2,)),
        ],
        compiler_params=pltpu.CompilerParams(vmem_limit_bytes=32 * 1024 * 1024),
        name="plan",
    )(ids, *[
        pltpu.with_memory_space_constraint(a, pltpu.HBM)
        for a in (src.reshape(1, tiles), rows.reshape(1, tiles), dst.reshape(1, tiles), tw, xo)
    ])


def select_kernel(groups, ids, lists, counts, adj, sel, front, adj_out):
    core, me = ids[0], ids[1]
    n = lists.shape[0]
    slots = lists.shape[1]
    total = n * slots
    q_n = lax.broadcasted_iota(jnp.int32, (total, n), 0)
    r_n = lax.broadcasted_iota(jnp.int32, (total, n), 1)
    mine = lists[me].astype(jnp.float32)
    cnt = counts[pl.ds(me, 1), :]
    picked = jnp.zeros((total, n), jnp.float32)
    k_n = jnp.bitwise_and(q_n, slots - 1)
    for k in range(slots):
        picked = jnp.where(k_n == k, mine[k:k + 1, :], picked)
    good = jnp.logical_and(n - 1 - lax.div(q_n, slots) == r_n, k_n < cnt)
    row = jnp.sum(jnp.where(good, picked + 1.0, 0.0), axis=1, keepdims=True) - 1.0
    lane = lax.broadcasted_iota(jnp.int32, (1, sel.shape[1]), 1)
    name = jnp.zeros(lane.shape, jnp.int32)
    names = [group_of(c, i, groups) for c in (core, 1 - core) for i in range(groups // 2)]
    for i, g in enumerate(names):
        name = jnp.where(lax.div(lane, UNIT) == i, g * UNIT + jnp.bitwise_and(lane, UNIT - 1), name)
    sel[...] = jnp.where(row == name.astype(jnp.float32), 1.0, 0.0).astype(jnp.bfloat16)
    tile, out_rows = groups * UNIT, adj.shape[0]
    placed = jnp.where(lax.broadcasted_iota(jnp.int32, (tile, tile), 0) == name, 1.0, 0.0).astype(jnp.bfloat16)
    front[:out_rows, :] = jnp.dot(adj[:, :tile], placed, preferred_element_type=jnp.float32).astype(jnp.bfloat16)
    front[out_rows:, :] = placed[:out_rows, :]
    column = lax.broadcasted_iota(jnp.int32, (1, total), 1)
    source = (n - 1 - lax.div(column, slots)) * slots + lax.rem(column, slots)
    moved = jnp.where(lax.broadcasted_iota(jnp.int32, (total, total), 0) == source, 1.0, 0.0).astype(jnp.bfloat16)
    adj_out[...] = jnp.dot(adj[:, groups * UNIT:], moved, preferred_element_type=jnp.float32).astype(jnp.bfloat16)


def selection(groups, ids, send_list, send_count, adj):
    n, _, slots = send_list.shape
    smem = pl.BlockSpec(memory_space=pltpu.SMEM)
    vmem = pl.BlockSpec(memory_space=pltpu.VMEM)
    return pl.pallas_call(
        functools.partial(select_kernel, groups),
        out_shape=[
            jax.ShapeDtypeStruct((n * slots, groups * UNIT), jnp.bfloat16),
            jax.ShapeDtypeStruct((2 * adj.shape[0], groups * UNIT), jnp.bfloat16),
            jax.ShapeDtypeStruct((adj.shape[0], n * slots), jnp.bfloat16),
        ],
        in_specs=[smem, vmem, vmem, vmem],
        out_specs=[vmem] * 3,
        compiler_params=pltpu.CompilerParams(vmem_limit_bytes=32 * 1024 * 1024),
        name="selection",
    )(ids, jnp.swapaxes(send_list, 1, 2), send_count, adj)


def tiles_kernel(chunk, per, ids, table_v, tbuf, xo, xp, *rest):
    parts = len(rest) - 3
    accs, (masks, table, sem) = rest[:parts], rest[parts:]
    tiles, groups, _, tile = tbuf.shape
    width = xo.shape[1]
    core = ids[0]
    to_scalar = pltpu.make_async_copy(table_v, table, sem)
    to_scalar.start()
    for acc in accs:
        acc[...] = jnp.zeros_like(acc)
    row_i = lax.broadcasted_iota(jnp.int32, (UNIT, tile), 0)
    for m in range(UNIT + 1):
        masks[m] = jnp.where(row_i < m, 1.0, 0.0).astype(jnp.bfloat16)
    columns = [(x, h) for x in (xo, xp) for h in range(0, width, PART)]
    to_scalar.wait()

    def blocks(first, count):
        for m in range(count):
            at = first + m
            base = pl.multiple_of(table[1, at] * tile, tile)
            rows, places = [], []
            for k in range(BLOCK):
                word = table[0, at * BLOCK + k]
                u = jnp.bitwise_and(lax.shift_right_logical(word, 5), 511)
                place = lax.div(u, tiles) + chunk * per
                odd = jnp.bitwise_and(place, 1)
                row = odd * groups + (1 - 2 * odd) * (place + core)
                rows.append(tbuf[lax.rem(u, tiles), row] * masks[jnp.bitwise_and(word, 31)])
                places.append(pl.multiple_of(lax.shift_right_logical(word, 14) * UNIT, UNIT))
            lhs = jnp.concatenate(rows, axis=0)
            for acc, (x, h) in zip(accs, columns):
                got = jnp.dot(lhs, x[pl.ds(base, tile), h:h + PART], preferred_element_type=jnp.float32)
                got = got.astype(jnp.bfloat16).astype(jnp.float32)
                for k in range(BLOCK):
                    acc[pl.ds(places[k], UNIT), :] += got[k * UNIT:(k + 1) * UNIT, :]

    half = STEP // 2
    halves = lax.div(table[1, table.shape[1] - 1] + half - 1, half)
    steps = lax.div(halves, 2)

    def step(i, carry):
        blocks(i * STEP, STEP)
        return carry

    def last(i, carry):
        blocks(steps * STEP, half)
        return carry

    lax.fori_loop(0, steps, step, 0)
    lax.fori_loop(0, lax.rem(halves, 2), last, 0)


def gathered_sums(chunk, per, n, ids, table, tbuf, xo, xp):
    width = xo.shape[1]
    tile = tbuf.shape[3]
    smem = pl.BlockSpec(memory_space=pltpu.SMEM)
    vmem = pl.BlockSpec(memory_space=pltpu.VMEM)
    flops = 2 * tbuf.shape[0] * per * UNIT * tile * 2 * width
    parts = 2 * width // PART
    sums = jax.ShapeDtypeStruct(((n * per + 1) * UNIT, PART), jnp.float32)
    return pl.pallas_call(
        functools.partial(tiles_kernel, chunk, per),
        out_shape=[sums] * parts,
        in_specs=[smem] + [vmem] * 4,
        out_specs=[vmem] * parts,
        scratch_shapes=[
            pltpu.VMEM((UNIT + 1, UNIT, tile), jnp.bfloat16),
            pltpu.SMEM(table.shape, jnp.int32),
            pltpu.SemaphoreType.DMA,
        ],
        compiler_params=pltpu.CompilerParams(vmem_limit_bytes=(12 << 20) + sums.size * 4 * parts),
        cost_estimate=pl.CostEstimate(flops=flops, bytes_accessed=8 << 20, transcendentals=0),
        name="gathered_sums",
    )(ids, table, tbuf, xo, xp)


def weigh(accs, weights, first, count, out):
    size = min(256, count)

    def piece(r, carry):
        at = r * size if isinstance(r, int) else pl.multiple_of(r * size, size)
        got = jnp.zeros((size, out.shape[1]), jnp.float32)
        for i, acc in enumerate(accs):
            w, h = weights[i * PART // weights[0].shape[0]], i * PART % weights[0].shape[0]
            value = acc[pl.ds(first + at, size), :]
            high = value.astype(jnp.bfloat16)
            low = (value - high.astype(jnp.float32)).astype(jnp.bfloat16)
            got = got + jnp.dot(high, w[h:h + PART, :], preferred_element_type=jnp.float32)
            got = got + jnp.dot(low, w[h:h + PART, :], preferred_element_type=jnp.float32)
        out[pl.ds(at, size), :] = got
        return carry

    if count == size:
        piece(0, 0)
    else:
        lax.fori_loop(0, count // size, piece, 0)


def sent_kernel(ks, slots, rows, parts, wo, wp, *refs):
    accs, outs, scratch = refs[:parts], refs[parts:parts + len(ks)], refs[parts + len(ks):]
    for i, k in enumerate(ks):
        sums, tail = scratch[2 * i:2 * i + 2]
        weigh(accs, (wo, wp), k * slots * rows, slots * rows, sums)
        write_coded(outs[i], tail, slots, rows, lambda s: sums[s * rows:(s + 1) * rows, :])


def sent_terms(ks, slots, rows, accs, wo, wp):
    hidden = wo.shape[1]
    vmem = pl.BlockSpec(memory_space=pltpu.VMEM)
    coded = jax.ShapeDtypeStruct((slots * rows + tail_rows(slots), hidden), jnp.int16)
    return pl.pallas_call(
        functools.partial(sent_kernel, ks, slots, rows, len(accs)),
        out_shape=[coded] * len(ks),
        in_specs=[vmem] * (2 + len(accs)),
        out_specs=[vmem] * len(ks),
        scratch_shapes=[
            pltpu.VMEM((slots * rows, hidden), jnp.float32),
            pltpu.VMEM((tail_rows(slots), hidden), jnp.float32),
        ] * len(ks),
        compiler_params=pltpu.CompilerParams(vmem_limit_bytes=(20 << 20) + accs[0].size * 4 * len(accs)),
        cost_estimate=pl.CostEstimate(
            flops=4 * len(ks) * slots * rows * PART * len(accs) * hidden, bytes_accessed=2 << 20, transcendentals=0),
        name="sent_terms",
    )(wo, wp, *accs)


def own_kernel(chunk, per, groups, parts, ids, wo, wp, xo, so, *refs):
    accs, (out, theirs, terms) = refs[:parts], refs[parts:]
    weigh(accs, (wo, wp), 0, out.shape[0], out)
    terms[...] = jnp.dot(xo[:groups * UNIT, :], so[...], preferred_element_type=jnp.float32)
    for j in range(per):
        here = slice(j * UNIT, (j + 1) * UNIT)
        at = pl.multiple_of(group_of(ids[0], chunk * per + j, groups) * UNIT, UNIT)
        out[here, :] += terms[pl.ds(at, UNIT), :]
        at = pl.multiple_of(group_of(1 - ids[0], chunk * per + j, groups) * UNIT, UNIT)
        theirs[here, :] = terms[pl.ds(at, UNIT), :]


def own_terms(chunk, per, groups, slots, ids, accs, wo, wp, xo, so):
    hidden = wo.shape[1]
    rows = per * UNIT
    smem = pl.BlockSpec(memory_space=pltpu.SMEM)
    vmem = pl.BlockSpec(memory_space=pltpu.VMEM)
    return pl.pallas_call(
        functools.partial(own_kernel, chunk, per, groups, len(accs)),
        out_shape=[
            jax.ShapeDtypeStruct((slots * rows, hidden), jnp.float32),
            jax.ShapeDtypeStruct((rows, hidden), jnp.float32),
        ],
        in_specs=[smem] + [vmem] * (4 + len(accs)),
        out_specs=[vmem] * 2,
        scratch_shapes=[pltpu.VMEM((groups * UNIT, hidden), jnp.float32)],
        compiler_params=pltpu.CompilerParams(vmem_limit_bytes=(12 << 20) + accs[0].size * 4 * len(accs)),
        cost_estimate=pl.CostEstimate(
            flops=4 * slots * rows * PART * len(accs) * hidden, bytes_accessed=2 << 20, transcendentals=0),
        name="own_terms",
    )(ids, wo, wp, xo, so, *accs)


def combine_kernel(slots, rows, ways, own, *refs):
    parts = len(refs) - ways - 1
    coded, outs, tail = refs[:parts], refs[parts:parts + ways], refs[parts + ways]
    values = [read_coded(a, slots, rows) for a in coded]

    def total(s):
        got = own[s * rows:(s + 1) * rows, :]
        for value in values:
            got = got + value(s)
        return got

    for i in range(slots // ways):
        outs[0][i * rows:(i + 1) * rows, :] = total(i * ways)
    for k in range(1, ways):
        write_coded(outs[k], tail, slots // ways, rows, lambda s: total(s * ways + k))


def combine(slots, rows, ways, own, coded):
    width = own.shape[1]
    left = slots // ways
    vmem = pl.BlockSpec(memory_space=pltpu.VMEM)
    out = jax.ShapeDtypeStruct((left * rows + tail_rows(left), width), jnp.int16)
    return pl.pallas_call(
        functools.partial(combine_kernel, slots, rows, ways),
        out_shape=[jax.ShapeDtypeStruct((left * rows, width), jnp.float32)] + [out] * (ways - 1),
        in_specs=[vmem] * (1 + len(coded)),
        out_specs=[vmem] * ways,
        scratch_shapes=[pltpu.VMEM((tail_rows(left), width), jnp.float32)],
        compiler_params=pltpu.CompilerParams(vmem_limit_bytes=32 * 1024 * 1024),
        name="combine",
    )(own, *coded)


def hidden_kernel(chunks, parts, rows, *refs):
    out = refs[chunks * parts + 1]
    for c in range(chunks):
        own, self, coded = refs[c * parts], refs[c * parts + 1], refs[c * parts + 2:(c + 1) * parts]
        total = own[:rows, :] + self[...]
        for a in coded:
            total = total + read_coded(a, 1, rows)(0)
        out[c * rows:(c + 1) * rows, :] = jnp.maximum(total, 0.0).astype(jnp.bfloat16)


def hidden_rows(chunk_parts, rows, sel):
    chunks, parts = len(chunk_parts), len(chunk_parts[0])
    width = chunk_parts[0][0].shape[1]
    vmem = pl.BlockSpec(memory_space=pltpu.VMEM)
    flat = [a for part in chunk_parts for a in part]
    return pl.pallas_call(
        functools.partial(hidden_kernel, chunks, parts, rows),
        out_shape=jax.ShapeDtypeStruct((chunks * rows, width), jnp.bfloat16),
        in_specs=[vmem] * (len(flat) + 1),
        out_specs=vmem,
        compiler_params=pltpu.CompilerParams(vmem_limit_bytes=32 * 1024 * 1024),
        name="hidden_rows",
    )(*flat, sel)


def send_kernel(own, other, sel, send):
    both = jnp.concatenate([own[...], other[...]], axis=0)
    send[...] = jnp.dot(sel[...], both, preferred_element_type=jnp.float32).astype(jnp.bfloat16)


def rows_to_send(own, other, sel):
    vmem = pl.BlockSpec(memory_space=pltpu.VMEM)
    return pl.pallas_call(
        send_kernel,
        out_shape=jax.ShapeDtypeStruct((sel.shape[0], own.shape[1]), jnp.bfloat16),
        in_specs=[vmem] * 3,
        out_specs=vmem,
        compiler_params=pltpu.CompilerParams(vmem_limit_bytes=32 * 1024 * 1024),
        name="rows_to_send",
    )(own, other, sel)


def logits_kernel(own, other, received, front, adj_received, w_self, w_neigh, out):
    rows = out.shape[0]
    both = jnp.concatenate([own[...], other[...]], axis=0)
    local = jnp.dot(front[...], both, preferred_element_type=jnp.float32)
    mean = local[:rows, :] + jnp.dot(adj_received[...], received[...], preferred_element_type=jnp.float32)
    dims = (((1,), (1,)), ((), ()))
    got = lax.dot_general(local[rows:, :].astype(jnp.bfloat16), w_self[...], dims, preferred_element_type=jnp.float32)
    got = got + lax.dot_general(mean.astype(jnp.bfloat16), w_neigh[...], dims, preferred_element_type=jnp.float32)
    out[...] = got


def logits_of(own, other, received, front, adj_received, w_self, w_neigh):
    vmem = pl.BlockSpec(memory_space=pltpu.VMEM)
    return pl.pallas_call(
        logits_kernel,
        out_shape=jax.ShapeDtypeStruct((adj_received.shape[0], w_self.shape[1]), jnp.float32),
        in_specs=[vmem] * 7,
        out_specs=vmem,
        compiler_params=pltpu.CompilerParams(vmem_limit_bytes=32 * 1024 * 1024),
        name="logits",
    )(own, other, received, front, adj_received, w_self.T, w_neigh.T)


def exchange(parts, stride, n, places):
    got = [parts[0]]
    for k in places:
        got.append(lax.ppermute(parts[k], "dom", [(i, i ^ (k * stride)) for i in range(n)]))
    return got


def body(
    features,
    tile_weight,
    tile_dst,
    tile_src,
    tile_rows,
    w_self1,
    neighbour_weight_first,
    send_list,
    send_count,
    adj_two,
    w_self2,
    w_neigh2,
):
    n = lax.axis_size("dom")
    tile = tile_weight.shape[1]
    groups = tile // UNIT
    per = groups // 2 // CHUNKS
    bits = n.bit_length() - 1
    assert n == 1 << bits and bits >= 2
    radices = [2] * (bits // 2) + [1] * (bits % 2)
    ids = jnp.stack([lax.axis_index("feat"), lax.axis_index("dom")]).astype(jnp.int32)
    swap = [(0, 1), (1, 0)]
    xp = lax.ppermute(features, "feat", swap)
    wp = lax.ppermute(neighbour_weight_first, "feat", swap)
    tw = tile_weight.reshape(tile_weight.shape[0], groups, UNIT, tile)
    planned = plan(
        CHUNKS, per, n, 4, ids, tile_src, tile_rows, tile_dst, tw, features,
    )
    tables, (tbuf, xo) = planned[:CHUNKS], planned[CHUNKS:]
    wo, so = neighbour_weight_first, w_self1
    done = []
    for chunk in range(CHUNKS):
        accs = gathered_sums(chunk, per, n, ids, tables[chunk], tbuf, xo, xp)
        slots, rows = n // 4, per * UNIT
        parts = {}
        (parts[3],) = sent_terms((3,), slots, rows, accs, wo, wp)
        parts[2], parts[1] = sent_terms((2, 1), slots, rows, accs, wo, wp)
        parts[0], theirs = own_terms(chunk, per, groups, slots, ids, accs, wo, wp, xo, so)
        self = lax.ppermute(theirs, "feat", swap)
        got = exchange(parts, 1, n, (1, 2, 3))
        stride = 4
        for radix in radices[1:]:
            ways = 1 << radix
            parts = combine(n // stride, per * UNIT, ways, got[0], got[1:])
            got = exchange(parts, stride, n, (2, 3, 1) if ways == 4 else (1,))
            stride *= ways
        done.append([got[0], self] + got[1:])
    sel, front, adj_received = selection(groups, ids, send_list, send_count, adj_two)
    own = hidden_rows(done, per * UNIT, sel)
    other = lax.ppermute(own, "feat", swap)
    send = rows_to_send(own, other, sel)
    received = lax.all_to_all(send, "dom", 0, 0, axis_index_groups=[group_order(n)], tiled=True)
    return logits_of(own, other, received, front, adj_received, w_self2, w_neigh2)


def solution(mesh):
    in_specs = (
        P("dom", "feat"),
        P("dom", None, None),
        P("dom"),
        P("dom"),
        P("dom"),
        P("feat", None),
        P("feat", None),
        P(),
        P(),
        P("dom", None),
        P(),
        P(),
    )
    out_specs = P("dom", None)
    return jax.shard_map(body, mesh=mesh, in_specs=in_specs, out_specs=out_specs, check_vma=False)
```

```python
import functools

import jax
import jax.numpy as jnp
from jax import lax
from jax.experimental import pallas as pl
from jax.experimental.pallas import tpu as pltpu
from jax.sharding import PartitionSpec as P

UNIT = 16
BLOCK = 4
STEP = 16
PART = 256
CHUNKS = 1


def group_of(core, place, groups):
    pair = 2 * (place // 2) + core
    return pair if place % 2 == 0 else groups - 1 - pair


def group_order(n):
    return list(range(n - 1, -1, -1))


LN2 = 0.6931471805599453


def tail_rows(slots):
    return -(-slots // 8) * 8


def encode(x):
    top = jnp.max(jnp.abs(x), axis=0, keepdims=True)
    power = jnp.ceil(jnp.log(jnp.maximum(top, 1e-30)) * (1.0 / LN2) + 1e-3) - 15.0
    return jnp.floor(x * jnp.exp(power * -LN2) + 0.5), power


def to_int16(x):
    return x.astype(jnp.int32).astype(jnp.int16)


def write_coded(out, tail, slots, rows, value_of):
    tail[...] = jnp.zeros_like(tail)
    for s in range(slots):
        whole, power = encode(value_of(s))
        out[s * rows:(s + 1) * rows, :] = to_int16(whole)
        tail[s:s + 1, :] = power
    out[slots * rows:, :] = to_int16(tail[...])


def read_coded(ref, slots, rows):
    powers = ref[slots * rows:, :].astype(jnp.int32).astype(jnp.float32)

    def value_of(s):
        whole = ref[s * rows:(s + 1) * rows, :].astype(jnp.int32).astype(jnp.float32)
        return whole * jnp.exp(powers[s:s + 1, :] * LN2)

    return value_of


def plan_kernel(chunks, per, n, radix, n_src, ids, src_h, rows_h, dst_h, tw, xo, *rest):
    tables, rest = rest[:chunks], rest[chunks:]
    tbufs, rest = rest[:chunks], rest[chunks:]
    xo_out, src_v, rows_v, dst_v, sems = rest
    core, me = ids[0], ids[1]
    tiles = src_v.shape[1]
    n_pos = tables[0].shape[1]
    units = per * tiles
    groups = 2 * per * chunks
    half = groups // 2
    gs = [group_of(core, i, groups) for i in range(half)]
    small = [(src_h, src_v), (rows_h, rows_v), (dst_h, dst_v)]
    large = [(tw.at[:, g], tbufs[i // per].at[pl.ds(i % per * tiles, tiles)]) for i, g in enumerate(gs)]
    large += [(xo, xo_out)]
    copies = [pltpu.make_async_copy(a, b, sems.at[i]) for i, (a, b) in enumerate(small + large)]
    for c in copies:
        c.start()
    lane = lax.broadcasted_iota(jnp.int32, (1, tiles), 1)
    block_i = lax.broadcasted_iota(jnp.int32, (n_src, tiles), 0)
    before = lax.broadcasted_iota(jnp.int32, (tiles, tiles), 0) < lax.broadcasted_iota(jnp.int32, (tiles, tiles), 1)
    before = jnp.where(before, 1.0, 0.0).astype(jnp.bfloat16)
    pos_i = lax.broadcasted_iota(jnp.int32, (tiles, n_pos), 1).astype(jnp.float32)
    place_i = lax.broadcasted_iota(jnp.int32, (1, n_pos), 1)
    trash = float(n * per << 14)
    for c in copies[:3]:
        c.wait()
    src, rows = src_v[...], rows_v[...]
    slot = jnp.bitwise_xor(dst_v[...], me)
    slot = jnp.bitwise_and(slot, radix - 1) * (n // radix) + lax.div(slot, radix)
    for c in range(chunks):
        hot, words, valid = [], [], []
        for j in range(per):
            limit = jnp.clip(rows - UNIT * gs[c * per + j], 0, UNIT)
            ok = limit > 0
            valid.append(ok)
            words.append(((slot * per + j) * 512 + (j * tiles + lane)) * 32 + limit)
            hot.append(jnp.where(jnp.logical_and(block_i == src, ok), 1.0, 0.0))
        stacked = jnp.concatenate(hot, axis=0)
        earlier = jnp.dot(stacked.astype(jnp.bfloat16), before, preferred_element_type=jnp.float32)
        counts = jnp.sum(stacked, axis=1, keepdims=True)
        counts = [counts[j * n_src:(j + 1) * n_src, :] for j in range(per)]
        blocks = jnp.floor((sum(counts) + (BLOCK - 1)) * (1.0 / BLOCK))
        ahead = jnp.zeros(blocks.shape, jnp.float32)
        source_i = lax.broadcasted_iota(jnp.int32, blocks.shape, 0)
        for s in range(n_src - 1):
            ahead = ahead + jnp.where(source_i > s, blocks[s:s + 1, :], 0.0)
        first, pos = ahead * BLOCK, []
        for j in range(per):
            place = hot[j] * (earlier[j * n_src:(j + 1) * n_src, :] + first)
            pos.append(jnp.sum(place, axis=0, keepdims=True))
            first = first + counts[j]
        behind = jnp.where(place_i.astype(jnp.float32) >= ahead + blocks, 1.0, 0.0)
        owner = jnp.sum(behind, axis=0, keepdims=True)
        run = ahead[n_src - 1:, :] + blocks[n_src - 1:, :]
        stack = [jnp.where(valid[j], pos[j], -1.0) for j in range(per)]
        stack += [w.astype(jnp.float32) - trash for w in words]
        stack += [jnp.zeros((1, tiles), jnp.float32)] * (-len(stack) % 8)
        cols = jnp.concatenate(stack, axis=0).T
        found = jnp.zeros((tiles, n_pos), jnp.float32)
        for j in range(per):
            found = found + jnp.where(cols[:, j:j + 1] == pos_i, cols[:, per + j:per + j + 1], 0.0)
        word = jnp.sum(found, axis=0, keepdims=True) + trash
        owner = jnp.where(place_i == n_pos - 1, run, jnp.minimum(owner, n_src - 1.0))
        word = word.astype(jnp.int32)
        tables[c][0:1, :] = jnp.bitwise_and(lax.shift_right_logical(word, 5), 511)
        tables[c][1:2, :] = owner.astype(jnp.int32)
        tables[c][2:3, :] = lax.shift_right_logical(word, 14)
        tables[c][3:4, :] = jnp.bitwise_and(word, 31)

    for c in copies[3:]:
        c.wait()


def plan(chunks, per, n, radix, ids, src, rows, dst, tw, xo):
    tiles, _, _, tile = tw.shape
    n_src = xo.shape[0] // tile
    blocks = -(-(per * tiles // BLOCK + n_src) // STEP) * STEP
    n_pos = -(-(blocks * BLOCK + 1) // 128) * 128
    smem = pl.BlockSpec(memory_space=pltpu.SMEM)
    vmem = pl.BlockSpec(memory_space=pltpu.VMEM)
    hbm = pl.BlockSpec(memory_space=pltpu.HBM)
    half = chunks * per
    return pl.pallas_call(
        functools.partial(plan_kernel, chunks, per, n, radix, n_src),
        out_shape=[jax.ShapeDtypeStruct((4, n_pos), jnp.int32)] * chunks
        + [jax.ShapeDtypeStruct((per * tiles, UNIT, tile), tw.dtype)] * chunks
        + [jax.ShapeDtypeStruct(xo.shape, xo.dtype)],
        in_specs=[smem] + [hbm] * 5,
        out_specs=[vmem] * (2 * chunks + 1),
        scratch_shapes=[
            pltpu.VMEM((1, tiles), jnp.int32),
            pltpu.VMEM((1, tiles), jnp.int32),
            pltpu.VMEM((1, tiles), jnp.int32),
            pltpu.SemaphoreType.DMA((3 + half + 1,)),
        ],
        compiler_params=pltpu.CompilerParams(vmem_limit_bytes=32 * 1024 * 1024),
        name="plan",
    )(ids, *[
        pltpu.with_memory_space_constraint(a, pltpu.HBM)
        for a in (src.reshape(1, tiles), rows.reshape(1, tiles), dst.reshape(1, tiles), tw, xo)
    ])


def select_kernel(groups, ids, lists, counts, adj, sel, front, adj_out):
    core, me = ids[0], ids[1]
    n = lists.shape[0]
    slots = lists.shape[1]
    total = n * slots
    q_n = lax.broadcasted_iota(jnp.int32, (total, n), 0)
    r_n = lax.broadcasted_iota(jnp.int32, (total, n), 1)
    mine = lists[me].astype(jnp.float32)
    cnt = counts[pl.ds(me, 1), :]
    picked = jnp.zeros((total, n), jnp.float32)
    k_n = jnp.bitwise_and(q_n, slots - 1)
    for k in range(slots):
        picked = jnp.where(k_n == k, mine[k:k + 1, :], picked)
    good = jnp.logical_and(n - 1 - lax.div(q_n, slots) == r_n, k_n < cnt)
    row = jnp.sum(jnp.where(good, picked + 1.0, 0.0), axis=1, keepdims=True) - 1.0
    lane = lax.broadcasted_iota(jnp.int32, (1, sel.shape[1]), 1)
    name = jnp.zeros(lane.shape, jnp.int32)
    names = [group_of(c, i, groups) for c in (core, 1 - core) for i in range(groups // 2)]
    for i, g in enumerate(names):
        name = jnp.where(lax.div(lane, UNIT) == i, g * UNIT + jnp.bitwise_and(lane, UNIT - 1), name)
    sel[...] = jnp.where(row == name.astype(jnp.float32), 1.0, 0.0).astype(jnp.bfloat16)
    tile, out_rows = groups * UNIT, adj.shape[0]
    placed = jnp.where(lax.broadcasted_iota(jnp.int32, (tile, tile), 0) == name, 1.0, 0.0).astype(jnp.bfloat16)
    front[:out_rows, :] = jnp.dot(adj[:, :tile], placed, preferred_element_type=jnp.float32).astype(jnp.bfloat16)
    front[out_rows:, :] = placed[:out_rows, :]
    column = lax.broadcasted_iota(jnp.int32, (1, total), 1)
    source = (n - 1 - lax.div(column, slots)) * slots + lax.rem(column, slots)
    moved = jnp.where(lax.broadcasted_iota(jnp.int32, (total, total), 0) == source, 1.0, 0.0).astype(jnp.bfloat16)
    adj_out[...] = jnp.dot(adj[:, groups * UNIT:], moved, preferred_element_type=jnp.float32).astype(jnp.bfloat16)


def selection(groups, ids, send_list, send_count, adj):
    n, _, slots = send_list.shape
    smem = pl.BlockSpec(memory_space=pltpu.SMEM)
    vmem = pl.BlockSpec(memory_space=pltpu.VMEM)
    return pl.pallas_call(
        functools.partial(select_kernel, groups),
        out_shape=[
            jax.ShapeDtypeStruct((n * slots, groups * UNIT), jnp.bfloat16),
            jax.ShapeDtypeStruct((2 * adj.shape[0], groups * UNIT), jnp.bfloat16),
            jax.ShapeDtypeStruct((adj.shape[0], n * slots), jnp.bfloat16),
        ],
        in_specs=[smem, vmem, vmem, vmem],
        out_specs=[vmem] * 3,
        compiler_params=pltpu.CompilerParams(vmem_limit_bytes=32 * 1024 * 1024),
        name="selection",
    )(ids, jnp.swapaxes(send_list, 1, 2), send_count, adj)


def tiles_kernel(table_v, tbuf, xo, xp, *rest):
    parts = len(rest) - 3
    accs, (masks, table, sem) = rest[:parts], rest[parts:]
    tile = tbuf.shape[2]
    width = xo.shape[1]
    to_scalar = pltpu.make_async_copy(table_v, table, sem)
    to_scalar.start()
    for acc in accs:
        acc[...] = jnp.zeros_like(acc)
    row_i = lax.broadcasted_iota(jnp.int32, (UNIT, tile), 0)
    for m in range(UNIT + 1):
        masks[m] = jnp.where(row_i < m, 1.0, 0.0).astype(jnp.bfloat16)
    columns = [(x, h) for x in (xo, xp) for h in range(0, width, PART)]
    to_scalar.wait()

    def blocks(first, count):
        for m in range(count):
            at = first + m
            base = pl.multiple_of(table[1, at] * tile, tile)
            rows, places = [], []
            for k in range(BLOCK):
                rows.append(tbuf[table[0, at * BLOCK + k]] * masks[table[3, at * BLOCK + k]])
                places.append(table[2, at * BLOCK + k])
            lhs = jnp.concatenate(rows, axis=0)
            for acc, (x, h) in zip(accs, columns):
                got = jnp.dot(lhs, x[pl.ds(base, tile), h:h + PART], preferred_element_type=jnp.float32)
                got = got.astype(jnp.bfloat16).astype(jnp.float32)
                for k in range(BLOCK):
                    acc[places[k]] += got[k * UNIT:(k + 1) * UNIT, :]

    half = STEP // 2
    halves = lax.div(table[1, table.shape[1] - 1] + half - 1, half)
    steps = lax.div(halves, 2)

    def step(i, carry):
        blocks(i * STEP, STEP)
        return carry

    def last(i, carry):
        blocks(steps * STEP, half)
        return carry

    lax.fori_loop(0, steps, step, 0)
    lax.fori_loop(0, lax.rem(halves, 2), last, 0)


def gathered_sums(per, n, table, tbuf, xo, xp):
    width = xo.shape[1]
    tile = tbuf.shape[2]
    vmem = pl.BlockSpec(memory_space=pltpu.VMEM)
    flops = 2 * tbuf.shape[0] * UNIT * tile * 2 * width
    parts = 2 * width // PART
    sums = jax.ShapeDtypeStruct((n * per + 1, UNIT, PART), jnp.float32)
    return pl.pallas_call(
        tiles_kernel,
        out_shape=[sums] * parts,
        in_specs=[vmem] * 4,
        out_specs=[vmem] * parts,
        scratch_shapes=[
            pltpu.VMEM((UNIT + 1, UNIT, tile), jnp.bfloat16),
            pltpu.SMEM(table.shape, jnp.int32),
            pltpu.SemaphoreType.DMA,
        ],
        compiler_params=pltpu.CompilerParams(vmem_limit_bytes=(12 << 20) + sums.size * 4 * parts),
        cost_estimate=pl.CostEstimate(flops=flops, bytes_accessed=8 << 20, transcendentals=0),
        name="gathered_sums",
    )(table, tbuf, xo, xp)


def weigh(accs, weights, first, count, out):
    size = min(256, count)

    def piece(r, carry):
        at = r * size if isinstance(r, int) else pl.multiple_of(r * size, size)
        got = jnp.zeros((size, out.shape[1]), jnp.float32)
        for i, acc in enumerate(accs):
            w, h = weights[i * PART // weights[0].shape[0]], i * PART % weights[0].shape[0]
            value = acc[pl.ds(first // UNIT + r * (size // UNIT), size // UNIT)].reshape(size, PART)
            high = value.astype(jnp.bfloat16)
            low = (value - high.astype(jnp.float32)).astype(jnp.bfloat16)
            got = got + jnp.dot(high, w[h:h + PART, :], preferred_element_type=jnp.float32)
            got = got + jnp.dot(low, w[h:h + PART, :], preferred_element_type=jnp.float32)
        out[pl.ds(at, size), :] = got
        return carry

    if count == size:
        piece(0, 0)
    else:
        lax.fori_loop(0, count // size, piece, 0)


def sent_kernel(ks, slots, rows, parts, wo, wp, *refs):
    accs, outs, scratch = refs[:parts], refs[parts:parts + len(ks)], refs[parts + len(ks):]
    for i, k in enumerate(ks):
        sums, tail = scratch[2 * i:2 * i + 2]
        weigh(accs, (wo, wp), k * slots * rows, slots * rows, sums)
        write_coded(outs[i], tail, slots, rows, lambda s: sums[s * rows:(s + 1) * rows, :])


def sent_terms(ks, slots, rows, accs, wo, wp):
    hidden = wo.shape[1]
    vmem = pl.BlockSpec(memory_space=pltpu.VMEM)
    coded = jax.ShapeDtypeStruct((slots * rows + tail_rows(slots), hidden), jnp.int16)
    return pl.pallas_call(
        functools.partial(sent_kernel, ks, slots, rows, len(accs)),
        out_shape=[coded] * len(ks),
        in_specs=[vmem] * (2 + len(accs)),
        out_specs=[vmem] * len(ks),
        scratch_shapes=[
            pltpu.VMEM((slots * rows, hidden), jnp.float32),
            pltpu.VMEM((tail_rows(slots), hidden), jnp.float32),
        ] * len(ks),
        compiler_params=pltpu.CompilerParams(vmem_limit_bytes=(20 << 20) + accs[0].size * 4 * len(accs)),
        cost_estimate=pl.CostEstimate(
            flops=4 * len(ks) * slots * rows * PART * len(accs) * hidden, bytes_accessed=2 << 20, transcendentals=0),
        name="sent_terms",
    )(wo, wp, *accs)


def own_kernel(chunk, per, groups, parts, ids, wo, wp, xo, so, *refs):
    accs, (out, theirs, terms) = refs[:parts], refs[parts:]
    weigh(accs, (wo, wp), 0, out.shape[0], out)
    terms[...] = jnp.dot(xo[:groups * UNIT, :], so[...], preferred_element_type=jnp.float32)
    for j in range(per):
        here = slice(j * UNIT, (j + 1) * UNIT)
        at = pl.multiple_of(group_of(ids[0], chunk * per + j, groups) * UNIT, UNIT)
        out[here, :] += terms[pl.ds(at, UNIT), :]
        at = pl.multiple_of(group_of(1 - ids[0], chunk * per + j, groups) * UNIT, UNIT)
        theirs[here, :] = terms[pl.ds(at, UNIT), :]


def own_terms(chunk, per, groups, slots, ids, accs, wo, wp, xo, so):
    hidden = wo.shape[1]
    rows = per * UNIT
    smem = pl.BlockSpec(memory_space=pltpu.SMEM)
    vmem = pl.BlockSpec(memory_space=pltpu.VMEM)
    return pl.pallas_call(
        functools.partial(own_kernel, chunk, per, groups, len(accs)),
        out_shape=[
            jax.ShapeDtypeStruct((slots * rows, hidden), jnp.float32),
            jax.ShapeDtypeStruct((rows, hidden), jnp.float32),
        ],
        in_specs=[smem] + [vmem] * (4 + len(accs)),
        out_specs=[vmem] * 2,
        scratch_shapes=[pltpu.VMEM((groups * UNIT, hidden), jnp.float32)],
        compiler_params=pltpu.CompilerParams(vmem_limit_bytes=(12 << 20) + accs[0].size * 4 * len(accs)),
        cost_estimate=pl.CostEstimate(
            flops=4 * slots * rows * PART * len(accs) * hidden, bytes_accessed=2 << 20, transcendentals=0),
        name="own_terms",
    )(ids, wo, wp, xo, so, *accs)


def combine_kernel(slots, rows, ways, own, *refs):
    parts = len(refs) - ways - 1
    coded, outs, tail = refs[:parts], refs[parts:parts + ways], refs[parts + ways]
    values = [read_coded(a, slots, rows) for a in coded]

    def total(s):
        got = own[s * rows:(s + 1) * rows, :]
        for value in values:
            got = got + value(s)
        return got

    for i in range(slots // ways):
        outs[0][i * rows:(i + 1) * rows, :] = total(i * ways)
    for k in range(1, ways):
        write_coded(outs[k], tail, slots // ways, rows, lambda s: total(s * ways + k))


def combine(slots, rows, ways, own, coded):
    width = own.shape[1]
    left = slots // ways
    vmem = pl.BlockSpec(memory_space=pltpu.VMEM)
    out = jax.ShapeDtypeStruct((left * rows + tail_rows(left), width), jnp.int16)
    return pl.pallas_call(
        functools.partial(combine_kernel, slots, rows, ways),
        out_shape=[jax.ShapeDtypeStruct((left * rows, width), jnp.float32)] + [out] * (ways - 1),
        in_specs=[vmem] * (1 + len(coded)),
        out_specs=[vmem] * ways,
        scratch_shapes=[pltpu.VMEM((tail_rows(left), width), jnp.float32)],
        compiler_params=pltpu.CompilerParams(vmem_limit_bytes=32 * 1024 * 1024),
        name="combine",
    )(own, *coded)


def hidden_kernel(chunks, parts, rows, *refs):
    out = refs[chunks * parts + 1]
    for c in range(chunks):
        own, self, coded = refs[c * parts], refs[c * parts + 1], refs[c * parts + 2:(c + 1) * parts]
        total = own[:rows, :] + self[...]
        for a in coded:
            total = total + read_coded(a, 1, rows)(0)
        out[c * rows:(c + 1) * rows, :] = jnp.maximum(total, 0.0).astype(jnp.bfloat16)


def hidden_rows(chunk_parts, rows, sel):
    chunks, parts = len(chunk_parts), len(chunk_parts[0])
    width = chunk_parts[0][0].shape[1]
    vmem = pl.BlockSpec(memory_space=pltpu.VMEM)
    flat = [a for part in chunk_parts for a in part]
    return pl.pallas_call(
        functools.partial(hidden_kernel, chunks, parts, rows),
        out_shape=jax.ShapeDtypeStruct((chunks * rows, width), jnp.bfloat16),
        in_specs=[vmem] * (len(flat) + 1),
        out_specs=vmem,
        compiler_params=pltpu.CompilerParams(vmem_limit_bytes=32 * 1024 * 1024),
        name="hidden_rows",
    )(*flat, sel)


def send_kernel(own, other, sel, send):
    both = jnp.concatenate([own[...], other[...]], axis=0)
    send[...] = jnp.dot(sel[...], both, preferred_element_type=jnp.float32).astype(jnp.bfloat16)


def rows_to_send(own, other, sel):
    vmem = pl.BlockSpec(memory_space=pltpu.VMEM)
    return pl.pallas_call(
        send_kernel,
        out_shape=jax.ShapeDtypeStruct((sel.shape[0], own.shape[1]), jnp.bfloat16),
        in_specs=[vmem] * 3,
        out_specs=vmem,
        compiler_params=pltpu.CompilerParams(vmem_limit_bytes=32 * 1024 * 1024),
        name="rows_to_send",
    )(own, other, sel)


def logits_kernel(own, other, received, front, adj_received, w_self, w_neigh, out):
    rows = out.shape[0]
    both = jnp.concatenate([own[...], other[...]], axis=0)
    local = jnp.dot(front[...], both, preferred_element_type=jnp.float32)
    mean = local[:rows, :] + jnp.dot(adj_received[...], received[...], preferred_element_type=jnp.float32)
    dims = (((1,), (1,)), ((), ()))
    got = lax.dot_general(local[rows:, :].astype(jnp.bfloat16), w_self[...], dims, preferred_element_type=jnp.float32)
    got = got + lax.dot_general(mean.astype(jnp.bfloat16), w_neigh[...], dims, preferred_element_type=jnp.float32)
    out[...] = got


def logits_of(own, other, received, front, adj_received, w_self, w_neigh):
    vmem = pl.BlockSpec(memory_space=pltpu.VMEM)
    return pl.pallas_call(
        logits_kernel,
        out_shape=jax.ShapeDtypeStruct((adj_received.shape[0], w_self.shape[1]), jnp.float32),
        in_specs=[vmem] * 7,
        out_specs=vmem,
        compiler_params=pltpu.CompilerParams(vmem_limit_bytes=32 * 1024 * 1024),
        name="logits",
    )(own, other, received, front, adj_received, w_self.T, w_neigh.T)


def exchange(parts, stride, n, places):
    got = [parts[0]]
    for k in places:
        got.append(lax.ppermute(parts[k], "dom", [(i, i ^ (k * stride)) for i in range(n)]))
    return got


def body(
    features,
    tile_weight,
    tile_dst,
    tile_src,
    tile_rows,
    w_self1,
    neighbour_weight_first,
    send_list,
    send_count,
    adj_two,
    w_self2,
    w_neigh2,
):
    n = lax.axis_size("dom")
    tile = tile_weight.shape[1]
    groups = tile // UNIT
    per = groups // 2 // CHUNKS
    bits = n.bit_length() - 1
    assert n == 1 << bits and bits >= 2
    radices = [2] * (bits // 2) + [1] * (bits % 2)
    ids = jnp.stack([lax.axis_index("feat"), lax.axis_index("dom")]).astype(jnp.int32)
    swap = [(0, 1), (1, 0)]
    xp = lax.ppermute(features, "feat", swap)
    wp = lax.ppermute(neighbour_weight_first, "feat", swap)
    tw = tile_weight.reshape(tile_weight.shape[0], groups, UNIT, tile)
    planned = plan(
        CHUNKS, per, n, 4, ids, tile_src, tile_rows, tile_dst, tw, features,
    )
    tables, tbufs, xo = planned[:CHUNKS], planned[CHUNKS:2 * CHUNKS], planned[2 * CHUNKS]
    wo, so = neighbour_weight_first, w_self1
    done = []
    for chunk in range(CHUNKS):
        accs = gathered_sums(per, n, tables[chunk], tbufs[chunk], xo, xp)
        slots, rows = n // 4, per * UNIT
        parts = {}
        (parts[3],) = sent_terms((3,), slots, rows, accs, wo, wp)
        parts[2], parts[1] = sent_terms((2, 1), slots, rows, accs, wo, wp)
        parts[0], theirs = own_terms(chunk, per, groups, slots, ids, accs, wo, wp, xo, so)
        self = lax.ppermute(theirs, "feat", swap)
        got = exchange(parts, 1, n, (1, 2, 3))
        stride = 4
        for radix in radices[1:]:
            ways = 1 << radix
            parts = combine(n // stride, per * UNIT, ways, got[0], got[1:])
            got = exchange(parts, stride, n, (2, 3, 1) if ways == 4 else (1,))
            stride *= ways
        done.append([got[0], self] + got[1:])
    sel, front, adj_received = selection(groups, ids, send_list, send_count, adj_two)
    own = hidden_rows(done, per * UNIT, sel)
    other = lax.ppermute(own, "feat", swap)
    send = rows_to_send(own, other, sel)
    received = lax.all_to_all(send, "dom", 0, 0, axis_index_groups=[group_order(n)], tiled=True)
    return logits_of(own, other, received, front, adj_received, w_self2, w_neigh2)


def solution(mesh):
    in_specs = (
        P("dom", "feat"),
        P("dom", None, None),
        P("dom"),
        P("dom"),
        P("dom"),
        P("feat", None),
        P("feat", None),
        P(),
        P(),
        P("dom", None),
        P(),
        P(),
    )
    out_specs = P("dom", None)
    return jax.shard_map(body, mesh=mesh, in_specs=in_specs, out_specs=out_specs, check_vma=False)
```

```python
import functools

import jax
import jax.numpy as jnp
from jax import lax
from jax.experimental import pallas as pl
from jax.experimental.pallas import tpu as pltpu
from jax.sharding import PartitionSpec as P

UNIT = 16
BLOCK = 8
STEP = 8
PART = 256
CHUNKS = 1


def group_of(core, place, groups):
    pair = 2 * (place // 2) + core
    return pair if place % 2 == 0 else groups - 1 - pair


def group_order(n):
    return list(range(n - 1, -1, -1))


LN2 = 0.6931471805599453


def tail_rows(slots):
    return -(-slots // 8) * 8


def encode(x):
    top = jnp.max(jnp.abs(x), axis=0, keepdims=True)
    power = jnp.ceil(jnp.log(jnp.maximum(top, 1e-30)) * (1.0 / LN2) + 1e-3) - 15.0
    return jnp.floor(x * jnp.exp(power * -LN2) + 0.5), power


def to_int16(x):
    return x.astype(jnp.int32).astype(jnp.int16)


def write_coded(out, tail, slots, rows, value_of):
    tail[...] = jnp.zeros_like(tail)
    for s in range(slots):
        whole, power = encode(value_of(s))
        out[s * rows:(s + 1) * rows, :] = to_int16(whole)
        tail[s:s + 1, :] = power
    out[slots * rows:, :] = to_int16(tail[...])


def read_coded(ref, slots, rows):
    powers = ref[slots * rows:, :].astype(jnp.int32).astype(jnp.float32)

    def value_of(s):
        whole = ref[s * rows:(s + 1) * rows, :].astype(jnp.int32).astype(jnp.float32)
        return whole * jnp.exp(powers[s:s + 1, :] * LN2)

    return value_of


def plan_kernel(chunks, per, n, radix, n_src, ids, src_h, rows_h, dst_h, tw, xo, *rest):
    tables, rest = rest[:chunks], rest[chunks:]
    tbufs, rest = rest[:chunks], rest[chunks:]
    xo_out, src_v, rows_v, dst_v, sems = rest
    core, me = ids[0], ids[1]
    tiles = src_v.shape[1]
    n_pos = tables[0].shape[1]
    units = per * tiles
    groups = 2 * per * chunks
    half = groups // 2
    gs = [group_of(core, i, groups) for i in range(half)]
    small = [(src_h, src_v), (rows_h, rows_v), (dst_h, dst_v)]
    large = [(tw.at[:, g], tbufs[i // per].at[pl.ds(i % per * tiles, tiles)]) for i, g in enumerate(gs)]
    large += [(xo, xo_out)]
    copies = [pltpu.make_async_copy(a, b, sems.at[i]) for i, (a, b) in enumerate(small + large)]
    for c in copies:
        c.start()
    lane = lax.broadcasted_iota(jnp.int32, (1, tiles), 1)
    block_i = lax.broadcasted_iota(jnp.int32, (n_src, tiles), 0)
    before = lax.broadcasted_iota(jnp.int32, (tiles, tiles), 0) < lax.broadcasted_iota(jnp.int32, (tiles, tiles), 1)
    before = jnp.where(before, 1.0, 0.0).astype(jnp.bfloat16)
    pos_i = lax.broadcasted_iota(jnp.int32, (tiles, n_pos), 1).astype(jnp.float32)
    place_i = lax.broadcasted_iota(jnp.int32, (1, n_pos), 1)
    trash = float(n * per << 14)
    for c in copies[:3]:
        c.wait()
    src, rows = src_v[...], rows_v[...]
    slot = jnp.bitwise_xor(dst_v[...], me)
    slot = jnp.bitwise_and(slot, radix - 1) * (n // radix) + lax.div(slot, radix)
    for c in range(chunks):
        hot, words, valid = [], [], []
        for j in range(per):
            limit = jnp.clip(rows - UNIT * gs[c * per + j], 0, UNIT)
            ok = limit > 0
            valid.append(ok)
            words.append(((slot * per + j) * 512 + (j * tiles + lane)) * 32 + limit)
            hot.append(jnp.where(jnp.logical_and(block_i == src, ok), 1.0, 0.0))
        stacked = jnp.concatenate(hot, axis=0)
        earlier = jnp.dot(stacked.astype(jnp.bfloat16), before, preferred_element_type=jnp.float32)
        counts = jnp.sum(stacked, axis=1, keepdims=True)
        counts = [counts[j * n_src:(j + 1) * n_src, :] for j in range(per)]
        blocks = jnp.floor((sum(counts) + (BLOCK - 1)) * (1.0 / BLOCK))
        ahead = jnp.zeros(blocks.shape, jnp.float32)
        source_i = lax.broadcasted_iota(jnp.int32, blocks.shape, 0)
        for s in range(n_src - 1):
            ahead = ahead + jnp.where(source_i > s, blocks[s:s + 1, :], 0.0)
        first, pos = ahead * BLOCK, []
        for j in range(per):
            place = hot[j] * (earlier[j * n_src:(j + 1) * n_src, :] + first)
            pos.append(jnp.sum(place, axis=0, keepdims=True))
            first = first + counts[j]
        behind = jnp.where(place_i.astype(jnp.float32) >= ahead + blocks, 1.0, 0.0)
        owner = jnp.sum(behind, axis=0, keepdims=True)
        run = ahead[n_src - 1:, :] + blocks[n_src - 1:, :]
        stack = [jnp.where(valid[j], pos[j], -1.0) for j in range(per)]
        stack += [w.astype(jnp.float32) - trash for w in words]
        stack += [jnp.zeros((1, tiles), jnp.float32)] * (-len(stack) % 8)
        cols = jnp.concatenate(stack, axis=0).T
        found = jnp.zeros((tiles, n_pos), jnp.float32)
        for j in range(per):
            found = found + jnp.where(cols[:, j:j + 1] == pos_i, cols[:, per + j:per + j + 1], 0.0)
        word = jnp.sum(found, axis=0, keepdims=True) + trash
        owner = jnp.where(place_i == n_pos - 1, run, jnp.minimum(owner, n_src - 1.0))
        word = word.astype(jnp.int32)
        tables[c][0:1, :] = jnp.bitwise_and(lax.shift_right_logical(word, 5), 511)
        tables[c][1:2, :] = owner.astype(jnp.int32)
        tables[c][2:3, :] = lax.shift_right_logical(word, 14)
        tables[c][3:4, :] = jnp.bitwise_and(word, 31)

    for c in copies[3:]:
        c.wait()


def plan(chunks, per, n, radix, ids, src, rows, dst, tw, xo):
    tiles, _, _, tile = tw.shape
    n_src = xo.shape[0] // tile
    blocks = -(-(per * tiles // BLOCK + n_src) // STEP) * STEP
    n_pos = -(-(blocks * BLOCK + 1) // 128) * 128
    smem = pl.BlockSpec(memory_space=pltpu.SMEM)
    vmem = pl.BlockSpec(memory_space=pltpu.VMEM)
    hbm = pl.BlockSpec(memory_space=pltpu.HBM)
    half = chunks * per
    return pl.pallas_call(
        functools.partial(plan_kernel, chunks, per, n, radix, n_src),
        out_shape=[jax.ShapeDtypeStruct((4, n_pos), jnp.int32)] * chunks
        + [jax.ShapeDtypeStruct((per * tiles, UNIT, tile), tw.dtype)] * chunks
        + [jax.ShapeDtypeStruct(xo.shape, xo.dtype)],
        in_specs=[smem] + [hbm] * 5,
        out_specs=[vmem] * (2 * chunks + 1),
        scratch_shapes=[
            pltpu.VMEM((1, tiles), jnp.int32),
            pltpu.VMEM((1, tiles), jnp.int32),
            pltpu.VMEM((1, tiles), jnp.int32),
            pltpu.SemaphoreType.DMA((3 + half + 1,)),
        ],
        compiler_params=pltpu.CompilerParams(vmem_limit_bytes=32 * 1024 * 1024),
        name="plan",
    )(ids, *[
        pltpu.with_memory_space_constraint(a, pltpu.HBM)
        for a in (src.reshape(1, tiles), rows.reshape(1, tiles), dst.reshape(1, tiles), tw, xo)
    ])


def select_kernel(groups, ids, lists, counts, adj, sel, front, adj_out):
    core, me = ids[0], ids[1]
    n = lists.shape[0]
    slots = lists.shape[1]
    total = n * slots
    q_n = lax.broadcasted_iota(jnp.int32, (total, n), 0)
    r_n = lax.broadcasted_iota(jnp.int32, (total, n), 1)
    mine = lists[me].astype(jnp.float32)
    cnt = counts[pl.ds(me, 1), :]
    picked = jnp.zeros((total, n), jnp.float32)
    k_n = jnp.bitwise_and(q_n, slots - 1)
    for k in range(slots):
        picked = jnp.where(k_n == k, mine[k:k + 1, :], picked)
    good = jnp.logical_and(n - 1 - lax.div(q_n, slots) == r_n, k_n < cnt)
    row = jnp.sum(jnp.where(good, picked + 1.0, 0.0), axis=1, keepdims=True) - 1.0
    lane = lax.broadcasted_iota(jnp.int32, (1, sel.shape[1]), 1)
    name = jnp.zeros(lane.shape, jnp.int32)
    names = [group_of(c, i, groups) for c in (core, 1 - core) for i in range(groups // 2)]
    for i, g in enumerate(names):
        name = jnp.where(lax.div(lane, UNIT) == i, g * UNIT + jnp.bitwise_and(lane, UNIT - 1), name)
    sel[...] = jnp.where(row == name.astype(jnp.float32), 1.0, 0.0).astype(jnp.bfloat16)
    tile, out_rows = groups * UNIT, adj.shape[0]
    placed = jnp.where(lax.broadcasted_iota(jnp.int32, (tile, tile), 0) == name, 1.0, 0.0).astype(jnp.bfloat16)
    front[:out_rows, :] = jnp.dot(adj[:, :tile], placed, preferred_element_type=jnp.float32).astype(jnp.bfloat16)
    front[out_rows:, :] = placed[:out_rows, :]
    column = lax.broadcasted_iota(jnp.int32, (1, total), 1)
    source = (n - 1 - lax.div(column, slots)) * slots + lax.rem(column, slots)
    moved = jnp.where(lax.broadcasted_iota(jnp.int32, (total, total), 0) == source, 1.0, 0.0).astype(jnp.bfloat16)
    adj_out[...] = jnp.dot(adj[:, groups * UNIT:], moved, preferred_element_type=jnp.float32).astype(jnp.bfloat16)


def selection(groups, ids, send_list, send_count, adj):
    n, _, slots = send_list.shape
    smem = pl.BlockSpec(memory_space=pltpu.SMEM)
    vmem = pl.BlockSpec(memory_space=pltpu.VMEM)
    return pl.pallas_call(
        functools.partial(select_kernel, groups),
        out_shape=[
            jax.ShapeDtypeStruct((n * slots, groups * UNIT), jnp.bfloat16),
            jax.ShapeDtypeStruct((2 * adj.shape[0], groups * UNIT), jnp.bfloat16),
            jax.ShapeDtypeStruct((adj.shape[0], n * slots), jnp.bfloat16),
        ],
        in_specs=[smem, vmem, vmem, vmem],
        out_specs=[vmem] * 3,
        compiler_params=pltpu.CompilerParams(vmem_limit_bytes=32 * 1024 * 1024),
        name="selection",
    )(ids, jnp.swapaxes(send_list, 1, 2), send_count, adj)


def tiles_kernel(table_v, tbuf, xo, xp, *rest):
    parts = len(rest) - 3
    accs, (masks, table, sem) = rest[:parts], rest[parts:]
    tile = tbuf.shape[2]
    width = xo.shape[1]
    to_scalar = pltpu.make_async_copy(table_v, table, sem)
    to_scalar.start()
    for acc in accs:
        acc[...] = jnp.zeros_like(acc)
    row_i = lax.broadcasted_iota(jnp.int32, (UNIT, tile), 0)
    for m in range(UNIT + 1):
        masks[m] = jnp.where(row_i < m, 1.0, 0.0).astype(jnp.bfloat16)
    columns = [(x, h) for x in (xo, xp) for h in range(0, width, PART)]
    to_scalar.wait()

    def blocks(first, count):
        for m in range(count):
            at = first + m
            base = pl.multiple_of(table[1, at] * tile, tile)
            rows, places = [], []
            for k in range(BLOCK):
                rows.append(tbuf[table[0, at * BLOCK + k]] * masks[table[3, at * BLOCK + k]])
                places.append(table[2, at * BLOCK + k])
            lhs = jnp.concatenate(rows, axis=0)
            for acc, (x, h) in zip(accs, columns):
                got = jnp.dot(lhs, x[pl.ds(base, tile), h:h + PART], preferred_element_type=jnp.float32)
                got = got.astype(jnp.bfloat16).astype(jnp.float32)
                for k in range(BLOCK):
                    acc[places[k]] += got[k * UNIT:(k + 1) * UNIT, :]

    half = STEP // 2
    halves = lax.div(table[1, table.shape[1] - 1] + half - 1, half)
    steps = lax.div(halves, 2)

    def step(i, carry):
        blocks(i * STEP, STEP)
        return carry

    def last(i, carry):
        blocks(steps * STEP, half)
        return carry

    lax.fori_loop(0, steps, step, 0)
    lax.fori_loop(0, lax.rem(halves, 2), last, 0)


def gathered_sums(per, n, table, tbuf, xo, xp):
    width = xo.shape[1]
    tile = tbuf.shape[2]
    vmem = pl.BlockSpec(memory_space=pltpu.VMEM)
    flops = 2 * tbuf.shape[0] * UNIT * tile * 2 * width
    parts = 2 * width // PART
    sums = jax.ShapeDtypeStruct((n * per + 1, UNIT, PART), jnp.float32)
    return pl.pallas_call(
        tiles_kernel,
        out_shape=[sums] * parts,
        in_specs=[vmem] * 4,
        out_specs=[vmem] * parts,
        scratch_shapes=[
            pltpu.VMEM((UNIT + 1, UNIT, tile), jnp.bfloat16),
            pltpu.SMEM(table.shape, jnp.int32),
            pltpu.SemaphoreType.DMA,
        ],
        compiler_params=pltpu.CompilerParams(vmem_limit_bytes=(12 << 20) + sums.size * 4 * parts),
        cost_estimate=pl.CostEstimate(flops=flops, bytes_accessed=8 << 20, transcendentals=0),
        name="gathered_sums",
    )(table, tbuf, xo, xp)


def weigh(accs, weights, first, count, out):
    size = min(256, count)

    def piece(r, carry):
        at = r * size if isinstance(r, int) else pl.multiple_of(r * size, size)
        got = jnp.zeros((size, out.shape[1]), jnp.float32)
        for i, acc in enumerate(accs):
            w, h = weights[i * PART // weights[0].shape[0]], i * PART % weights[0].shape[0]
            value = acc[pl.ds(first // UNIT + r * (size // UNIT), size // UNIT)].reshape(size, PART)
            high = value.astype(jnp.bfloat16)
            low = (value - high.astype(jnp.float32)).astype(jnp.bfloat16)
            got = got + jnp.dot(high, w[h:h + PART, :], preferred_element_type=jnp.float32)
            got = got + jnp.dot(low, w[h:h + PART, :], preferred_element_type=jnp.float32)
        out[pl.ds(at, size), :] = got
        return carry

    if count == size:
        piece(0, 0)
    else:
        lax.fori_loop(0, count // size, piece, 0)


def sent_kernel(ks, slots, rows, parts, wo, wp, *refs):
    accs, outs, scratch = refs[:parts], refs[parts:parts + len(ks)], refs[parts + len(ks):]
    for i, k in enumerate(ks):
        sums, tail = scratch[2 * i:2 * i + 2]
        weigh(accs, (wo, wp), k * slots * rows, slots * rows, sums)
        write_coded(outs[i], tail, slots, rows, lambda s: sums[s * rows:(s + 1) * rows, :])


def sent_terms(ks, slots, rows, accs, wo, wp):
    hidden = wo.shape[1]
    vmem = pl.BlockSpec(memory_space=pltpu.VMEM)
    coded = jax.ShapeDtypeStruct((slots * rows + tail_rows(slots), hidden), jnp.int16)
    return pl.pallas_call(
        functools.partial(sent_kernel, ks, slots, rows, len(accs)),
        out_shape=[coded] * len(ks),
        in_specs=[vmem] * (2 + len(accs)),
        out_specs=[vmem] * len(ks),
        scratch_shapes=[
            pltpu.VMEM((slots * rows, hidden), jnp.float32),
            pltpu.VMEM((tail_rows(slots), hidden), jnp.float32),
        ] * len(ks),
        compiler_params=pltpu.CompilerParams(vmem_limit_bytes=(20 << 20) + accs[0].size * 4 * len(accs)),
        cost_estimate=pl.CostEstimate(
            flops=4 * len(ks) * slots * rows * PART * len(accs) * hidden, bytes_accessed=2 << 20, transcendentals=0),
        name="sent_terms",
    )(wo, wp, *accs)


def own_kernel(chunk, per, groups, parts, ids, wo, wp, xo, so, *refs):
    accs, (out, theirs, terms) = refs[:parts], refs[parts:]
    weigh(accs, (wo, wp), 0, out.shape[0], out)
    terms[...] = jnp.dot(xo[:groups * UNIT, :], so[...], preferred_element_type=jnp.float32)
    for j in range(per):
        here = slice(j * UNIT, (j + 1) * UNIT)
        at = pl.multiple_of(group_of(ids[0], chunk * per + j, groups) * UNIT, UNIT)
        out[here, :] += terms[pl.ds(at, UNIT), :]
        at = pl.multiple_of(group_of(1 - ids[0], chunk * per + j, groups) * UNIT, UNIT)
        theirs[here, :] = terms[pl.ds(at, UNIT), :]


def own_terms(chunk, per, groups, slots, ids, accs, wo, wp, xo, so):
    hidden = wo.shape[1]
    rows = per * UNIT
    smem = pl.BlockSpec(memory_space=pltpu.SMEM)
    vmem = pl.BlockSpec(memory_space=pltpu.VMEM)
    return pl.pallas_call(
        functools.partial(own_kernel, chunk, per, groups, len(accs)),
        out_shape=[
            jax.ShapeDtypeStruct((slots * rows, hidden), jnp.float32),
            jax.ShapeDtypeStruct((rows, hidden), jnp.float32),
        ],
        in_specs=[smem] + [vmem] * (4 + len(accs)),
        out_specs=[vmem] * 2,
        scratch_shapes=[pltpu.VMEM((groups * UNIT, hidden), jnp.float32)],
        compiler_params=pltpu.CompilerParams(vmem_limit_bytes=(12 << 20) + accs[0].size * 4 * len(accs)),
        cost_estimate=pl.CostEstimate(
            flops=4 * slots * rows * PART * len(accs) * hidden, bytes_accessed=2 << 20, transcendentals=0),
        name="own_terms",
    )(ids, wo, wp, xo, so, *accs)


def combine_kernel(slots, rows, ways, own, *refs):
    parts = len(refs) - ways - 1
    coded, outs, tail = refs[:parts], refs[parts:parts + ways], refs[parts + ways]
    values = [read_coded(a, slots, rows) for a in coded]

    def total(s):
        got = own[s * rows:(s + 1) * rows, :]
        for value in values:
            got = got + value(s)
        return got

    for i in range(slots // ways):
        outs[0][i * rows:(i + 1) * rows, :] = total(i * ways)
    for k in range(1, ways):
        write_coded(outs[k], tail, slots // ways, rows, lambda s: total(s * ways + k))


def combine(slots, rows, ways, own, coded):
    width = own.shape[1]
    left = slots // ways
    vmem = pl.BlockSpec(memory_space=pltpu.VMEM)
    out = jax.ShapeDtypeStruct((left * rows + tail_rows(left), width), jnp.int16)
    return pl.pallas_call(
        functools.partial(combine_kernel, slots, rows, ways),
        out_shape=[jax.ShapeDtypeStruct((left * rows, width), jnp.float32)] + [out] * (ways - 1),
        in_specs=[vmem] * (1 + len(coded)),
        out_specs=[vmem] * ways,
        scratch_shapes=[pltpu.VMEM((tail_rows(left), width), jnp.float32)],
        compiler_params=pltpu.CompilerParams(vmem_limit_bytes=32 * 1024 * 1024),
        name="combine",
    )(own, *coded)


def hidden_kernel(chunks, parts, rows, *refs):
    out = refs[chunks * parts + 1]
    for c in range(chunks):
        own, self, coded = refs[c * parts], refs[c * parts + 1], refs[c * parts + 2:(c + 1) * parts]
        total = own[:rows, :] + self[...]
        for a in coded:
            total = total + read_coded(a, 1, rows)(0)
        out[c * rows:(c + 1) * rows, :] = jnp.maximum(total, 0.0).astype(jnp.bfloat16)


def hidden_rows(chunk_parts, rows, sel):
    chunks, parts = len(chunk_parts), len(chunk_parts[0])
    width = chunk_parts[0][0].shape[1]
    vmem = pl.BlockSpec(memory_space=pltpu.VMEM)
    flat = [a for part in chunk_parts for a in part]
    return pl.pallas_call(
        functools.partial(hidden_kernel, chunks, parts, rows),
        out_shape=jax.ShapeDtypeStruct((chunks * rows, width), jnp.bfloat16),
        in_specs=[vmem] * (len(flat) + 1),
        out_specs=vmem,
        compiler_params=pltpu.CompilerParams(vmem_limit_bytes=32 * 1024 * 1024),
        name="hidden_rows",
    )(*flat, sel)


def send_kernel(own, other, sel, send):
    both = jnp.concatenate([own[...], other[...]], axis=0)
    send[...] = jnp.dot(sel[...], both, preferred_element_type=jnp.float32).astype(jnp.bfloat16)


def rows_to_send(own, other, sel):
    vmem = pl.BlockSpec(memory_space=pltpu.VMEM)
    return pl.pallas_call(
        send_kernel,
        out_shape=jax.ShapeDtypeStruct((sel.shape[0], own.shape[1]), jnp.bfloat16),
        in_specs=[vmem] * 3,
        out_specs=vmem,
        compiler_params=pltpu.CompilerParams(vmem_limit_bytes=32 * 1024 * 1024),
        name="rows_to_send",
    )(own, other, sel)


def logits_kernel(own, other, received, front, adj_received, w_self, w_neigh, out):
    rows = out.shape[0]
    both = jnp.concatenate([own[...], other[...]], axis=0)
    local = jnp.dot(front[...], both, preferred_element_type=jnp.float32)
    mean = local[:rows, :] + jnp.dot(adj_received[...], received[...], preferred_element_type=jnp.float32)
    dims = (((1,), (1,)), ((), ()))
    got = lax.dot_general(local[rows:, :].astype(jnp.bfloat16), w_self[...], dims, preferred_element_type=jnp.float32)
    got = got + lax.dot_general(mean.astype(jnp.bfloat16), w_neigh[...], dims, preferred_element_type=jnp.float32)
    out[...] = got


def logits_of(own, other, received, front, adj_received, w_self, w_neigh):
    vmem = pl.BlockSpec(memory_space=pltpu.VMEM)
    return pl.pallas_call(
        logits_kernel,
        out_shape=jax.ShapeDtypeStruct((adj_received.shape[0], w_self.shape[1]), jnp.float32),
        in_specs=[vmem] * 7,
        out_specs=vmem,
        compiler_params=pltpu.CompilerParams(vmem_limit_bytes=32 * 1024 * 1024),
        name="logits",
    )(own, other, received, front, adj_received, w_self.T, w_neigh.T)


def exchange(parts, stride, n, places):
    got = [parts[0]]
    for k in places:
        got.append(lax.ppermute(parts[k], "dom", [(i, i ^ (k * stride)) for i in range(n)]))
    return got


def body(
    features,
    tile_weight,
    tile_dst,
    tile_src,
    tile_rows,
    w_self1,
    neighbour_weight_first,
    send_list,
    send_count,
    adj_two,
    w_self2,
    w_neigh2,
):
    n = lax.axis_size("dom")
    tile = tile_weight.shape[1]
    groups = tile // UNIT
    per = groups // 2 // CHUNKS
    bits = n.bit_length() - 1
    assert n == 1 << bits and bits >= 2
    radices = [2] * (bits // 2) + [1] * (bits % 2)
    ids = jnp.stack([lax.axis_index("feat"), lax.axis_index("dom")]).astype(jnp.int32)
    swap = [(0, 1), (1, 0)]
    xp = lax.ppermute(features, "feat", swap)
    wp = lax.ppermute(neighbour_weight_first, "feat", swap)
    tw = tile_weight.reshape(tile_weight.shape[0], groups, UNIT, tile)
    planned = plan(
        CHUNKS, per, n, 4, ids, tile_src, tile_rows, tile_dst, tw, features,
    )
    tables, tbufs, xo = planned[:CHUNKS], planned[CHUNKS:2 * CHUNKS], planned[2 * CHUNKS]
    wo, so = neighbour_weight_first, w_self1
    done = []
    for chunk in range(CHUNKS):
        accs = gathered_sums(per, n, tables[chunk], tbufs[chunk], xo, xp)
        slots, rows = n // 4, per * UNIT
        parts = {}
        (parts[3],) = sent_terms((3,), slots, rows, accs, wo, wp)
        parts[2], parts[1] = sent_terms((2, 1), slots, rows, accs, wo, wp)
        parts[0], theirs = own_terms(chunk, per, groups, slots, ids, accs, wo, wp, xo, so)
        self = lax.ppermute(theirs, "feat", swap)
        got = exchange(parts, 1, n, (1, 2, 3))
        stride = 4
        for radix in radices[1:]:
            ways = 1 << radix
            parts = combine(n // stride, per * UNIT, ways, got[0], got[1:])
            got = exchange(parts, stride, n, (2, 3, 1) if ways == 4 else (1,))
            stride *= ways
        done.append([got[0], self] + got[1:])
    sel, front, adj_received = selection(groups, ids, send_list, send_count, adj_two)
    own = hidden_rows(done, per * UNIT, sel)
    other = lax.ppermute(own, "feat", swap)
    send = rows_to_send(own, other, sel)
    received = lax.all_to_all(send, "dom", 0, 0, axis_index_groups=[group_order(n)], tiled=True)
    return logits_of(own, other, received, front, adj_received, w_self2, w_neigh2)


def solution(mesh):
    in_specs = (
        P("dom", "feat"),
        P("dom", None, None),
        P("dom"),
        P("dom"),
        P("dom"),
        P("feat", None),
        P("feat", None),
        P(),
        P(),
        P("dom", None),
        P(),
        P(),
    )
    out_specs = P("dom", None)
    return jax.shard_map(body, mesh=mesh, in_specs=in_specs, out_specs=out_specs, check_vma=False)
```

```python
import functools

import jax
import jax.numpy as jnp
from jax import lax
from jax.experimental import pallas as pl
from jax.experimental.pallas import tpu as pltpu
from jax.sharding import PartitionSpec as P

UNIT = 16
BLOCK = 8
STEP = 12
PART = 256
CHUNKS = 1


def group_of(core, place, groups):
    pair = 2 * (place // 2) + core
    return pair if place % 2 == 0 else groups - 1 - pair


def group_order(n):
    return list(range(n - 1, -1, -1))


LN2 = 0.6931471805599453


def tail_rows(slots):
    return -(-slots // 8) * 8


def encode(x):
    top = jnp.max(jnp.abs(x), axis=0, keepdims=True)
    power = jnp.ceil(jnp.log(jnp.maximum(top, 1e-30)) * (1.0 / LN2) + 1e-3) - 15.0
    return jnp.floor(x * jnp.exp(power * -LN2) + 0.5), power


def to_int16(x):
    return x.astype(jnp.int32).astype(jnp.int16)


def write_coded(out, tail, slots, rows, value_of):
    tail[...] = jnp.zeros_like(tail)
    for s in range(slots):
        whole, power = encode(value_of(s))
        out[s * rows:(s + 1) * rows, :] = to_int16(whole)
        tail[s:s + 1, :] = power
    out[slots * rows:, :] = to_int16(tail[...])


def read_coded(ref, slots, rows):
    powers = ref[slots * rows:, :].astype(jnp.int32).astype(jnp.float32)

    def value_of(s):
        whole = ref[s * rows:(s + 1) * rows, :].astype(jnp.int32).astype(jnp.float32)
        return whole * jnp.exp(powers[s:s + 1, :] * LN2)

    return value_of


def plan_kernel(chunks, per, n, radix, n_src, ids, src_h, rows_h, dst_h, tw, xo, *rest):
    tables, rest = rest[:chunks], rest[chunks:]
    tbufs, rest = rest[:chunks], rest[chunks:]
    xo_out, src_v, rows_v, dst_v, sems = rest
    core, me = ids[0], ids[1]
    tiles = src_v.shape[1]
    n_pos = tables[0].shape[1]
    units = per * tiles
    groups = 2 * per * chunks
    half = groups // 2
    gs = [group_of(core, i, groups) for i in range(half)]
    small = [(src_h, src_v), (rows_h, rows_v), (dst_h, dst_v)]
    large = [(tw.at[:, g], tbufs[i // per].at[pl.ds(i % per * tiles, tiles)]) for i, g in enumerate(gs)]
    large += [(xo, xo_out)]
    copies = [pltpu.make_async_copy(a, b, sems.at[i]) for i, (a, b) in enumerate(small + large)]
    for c in copies:
        c.start()
    lane = lax.broadcasted_iota(jnp.int32, (1, tiles), 1)
    block_i = lax.broadcasted_iota(jnp.int32, (n_src, tiles), 0)
    before = lax.broadcasted_iota(jnp.int32, (tiles, tiles), 0) < lax.broadcasted_iota(jnp.int32, (tiles, tiles), 1)
    before = jnp.where(before, 1.0, 0.0).astype(jnp.bfloat16)
    pos_i = lax.broadcasted_iota(jnp.int32, (tiles, n_pos), 1).astype(jnp.float32)
    place_i = lax.broadcasted_iota(jnp.int32, (1, n_pos), 1)
    trash = float(n * per << 14)
    for c in copies[:3]:
        c.wait()
    src, rows = src_v[...], rows_v[...]
    slot = jnp.bitwise_xor(dst_v[...], me)
    slot = jnp.bitwise_and(slot, radix - 1) * (n // radix) + lax.div(slot, radix)
    for c in range(chunks):
        hot, words, valid = [], [], []
        for j in range(per):
            limit = jnp.clip(rows - UNIT * gs[c * per + j], 0, UNIT)
            ok = limit > 0
            valid.append(ok)
            words.append(((slot * per + j) * 512 + (j * tiles + lane)) * 32 + limit)
            hot.append(jnp.where(jnp.logical_and(block_i == src, ok), 1.0, 0.0))
        stacked = jnp.concatenate(hot, axis=0)
        earlier = jnp.dot(stacked.astype(jnp.bfloat16), before, preferred_element_type=jnp.float32)
        counts = jnp.sum(stacked, axis=1, keepdims=True)
        counts = [counts[j * n_src:(j + 1) * n_src, :] for j in range(per)]
        blocks = jnp.floor((sum(counts) + (BLOCK - 1)) * (1.0 / BLOCK))
        ahead = jnp.zeros(blocks.shape, jnp.float32)
        source_i = lax.broadcasted_iota(jnp.int32, blocks.shape, 0)
        for s in range(n_src - 1):
            ahead = ahead + jnp.where(source_i > s, blocks[s:s + 1, :], 0.0)
        first, pos = ahead * BLOCK, []
        for j in range(per):
            place = hot[j] * (earlier[j * n_src:(j + 1) * n_src, :] + first)
            pos.append(jnp.sum(place, axis=0, keepdims=True))
            first = first + counts[j]
        behind = jnp.where(place_i.astype(jnp.float32) >= ahead + blocks, 1.0, 0.0)
        owner = jnp.sum(behind, axis=0, keepdims=True)
        run = ahead[n_src - 1:, :] + blocks[n_src - 1:, :]
        stack = [jnp.where(valid[j], pos[j], -1.0) for j in range(per)]
        stack += [w.astype(jnp.float32) - trash for w in words]
        stack += [jnp.zeros((1, tiles), jnp.float32)] * (-len(stack) % 8)
        cols = jnp.concatenate(stack, axis=0).T
        found = jnp.zeros((tiles, n_pos), jnp.float32)
        for j in range(per):
            found = found + jnp.where(cols[:, j:j + 1] == pos_i, cols[:, per + j:per + j + 1], 0.0)
        word = jnp.sum(found, axis=0, keepdims=True) + trash
        owner = jnp.where(place_i == n_pos - 1, run, jnp.minimum(owner, n_src - 1.0))
        word = word.astype(jnp.int32)
        tables[c][0:1, :] = jnp.bitwise_and(lax.shift_right_logical(word, 5), 511)
        tables[c][1:2, :] = owner.astype(jnp.int32)
        tables[c][2:3, :] = lax.shift_right_logical(word, 14)
        tables[c][3:4, :] = jnp.bitwise_and(word, 31)

    for c in copies[3:]:
        c.wait()


def plan(chunks, per, n, radix, ids, src, rows, dst, tw, xo):
    tiles, _, _, tile = tw.shape
    n_src = xo.shape[0] // tile
    blocks = -(-(per * tiles // BLOCK + n_src) // STEP) * STEP
    n_pos = -(-(blocks * BLOCK + 1) // 128) * 128
    smem = pl.BlockSpec(memory_space=pltpu.SMEM)
    vmem = pl.BlockSpec(memory_space=pltpu.VMEM)
    hbm = pl.BlockSpec(memory_space=pltpu.HBM)
    half = chunks * per
    return pl.pallas_call(
        functools.partial(plan_kernel, chunks, per, n, radix, n_src),
        out_shape=[jax.ShapeDtypeStruct((4, n_pos), jnp.int32)] * chunks
        + [jax.ShapeDtypeStruct((per * tiles, UNIT, tile), tw.dtype)] * chunks
        + [jax.ShapeDtypeStruct(xo.shape, xo.dtype)],
        in_specs=[smem] + [hbm] * 5,
        out_specs=[vmem] * (2 * chunks + 1),
        scratch_shapes=[
            pltpu.VMEM((1, tiles), jnp.int32),
            pltpu.VMEM((1, tiles), jnp.int32),
            pltpu.VMEM((1, tiles), jnp.int32),
            pltpu.SemaphoreType.DMA((3 + half + 1,)),
        ],
        compiler_params=pltpu.CompilerParams(vmem_limit_bytes=32 * 1024 * 1024),
        name="plan",
    )(ids, *[
        pltpu.with_memory_space_constraint(a, pltpu.HBM)
        for a in (src.reshape(1, tiles), rows.reshape(1, tiles), dst.reshape(1, tiles), tw, xo)
    ])


def select_kernel(groups, ids, lists, counts, adj, sel, front, adj_out):
    core, me = ids[0], ids[1]
    n = lists.shape[0]
    slots = lists.shape[1]
    total = n * slots
    q_n = lax.broadcasted_iota(jnp.int32, (total, n), 0)
    r_n = lax.broadcasted_iota(jnp.int32, (total, n), 1)
    mine = lists[me].astype(jnp.float32)
    cnt = counts[pl.ds(me, 1), :]
    picked = jnp.zeros((total, n), jnp.float32)
    k_n = jnp.bitwise_and(q_n, slots - 1)
    for k in range(slots):
        picked = jnp.where(k_n == k, mine[k:k + 1, :], picked)
    good = jnp.logical_and(n - 1 - lax.div(q_n, slots) == r_n, k_n < cnt)
    row = jnp.sum(jnp.where(good, picked + 1.0, 0.0), axis=1, keepdims=True) - 1.0
    lane = lax.broadcasted_iota(jnp.int32, (1, sel.shape[1]), 1)
    name = jnp.zeros(lane.shape, jnp.int32)
    names = [group_of(c, i, groups) for c in (core, 1 - core) for i in range(groups // 2)]
    for i, g in enumerate(names):
        name = jnp.where(lax.div(lane, UNIT) == i, g * UNIT + jnp.bitwise_and(lane, UNIT - 1), name)
    sel[...] = jnp.where(row == name.astype(jnp.float32), 1.0, 0.0).astype(jnp.bfloat16)
    tile, out_rows = groups * UNIT, adj.shape[0]
    placed = jnp.where(lax.broadcasted_iota(jnp.int32, (tile, tile), 0) == name, 1.0, 0.0).astype(jnp.bfloat16)
    front[:out_rows, :] = jnp.dot(adj[:, :tile], placed, preferred_element_type=jnp.float32).astype(jnp.bfloat16)
    front[out_rows:, :] = placed[:out_rows, :]
    column = lax.broadcasted_iota(jnp.int32, (1, total), 1)
    source = (n - 1 - lax.div(column, slots)) * slots + lax.rem(column, slots)
    moved = jnp.where(lax.broadcasted_iota(jnp.int32, (total, total), 0) == source, 1.0, 0.0).astype(jnp.bfloat16)
    adj_out[...] = jnp.dot(adj[:, groups * UNIT:], moved, preferred_element_type=jnp.float32).astype(jnp.bfloat16)


def selection(groups, ids, send_list, send_count, adj):
    n, _, slots = send_list.shape
    smem = pl.BlockSpec(memory_space=pltpu.SMEM)
    vmem = pl.BlockSpec(memory_space=pltpu.VMEM)
    return pl.pallas_call(
        functools.partial(select_kernel, groups),
        out_shape=[
            jax.ShapeDtypeStruct((n * slots, groups * UNIT), jnp.bfloat16),
            jax.ShapeDtypeStruct((2 * adj.shape[0], groups * UNIT), jnp.bfloat16),
            jax.ShapeDtypeStruct((adj.shape[0], n * slots), jnp.bfloat16),
        ],
        in_specs=[smem, vmem, vmem, vmem],
        out_specs=[vmem] * 3,
        compiler_params=pltpu.CompilerParams(vmem_limit_bytes=32 * 1024 * 1024),
        name="selection",
    )(ids, jnp.swapaxes(send_list, 1, 2), send_count, adj)


def tiles_kernel(table_v, tbuf, xo, xp, *rest):
    parts = len(rest) - 3
    accs, (masks, table, sem) = rest[:parts], rest[parts:]
    tile = tbuf.shape[2]
    width = xo.shape[1]
    to_scalar = pltpu.make_async_copy(table_v, table, sem)
    to_scalar.start()
    for acc in accs:
        acc[...] = jnp.zeros_like(acc)
    row_i = lax.broadcasted_iota(jnp.int32, (UNIT, tile), 0)
    for m in range(UNIT + 1):
        masks[m] = jnp.where(row_i < m, 1.0, 0.0).astype(jnp.bfloat16)
    columns = [(x, h) for x in (xo, xp) for h in range(0, width, PART)]
    to_scalar.wait()

    def blocks(first, count):
        for m in range(count):
            at = first + m
            base = pl.multiple_of(table[1, at] * tile, tile)
            rows, places = [], []
            for k in range(BLOCK):
                rows.append(tbuf[table[0, at * BLOCK + k]] * masks[table[3, at * BLOCK + k]])
                places.append(table[2, at * BLOCK + k])
            lhs = jnp.concatenate(rows, axis=0)
            for acc, (x, h) in zip(accs, columns):
                got = jnp.dot(lhs, x[pl.ds(base, tile), h:h + PART], preferred_element_type=jnp.float32)
                got = got.astype(jnp.bfloat16).astype(jnp.float32)
                for k in range(BLOCK):
                    acc[places[k]] += got[k * UNIT:(k + 1) * UNIT, :]

    half = STEP // 2
    halves = lax.div(table[1, table.shape[1] - 1] + half - 1, half)
    steps = lax.div(halves, 2)

    def step(i, carry):
        blocks(i * STEP, STEP)
        return carry

    def last(i, carry):
        blocks(steps * STEP, half)
        return carry

    lax.fori_loop(0, steps, step, 0)
    lax.fori_loop(0, lax.rem(halves, 2), last, 0)


def gathered_sums(per, n, table, tbuf, xo, xp):
    width = xo.shape[1]
    tile = tbuf.shape[2]
    vmem = pl.BlockSpec(memory_space=pltpu.VMEM)
    flops = 2 * tbuf.shape[0] * UNIT * tile * 2 * width
    parts = 2 * width // PART
    sums = jax.ShapeDtypeStruct((n * per + 1, UNIT, PART), jnp.float32)
    return pl.pallas_call(
        tiles_kernel,
        out_shape=[sums] * parts,
        in_specs=[vmem] * 4,
        out_specs=[vmem] * parts,
        scratch_shapes=[
            pltpu.VMEM((UNIT + 1, UNIT, tile), jnp.bfloat16),
            pltpu.SMEM(table.shape, jnp.int32),
            pltpu.SemaphoreType.DMA,
        ],
        compiler_params=pltpu.CompilerParams(vmem_limit_bytes=(12 << 20) + sums.size * 4 * parts),
        cost_estimate=pl.CostEstimate(flops=flops, bytes_accessed=8 << 20, transcendentals=0),
        name="gathered_sums",
    )(table, tbuf, xo, xp)


def weigh(accs, weights, first, count, out):
    size = min(256, count)

    def piece(r, carry):
        at = r * size if isinstance(r, int) else pl.multiple_of(r * size, size)
        got = jnp.zeros((size, out.shape[1]), jnp.float32)
        for i, acc in enumerate(accs):
            w, h = weights[i * PART // weights[0].shape[0]], i * PART % weights[0].shape[0]
            value = acc[pl.ds(first // UNIT + r * (size // UNIT), size // UNIT)].reshape(size, PART)
            high = value.astype(jnp.bfloat16)
            low = (value - high.astype(jnp.float32)).astype(jnp.bfloat16)
            got = got + jnp.dot(high, w[h:h + PART, :], preferred_element_type=jnp.float32)
            got = got + jnp.dot(low, w[h:h + PART, :], preferred_element_type=jnp.float32)
        out[pl.ds(at, size), :] = got
        return carry

    if count == size:
        piece(0, 0)
    else:
        lax.fori_loop(0, count // size, piece, 0)


def sent_kernel(ks, slots, rows, parts, wo, wp, *refs):
    accs, outs, scratch = refs[:parts], refs[parts:parts + len(ks)], refs[parts + len(ks):]
    for i, k in enumerate(ks):
        sums, tail = scratch[2 * i:2 * i + 2]
        weigh(accs, (wo, wp), k * slots * rows, slots * rows, sums)
        write_coded(outs[i], tail, slots, rows, lambda s: sums[s * rows:(s + 1) * rows, :])


def sent_terms(ks, slots, rows, accs, wo, wp):
    hidden = wo.shape[1]
    vmem = pl.BlockSpec(memory_space=pltpu.VMEM)
    coded = jax.ShapeDtypeStruct((slots * rows + tail_rows(slots), hidden), jnp.int16)
    return pl.pallas_call(
        functools.partial(sent_kernel, ks, slots, rows, len(accs)),
        out_shape=[coded] * len(ks),
        in_specs=[vmem] * (2 + len(accs)),
        out_specs=[vmem] * len(ks),
        scratch_shapes=[
            pltpu.VMEM((slots * rows, hidden), jnp.float32),
            pltpu.VMEM((tail_rows(slots), hidden), jnp.float32),
        ] * len(ks),
        compiler_params=pltpu.CompilerParams(vmem_limit_bytes=(20 << 20) + accs[0].size * 4 * len(accs)),
        cost_estimate=pl.CostEstimate(
            flops=4 * len(ks) * slots * rows * PART * len(accs) * hidden, bytes_accessed=2 << 20, transcendentals=0),
        name="sent_terms",
    )(wo, wp, *accs)


def own_kernel(chunk, per, groups, parts, ids, wo, wp, xo, so, *refs):
    accs, (out, theirs, terms) = refs[:parts], refs[parts:]
    weigh(accs, (wo, wp), 0, out.shape[0], out)
    terms[...] = jnp.dot(xo[:groups * UNIT, :], so[...], preferred_element_type=jnp.float32)
    for j in range(per):
        here = slice(j * UNIT, (j + 1) * UNIT)
        at = pl.multiple_of(group_of(ids[0], chunk * per + j, groups) * UNIT, UNIT)
        out[here, :] += terms[pl.ds(at, UNIT), :]
        at = pl.multiple_of(group_of(1 - ids[0], chunk * per + j, groups) * UNIT, UNIT)
        theirs[here, :] = terms[pl.ds(at, UNIT), :]


def own_terms(chunk, per, groups, slots, ids, accs, wo, wp, xo, so):
    hidden = wo.shape[1]
    rows = per * UNIT
    smem = pl.BlockSpec(memory_space=pltpu.SMEM)
    vmem = pl.BlockSpec(memory_space=pltpu.VMEM)
    return pl.pallas_call(
        functools.partial(own_kernel, chunk, per, groups, len(accs)),
        out_shape=[
            jax.ShapeDtypeStruct((slots * rows, hidden), jnp.float32),
            jax.ShapeDtypeStruct((rows, hidden), jnp.float32),
        ],
        in_specs=[smem] + [vmem] * (4 + len(accs)),
        out_specs=[vmem] * 2,
        scratch_shapes=[pltpu.VMEM((groups * UNIT, hidden), jnp.float32)],
        compiler_params=pltpu.CompilerParams(vmem_limit_bytes=(12 << 20) + accs[0].size * 4 * len(accs)),
        cost_estimate=pl.CostEstimate(
            flops=4 * slots * rows * PART * len(accs) * hidden, bytes_accessed=2 << 20, transcendentals=0),
        name="own_terms",
    )(ids, wo, wp, xo, so, *accs)


def combine_kernel(slots, rows, ways, own, *refs):
    parts = len(refs) - ways - 1
    coded, outs, tail = refs[:parts], refs[parts:parts + ways], refs[parts + ways]
    values = [read_coded(a, slots, rows) for a in coded]

    def total(s):
        got = own[s * rows:(s + 1) * rows, :]
        for value in values:
            got = got + value(s)
        return got

    for i in range(slots // ways):
        outs[0][i * rows:(i + 1) * rows, :] = total(i * ways)
    for k in range(1, ways):
        write_coded(outs[k], tail, slots // ways, rows, lambda s: total(s * ways + k))


def combine(slots, rows, ways, own, coded):
    width = own.shape[1]
    left = slots // ways
    vmem = pl.BlockSpec(memory_space=pltpu.VMEM)
    out = jax.ShapeDtypeStruct((left * rows + tail_rows(left), width), jnp.int16)
    return pl.pallas_call(
        functools.partial(combine_kernel, slots, rows, ways),
        out_shape=[jax.ShapeDtypeStruct((left * rows, width), jnp.float32)] + [out] * (ways - 1),
        in_specs=[vmem] * (1 + len(coded)),
        out_specs=[vmem] * ways,
        scratch_shapes=[pltpu.VMEM((tail_rows(left), width), jnp.float32)],
        compiler_params=pltpu.CompilerParams(vmem_limit_bytes=32 * 1024 * 1024),
        name="combine",
    )(own, *coded)


def hidden_kernel(chunks, parts, rows, *refs):
    out = refs[chunks * parts + 1]
    for c in range(chunks):
        own, self, coded = refs[c * parts], refs[c * parts + 1], refs[c * parts + 2:(c + 1) * parts]
        total = own[:rows, :] + self[...]
        for a in coded:
            total = total + read_coded(a, 1, rows)(0)
        out[c * rows:(c + 1) * rows, :] = jnp.maximum(total, 0.0).astype(jnp.bfloat16)


def hidden_rows(chunk_parts, rows, sel):
    chunks, parts = len(chunk_parts), len(chunk_parts[0])
    width = chunk_parts[0][0].shape[1]
    vmem = pl.BlockSpec(memory_space=pltpu.VMEM)
    flat = [a for part in chunk_parts for a in part]
    return pl.pallas_call(
        functools.partial(hidden_kernel, chunks, parts, rows),
        out_shape=jax.ShapeDtypeStruct((chunks * rows, width), jnp.bfloat16),
        in_specs=[vmem] * (len(flat) + 1),
        out_specs=vmem,
        compiler_params=pltpu.CompilerParams(vmem_limit_bytes=32 * 1024 * 1024),
        name="hidden_rows",
    )(*flat, sel)


def send_kernel(own, other, sel, send):
    both = jnp.concatenate([own[...], other[...]], axis=0)
    send[...] = jnp.dot(sel[...], both, preferred_element_type=jnp.float32).astype(jnp.bfloat16)


def rows_to_send(own, other, sel):
    vmem = pl.BlockSpec(memory_space=pltpu.VMEM)
    return pl.pallas_call(
        send_kernel,
        out_shape=jax.ShapeDtypeStruct((sel.shape[0], own.shape[1]), jnp.bfloat16),
        in_specs=[vmem] * 3,
        out_specs=vmem,
        compiler_params=pltpu.CompilerParams(vmem_limit_bytes=32 * 1024 * 1024),
        name="rows_to_send",
    )(own, other, sel)


def logits_kernel(own, other, received, front, adj_received, w_self, w_neigh, out):
    rows = out.shape[0]
    both = jnp.concatenate([own[...], other[...]], axis=0)
    local = jnp.dot(front[...], both, preferred_element_type=jnp.float32)
    mean = local[:rows, :] + jnp.dot(adj_received[...], received[...], preferred_element_type=jnp.float32)
    dims = (((1,), (1,)), ((), ()))
    got = lax.dot_general(local[rows:, :].astype(jnp.bfloat16), w_self[...], dims, preferred_element_type=jnp.float32)
    got = got + lax.dot_general(mean.astype(jnp.bfloat16), w_neigh[...], dims, preferred_element_type=jnp.float32)
    out[...] = got


def logits_of(own, other, received, front, adj_received, w_self, w_neigh):
    vmem = pl.BlockSpec(memory_space=pltpu.VMEM)
    return pl.pallas_call(
        logits_kernel,
        out_shape=jax.ShapeDtypeStruct((adj_received.shape[0], w_self.shape[1]), jnp.float32),
        in_specs=[vmem] * 7,
        out_specs=vmem,
        compiler_params=pltpu.CompilerParams(vmem_limit_bytes=32 * 1024 * 1024),
        name="logits",
    )(own, other, received, front, adj_received, w_self.T, w_neigh.T)


def exchange(parts, stride, n, places):
    got = [parts[0]]
    for k in places:
        got.append(lax.ppermute(parts[k], "dom", [(i, i ^ (k * stride)) for i in range(n)]))
    return got


def body(
    features,
    tile_weight,
    tile_dst,
    tile_src,
    tile_rows,
    w_self1,
    neighbour_weight_first,
    send_list,
    send_count,
    adj_two,
    w_self2,
    w_neigh2,
):
    n = lax.axis_size("dom")
    tile = tile_weight.shape[1]
    groups = tile // UNIT
    per = groups // 2 // CHUNKS
    bits = n.bit_length() - 1
    assert n == 1 << bits and bits >= 2
    radices = [2] * (bits // 2) + [1] * (bits % 2)
    ids = jnp.stack([lax.axis_index("feat"), lax.axis_index("dom")]).astype(jnp.int32)
    swap = [(0, 1), (1, 0)]
    xp = lax.ppermute(features, "feat", swap)
    wp = lax.ppermute(neighbour_weight_first, "feat", swap)
    tw = tile_weight.reshape(tile_weight.shape[0], groups, UNIT, tile)
    planned = plan(
        CHUNKS, per, n, 4, ids, tile_src, tile_rows, tile_dst, tw, features,
    )
    tables, tbufs, xo = planned[:CHUNKS], planned[CHUNKS:2 * CHUNKS], planned[2 * CHUNKS]
    wo, so = neighbour_weight_first, w_self1
    done = []
    for chunk in range(CHUNKS):
        accs = gathered_sums(per, n, tables[chunk], tbufs[chunk], xo, xp)
        slots, rows = n // 4, per * UNIT
        parts = {}
        (parts[3],) = sent_terms((3,), slots, rows, accs, wo, wp)
        parts[2], parts[1] = sent_terms((2, 1), slots, rows, accs, wo, wp)
        parts[0], theirs = own_terms(chunk, per, groups, slots, ids, accs, wo, wp, xo, so)
        self = lax.ppermute(theirs, "feat", swap)
        got = exchange(parts, 1, n, (1, 2, 3))
        stride = 4
        for radix in radices[1:]:
            ways = 1 << radix
            parts = combine(n // stride, per * UNIT, ways, got[0], got[1:])
            got = exchange(parts, stride, n, (2, 3, 1) if ways == 4 else (1,))
            stride *= ways
        done.append([got[0], self] + got[1:])
    sel, front, adj_received = selection(groups, ids, send_list, send_count, adj_two)
    own = hidden_rows(done, per * UNIT, sel)
    other = lax.ppermute(own, "feat", swap)
    send = rows_to_send(own, other, sel)
    received = lax.all_to_all(send, "dom", 0, 0, axis_index_groups=[group_order(n)], tiled=True)
    return logits_of(own, other, received, front, adj_received, w_self2, w_neigh2)


def solution(mesh):
    in_specs = (
        P("dom", "feat"),
        P("dom", None, None),
        P("dom"),
        P("dom"),
        P("dom"),
        P("feat", None),
        P("feat", None),
        P(),
        P(),
        P("dom", None),
        P(),
        P(),
    )
    out_specs = P("dom", None)
    return jax.shard_map(body, mesh=mesh, in_specs=in_specs, out_specs=out_specs, check_vma=False)
```
